32 devices in a mesh: seq: 8 (over z, x), group: 4 (over y, core).
Axes of the slice: x: 2, y: 2, z: 4, core: 2. Of those that a mesh axis runs over, the one named last changes fastest.
Arguments:
- tokens: bfloat16 [4, 4096, 768], P('group', 'seq'), may hold values from -6 to 6
- cotangent: bfloat16 [4, 4096, 768], P('group', 'seq'), may hold values from -6 to 6
- skip_table: int32 [4, 16, 16], P('group'), may hold values from 0 to 1, as said below
- gain_attn: float32 [768], replicated, may hold values from 0.5 to 1.5
- w_attn: bfloat16 [768, 3072], replicated, may hold values from -0.21875 to 0.21875
- w_heads: bfloat16 [768, 36], replicated, may hold values from -0.21875 to 0.21875
- forget_bias: float32 [12], replicated, may hold values from 3 to 10
- query_gain: float32 [768], replicated, may hold values from 0.1 to 1.9
- key_gain: float32 [768], replicated, may hold values from 0.1 to 1.9
- w_out: bfloat16 [768, 768], replicated, may hold values from -0.875 to 0.875
- gain_ffn: float32 [768], replicated, may hold values from 0.4 to 1.6
- w_gate_up: bfloat16 [768, 4096], replicated, may hold values from -0.21875 to 0.21875
- w_down: bfloat16 [2048, 768], replicated, may hold values from -0.125 to 0.125
Outputs:
- activations: bfloat16 [4, 4096, 768], P('group', 'seq')
- grad_tokens: float32 [4, 4096, 768], P('group', 'seq')
- grad_gain_attn: float32 [768], replicated
- grad_w_attn: float32 [768, 3072], replicated
- grad_w_heads: float32 [768, 36], replicated
- grad_forget_bias: float32 [12], replicated
- grad_query_gain: float32 [768], replicated
- grad_key_gain: float32 [768], replicated
- grad_w_out: float32 [768, 768], replicated
- grad_gain_ffn: float32 [768], replicated
- grad_w_gate_up: float32 [768, 4096], replicated
- grad_w_down: float32 [2048, 768], replicated
The draws below stay inside these ranges and needn't reach their ends.
Inputs may be any that keep to these rules, and one draw needn't show every extreme that they name: `skip_table`: 1 marks a key block that a query block drops; only key blocks two or more before the query block are dropped, and the last query block of every group drops none.
All inputs are finite; a program needn't handle non-finite values.
Results may differ from the reference program's by a relative error of at most 0.019.
Values may be sent and summed in bfloat16 or wider, within the bound.
A program may use at most 384 MiB of HBM per device.

```python
import jax
import jax.numpy as jnp
from jax import lax

D = 768
HEADS = 12
HDIM = 64
FF = 2048
BLK = 256
GROUPS = 4
NBLK = 16
SEQLEN = 4096
N_SEQ = 8


def draw_skip_table(key, part):
    key = jax.random.fold_in(key, 7)
    coins = jax.random.randint(key, (GROUPS, NBLK, NBLK), 0, 10)
    row_ids = lax.broadcasted_iota(jnp.int32, (GROUPS, NBLK, NBLK), 1)
    column_ids = lax.broadcasted_iota(jnp.int32, (GROUPS, NBLK, NBLK), 2)
    dropped = (coins < 3) & (column_ids <= row_ids - 2) & (row_ids < NBLK - 1)
    return jnp.where(dropped, 1, 0).astype(jnp.int32)


def levels(stream_key, shape, pieces, least, top_value):
    loudness, own = 1.0, jax.random.fold_in(stream_key, 6)
    for dim, shards_of in pieces:
        steps = jnp.exp(jax.random.uniform(jax.random.fold_in(own, dim), (shards_of,), jnp.float32, least / len(pieces), top_value / len(pieces)))
        loudness = loudness * jnp.repeat(steps, shape[dim] // shards_of).reshape([-1 if axis == dim else 1 for axis in range(len(shape))])
    return loudness


def noise(key, dims, scale, limit, pieces=(), kind=jnp.bfloat16):
    factor_of = levels(key, dims, pieces, -0.22, 0.18) if pieces else 1.0
    entries = jax.random.normal(key, dims, jnp.float32) * scale * factor_of
    return jnp.minimum(jnp.maximum(entries, -limit), limit).astype(kind)


def setup_inputs(seed: int = 0) -> dict:
    splits = jax.random.split(jax.random.key(seed), 14)
    return {
        "tokens": noise(splits[0], (GROUPS, SEQLEN, D), 1.0, 6.0, ((0, 4), (1, 8))),
        "cotangent": noise(splits[1], (GROUPS, SEQLEN, D), 1.0, 6.0, ((0, 4), (1, 8))),
        "skip_table": draw_skip_table(jax.random.fold_in(splits[13], 71), 0),
        "gain_attn": jnp.clip(1.0 + 0.1 * jax.random.normal(splits[3], (D,), jnp.float32), 0.5, 1.5),
        "w_attn": noise(splits[4], (D, 4 * D), D ** -0.5, 0.21875),
        "w_heads": noise(splits[5], (D, 3 * HEADS), D ** -0.5, 0.21875),
        "forget_bias": jnp.clip(jax.random.uniform(splits[6], (HEADS,), jnp.float32, 3.0, 10.0), 3.0, 10.0),
        "query_gain": jnp.clip(1.0 + 0.18 * jax.random.normal(splits[7], (D,), jnp.float32), 0.1, 1.9),
        "key_gain": jnp.clip(1.0 + 0.18 * jax.random.normal(splits[8], (D,), jnp.float32), 0.1, 1.9),
        "w_out": noise(splits[9], (D, D), (D // 16) ** -0.5, 0.875),
        "gain_ffn": jnp.clip(1.0 + 0.12 * jax.random.normal(splits[10], (D,), jnp.float32), 0.4, 1.6),
        "w_gate_up": noise(splits[11], (D, 2 * FF), D ** -0.5, 0.21875),
        "w_down": noise(splits[12], (FF, D), FF ** -0.5, 0.125),
    }


@jax.custom_vjp
def low(v):
    return lax.optimization_barrier(v.astype(jnp.bfloat16)).astype(jnp.float32)

@jax.custom_vjp
def low_back(v):
    return v

def low_keep(v):
    return (low(v), None)

def low_pass(kept, grad):
    return (grad,)

def back_keep(v):
    return (v, None)

def back_low(kept, grad):
    return (low(grad),)
low.defvjp(low_keep, low_pass)
low_back.defvjp(back_keep, back_low)
NEG = -1e+30
EPS = 1e-06

def product(left, right):
    return jnp.dot(left, right, precision=lax.Precision.HIGHEST, preferred_element_type=jnp.float32)

def rms_scale(values, gains):
    inverse = lax.rsqrt(lax.optimization_barrier(jnp.mean(values * values, axis=-1, keepdims=True)) + EPS)
    return values * inverse * gains

def head_scale(values, gains):
    shaped = values.reshape(values.shape[0], HEADS, HDIM)
    inverse = lax.rsqrt(lax.optimization_barrier(jnp.mean(shaped * shaped, axis=-1, keepdims=True)) + EPS)
    return (shaped * inverse).reshape(values.shape) * gains

def attend(queries, keys, values, cum_forget, pruning):
    length = queries.shape[0]
    query_rows = min(512, length)
    key_pos = jnp.arange(length, dtype=jnp.int32)
    key_heads = keys.reshape(length, HEADS, HDIM)
    value_heads = values.reshape(length, HEADS, HDIM)
    score_scale = HDIM ** (-0.5)

    def one_block(block_item):
        query_tile, cum_tile, start = block_item
        query_pos = start + jnp.arange(query_rows, dtype=jnp.int32)
        scores = jnp.einsum('qhd,khd->hqk', query_tile, key_heads, precision=lax.Precision.HIGHEST) * score_scale
        scores = scores + cum_tile.T[:, :, None] - cum_forget.T[:, None, :]
        scores = low_back(scores)
        dropped = pruning[query_pos // BLK][:, key_pos // BLK]
        allowed = (key_pos[None, :] <= query_pos[:, None]) & (dropped == 0)
        weights = low(jax.nn.softmax(jnp.where(allowed[None], scores, NEG), axis=-1))
        mixed = jnp.einsum('hqk,khd->qhd', weights, value_heads, precision=lax.Precision.HIGHEST)
        return mixed.reshape(query_rows, D)
    starts = jnp.arange(0, length, query_rows, dtype=jnp.int32)
    mixed_all = lax.map(jax.checkpoint(one_block), (queries.reshape(-1, query_rows, HEADS, HDIM), cum_forget.reshape(-1, query_rows, HEADS), starts))
    return low_back(mixed_all.reshape(length, D))

def group_forward(inputs, pruning, gain_attn, w_attn, w_heads, forget_bias, query_gain, key_gain, w_out, gain_ffn, w_gate_up, w_down):
    h_first = low(rms_scale(inputs, gain_attn))
    projected = low_back(product(h_first, w_attn))
    head_logits = low_back(product(h_first, w_heads))
    kv_raw = projected[:, D:3 * D]
    before = jnp.concatenate([jnp.zeros((1, 2 * D), jnp.float32), kv_raw[:-1]], 0)
    shift_rate = jnp.repeat(jax.nn.sigmoid(head_logits[:, HEADS:]), HDIM, axis=1)
    kv_mixed = kv_raw + shift_rate * (before - kv_raw)
    queries = low(head_scale(projected[:, :D], query_gain))
    keys = low(head_scale(kv_mixed[:, :D], key_gain))
    values = low(kv_mixed[:, D:])
    cum_forget = jnp.cumsum(jax.nn.log_sigmoid(head_logits[:, :HEADS] + forget_bias), axis=0)
    mixed = attend(queries, keys, values, cum_forget, pruning)
    gated = low(jax.nn.sigmoid(projected[:, 3 * D:]) * mixed)
    resid = inputs + low_back(product(gated, w_out))
    h_second = low(rms_scale(resid, gain_ffn))
    gate_up = low_back(product(h_second, w_gate_up))
    hidden = low(jax.nn.silu(gate_up[:, :FF]) * gate_up[:, FF:])
    return resid + low_back(product(hidden, w_down))

def group_order(values):
    shaped = values.reshape(values.shape[0], N_SEQ, 2, BLK, values.shape[-1])
    joined = jnp.concatenate([shaped[:, :, 0], shaped[:, ::-1, 1]], axis=1)
    return joined.reshape(values.shape)

def device_order(values):
    middle = values.shape[1] // 2
    front = values[:, :middle].reshape(values.shape[0], N_SEQ, BLK, values.shape[-1])
    back_part = values[:, middle:].reshape(values.shape[0], N_SEQ, BLK, values.shape[-1])[:, ::-1]
    return jnp.stack([front, back_part], axis=2).reshape(values.shape)

def reference(tokens, cotangent, skip_table, gain_attn, w_attn, w_heads, forget_bias, query_gain, key_gain, w_out, gain_ffn, w_gate_up, w_down):
    params = (gain_attn.astype(jnp.float32), w_attn.astype(jnp.float32), w_heads.astype(jnp.float32), forget_bias.astype(jnp.float32), query_gain.astype(jnp.float32), key_gain.astype(jnp.float32), w_out.astype(jnp.float32), gain_ffn.astype(jnp.float32), w_gate_up.astype(jnp.float32), w_down.astype(jnp.float32))
    inputs = group_order(tokens.astype(jnp.float32))
    incoming = group_order(cotangent.astype(jnp.float32))

    def forward(group_inputs, weights):

        def one_group(group_item):
            return group_forward(group_item[0], group_item[1], *weights)
        return lax.map(jax.checkpoint(one_group), (group_inputs, skip_table))
    outputs, pullback = jax.vjp(forward, inputs, params)
    d_inputs, grads = pullback(incoming)
    return (device_order(outputs).astype(jnp.bfloat16), device_order(d_inputs), grads[0], grads[1], grads[2], grads[3], grads[4], grads[5], grads[6], grads[7], grads[8], grads[9])
```

```python
import functools

import jax
import jax.numpy as jnp
from jax import lax
from jax.experimental import pallas as pl
from jax.experimental.pallas import tpu as pltpu
from jax.sharding import PartitionSpec as P

D, FF = 768, 2048
MESH = pl.DeviceIdType.MESH
ANY = pl.BlockSpec(memory_space=pl.ANY)

HEADS, HDIM, BLK = 12, 64, 256
EPS = 1e-06
LOG2E = 1.4426950408889634
LN2 = 0.6931471805599453
SCORE = HDIM ** -0.5
f32, bf16 = jnp.float32, jnp.bfloat16
UNROLL = 8
UNROLL_BACK = 4
NN = (((1,), (0,)), ((), ()))
NT = (((1,), (1,)), ((), ()))


def mm(a, b, dims=NN):
    return lax.dot_general(a, b, dims, preferred_element_type=f32)


def split3(v):
    hi = v.astype(bf16).astype(f32)
    rest = v - hi
    mid = rest.astype(bf16).astype(f32)
    return hi, mid, rest - mid


def place_of(block, count):
    return jnp.where(block < count, block, 2 * count - 1 - block)


def lanes_of(block, count):
    return pl.ds(pl.multiple_of(jnp.where(block < count, 0, BLK), BLK), BLK)


def first_head(device, count):
    return jnp.minimum(HEADS * device // count, HEADS - 2)


def is_mine(device, slot, place, count):
    chunk = (first_head(device, count) + slot) * count + place
    return (chunk >= HEADS * device) & (chunk < HEADS * device + HEADS)


def list_pairs(skip_ref, pairs_ref, own_ref, device, slot, count, unroll):
    spare = 2 * count

    def row(number, found):
        def column(other, found):
            pairs_ref[found] = number * 1024 + other
            return found + jnp.where(skip_ref[number, other] == 0, 1, 0)

        mine = is_mine(device, slot, place_of(number, count), count)
        own_ref[found[1]] = number
        below = lax.fori_loop(0, jnp.where(mine, number, 0), column, found[0])
        return below, found[1] + jnp.where(mine, 1, 0)

    below, own = lax.fori_loop(0, spare, row, (0, 0))
    for extra in range(unroll):
        pairs_ref[below + extra] = spare * 1024
        own_ref[own + extra] = spare
    return pl.cdiv(below, unroll), pl.cdiv(own, unroll)


def running_sum(values, count, reverse):
    t = lax.broadcasted_iota(jnp.int32, (BLK, BLK), 0)
    p = lax.broadcasted_iota(jnp.int32, (BLK, BLK), 1)
    ones = jnp.where(t >= p if reverse else t <= p, 1.0, 0.0).astype(bf16)
    halves = []
    for half in range(2):
        part = values[:, half * BLK : (half + 1) * BLK]
        halves.append(sum(mm(piece.astype(bf16), ones) for piece in split3(part)))
    edge = 0 if reverse else BLK - 1
    first, last = (jnp.broadcast_to(h[:, edge : edge + 1], (count, 128)) for h in halves)
    rows = lax.broadcasted_iota(jnp.int32, (count, 128), 0)

    def scan(total, down):
        own = total
        step = 1
        while step < count:
            moved = pltpu.roll(total, step if down else count - step, 0)
            total = total + jnp.where(rows >= step if down else rows < count - step, moved, 0.0)
            step *= 2
        return total - own

    if reverse:
        all_last = jnp.sum(last, axis=0, keepdims=True)
        offsets = scan(first, False) + all_last, scan(last, True)
    else:
        all_first = jnp.sum(first, axis=0, keepdims=True)
        offsets = scan(first, True), scan(last, False) + all_first
    return jnp.concatenate([halves[0] + offsets[0][:, :1], halves[1] + offsets[1][:, :1]], 1)


def shifted(current, before):
    lane = lax.broadcasted_iota(jnp.int32, current.shape, 1)
    return jnp.where(lane == 0, pltpu.roll(before, 1, 1), pltpu.roll(current, 1, 1))


def shifted_back(current, after):
    lane = lax.broadcasted_iota(jnp.int32, current.shape, 1)
    return jnp.where(lane == BLK - 1, pltpu.roll(after, BLK - 1, 1), pltpu.roll(current, BLK - 1, 1))


def stack_rows(top, rows, size):
    extra = size if top is None else size - top.shape[0]
    number = lax.broadcasted_iota(jnp.int32, (extra, BLK), 0)
    bottom = jnp.zeros((extra, BLK), f32)
    for i, r in enumerate(rows):
        bottom = jnp.where(number == i, r, bottom)
    return bottom if top is None else jnp.concatenate([top, bottom], 0)


def forward_kernel(count, device_ref, skip_ref, bias_ref, raw_ref, logit_ref, gain_ref,
                   mixed_ref, mixed_full_ref, q_ref, k_ref, kt_ref, vt_ref,
                   cum_ref, acc_ref, pairs_ref, own_ref):
    slot = pl.program_id(0)
    device = device_ref[0]
    blocks = 2 * count
    pair_steps, own_steps = list_pairs(skip_ref, pairs_ref, own_ref, device, slot, count, UNROLL)
    logits = logit_ref[:, 0, :] + bias_ref[slot]
    log_forget = jnp.minimum(logits, 0.0) - jnp.log1p(jnp.exp(-jnp.abs(logits)))
    cum_ref[...] = running_sum(log_forget, count, False) * LOG2E
    gain_q, gain_k = gain_ref[:, 0:1], gain_ref[:, 1:2]

    def prepare(block, carried):
        place, lanes = place_of(block, count), lanes_of(block, count)
        q_raw, k_raw, v_raw = (raw_ref[place, i, :, lanes].astype(f32) for i in range(3))
        cum = cum_ref[pl.ds(place, 1), lanes]
        parts = split3(cum)
        one = jnp.ones_like(cum)
        query = q_raw * lax.rsqrt(jnp.mean(q_raw * q_raw, 0, keepdims=True) + EPS) * (gain_q * (SCORE * LOG2E))
        q_ref[block] = stack_rows(query, (*parts, one, one, one), 128).astype(bf16)
        rate_k = jax.nn.sigmoid(logit_ref[place, 1:2, lanes])
        rate_v = jax.nn.sigmoid(logit_ref[place, 2:3, lanes])
        key = k_raw + rate_k * (shifted(k_raw, carried[0]) - k_raw)
        key = key * lax.rsqrt(jnp.mean(key * key, 0, keepdims=True) + EPS) * gain_k
        value = v_raw + rate_v * (shifted(v_raw, carried[1]) - v_raw)
        k_ref[block] = stack_rows(key, (one, one, one, *(-c for c in parts)), 128).T.astype(bf16)
        kt_ref[block] = stack_rows(key, (one,), 80).astype(bf16)
        vt_ref[block] = stack_rows(value, (one, one, one), 80).astype(bf16)
        return k_raw, v_raw

    zero = jnp.zeros((HDIM, BLK), f32)
    lax.fori_loop(0, blocks, prepare, (zero, zero))
    q_ref[blocks] = jnp.zeros(q_ref.shape[1:], bf16)

    t = lax.broadcasted_iota(jnp.int32, (BLK, BLK), 0)
    p = lax.broadcasted_iota(jnp.int32, (BLK, BLK), 1)

    def together(pairs, diagonal):
        scores = [mm(k_ref[column], q_ref[row]) for row, column in pairs]
        weights = [jnp.exp2(score) for score in scores]
        if diagonal:
            weights = [jnp.where(t <= p, weight, 0.0) for weight in weights]
        weights = [weight.astype(bf16) for weight in weights]
        parts = [mm(vt_ref[column], weight) for (row, column), weight in zip(pairs, weights)]
        for (row, column), part in zip(pairs, parts):
            acc_ref[row] = part if diagonal else acc_ref[row] + part

    def own_rows(step, carried):
        rows = [own_ref[step * UNROLL + i] for i in range(UNROLL)]
        together([(row, jnp.minimum(row, blocks - 1)) for row in rows], True)
        return carried

    def kept_pairs(step, carried):
        codes = [pairs_ref[step * UNROLL + i] for i in range(UNROLL)]
        together([(code >> 10, code & 1023) for code in codes], False)
        return carried

    lax.fori_loop(0, own_steps, own_rows, 0)
    lax.fori_loop(0, pair_steps, kept_pairs, 0)

    def finish(block, carried):
        place, lanes = place_of(block, count), lanes_of(block, count)
        total = acc_ref[block]
        norm = total[HDIM : HDIM + 1]
        mixed = total[:HDIM] * (1.0 / norm)
        mixed_full_ref[block] = mixed
        mixed_ref[place, :, lanes] = mixed.astype(bf16)
        parts = split3(cum_ref[pl.ds(place, 1), lanes] - jnp.log2(norm))
        one = jnp.ones_like(norm)
        q_ref[block, HDIM : HDIM + 16, :] = stack_rows(None, (*parts, one, one, one), 16).astype(bf16)
        return carried

    lax.fori_loop(0, blocks, finish, 0)


def buffers(count):
    return pl.Buffered(1 if count > 8 else 2)


def attend_forward(device, skip, bias, raw, logits, gains):
    count = raw.shape[0]
    blocks = 2 * count
    most = blocks * (blocks - 1) // 2 + UNROLL
    mode = buffers(count)
    by_slot = lambda *shape: pl.BlockSpec((None,) + shape, lambda s, *_: (s,) + (0,) * len(shape), pipeline_mode=mode)
    out = lambda shape, dtype: jax.ShapeDtypeStruct((2,) + shape, dtype)
    return pl.pallas_call(
        functools.partial(forward_kernel, count),
        grid_spec=pltpu.PrefetchScalarGridSpec(
            num_scalar_prefetch=3,
            grid=(2,),
            in_specs=[
                pl.BlockSpec((count, 3, None, HDIM, 2 * BLK), lambda s, *_: (0, 0, s, 0, 0), pipeline_mode=mode),
                pl.BlockSpec((count, None, 8, 2 * BLK), lambda s, *_: (0, s, 0, 0), pipeline_mode=mode),
                by_slot(HDIM, 2),
            ],
            out_specs=[
                by_slot(count, HDIM, 2 * BLK),
                by_slot(blocks, HDIM, BLK),
                by_slot(blocks + 1, 128, BLK),
                by_slot(blocks, BLK, 128),
                by_slot(blocks, 80, BLK),
                by_slot(blocks, 80, BLK),
            ],
            scratch_shapes=[
                pltpu.VMEM((count, 2 * BLK), f32),
                pltpu.VMEM((blocks + 1, 80, BLK), f32),
                pltpu.SMEM((most,), jnp.int32),
                pltpu.SMEM((blocks + UNROLL,), jnp.int32),
            ],
        ),
        out_shape=[
            out((count, HDIM, 2 * BLK), bf16),
            out((blocks, HDIM, BLK), f32),
            out((blocks + 1, 128, BLK), bf16),
            out((blocks, BLK, 128), bf16),
            out((blocks, 80, BLK), bf16),
            out((blocks, 80, BLK), bf16),
        ],
        compiler_params=pltpu.CompilerParams(vmem_limit_bytes=60 * 2**20),
        name="attend_forward",
    )(device, skip, bias, raw, logits, gains)


def norm_back(v, gain, u):
    scale = lax.rsqrt(jnp.mean(v * v, 0, keepdims=True) + EPS)
    hat = v * scale
    gu = gain * u
    return scale * (gu - hat * jnp.mean(hat * gu, 0, keepdims=True)), hat * u


def backward_kernel(count, device_ref, skip_ref, bias_ref, raw_ref, logit_ref, gain_ref, dmixed_ref, mixed_ref,
                    q_ref, k_ref, kt_ref, vt_ref, draw_ref, dlogit_ref, dgain_ref,
                    do_ref, v_ref, cum_ref, dq_ref, dk_ref, dv_ref, pairs_ref, own_ref):
    slot = pl.program_id(0)
    device = device_ref[0]
    blocks = 2 * count
    pair_steps, own_steps = list_pairs(skip_ref, pairs_ref, own_ref, device, slot, count, UNROLL_BACK)
    gain_q, gain_k = gain_ref[:, 0:1], gain_ref[:, 1:2]
    wide = jnp.zeros((128 - 80, BLK), f32)

    def prepare(block, carried):
        place, lanes = place_of(block, count), lanes_of(block, count)
        d_out = dmixed_ref[place, :, lanes].astype(f32)
        delta = jnp.sum(d_out * mixed_ref[block], 0, keepdims=True)
        do_ref[block] = stack_rows(d_out, [-d for d in split3(delta)], 128).astype(bf16)
        v_ref[block] = jnp.concatenate([vt_ref[block].astype(f32), wide], 0).T.astype(bf16)
        dq_ref[block] = jnp.zeros(dq_ref.shape[1:], f32)
        dk_ref[block] = jnp.zeros(dk_ref.shape[1:], f32)
        dv_ref[block] = jnp.zeros(dv_ref.shape[1:], f32)
        return carried

    lax.fori_loop(0, blocks, prepare, 0)
    do_ref[blocks] = jnp.zeros(do_ref.shape[1:], bf16)
    dq_ref[blocks] = jnp.zeros(dq_ref.shape[1:], f32)

    t = lax.broadcasted_iota(jnp.int32, (BLK, BLK), 0)
    p = lax.broadcasted_iota(jnp.int32, (BLK, BLK), 1)

    def together(pairs, diagonal):
        scores = [mm(k_ref[column], q_ref[row]) for row, column in pairs]
        weights = [jnp.exp2(score) for score in scores]
        if diagonal:
            weights = [jnp.where(t <= p, weight, 0.0) for weight in weights]
        d_weights = [mm(v_ref[column], do_ref[row]) for row, column in pairs]
        low_weights = [weight.astype(bf16) for weight in weights]
        d_scores = [(weight * d_weight).astype(bf16) for weight, d_weight in zip(weights, d_weights)]
        parts = [mm(do_ref[row, :HDIM], weight, NT) for (row, _), weight in zip(pairs, low_weights)]
        for (_, column), part in zip(pairs, parts):
            dv_ref[column] += part
        parts = [mm(kt_ref[column], d_score) for (_, column), d_score in zip(pairs, d_scores)]
        for (row, _), part in zip(pairs, parts):
            dq_ref[row] += part
        parts = [mm(q_ref[row, :80], d_score, NT) for (row, _), d_score in zip(pairs, d_scores)]
        for (_, column), part in zip(pairs, parts):
            dk_ref[column] += part

    def own_rows(step, carried):
        rows = [own_ref[step * UNROLL_BACK + i] for i in range(UNROLL_BACK)]
        together([(row, jnp.minimum(row, blocks - 1)) for row in rows], True)
        return carried

    def kept_pairs(step, carried):
        codes = [pairs_ref[step * UNROLL_BACK + i] for i in range(UNROLL_BACK)]
        together([(code >> 10, code & 1023) for code in codes], False)
        return carried

    lax.fori_loop(0, own_steps, own_rows, 0)
    lax.fori_loop(0, pair_steps, kept_pairs, 0)

    def finish(step, carried):
        next_k, next_v, sum_q, sum_k = carried
        block = blocks - 1 - step
        place, lanes = place_of(block, count), lanes_of(block, count)
        earlier = jnp.maximum(block - 1, 0)
        place_before, lanes_before = place_of(earlier, count), lanes_of(earlier, count)
        exists = jnp.where(block > 0, 1.0, 0.0)
        q_raw, k_raw, v_raw = (raw_ref[place, i, :, lanes].astype(f32) for i in range(3))
        k_step = shifted(k_raw, raw_ref[place_before, 1, :, lanes_before].astype(f32) * exists) - k_raw
        v_step = shifted(v_raw, raw_ref[place_before, 2, :, lanes_before].astype(f32) * exists) - v_raw
        rate_k = jax.nn.sigmoid(logit_ref[place, 1:2, lanes])
        rate_v = jax.nn.sigmoid(logit_ref[place, 2:3, lanes])
        dq, dk, dv = dq_ref[block], dk_ref[block], dv_ref[block]
        dq_raw, part_q = norm_back(q_raw, gain_q, dq[:HDIM] * SCORE)
        dk_mixed, part_k = norm_back(k_raw + rate_k * k_step, gain_k, dk[:HDIM] * LN2)
        send_k, send_v = rate_k * dk_mixed, rate_v * dv
        draw_ref[place, 0, :, lanes] = dq_raw.astype(bf16)
        draw_ref[place, 1, :, lanes] = (dk_mixed - send_k + shifted_back(send_k, next_k)).astype(bf16)
        draw_ref[place, 2, :, lanes] = (dv - send_v + shifted_back(send_v, next_v)).astype(bf16)
        dlogit_ref[place, 1:2, lanes] = (1.0 - rate_k) * jnp.sum(k_step * send_k, 0, keepdims=True)
        dlogit_ref[place, 2:3, lanes] = (1.0 - rate_v) * jnp.sum(v_step * send_v, 0, keepdims=True)
        cum_ref[pl.ds(place, 1), lanes] = dq[HDIM : HDIM + 1] - dk[HDIM + 3 : HDIM + 4]
        part_q = jnp.where(is_mine(device, slot, place, count), part_q, 0.0)
        return send_k, send_v, sum_q + part_q, sum_k + part_k

    zero = jnp.zeros((HDIM, BLK), f32)
    _, _, sum_q, sum_k = lax.fori_loop(0, blocks, finish, (zero, zero, zero, zero))
    dgain_ref[:, 0:1] = jnp.sum(sum_q, 1, keepdims=True)
    dgain_ref[:, 1:2] = jnp.sum(sum_k, 1, keepdims=True)
    d_log = running_sum(cum_ref[...], count, True)
    dlogit_ref[:, 0, :] = d_log * jax.nn.sigmoid(-(logit_ref[:, 0, :] + bias_ref[slot]))
    dlogit_ref[:, 3:, :] = jnp.zeros((count, 5, 2 * BLK), f32)


def attend_backward(device, skip, bias, raw, logits, gains, dmixed, mixed, q, k, kt, vt):
    count = raw.shape[0]
    blocks = 2 * count
    most = blocks * (blocks - 1) // 2 + UNROLL_BACK
    mode = buffers(count)
    by_slot = lambda *shape: pl.BlockSpec((None,) + shape, lambda s, *_: (s,) + (0,) * len(shape), pipeline_mode=mode)
    raw_spec = pl.BlockSpec((count, 3, None, HDIM, 2 * BLK), lambda s, *_: (0, 0, s, 0, 0), pipeline_mode=mode)
    place_spec = lambda rows: pl.BlockSpec((count, None, rows, 2 * BLK), lambda s, *_: (0, s, 0, 0), pipeline_mode=mode)
    return pl.pallas_call(
        functools.partial(backward_kernel, count),
        grid_spec=pltpu.PrefetchScalarGridSpec(
            num_scalar_prefetch=3,
            grid=(2,),
            in_specs=[
                raw_spec,
                place_spec(8),
                by_slot(HDIM, 2),
                place_spec(HDIM),
                by_slot(blocks, HDIM, BLK),
                by_slot(blocks + 1, 128, BLK),
                by_slot(blocks, BLK, 128),
                by_slot(blocks, 80, BLK),
                by_slot(blocks, 80, BLK),
            ],
            out_specs=[raw_spec, place_spec(8), by_slot(HDIM, 2)],
            scratch_shapes=[
                pltpu.VMEM((blocks + 1, 128, BLK), bf16),
                pltpu.VMEM((blocks, BLK, 128), bf16),
                pltpu.VMEM((count, 2 * BLK), f32),
                pltpu.VMEM((blocks + 1, 80, BLK), f32),
                pltpu.VMEM((blocks, 80, BLK), f32),
                pltpu.VMEM((blocks, HDIM, BLK), f32),
                pltpu.SMEM((most,), jnp.int32),
                pltpu.SMEM((blocks + UNROLL_BACK,), jnp.int32),
            ],
        ),
        out_shape=[
            jax.ShapeDtypeStruct(raw.shape, bf16),
            jax.ShapeDtypeStruct(logits.shape, f32),
            jax.ShapeDtypeStruct(gains.shape, f32),
        ],
        compiler_params=pltpu.CompilerParams(vmem_limit_bytes=60 * 2**20),
        name="attend_backward",
    )(device, skip, bias, raw, logits, gains, dmixed, mixed, q, k, kt, vt)


def holder(head, place, count):
    return (head * count + place) // HEADS


def greet(count):
    me = lax.axis_index("seq")
    barrier = pltpu.get_barrier_semaphore()
    for k in range(1, count):
        peer = lax.rem(me + k, count)
        pl.semaphore_signal(barrier, inc=1, device_id={"seq": peer}, device_id_type=MESH)
    pl.semaphore_wait(barrier, count - 1)
    return me


def far_first(count):
    return sorted(range(1, count), key=lambda k: -min(k, count - k))


def push(src, dst, send, recv, peer):
    return pltpu.make_async_remote_copy(
        src_ref=src, dst_ref=dst, send_sem=send, recv_sem=recv, device_id={"seq": peer}, device_id_type=MESH
    )


def heads_out_kernel(count, x_ref, logit_in, raw_ref, logit_ref, send, recv, local):
    me = greet(count)

    def copies(peer, source, k):
        head = first_head(peer, count)
        items = []
        for slot in range(2):
            items.append((is_mine(peer, slot, me, count), is_mine(me, slot, source, count),
                          push(x_ref.at[0, head + slot], raw_ref.at[me, 0, slot], send.at[k, slot], recv.at[k, slot], peer)))
        items.append((None, None, push(x_ref.at[pl.ds(1, 2), pl.ds(head, 2)], raw_ref.at[me, pl.ds(1, 2)], send.at[k, 2], recv.at[k, 2], peer)))
        items.append((None, None, push(logit_in.at[pl.ds(head, 2)], logit_ref.at[me], send.at[k, 3], recv.at[k, 3], peer)))
        return items

    every = []
    for k in far_first(count):
        items = copies(lax.rem(me + k, count), lax.rem(me + count - k, count), k)
        every.append(items)
        for out, _, copy in items:
            if out is None:
                copy.start()
            else:
                pl.when(out)(copy.start)
    head = first_head(me, count)
    own = [
        pltpu.make_async_copy(x_ref.at[:, pl.ds(head, 2)], raw_ref.at[me], local.at[0]),
        pltpu.make_async_copy(logit_in.at[pl.ds(head, 2)], logit_ref.at[me], local.at[1]),
    ]
    for copy in own:
        copy.start()
    for items in every:
        for out, into, copy in items:
            if out is None:
                copy.wait()
            else:
                pl.when(out)(copy.wait_send)
                pl.when(into)(copy.wait_recv)
    for copy in own:
        copy.wait()


def heads_out(qkv, logits, count):
    return pl.pallas_call(
        functools.partial(heads_out_kernel, count),
        out_shape=[
            jax.ShapeDtypeStruct((count, 3, 2, HDIM, 2 * BLK), bf16),
            jax.ShapeDtypeStruct((count, 2, 8, 2 * BLK), f32),
        ],
        in_specs=[ANY, ANY],
        out_specs=[ANY, ANY],
        scratch_shapes=[pltpu.SemaphoreType.DMA((count, 4)), pltpu.SemaphoreType.DMA((count, 4)), pltpu.SemaphoreType.DMA((2,))],
        compiler_params=pltpu.CompilerParams(collective_id=0, has_side_effects=True),
        name="heads_out",
    )(qkv, logits)


def mixed_back_kernel(count, x_ref, o_ref, send, recv, local):
    me = greet(count)
    first = first_head(me, count)
    started = []
    for k in far_first(count) + [0]:
        peer = lax.rem(me + k, count)
        for slot in range(2):
            mine = is_mine(me, slot, peer, count)
            src, dst = x_ref.at[slot, peer], o_ref.at[first + slot]
            if k:
                copy = push(src, dst, send.at[k, slot], recv.at[first + slot], peer)
            else:
                copy = pltpu.make_async_copy(src, dst, local.at[slot])
            started.append((mine, k, copy))
            pl.when(mine)(copy.start)
    for mine, k, copy in started:
        pl.when(mine)(copy.wait_send if k else copy.wait)
    for head in range(HEADS):
        source = holder(head, me, count)
        copy = push(x_ref.at[0, 0], o_ref.at[head], send.at[0, 0], recv.at[head], lax.rem(me + 1, count))
        pl.when(source != me)(copy.wait_recv)


def mixed_back(mixed, count):
    return pl.pallas_call(
        functools.partial(mixed_back_kernel, count),
        out_shape=jax.ShapeDtypeStruct((HEADS, HDIM, 2 * BLK), bf16),
        in_specs=[ANY],
        out_specs=ANY,
        scratch_shapes=[pltpu.SemaphoreType.DMA((count, 2)), pltpu.SemaphoreType.DMA((HEADS,)), pltpu.SemaphoreType.DMA((2,))],
        compiler_params=pltpu.CompilerParams(collective_id=1, has_side_effects=True),
        name="mixed_back",
    )(mixed)


def grads_out_kernel(count, x_ref, o_ref, send, recv, local):
    me = greet(count)
    started = []
    for head in range(HEADS):
        peer = holder(head, me, count)
        slot = head - first_head(peer, count)
        away = peer != me
        there = jnp.where(away, peer, lax.rem(me + 1, count))
        copy = push(x_ref.at[head], o_ref.at[me, slot], send.at[head], recv.at[me, slot], there)
        own = pltpu.make_async_copy(x_ref.at[head], o_ref.at[me, slot], local.at[slot])
        pl.when(away)(copy.start)
        pl.when(peer == me)(own.start)
        started.append((away, peer == me, copy, own))
    for away, here, copy, own in started:
        pl.when(away)(copy.wait_send)
        pl.when(here)(own.wait)
    for k in range(1, count):
        source = lax.rem(me + k, count)
        for slot in range(2):
            copy = push(x_ref.at[0], o_ref.at[source, slot], send.at[0], recv.at[source, slot], source)
            pl.when(is_mine(me, slot, source, count))(copy.wait_recv)


def grads_out(d_mixed, count):
    return pl.pallas_call(
        functools.partial(grads_out_kernel, count),
        out_shape=jax.ShapeDtypeStruct((count, 2, HDIM, 2 * BLK), bf16),
        in_specs=[ANY],
        out_specs=ANY,
        scratch_shapes=[pltpu.SemaphoreType.DMA((HEADS,)), pltpu.SemaphoreType.DMA((count, 2)), pltpu.SemaphoreType.DMA((2,))],
        compiler_params=pltpu.CompilerParams(collective_id=2, has_side_effects=True),
        name="grads_out",
    )(d_mixed)


def heads_back_kernel(count, x_ref, logit_in, q_ref, kv_ref, logit_ref, send, recv, recv_q, local):
    me = greet(count)
    first = first_head(me, count)
    started = []
    for k in far_first(count) + [0]:
        peer = lax.rem(me + k, count)
        pairs = [
            (None, x_ref.at[peer, pl.ds(1, 2)], kv_ref.at[me], recv.at[k, 0]),
            (None, logit_in.at[peer], logit_ref.at[me], recv.at[k, 1]),
        ]
        for slot in range(2):
            pairs.append((is_mine(me, slot, peer, count), x_ref.at[peer, 0, slot], q_ref.at[first + slot], recv_q.at[first + slot]))
        for i, (mine, src, dst, sem) in enumerate(pairs):
            copy = push(src, dst, send.at[k, i], sem, peer) if k else pltpu.make_async_copy(src, dst, local.at[i])
            started.append((mine, k, copy))
            if mine is None:
                copy.start()
            else:
                pl.when(mine)(copy.start)
    for mine, k, copy in started:
        if mine is not None:
            pl.when(mine)(copy.wait_send if k else copy.wait)
        else:
            copy.wait()
    for head in range(HEADS):
        source = holder(head, me, count)
        copy = push(x_ref.at[0, 0, 0], q_ref.at[head], send.at[0, 0], recv_q.at[head], lax.rem(me + 1, count))
        pl.when(source != me)(copy.wait_recv)


def heads_back(d_raw, d_logits, count):
    return pl.pallas_call(
        functools.partial(heads_back_kernel, count),
        out_shape=[
            jax.ShapeDtypeStruct((HEADS, HDIM, 2 * BLK), bf16),
            jax.ShapeDtypeStruct((count, 2, 2, HDIM, 2 * BLK), bf16),
            jax.ShapeDtypeStruct((count, 2, 8, 2 * BLK), f32),
        ],
        in_specs=[ANY, ANY],
        out_specs=[ANY, ANY, ANY],
        scratch_shapes=[
            pltpu.SemaphoreType.DMA((count, 4)),
            pltpu.SemaphoreType.DMA((count, 2)),
            pltpu.SemaphoreType.DMA((HEADS,)),
            pltpu.SemaphoreType.DMA((4,)),
        ],
        compiler_params=pltpu.CompilerParams(collective_id=3, has_side_effects=True),
        name="heads_back",
    )(d_raw, d_logits)


def dot(a, b, i, j):
    return lax.dot_general(a, b, (((i,), (j,)), ((), ())), preferred_element_type=f32)


def rms_scale(values, gains):
    inverse = lax.rsqrt(jnp.mean(values * values, axis=-1, keepdims=True) + EPS)
    return values * inverse * gains


def swiglu(gate_up):
    return jax.nn.silu(gate_up[:, :FF]) * gate_up[:, FF:]


def held_heads(count):
    first = [min(HEADS * d // count, HEADS - 2) for d in range(count)]
    return [
        [(d, h - first[d]) for d in range(h * count // HEADS, ((h + 1) * count - 1) // HEADS + 1)]
        for h in range(HEADS)
    ]


def total(parts):
    return functools.reduce(jnp.add, parts)


def local(tokens, cotangent, skip_table, gain_attn, w_attn, w_heads, forget_bias, query_gain, key_gain,
          w_out, gain_ffn, w_gate_up, w_down):
    count = lax.axis_size("seq")
    me = lax.axis_index("seq")
    rows = tokens.shape[1]
    both = ("seq", "group")
    inputs = tokens[0].astype(f32)
    device = me.astype(jnp.int32)[None]
    head = first_head(me, count)
    skip = skip_table[0]
    gains = jnp.stack([query_gain.reshape(HEADS, HDIM), key_gain.reshape(HEADS, HDIM)], 2)
    gains = lax.dynamic_slice_in_dim(gains, head, 2, 0)
    bias = lax.dynamic_slice_in_dim(forget_bias, head, 2, 0)
    w_small = jnp.pad(w_heads.reshape(D, 3, HEADS).transpose(0, 2, 1), ((0, 0), (0, 0), (0, 5))).reshape(D, HEADS * 8)

    normed_attn, norm_back_attn = jax.vjp(rms_scale, inputs, gain_attn)
    h_first = normed_attn.astype(bf16)
    qkv = dot(w_attn[:, : 3 * D], h_first, 0, 1).astype(bf16).reshape(3, HEADS, HDIM, rows)
    gate_logit = dot(w_attn[:, 3 * D :], h_first, 0, 1)
    logits_here = dot(w_small, h_first, 0, 1).reshape(HEADS, 8, rows)

    raw, logits = heads_out(qkv, logits_here, count)
    mixed_low, mixed, q, k, kt, vt = attend_forward(device, skip, bias, raw, logits, gains)
    attended = mixed_back(mixed_low, count).reshape(D, rows).astype(f32)

    gate_open = jax.nn.sigmoid(gate_logit)
    gated = (gate_open * attended).astype(bf16)
    resid = inputs + dot(gated, w_out, 0, 0)
    normed_ffn, norm_back_ffn = jax.vjp(rms_scale, resid, gain_ffn)
    h_second = normed_ffn.astype(bf16)
    gate_up = dot(h_second, w_gate_up, 1, 0)
    hidden, hidden_back = jax.vjp(swiglu, gate_up)
    hidden_low = hidden.astype(bf16)
    output = resid + dot(hidden_low, w_down, 1, 0)
    d_low = cotangent[0]
    d_output = d_low.astype(f32)
    (d_gate_up,) = hidden_back(dot(d_low, w_down, 1, 1))
    d_gate_low = d_gate_up.astype(bf16)
    d_resid_norm, grad_gain_ffn = norm_back_ffn(dot(d_gate_low, w_gate_up, 1, 1))
    d_resid = d_output + d_resid_norm
    d_branch = d_resid.astype(bf16)
    d_gated = dot(w_out, d_branch, 1, 1)
    d_gate_logit = (d_gated * attended * gate_open * (1.0 - gate_open)).astype(bf16)
    d_mixed = (d_gated * gate_open).astype(bf16).reshape(HEADS, HDIM, rows)

    grad_w_down = dot(hidden_low, d_low, 0, 0).astype(bf16)
    grad_w_gate_up = dot(h_second, d_gate_low, 0, 0).astype(bf16)
    grad_w_out = dot(gated, d_branch, 1, 0).astype(bf16)
    grad_gate = dot(h_first, d_gate_logit, 0, 1).astype(bf16)
    early = lax.psum((grad_w_down, grad_w_gate_up, grad_w_out, grad_gate), both)

    d_mixed_all = grads_out(d_mixed, count)
    d_raw, d_logits, d_gains = attend_backward(device, skip, bias, raw, logits, gains, d_mixed_all, mixed, q, k, kt, vt)
    d_q, d_kv_parts, d_logit_parts = heads_back(d_raw, d_logits, count)

    holders = held_heads(count)
    d_kv = [
        jnp.concatenate([total([d_kv_parts[d, i, s].astype(f32) for d, s in held]) for held in holders], 0).astype(bf16)
        for i in range(2)
    ]
    d_small = jnp.concatenate([total([d_logit_parts[d, s] for d, s in held]) for held in holders], 0)
    d_small_low = d_small.astype(bf16)
    d_projected = jnp.concatenate([d_q.reshape(D, rows), d_kv[0], d_kv[1], d_gate_logit], 0)
    grad_qkv = dot(h_first, d_projected[: 3 * D], 0, 1).astype(bf16)
    grad_small = dot(h_first, d_small_low, 0, 1)
    d_normed = dot(d_projected, w_attn, 0, 1) + dot(d_small_low, w_small, 0, 1)
    d_inputs_norm, grad_gain_attn = norm_back_attn(d_normed)
    d_inputs = d_resid + d_inputs_norm

    grad_bias = jnp.sum(d_small.reshape(HEADS, 8, rows)[:, 0], axis=1)
    placed = jnp.zeros((HEADS, HDIM, 2), f32)
    placed = lax.dynamic_update_slice(placed, d_gains, (head, 0, 0)).reshape(D, 2)
    grad_qkv, early = lax.optimization_barrier((grad_qkv, early))
    late, small = lax.psum((grad_qkv, (grad_small, grad_gain_ffn, grad_gain_attn, grad_bias, placed)), both)
    grad_small, grad_gain_ffn, grad_gain_attn, grad_bias, placed = small
    grad_w_heads = grad_small.reshape(D, HEADS, 8)[:, :, :3].transpose(0, 2, 1).reshape(D, 3 * HEADS)
    grad_w_attn = jnp.concatenate([late, early[3]], 1).astype(f32)
    return (
        output[None].astype(bf16),
        d_inputs[None],
        grad_gain_attn,
        grad_w_attn,
        grad_w_heads,
        grad_bias,
        placed[:, 0],
        placed[:, 1],
        early[2].astype(f32),
        grad_gain_ffn,
        early[1].astype(f32),
        early[0].astype(f32),
    )


def solution(mesh):
    rows = P("group", "seq", None)
    return jax.shard_map(
        local,
        mesh=mesh,
        in_specs=(rows, rows, P("group", None, None)) + (P(),) * 10,
        out_specs=(rows, rows) + (P(),) * 10,
        check_vma=False,
    )
```

```python
import functools

import jax
import jax.numpy as jnp
from jax import lax
from jax.experimental import pallas as pl
from jax.experimental.pallas import tpu as pltpu
from jax.sharding import PartitionSpec as P

D, FF = 768, 2048
MESH = pl.DeviceIdType.MESH
ANY = pl.BlockSpec(memory_space=pl.ANY)

HEADS, HDIM, BLK = 12, 64, 256
EPS = 1e-06
LOG2E = 1.4426950408889634
LN2 = 0.6931471805599453
SCORE = HDIM ** -0.5
f32, bf16 = jnp.float32, jnp.bfloat16
UNROLL = 8
UNROLL_BACK = 4
NN = (((1,), (0,)), ((), ()))
NT = (((1,), (1,)), ((), ()))


def mm(a, b, dims=NN):
    return lax.dot_general(a, b, dims, preferred_element_type=f32)


def split3(v):
    hi = v.astype(bf16).astype(f32)
    rest = v - hi
    mid = rest.astype(bf16).astype(f32)
    return hi, mid, rest - mid


def place_of(block, count):
    return jnp.where(block < count, block, 2 * count - 1 - block)


def lanes_of(block, count):
    return pl.ds(pl.multiple_of(jnp.where(block < count, 0, BLK), BLK), BLK)


def first_head(device, count):
    return jnp.minimum(HEADS * device // count, HEADS - 2)


def is_mine(device, slot, place, count):
    chunk = (first_head(device, count) + slot) * count + place
    return (chunk >= HEADS * device) & (chunk < HEADS * device + HEADS)


def list_pairs(skip_ref, pairs_ref, own_ref, device, slot, count, unroll):
    spare = 2 * count

    def row(number, found):
        def column(other, found):
            pairs_ref[found] = number * 1024 + other
            return found + jnp.where(skip_ref[number, other] == 0, 1, 0)

        mine = is_mine(device, slot, place_of(number, count), count)
        own_ref[found[1]] = number
        below = lax.fori_loop(0, jnp.where(mine, number, 0), column, found[0])
        return below, found[1] + jnp.where(mine, 1, 0)

    below, own = lax.fori_loop(0, spare, row, (0, 0))
    for extra in range(unroll):
        pairs_ref[below + extra] = spare * 1024
        own_ref[own + extra] = spare
    return pl.cdiv(below, unroll), pl.cdiv(own, unroll)


def running_sum(values, count, reverse):
    t = lax.broadcasted_iota(jnp.int32, (BLK, BLK), 0)
    p = lax.broadcasted_iota(jnp.int32, (BLK, BLK), 1)
    ones = jnp.where(t >= p if reverse else t <= p, 1.0, 0.0).astype(bf16)
    halves = []
    for half in range(2):
        part = values[:, half * BLK : (half + 1) * BLK]
        halves.append(sum(mm(piece.astype(bf16), ones) for piece in split3(part)))
    edge = 0 if reverse else BLK - 1
    first, last = (jnp.broadcast_to(h[:, edge : edge + 1], (count, 128)) for h in halves)
    rows = lax.broadcasted_iota(jnp.int32, (count, 128), 0)

    def scan(total, down):
        own = total
        step = 1
        while step < count:
            moved = pltpu.roll(total, step if down else count - step, 0)
            total = total + jnp.where(rows >= step if down else rows < count - step, moved, 0.0)
            step *= 2
        return total - own

    if reverse:
        all_last = jnp.sum(last, axis=0, keepdims=True)
        offsets = scan(first, False) + all_last, scan(last, True)
    else:
        all_first = jnp.sum(first, axis=0, keepdims=True)
        offsets = scan(first, True), scan(last, False) + all_first
    return jnp.concatenate([halves[0] + offsets[0][:, :1], halves[1] + offsets[1][:, :1]], 1)


def shifted(current, before):
    lane = lax.broadcasted_iota(jnp.int32, current.shape, 1)
    return jnp.where(lane == 0, pltpu.roll(before, 1, 1), pltpu.roll(current, 1, 1))


def shifted_back(current, after):
    lane = lax.broadcasted_iota(jnp.int32, current.shape, 1)
    return jnp.where(lane == BLK - 1, pltpu.roll(after, BLK - 1, 1), pltpu.roll(current, BLK - 1, 1))


def stack_rows(top, rows, size):
    extra = size if top is None else size - top.shape[0]
    number = lax.broadcasted_iota(jnp.int32, (extra, BLK), 0)
    bottom = jnp.zeros((extra, BLK), f32)
    for i, r in enumerate(rows):
        bottom = jnp.where(number == i, r, bottom)
    return bottom if top is None else jnp.concatenate([top, bottom], 0)


def forward_kernel(count, device_ref, skip_ref, bias_ref, raw_ref, logit_ref, gain_ref,
                   mixed_ref, mixed_full_ref, q_ref, k_ref, kt_ref, vt_ref,
                   cum_ref, acc_ref, pairs_ref, own_ref):
    slot = pl.program_id(0)
    device = device_ref[0]
    blocks = 2 * count
    pair_steps, own_steps = list_pairs(skip_ref, pairs_ref, own_ref, device, slot, count, UNROLL)
    logits = logit_ref[:, 0, :] + bias_ref[slot]
    log_forget = jnp.minimum(logits, 0.0) - jnp.log1p(jnp.exp(-jnp.abs(logits)))
    cum_ref[...] = running_sum(log_forget, count, False) * LOG2E
    gain_q, gain_k = gain_ref[:, 0:1], gain_ref[:, 1:2]

    def prepare(block, carried):
        place, lanes = place_of(block, count), lanes_of(block, count)
        q_raw, k_raw, v_raw = (raw_ref[place, i, :, lanes].astype(f32) for i in range(3))
        cum = cum_ref[pl.ds(place, 1), lanes]
        parts = split3(cum)
        one = jnp.ones_like(cum)
        query = q_raw * lax.rsqrt(jnp.mean(q_raw * q_raw, 0, keepdims=True) + EPS) * (gain_q * (SCORE * LOG2E))
        q_ref[block] = stack_rows(query, (*parts, one, one, one), 128).astype(bf16)
        rate_k = jax.nn.sigmoid(logit_ref[place, 1:2, lanes])
        rate_v = jax.nn.sigmoid(logit_ref[place, 2:3, lanes])
        key = k_raw + rate_k * (shifted(k_raw, carried[0]) - k_raw)
        key = key * lax.rsqrt(jnp.mean(key * key, 0, keepdims=True) + EPS) * gain_k
        value = v_raw + rate_v * (shifted(v_raw, carried[1]) - v_raw)
        k_ref[block] = stack_rows(key, (one, one, one, *(-c for c in parts)), 128).T.astype(bf16)
        kt_ref[block] = stack_rows(key, (one,), 80).astype(bf16)
        vt_ref[block] = stack_rows(value, (one, one, one), 80).astype(bf16)
        return k_raw, v_raw

    zero = jnp.zeros((HDIM, BLK), f32)
    lax.fori_loop(0, blocks, prepare, (zero, zero))
    q_ref[blocks] = jnp.zeros(q_ref.shape[1:], bf16)

    t = lax.broadcasted_iota(jnp.int32, (BLK, BLK), 0)
    p = lax.broadcasted_iota(jnp.int32, (BLK, BLK), 1)

    def together(pairs, diagonal):
        scores = [mm(k_ref[column], q_ref[row]) for row, column in pairs]
        weights = [jnp.exp2(score) for score in scores]
        if diagonal:
            weights = [jnp.where(t <= p, weight, 0.0) for weight in weights]
        weights = [weight.astype(bf16) for weight in weights]
        parts = [mm(vt_ref[column], weight) for (row, column), weight in zip(pairs, weights)]
        for (row, column), part in zip(pairs, parts):
            acc_ref[row] = part if diagonal else acc_ref[row] + part

    def own_rows(step, carried):
        rows = [own_ref[step * UNROLL + i] for i in range(UNROLL)]
        together([(row, jnp.minimum(row, blocks - 1)) for row in rows], True)
        return carried

    def kept_pairs(step, carried):
        codes = [pairs_ref[step * UNROLL + i] for i in range(UNROLL)]
        together([(code >> 10, code & 1023) for code in codes], False)
        return carried

    lax.fori_loop(0, own_steps, own_rows, 0)
    lax.fori_loop(0, pair_steps, kept_pairs, 0)

    def finish(block, carried):
        place, lanes = place_of(block, count), lanes_of(block, count)
        total = acc_ref[block]
        norm = total[HDIM : HDIM + 1]
        mixed = total[:HDIM] * (1.0 / norm)
        mixed_full_ref[block] = mixed
        mixed_ref[place, :, lanes] = mixed.astype(bf16)
        parts = split3(cum_ref[pl.ds(place, 1), lanes] - jnp.log2(norm))
        one = jnp.ones_like(norm)
        q_ref[block, HDIM : HDIM + 16, :] = stack_rows(None, (*parts, one, one, one), 16).astype(bf16)
        return carried

    lax.fori_loop(0, blocks, finish, 0)


def buffers(count):
    return pl.Buffered(1 if count > 8 else 2)


def attend_forward(device, skip, bias, raw, logits, gains):
    count = raw.shape[0]
    blocks = 2 * count
    most = blocks * (blocks - 1) // 2 + UNROLL
    mode = buffers(count)
    by_slot = lambda *shape: pl.BlockSpec((None,) + shape, lambda s, *_: (s,) + (0,) * len(shape), pipeline_mode=mode)
    out = lambda shape, dtype: jax.ShapeDtypeStruct((2,) + shape, dtype)
    return pl.pallas_call(
        functools.partial(forward_kernel, count),
        grid_spec=pltpu.PrefetchScalarGridSpec(
            num_scalar_prefetch=3,
            grid=(2,),
            in_specs=[
                pl.BlockSpec((count, 3, None, HDIM, 2 * BLK), lambda s, *_: (0, 0, s, 0, 0), pipeline_mode=mode),
                pl.BlockSpec((count, None, 8, 2 * BLK), lambda s, *_: (0, s, 0, 0), pipeline_mode=mode),
                by_slot(HDIM, 2),
            ],
            out_specs=[
                by_slot(count, HDIM, 2 * BLK),
                by_slot(blocks, HDIM, BLK),
                by_slot(blocks + 1, 128, BLK),
                by_slot(blocks, BLK, 128),
                by_slot(blocks, 80, BLK),
                by_slot(blocks, 80, BLK),
            ],
            scratch_shapes=[
                pltpu.VMEM((count, 2 * BLK), f32),
                pltpu.VMEM((blocks + 1, 80, BLK), f32),
                pltpu.SMEM((most,), jnp.int32),
                pltpu.SMEM((blocks + UNROLL,), jnp.int32),
            ],
        ),
        out_shape=[
            out((count, HDIM, 2 * BLK), bf16),
            out((blocks, HDIM, BLK), f32),
            out((blocks + 1, 128, BLK), bf16),
            out((blocks, BLK, 128), bf16),
            out((blocks, 80, BLK), bf16),
            out((blocks, 80, BLK), bf16),
        ],
        compiler_params=pltpu.CompilerParams(vmem_limit_bytes=60 * 2**20),
        name="attend_forward",
    )(device, skip, bias, raw, logits, gains)


def norm_back(v, gain, u):
    scale = lax.rsqrt(jnp.mean(v * v, 0, keepdims=True) + EPS)
    hat = v * scale
    gu = gain * u
    return scale * (gu - hat * jnp.mean(hat * gu, 0, keepdims=True)), hat * u


def backward_kernel(count, device_ref, skip_ref, bias_ref, raw_ref, logit_ref, gain_ref, dmixed_ref, mixed_ref,
                    q_ref, k_ref, kt_ref, vt_ref, draw_ref, dlogit_ref, dgain_ref,
                    do_ref, v_ref, cum_ref, dq_ref, dk_ref, dv_ref, pairs_ref, own_ref):
    slot = pl.program_id(0)
    device = device_ref[0]
    blocks = 2 * count
    pair_steps, own_steps = list_pairs(skip_ref, pairs_ref, own_ref, device, slot, count, UNROLL_BACK)
    gain_q, gain_k = gain_ref[:, 0:1], gain_ref[:, 1:2]
    wide = jnp.zeros((128 - 80, BLK), f32)

    def prepare(block, carried):
        place, lanes = place_of(block, count), lanes_of(block, count)
        d_out = dmixed_ref[place, :, lanes].astype(f32)
        delta = jnp.sum(d_out * mixed_ref[block], 0, keepdims=True)
        do_ref[block] = stack_rows(d_out, [-d for d in split3(delta)], 128).astype(bf16)
        v_ref[block] = jnp.concatenate([vt_ref[block].astype(f32), wide], 0).T.astype(bf16)
        dq_ref[block] = jnp.zeros(dq_ref.shape[1:], f32)
        dk_ref[block] = jnp.zeros(dk_ref.shape[1:], f32)
        dv_ref[block] = jnp.zeros(dv_ref.shape[1:], f32)
        return carried

    lax.fori_loop(0, blocks, prepare, 0)
    do_ref[blocks] = jnp.zeros(do_ref.shape[1:], bf16)
    dq_ref[blocks] = jnp.zeros(dq_ref.shape[1:], f32)

    t = lax.broadcasted_iota(jnp.int32, (BLK, BLK), 0)
    p = lax.broadcasted_iota(jnp.int32, (BLK, BLK), 1)

    def together(pairs, diagonal):
        scores = [mm(k_ref[column], q_ref[row]) for row, column in pairs]
        weights = [jnp.exp2(score) for score in scores]
        if diagonal:
            weights = [jnp.where(t <= p, weight, 0.0) for weight in weights]
        d_weights = [mm(v_ref[column], do_ref[row]) for row, column in pairs]
        low_weights = [weight.astype(bf16) for weight in weights]
        d_scores = [(weight * d_weight).astype(bf16) for weight, d_weight in zip(weights, d_weights)]
        parts = [mm(do_ref[row, :HDIM], weight, NT) for (row, _), weight in zip(pairs, low_weights)]
        for (_, column), part in zip(pairs, parts):
            dv_ref[column] += part
        parts = [mm(kt_ref[column], d_score) for (_, column), d_score in zip(pairs, d_scores)]
        for (row, _), part in zip(pairs, parts):
            dq_ref[row] += part
        parts = [mm(q_ref[row, :80], d_score, NT) for (row, _), d_score in zip(pairs, d_scores)]
        for (_, column), part in zip(pairs, parts):
            dk_ref[column] += part

    def own_rows(step, carried):
        rows = [own_ref[step * UNROLL_BACK + i] for i in range(UNROLL_BACK)]
        together([(row, jnp.minimum(row, blocks - 1)) for row in rows], True)
        return carried

    def kept_pairs(step, carried):
        codes = [pairs_ref[step * UNROLL_BACK + i] for i in range(UNROLL_BACK)]
        together([(code >> 10, code & 1023) for code in codes], False)
        return carried

    lax.fori_loop(0, own_steps, own_rows, 0)
    lax.fori_loop(0, pair_steps, kept_pairs, 0)

    def finish(step, carried):
        next_k, next_v, sum_q, sum_k = carried
        block = blocks - 1 - step
        place, lanes = place_of(block, count), lanes_of(block, count)
        earlier = jnp.maximum(block - 1, 0)
        place_before, lanes_before = place_of(earlier, count), lanes_of(earlier, count)
        exists = jnp.where(block > 0, 1.0, 0.0)
        q_raw, k_raw, v_raw = (raw_ref[place, i, :, lanes].astype(f32) for i in range(3))
        k_step = shifted(k_raw, raw_ref[place_before, 1, :, lanes_before].astype(f32) * exists) - k_raw
        v_step = shifted(v_raw, raw_ref[place_before, 2, :, lanes_before].astype(f32) * exists) - v_raw
        rate_k = jax.nn.sigmoid(logit_ref[place, 1:2, lanes])
        rate_v = jax.nn.sigmoid(logit_ref[place, 2:3, lanes])
        dq, dk, dv = dq_ref[block], dk_ref[block], dv_ref[block]
        dq_raw, part_q = norm_back(q_raw, gain_q, dq[:HDIM] * SCORE)
        dk_mixed, part_k = norm_back(k_raw + rate_k * k_step, gain_k, dk[:HDIM] * LN2)
        send_k, send_v = rate_k * dk_mixed, rate_v * dv
        draw_ref[place, 0, :, lanes] = dq_raw.astype(bf16)
        draw_ref[place, 1, :, lanes] = (dk_mixed - send_k + shifted_back(send_k, next_k)).astype(bf16)
        draw_ref[place, 2, :, lanes] = (dv - send_v + shifted_back(send_v, next_v)).astype(bf16)
        dlogit_ref[place, 1:2, lanes] = (1.0 - rate_k) * jnp.sum(k_step * send_k, 0, keepdims=True)
        dlogit_ref[place, 2:3, lanes] = (1.0 - rate_v) * jnp.sum(v_step * send_v, 0, keepdims=True)
        cum_ref[pl.ds(place, 1), lanes] = dq[HDIM : HDIM + 1] - dk[HDIM + 3 : HDIM + 4]
        part_q = jnp.where(is_mine(device, slot, place, count), part_q, 0.0)
        return send_k, send_v, sum_q + part_q, sum_k + part_k

    zero = jnp.zeros((HDIM, BLK), f32)
    _, _, sum_q, sum_k = lax.fori_loop(0, blocks, finish, (zero, zero, zero, zero))
    dgain_ref[:, 0:1] = jnp.sum(sum_q, 1, keepdims=True)
    dgain_ref[:, 1:2] = jnp.sum(sum_k, 1, keepdims=True)
    d_log = running_sum(cum_ref[...], count, True)
    dlogit_ref[:, 0, :] = d_log * jax.nn.sigmoid(-(logit_ref[:, 0, :] + bias_ref[slot]))
    dlogit_ref[:, 3:, :] = jnp.zeros((count, 5, 2 * BLK), f32)


def attend_backward(device, skip, bias, raw, logits, gains, dmixed, mixed, q, k, kt, vt):
    count = raw.shape[0]
    blocks = 2 * count
    most = blocks * (blocks - 1) // 2 + UNROLL_BACK
    mode = buffers(count)
    by_slot = lambda *shape: pl.BlockSpec((None,) + shape, lambda s, *_: (s,) + (0,) * len(shape), pipeline_mode=mode)
    raw_spec = pl.BlockSpec((count, 3, None, HDIM, 2 * BLK), lambda s, *_: (0, 0, s, 0, 0), pipeline_mode=mode)
    place_spec = lambda rows: pl.BlockSpec((count, None, rows, 2 * BLK), lambda s, *_: (0, s, 0, 0), pipeline_mode=mode)
    return pl.pallas_call(
        functools.partial(backward_kernel, count),
        grid_spec=pltpu.PrefetchScalarGridSpec(
            num_scalar_prefetch=3,
            grid=(2,),
            in_specs=[
                raw_spec,
                place_spec(8),
                by_slot(HDIM, 2),
                place_spec(HDIM),
                by_slot(blocks, HDIM, BLK),
                by_slot(blocks + 1, 128, BLK),
                by_slot(blocks, BLK, 128),
                by_slot(blocks, 80, BLK),
                by_slot(blocks, 80, BLK),
            ],
            out_specs=[raw_spec, place_spec(8), by_slot(HDIM, 2)],
            scratch_shapes=[
                pltpu.VMEM((blocks + 1, 128, BLK), bf16),
                pltpu.VMEM((blocks, BLK, 128), bf16),
                pltpu.VMEM((count, 2 * BLK), f32),
                pltpu.VMEM((blocks + 1, 80, BLK), f32),
                pltpu.VMEM((blocks, 80, BLK), f32),
                pltpu.VMEM((blocks, HDIM, BLK), f32),
                pltpu.SMEM((most,), jnp.int32),
                pltpu.SMEM((blocks + UNROLL_BACK,), jnp.int32),
            ],
        ),
        out_shape=[
            jax.ShapeDtypeStruct(raw.shape, bf16),
            jax.ShapeDtypeStruct(logits.shape, f32),
            jax.ShapeDtypeStruct(gains.shape, f32),
        ],
        compiler_params=pltpu.CompilerParams(vmem_limit_bytes=60 * 2**20),
        name="attend_backward",
    )(device, skip, bias, raw, logits, gains, dmixed, mixed, q, k, kt, vt)


def holder(head, place, count):
    return (head * count + place) // HEADS


def greet(count):
    me = lax.axis_index("seq")
    barrier = pltpu.get_barrier_semaphore()
    for k in range(1, count):
        peer = lax.rem(me + k, count)
        pl.semaphore_signal(barrier, inc=1, device_id={"seq": peer}, device_id_type=MESH)
    pl.semaphore_wait(barrier, count - 1)
    return me


def far_first(count):
    return sorted(range(1, count), key=lambda k: -min(k, count - k))


def push(src, dst, send, recv, peer):
    return pltpu.make_async_remote_copy(
        src_ref=src, dst_ref=dst, send_sem=send, recv_sem=recv, device_id={"seq": peer}, device_id_type=MESH
    )


def heads_out_kernel(count, x_ref, logit_in, raw_ref, logit_ref, send, recv, local):
    me = greet(count)

    def copies(peer, source, k):
        head = first_head(peer, count)
        items = []
        for slot in range(2):
            items.append((is_mine(peer, slot, me, count), is_mine(me, slot, source, count),
                          push(x_ref.at[0, head + slot], raw_ref.at[me, 0, slot], send.at[k, slot], recv.at[k, slot], peer)))
        items.append((None, None, push(x_ref.at[pl.ds(1, 2), pl.ds(head, 2)], raw_ref.at[me, pl.ds(1, 2)], send.at[k, 2], recv.at[k, 2], peer)))
        items.append((None, None, push(logit_in.at[pl.ds(head, 2)], logit_ref.at[me], send.at[k, 3], recv.at[k, 3], peer)))
        return items

    every = []
    for k in far_first(count):
        items = copies(lax.rem(me + k, count), lax.rem(me + count - k, count), k)
        every.append(items)
        for out, _, copy in items:
            if out is None:
                copy.start()
            else:
                pl.when(out)(copy.start)
    head = first_head(me, count)
    own = [
        pltpu.make_async_copy(x_ref.at[:, pl.ds(head, 2)], raw_ref.at[me], local.at[0]),
        pltpu.make_async_copy(logit_in.at[pl.ds(head, 2)], logit_ref.at[me], local.at[1]),
    ]
    for copy in own:
        copy.start()
    for items in every:
        for out, into, copy in items:
            if out is None:
                copy.wait()
            else:
                pl.when(out)(copy.wait_send)
                pl.when(into)(copy.wait_recv)
    for copy in own:
        copy.wait()


def heads_out(qkv, logits, count):
    return pl.pallas_call(
        functools.partial(heads_out_kernel, count),
        out_shape=[
            jax.ShapeDtypeStruct((count, 3, 2, HDIM, 2 * BLK), bf16),
            jax.ShapeDtypeStruct((count, 2, 8, 2 * BLK), f32),
        ],
        in_specs=[ANY, ANY],
        out_specs=[ANY, ANY],
        scratch_shapes=[pltpu.SemaphoreType.DMA((count, 4)), pltpu.SemaphoreType.DMA((count, 4)), pltpu.SemaphoreType.DMA((2,))],
        compiler_params=pltpu.CompilerParams(collective_id=0, has_side_effects=True),
        name="heads_out",
    )(qkv, logits)


def mixed_back_kernel(count, x_ref, o_ref, send, recv, local):
    me = greet(count)
    first = first_head(me, count)
    started = []
    for k in far_first(count) + [0]:
        peer = lax.rem(me + k, count)
        for slot in range(2):
            mine = is_mine(me, slot, peer, count)
            src, dst = x_ref.at[slot, peer], o_ref.at[first + slot]
            if k:
                copy = push(src, dst, send.at[k, slot], recv.at[first + slot], peer)
            else:
                copy = pltpu.make_async_copy(src, dst, local.at[slot])
            started.append((mine, k, copy))
            pl.when(mine)(copy.start)
    for mine, k, copy in started:
        pl.when(mine)(copy.wait_send if k else copy.wait)
    for head in range(HEADS):
        source = holder(head, me, count)
        copy = push(x_ref.at[0, 0], o_ref.at[head], send.at[0, 0], recv.at[head], lax.rem(me + 1, count))
        pl.when(source != me)(copy.wait_recv)


def mixed_back(mixed, count):
    return pl.pallas_call(
        functools.partial(mixed_back_kernel, count),
        out_shape=jax.ShapeDtypeStruct((HEADS, HDIM, 2 * BLK), bf16),
        in_specs=[ANY],
        out_specs=ANY,
        scratch_shapes=[pltpu.SemaphoreType.DMA((count, 2)), pltpu.SemaphoreType.DMA((HEADS,)), pltpu.SemaphoreType.DMA((2,))],
        compiler_params=pltpu.CompilerParams(collective_id=1, has_side_effects=True),
        name="mixed_back",
    )(mixed)


def grads_out_kernel(count, x_ref, o_ref, send, recv, local):
    me = greet(count)
    started = []
    for head in range(HEADS):
        peer = holder(head, me, count)
        slot = head - first_head(peer, count)
        away = peer != me
        there = jnp.where(away, peer, lax.rem(me + 1, count))
        copy = push(x_ref.at[head], o_ref.at[me, slot], send.at[head], recv.at[me, slot], there)
        own = pltpu.make_async_copy(x_ref.at[head], o_ref.at[me, slot], local.at[slot])
        pl.when(away)(copy.start)
        pl.when(peer == me)(own.start)
        started.append((away, peer == me, copy, own))
    for away, here, copy, own in started:
        pl.when(away)(copy.wait_send)
        pl.when(here)(own.wait)
    for k in range(1, count):
        source = lax.rem(me + k, count)
        for slot in range(2):
            copy = push(x_ref.at[0], o_ref.at[source, slot], send.at[0], recv.at[source, slot], source)
            pl.when(is_mine(me, slot, source, count))(copy.wait_recv)


def grads_out(d_mixed, count):
    return pl.pallas_call(
        functools.partial(grads_out_kernel, count),
        out_shape=jax.ShapeDtypeStruct((count, 2, HDIM, 2 * BLK), bf16),
        in_specs=[ANY],
        out_specs=ANY,
        scratch_shapes=[pltpu.SemaphoreType.DMA((HEADS,)), pltpu.SemaphoreType.DMA((count, 2)), pltpu.SemaphoreType.DMA((2,))],
        compiler_params=pltpu.CompilerParams(collective_id=2, has_side_effects=True),
        name="grads_out",
    )(d_mixed)


def heads_back_kernel(count, x_ref, logit_in, q_ref, kv_ref, logit_ref, send, recv, recv_q, local):
    me = greet(count)
    first = first_head(me, count)
    started = []
    for k in far_first(count) + [0]:
        peer = lax.rem(me + k, count)
        pairs = [
            (None, x_ref.at[peer, pl.ds(1, 2)], kv_ref.at[me], recv.at[k, 0]),
            (None, logit_in.at[peer], logit_ref.at[me], recv.at[k, 1]),
        ]
        for slot in range(2):
            pairs.append((is_mine(me, slot, peer, count), x_ref.at[peer, 0, slot], q_ref.at[first + slot], recv_q.at[first + slot]))
        for i, (mine, src, dst, sem) in enumerate(pairs):
            copy = push(src, dst, send.at[k, i], sem, peer) if k else pltpu.make_async_copy(src, dst, local.at[i])
            started.append((mine, k, copy))
            if mine is None:
                copy.start()
            else:
                pl.when(mine)(copy.start)
    for mine, k, copy in started:
        if mine is not None:
            pl.when(mine)(copy.wait_send if k else copy.wait)
        else:
            copy.wait()
    for head in range(HEADS):
        source = holder(head, me, count)
        copy = push(x_ref.at[0, 0, 0], q_ref.at[head], send.at[0, 0], recv_q.at[head], lax.rem(me + 1, count))
        pl.when(source != me)(copy.wait_recv)


def heads_back(d_raw, d_logits, count):
    return pl.pallas_call(
        functools.partial(heads_back_kernel, count),
        out_shape=[
            jax.ShapeDtypeStruct((HEADS, HDIM, 2 * BLK), bf16),
            jax.ShapeDtypeStruct((count, 2, 2, HDIM, 2 * BLK), bf16),
            jax.ShapeDtypeStruct((count, 2, 8, 2 * BLK), f32),
        ],
        in_specs=[ANY, ANY],
        out_specs=[ANY, ANY, ANY],
        scratch_shapes=[
            pltpu.SemaphoreType.DMA((count, 4)),
            pltpu.SemaphoreType.DMA((count, 2)),
            pltpu.SemaphoreType.DMA((HEADS,)),
            pltpu.SemaphoreType.DMA((4,)),
        ],
        compiler_params=pltpu.CompilerParams(collective_id=3, has_side_effects=True),
        name="heads_back",
    )(d_raw, d_logits)


def dot(a, b, i, j):
    return lax.dot_general(a, b, (((i,), (j,)), ((), ())), preferred_element_type=f32)


SMALL = 48
UNIT = 16
PIECE = 8


def group_bits(group_count, count):
    bits = [("group", 1 << i) for i in range(group_count.bit_length() - 1)]
    return bits, [("seq", 1 << i) for i in range(count.bit_length() - 1)]


def partner(bit):
    axis, step = bit
    here = lax.axis_index(axis)
    side = lax.rem(here // step, 2)
    return {axis: here + step - 2 * step * side}, side


def greet_all(bits):
    barrier = pltpu.get_barrier_semaphore()
    for bit in bits:
        there, _ = partner(bit)
        pl.semaphore_signal(barrier, inc=1, device_id=there, device_id_type=MESH)
    pl.semaphore_wait(barrier, len(bits))


def orders(near, far, seq):
    rest = [far] + seq
    return [[near] + rest[i:] + rest[:i] for i in range(3)]


class Summing:
    def __init__(self, base, size, order, own, landing, result, send, recv):
        self.start, self.size, self.order = base, size, order
        self.own, self.landing, self.result, self.send, self.recv = own, landing, result, send, recv
        self.base, self.at, self.stage, self.copy = base, base, 0, None

    def give(self):
        there, side = partner(self.order[self.stage])
        half = self.size // 2
        self.keep = self.start + side * half
        self.copy = pltpu.make_async_remote_copy(
            src_ref=self.own.at[pl.ds(self.start + (1 - side) * half, half)],
            dst_ref=self.landing.at[pl.ds(self.at, half)],
            send_sem=self.send.at[self.stage], recv_sem=self.recv.at[self.stage],
            device_id=there, device_id_type=MESH,
        )
        self.copy.start()

    def add(self):
        self.copy.wait()
        half = self.size // 2
        step = PIECE if half % PIECE == 0 else 1
        keep, at, own, landing = self.keep, self.at, self.own, self.landing

        def piece(i, carried):
            mine = pl.ds(keep + i * step, step)
            theirs = landing[pl.ds(at + i * step, step)].astype(f32)
            own[mine] = (own[mine].astype(f32) + theirs).astype(bf16)
            return carried

        lax.fori_loop(0, half // step, piece, 0)
        self.start, self.size, self.at, self.stage = keep, half, at + half, self.stage + 1

    def settle(self, sem):
        copy = pltpu.make_async_copy(
            self.own.at[pl.ds(self.start, self.size)], self.result.at[pl.ds(self.start, self.size)], sem
        )
        copy.start()
        copy.wait()
        self.left = len(self.order)

    def spread(self):
        self.left -= 1
        there, side = partner(self.order[self.left])
        part = self.result.at[pl.ds(self.start, self.size)]
        stage = 2 * len(self.order) - 1 - self.left
        self.copy = pltpu.make_async_remote_copy(
            src_ref=part, dst_ref=part, send_sem=self.send.at[stage], recv_sem=self.recv.at[stage],
            device_id=there, device_id_type=MESH,
        )
        self.copy.start()
        self.start, self.size = self.start - side * self.size, 2 * self.size

    def gathered(self):
        self.copy.wait()


def total(parts):
    return functools.reduce(jnp.add, parts)


def held_heads(count):
    first = [min(HEADS * d // count, HEADS - 2) for d in range(count)]
    return [
        [(d, h - first[d]) for d in range(h * count // HEADS, ((h + 1) * count - 1) // HEADS + 1)]
        for h in range(HEADS)
    ]


def part_sizes(units, least):
    pieces = units // least
    return [least * ((pieces + 2 - i) // 3) for i in range(3)]


def last_kernel(count, sets, h_ref, dq_ref, dkv_ref, dlogit_ref, dgate_ref, w_ref, wsmall_ref, x_ref, gain_ref,
                dresid_ref, extra_ref, grads_ref, dx_ref, small_ref,
                proj_ref, ht_ref, dsmall_ref, rows_ref, dn_ref, g_ref, land_ref, small_land, send, recv, ssend, srecv, local):
    near, far, seq = sets
    bits = [near, far] + seq
    greet_all(bits)
    rows = h_ref.shape[0]
    holders = held_heads(count)
    proj_ref[0:D] = dq_ref[...].reshape(D, rows)
    for head, held in enumerate(holders):
        for i in range(2):
            start = D * (1 + i) + head * HDIM
            if len(held) == 1:
                d, s = held[0]
                proj_ref[start : start + HDIM] = dkv_ref[d, i, s]
            else:
                proj_ref[start : start + HDIM] = total([dkv_ref[d, i, s].astype(f32) for d, s in held]).astype(bf16)
        dsmall_ref[8 * head : 8 * head + 8] = total([dlogit_ref[d, s] for d, s in held])
    proj_ref[3 * D :] = dgate_ref[...]
    for i in range(3):
        cols = slice(256 * i, 256 * i + 256)
        ht_ref[cols, :] = h_ref[:, cols].astype(f32).T.astype(bf16)

    def block(i, carried):
        part = mm(ht_ref[...], proj_ref[pl.ds(pl.multiple_of(i * 256, 256), 256)], NT).astype(bf16)
        g_ref[pl.ds(i * (D // UNIT), D // UNIT)] = part.reshape(D // UNIT, UNIT, 256)
        return carried

    lax.fori_loop(0, 9, block, 0)
    used = 9 * (D // UNIT)
    units = g_ref.shape[0]
    g_ref[used:] = jnp.zeros((units - used, UNIT, 256), bf16)

    sums, base = [], 0
    for i, size in enumerate(part_sizes(units, 1 << len(bits))):
        sums.append(Summing(base, size, orders(near, far, seq)[i], g_ref, land_ref, grads_ref, send.at[i], recv.at[i]))
        base += size
    for part in sums:
        part.give()

    low_small = dsmall_ref[...].astype(bf16)
    for i in range(3):
        cols = slice(256 * i, 256 * i + 256)
        part = mm(w_ref[cols, :], proj_ref[...]) + mm(wsmall_ref[cols, :], low_small)
        dn_ref[:, cols] = part.T
    small = mm(low_small, h_ref[...])
    for head in range(HEADS):
        rows_ref[3 * head : 3 * head + 3] = small[8 * head : 8 * head + 3]
    rows_ref[3 * HEADS :] = extra_ref[...]
    gain = gain_ref[...]
    dgain = jnp.zeros((1, D), f32)
    for i in range(rows // 128):
        here = slice(128 * i, 128 * i + 128)
        v, u = x_ref[here].astype(f32), dn_ref[here]
        scale = lax.rsqrt(jnp.mean(v * v, 1, keepdims=True) + EPS)
        hat, gu = v * scale, u * gain
        dx_ref[here] = dresid_ref[here] + scale * (gu - hat * jnp.mean(hat * gu, 1, keepdims=True))
        dgain = dgain + jnp.sum(hat * u, 0, keepdims=True)
    rows_ref[3 * HEADS : 3 * HEADS + 1] = dgain
    bias_rows = jnp.concatenate([dsmall_ref[8 * head : 8 * head + 1] for head in range(HEADS)], 0)
    bias_sum = jnp.sum(bias_rows, 1, keepdims=True)
    lane = lax.broadcasted_iota(jnp.int32, (HEADS, 128), 1)
    row = lax.broadcasted_iota(jnp.int32, (HEADS, 128), 0)
    rows_ref[3 * HEADS + 4 : 3 * HEADS + 5, 0:128] = jnp.sum(jnp.where(lane == row, bias_sum, 0.0), 0, keepdims=True)

    for stage, bit in enumerate(bits):
        there, _ = partner(bit)
        swap = pltpu.make_async_remote_copy(
            src_ref=rows_ref, dst_ref=small_land.at[stage], send_sem=ssend.at[stage], recv_sem=srecv.at[stage],
            device_id=there, device_id_type=MESH,
        )
        swap.start()
        for part in sums:
            part.add()
            if stage + 1 < len(bits):
                part.give()
            else:
                part.settle(local)
                part.spread()
        swap.wait()
        rows_ref[...] += small_land[stage]
    for stage in range(len(bits)):
        for part in sums:
            part.gathered()
            if stage + 1 < len(bits):
                part.spread()
    small_ref[...] = rows_ref[...]


def last(count, groups, h, d_q, d_kv, d_logits, d_gate, w_attn, w_small, x, gain, d_resid, extra):
    bits = group_bits(groups, count)
    sets = (bits[0][0], bits[0][1], bits[1])
    stages = len(bits[0]) + len(bits[1])
    least = 1 << stages
    units = -(-9 * (D // UNIT) // least) * least
    rows = h.shape[0]
    vmem = pl.BlockSpec(memory_space=pltpu.VMEM)
    dma = pltpu.SemaphoreType.DMA
    return pl.pallas_call(
        functools.partial(last_kernel, count, sets),
        out_shape=[
            jax.ShapeDtypeStruct((units, UNIT, 256), bf16),
            jax.ShapeDtypeStruct((rows, D), f32),
            jax.ShapeDtypeStruct((SMALL, D), f32),
        ],
        in_specs=[vmem] * 11,
        out_specs=[ANY, vmem, vmem],
        scratch_shapes=[
            pltpu.VMEM((4 * D, rows), bf16),
            pltpu.VMEM((D, rows), bf16),
            pltpu.VMEM((8 * HEADS, rows), f32),
            pltpu.VMEM((SMALL, D), f32),
            pltpu.VMEM((rows, D), f32),
            pltpu.VMEM((units, UNIT, 256), bf16),
            pltpu.VMEM((units, UNIT, 256), bf16),
            pltpu.VMEM((stages, SMALL, D), f32),
            dma((3, 2 * stages)), dma((3, 2 * stages)), dma((stages,)), dma((stages,)), dma,
        ],
        compiler_params=pltpu.CompilerParams(collective_id=4, has_side_effects=True, vmem_limit_bytes=62 * 2**20),
        name="last",
    )(h, d_q, d_kv, d_logits, d_gate, w_attn, w_small, x, gain, d_resid, extra)


def rms_scale(values, gains):
    inverse = lax.rsqrt(jnp.mean(values * values, axis=-1, keepdims=True) + EPS)
    return values * inverse * gains


def swiglu(gate_up):
    return jax.nn.silu(gate_up[:, :FF]) * gate_up[:, FF:]


def local(tokens, cotangent, skip_table, gain_attn, w_attn, w_heads, forget_bias, query_gain, key_gain,
          w_out, gain_ffn, w_gate_up, w_down):
    count = lax.axis_size("seq")
    me = lax.axis_index("seq")
    rows = tokens.shape[1]
    both = ("seq", "group")
    inputs = tokens[0].astype(f32)
    device = me.astype(jnp.int32)[None]
    head = first_head(me, count)
    skip = skip_table[0]
    gains = jnp.stack([query_gain.reshape(HEADS, HDIM), key_gain.reshape(HEADS, HDIM)], 2)
    gains = lax.dynamic_slice_in_dim(gains, head, 2, 0)
    bias = lax.dynamic_slice_in_dim(forget_bias, head, 2, 0)
    w_small = jnp.pad(w_heads.reshape(D, 3, HEADS).transpose(0, 2, 1), ((0, 0), (0, 0), (0, 5))).reshape(D, HEADS * 8)

    normed_attn, norm_back_attn = jax.vjp(rms_scale, inputs, gain_attn)
    h_first = normed_attn.astype(bf16)
    qkv = dot(w_attn[:, : 3 * D], h_first, 0, 1).astype(bf16).reshape(3, HEADS, HDIM, rows)
    gate_logit = dot(w_attn[:, 3 * D :], h_first, 0, 1)
    logits_here = dot(w_small, h_first, 0, 1).reshape(HEADS, 8, rows)

    raw, logits = heads_out(qkv, logits_here, count)
    mixed_low, mixed, q, k, kt, vt = attend_forward(device, skip, bias, raw, logits, gains)
    attended = mixed_back(mixed_low, count).reshape(D, rows).astype(f32)

    gate_open = jax.nn.sigmoid(gate_logit)
    gated = (gate_open * attended).astype(bf16)
    resid = inputs + dot(gated, w_out, 0, 0)
    normed_ffn, norm_back_ffn = jax.vjp(rms_scale, resid, gain_ffn)
    h_second = normed_ffn.astype(bf16)
    gate_up = dot(h_second, w_gate_up, 1, 0)
    hidden, hidden_back = jax.vjp(swiglu, gate_up)
    hidden_low = hidden.astype(bf16)
    output = resid + dot(hidden_low, w_down, 1, 0)
    d_low = cotangent[0]
    d_output = d_low.astype(f32)
    (d_gate_up,) = hidden_back(dot(d_low, w_down, 1, 1))
    d_gate_low = d_gate_up.astype(bf16)
    d_resid_norm, grad_gain_ffn = norm_back_ffn(dot(d_gate_low, w_gate_up, 1, 1))
    d_resid = d_output + d_resid_norm
    d_branch = d_resid.astype(bf16)
    d_gated = dot(w_out, d_branch, 1, 1)
    d_gate_logit = (d_gated * attended * gate_open * (1.0 - gate_open)).astype(bf16)
    d_mixed = (d_gated * gate_open).astype(bf16).reshape(HEADS, HDIM, rows)

    grad_w_down = dot(hidden_low, d_low, 0, 0).astype(bf16)
    grad_w_gate_up = dot(h_second, d_gate_low, 0, 0).astype(bf16)
    grad_w_out = dot(gated, d_branch, 1, 0).astype(bf16)
    grad_gate = dot(h_first, d_gate_logit, 0, 1).astype(bf16)
    early = lax.psum((grad_w_down, grad_w_gate_up, grad_w_out, grad_gate), both)

    d_mixed_all = grads_out(d_mixed, count)
    d_raw, d_logits, d_gains = attend_backward(device, skip, bias, raw, logits, gains, d_mixed_all, mixed, q, k, kt, vt)
    d_q, d_kv_parts, d_logit_parts = heads_back(d_raw, d_logits, count)

    placed = jnp.zeros((HEADS, HDIM, 2), f32)
    placed = lax.dynamic_update_slice(placed, d_gains, (head, 0, 0)).reshape(D, 2).T
    extra = jnp.concatenate([jnp.zeros((1, D), f32), grad_gain_ffn[None], placed, jnp.zeros((SMALL - 3 * HEADS - 4, D), f32)], 0)
    late, d_inputs, small = last(
        count, lax.axis_size("group"), h_first, d_q, d_kv_parts, d_logit_parts, d_gate_logit, w_attn, w_small,
        tokens[0], gain_attn[None], d_resid, extra,
    )
    late = late[: 9 * (D // UNIT)].reshape(9, D, 256).transpose(1, 0, 2).reshape(D, 3 * D)
    grad_w_attn = jnp.concatenate([late, early[3]], 1).astype(f32)
    row = 3 * HEADS
    return (
        output[None].astype(bf16),
        d_inputs[None],
        small[row],
        grad_w_attn,
        small[:row].reshape(HEADS, 3, D).transpose(2, 1, 0).reshape(D, row),
        small[row + 4, :HEADS],
        small[row + 2],
        small[row + 3],
        early[2].astype(f32),
        small[row + 1],
        early[1].astype(f32),
        early[0].astype(f32),
    )


def solution(mesh):
    rows = P("group", "seq", None)
    return jax.shard_map(
        local,
        mesh=mesh,
        in_specs=(rows, rows, P("group", None, None)) + (P(),) * 10,
        out_specs=(rows, rows) + (P(),) * 10,
        check_vma=False,
    )
```

```python
import functools

import jax
import jax.numpy as jnp
from jax import lax
from jax.experimental import pallas as pl
from jax.experimental.pallas import tpu as pltpu
from jax.sharding import PartitionSpec as P

D, FF = 768, 2048
MESH = pl.DeviceIdType.MESH
ANY = pl.BlockSpec(memory_space=pl.ANY)

HEADS, HDIM, BLK = 12, 64, 256
EPS = 1e-06
LOG2E = 1.4426950408889634
LN2 = 0.6931471805599453
SCORE = HDIM ** -0.5
f32, bf16 = jnp.float32, jnp.bfloat16
UNROLL = 8
UNROLL_BACK = 4
NN = (((1,), (0,)), ((), ()))
NT = (((1,), (1,)), ((), ()))


def mm(a, b, dims=NN):
    return lax.dot_general(a, b, dims, preferred_element_type=f32)


def split3(v):
    hi = v.astype(bf16).astype(f32)
    rest = v - hi
    mid = rest.astype(bf16).astype(f32)
    return hi, mid, rest - mid


def place_of(block, count):
    return jnp.where(block < count, block, 2 * count - 1 - block)


def lanes_of(block, count):
    return pl.ds(pl.multiple_of(jnp.where(block < count, 0, BLK), BLK), BLK)


def first_head(device, count):
    return jnp.minimum(HEADS * device // count, HEADS - 2)


def is_mine(device, slot, place, count):
    chunk = (first_head(device, count) + slot) * count + place
    return (chunk >= HEADS * device) & (chunk < HEADS * device + HEADS)


def list_pairs(skip_ref, pairs_ref, own_ref, device, slot, count, unroll):
    spare = 2 * count

    def row(number, found):
        def column(other, found):
            pairs_ref[found] = number * 1024 + other
            return found + jnp.where(skip_ref[number, other] == 0, 1, 0)

        mine = is_mine(device, slot, place_of(number, count), count)
        own_ref[found[1]] = number
        below = lax.fori_loop(0, jnp.where(mine, number, 0), column, found[0])
        return below, found[1] + jnp.where(mine, 1, 0)

    below, own = lax.fori_loop(0, spare, row, (0, 0))
    for extra in range(unroll):
        pairs_ref[below + extra] = spare * 1024
        own_ref[own + extra] = spare
    return pl.cdiv(below, unroll), pl.cdiv(own, unroll)


def running_sum(values, count, reverse):
    t = lax.broadcasted_iota(jnp.int32, (BLK, BLK), 0)
    p = lax.broadcasted_iota(jnp.int32, (BLK, BLK), 1)
    ones = jnp.where(t >= p if reverse else t <= p, 1.0, 0.0).astype(bf16)
    halves = []
    for half in range(2):
        part = values[:, half * BLK : (half + 1) * BLK]
        halves.append(sum(mm(piece.astype(bf16), ones) for piece in split3(part)))
    edge = 0 if reverse else BLK - 1
    first, last = (jnp.broadcast_to(h[:, edge : edge + 1], (count, 128)) for h in halves)
    rows = lax.broadcasted_iota(jnp.int32, (count, 128), 0)

    def scan(total, down):
        own = total
        step = 1
        while step < count:
            moved = pltpu.roll(total, step if down else count - step, 0)
            total = total + jnp.where(rows >= step if down else rows < count - step, moved, 0.0)
            step *= 2
        return total - own

    if reverse:
        all_last = jnp.sum(last, axis=0, keepdims=True)
        offsets = scan(first, False) + all_last, scan(last, True)
    else:
        all_first = jnp.sum(first, axis=0, keepdims=True)
        offsets = scan(first, True), scan(last, False) + all_first
    return jnp.concatenate([halves[0] + offsets[0][:, :1], halves[1] + offsets[1][:, :1]], 1)


def shifted(current, before):
    lane = lax.broadcasted_iota(jnp.int32, current.shape, 1)
    return jnp.where(lane == 0, pltpu.roll(before, 1, 1), pltpu.roll(current, 1, 1))


def shifted_back(current, after):
    lane = lax.broadcasted_iota(jnp.int32, current.shape, 1)
    return jnp.where(lane == BLK - 1, pltpu.roll(after, BLK - 1, 1), pltpu.roll(current, BLK - 1, 1))


def stack_rows(top, rows, size):
    extra = size if top is None else size - top.shape[0]
    number = lax.broadcasted_iota(jnp.int32, (extra, BLK), 0)
    bottom = jnp.zeros((extra, BLK), f32)
    for i, r in enumerate(rows):
        bottom = jnp.where(number == i, r, bottom)
    return bottom if top is None else jnp.concatenate([top, bottom], 0)


def forward_kernel(count, device_ref, skip_ref, bias_ref, raw_ref, logit_ref, gain_ref,
                   mixed_ref, mixed_full_ref, q_ref, k_ref, kt_ref, vt_ref,
                   cum_ref, acc_ref, pairs_ref, own_ref):
    slot = pl.program_id(0)
    device = device_ref[0]
    blocks = 2 * count
    pair_steps, own_steps = list_pairs(skip_ref, pairs_ref, own_ref, device, slot, count, UNROLL)
    logits = logit_ref[:, 0, :] + bias_ref[slot]
    log_forget = jnp.minimum(logits, 0.0) - jnp.log1p(jnp.exp(-jnp.abs(logits)))
    cum_ref[...] = running_sum(log_forget, count, False) * LOG2E
    gain_q, gain_k = gain_ref[:, 0:1], gain_ref[:, 1:2]

    def prepare(block, carried):
        place, lanes = place_of(block, count), lanes_of(block, count)
        q_raw, k_raw, v_raw = (raw_ref[place, i, :, lanes].astype(f32) for i in range(3))
        cum = cum_ref[pl.ds(place, 1), lanes]
        parts = split3(cum)
        one = jnp.ones_like(cum)
        query = q_raw * lax.rsqrt(jnp.mean(q_raw * q_raw, 0, keepdims=True) + EPS) * (gain_q * (SCORE * LOG2E))
        q_ref[block] = stack_rows(query, (*parts, one, one, one), 128).astype(bf16)
        rate_k = jax.nn.sigmoid(logit_ref[place, 1:2, lanes])
        rate_v = jax.nn.sigmoid(logit_ref[place, 2:3, lanes])
        key = k_raw + rate_k * (shifted(k_raw, carried[0]) - k_raw)
        key = key * lax.rsqrt(jnp.mean(key * key, 0, keepdims=True) + EPS) * gain_k
        value = v_raw + rate_v * (shifted(v_raw, carried[1]) - v_raw)
        k_ref[block] = stack_rows(key, (one, one, one, *(-c for c in parts)), 128).T.astype(bf16)
        kt_ref[block] = stack_rows(key, (one,), 80).astype(bf16)
        vt_ref[block] = stack_rows(value, (one, one, one), 80).astype(bf16)
        return k_raw, v_raw

    zero = jnp.zeros((HDIM, BLK), f32)
    lax.fori_loop(0, blocks, prepare, (zero, zero))
    q_ref[blocks] = jnp.zeros(q_ref.shape[1:], bf16)

    t = lax.broadcasted_iota(jnp.int32, (BLK, BLK), 0)
    p = lax.broadcasted_iota(jnp.int32, (BLK, BLK), 1)

    def together(pairs, diagonal):
        scores = [mm(k_ref[column], q_ref[row]) for row, column in pairs]
        weights = [jnp.exp2(score) for score in scores]
        if diagonal:
            weights = [jnp.where(t <= p, weight, 0.0) for weight in weights]
        weights = [weight.astype(bf16) for weight in weights]
        parts = [mm(vt_ref[column], weight) for (row, column), weight in zip(pairs, weights)]
        for (row, column), part in zip(pairs, parts):
            acc_ref[row] = part if diagonal else acc_ref[row] + part

    def own_rows(step, carried):
        rows = [own_ref[step * UNROLL + i] for i in range(UNROLL)]
        together([(row, jnp.minimum(row, blocks - 1)) for row in rows], True)
        return carried

    def kept_pairs(step, carried):
        codes = [pairs_ref[step * UNROLL + i] for i in range(UNROLL)]
        together([(code >> 10, code & 1023) for code in codes], False)
        return carried

    lax.fori_loop(0, own_steps, own_rows, 0)
    lax.fori_loop(0, pair_steps, kept_pairs, 0)

    def finish(block, carried):
        place, lanes = place_of(block, count), lanes_of(block, count)
        total = acc_ref[block]
        norm = total[HDIM : HDIM + 1]
        mixed = total[:HDIM] * (1.0 / norm)
        mixed_full_ref[block] = mixed
        mixed_ref[place, :, lanes] = mixed.astype(bf16)
        parts = split3(cum_ref[pl.ds(place, 1), lanes] - jnp.log2(norm))
        one = jnp.ones_like(norm)
        q_ref[block, HDIM : HDIM + 16, :] = stack_rows(None, (*parts, one, one, one), 16).astype(bf16)
        return carried

    lax.fori_loop(0, blocks, finish, 0)


def buffers(count):
    return pl.Buffered(1 if count > 8 else 2)


def attend_forward(device, skip, bias, raw, logits, gains):
    count = raw.shape[0]
    blocks = 2 * count
    most = blocks * (blocks - 1) // 2 + UNROLL
    mode = buffers(count)
    by_slot = lambda *shape: pl.BlockSpec((None,) + shape, lambda s, *_: (s,) + (0,) * len(shape), pipeline_mode=mode)
    out = lambda shape, dtype: jax.ShapeDtypeStruct((2,) + shape, dtype)
    return pl.pallas_call(
        functools.partial(forward_kernel, count),
        grid_spec=pltpu.PrefetchScalarGridSpec(
            num_scalar_prefetch=3,
            grid=(2,),
            in_specs=[
                pl.BlockSpec((count, 3, None, HDIM, 2 * BLK), lambda s, *_: (0, 0, s, 0, 0), pipeline_mode=mode),
                pl.BlockSpec((count, None, 8, 2 * BLK), lambda s, *_: (0, s, 0, 0), pipeline_mode=mode),
                by_slot(HDIM, 2),
            ],
            out_specs=[
                by_slot(count, HDIM, 2 * BLK),
                by_slot(blocks, HDIM, BLK),
                by_slot(blocks + 1, 128, BLK),
                by_slot(blocks, BLK, 128),
                by_slot(blocks, 80, BLK),
                by_slot(blocks, 80, BLK),
            ],
            scratch_shapes=[
                pltpu.VMEM((count, 2 * BLK), f32),
                pltpu.VMEM((blocks + 1, 80, BLK), f32),
                pltpu.SMEM((most,), jnp.int32),
                pltpu.SMEM((blocks + UNROLL,), jnp.int32),
            ],
        ),
        out_shape=[
            out((count, HDIM, 2 * BLK), bf16),
            out((blocks, HDIM, BLK), f32),
            out((blocks + 1, 128, BLK), bf16),
            out((blocks, BLK, 128), bf16),
            out((blocks, 80, BLK), bf16),
            out((blocks, 80, BLK), bf16),
        ],
        compiler_params=pltpu.CompilerParams(vmem_limit_bytes=60 * 2**20),
        name="attend_forward",
    )(device, skip, bias, raw, logits, gains)


def norm_back(v, gain, u):
    scale = lax.rsqrt(jnp.mean(v * v, 0, keepdims=True) + EPS)
    hat = v * scale
    gu = gain * u
    return scale * (gu - hat * jnp.mean(hat * gu, 0, keepdims=True)), hat * u


def backward_kernel(count, device_ref, skip_ref, bias_ref, raw_ref, logit_ref, gain_ref, dmixed_ref, mixed_ref,
                    q_ref, k_ref, kt_ref, vt_ref, draw_ref, dlogit_ref, dgain_ref,
                    do_ref, v_ref, cum_ref, dq_ref, dk_ref, dv_ref, pairs_ref, own_ref):
    slot = pl.program_id(0)
    device = device_ref[0]
    blocks = 2 * count
    pair_steps, own_steps = list_pairs(skip_ref, pairs_ref, own_ref, device, slot, count, UNROLL_BACK)
    gain_q, gain_k = gain_ref[:, 0:1], gain_ref[:, 1:2]
    wide = jnp.zeros((128 - 80, BLK), f32)

    def prepare(block, carried):
        place, lanes = place_of(block, count), lanes_of(block, count)
        d_out = dmixed_ref[place, :, lanes].astype(f32)
        delta = jnp.sum(d_out * mixed_ref[block], 0, keepdims=True)
        do_ref[block] = stack_rows(d_out, [-d for d in split3(delta)], 128).astype(bf16)
        v_ref[block] = jnp.concatenate([vt_ref[block].astype(f32), wide], 0).T.astype(bf16)
        dq_ref[block] = jnp.zeros(dq_ref.shape[1:], f32)
        dk_ref[block] = jnp.zeros(dk_ref.shape[1:], f32)
        dv_ref[block] = jnp.zeros(dv_ref.shape[1:], f32)
        return carried

    lax.fori_loop(0, blocks, prepare, 0)
    do_ref[blocks] = jnp.zeros(do_ref.shape[1:], bf16)
    dq_ref[blocks] = jnp.zeros(dq_ref.shape[1:], f32)

    t = lax.broadcasted_iota(jnp.int32, (BLK, BLK), 0)
    p = lax.broadcasted_iota(jnp.int32, (BLK, BLK), 1)

    def together(pairs, diagonal):
        scores = [mm(k_ref[column], q_ref[row]) for row, column in pairs]
        weights = [jnp.exp2(score) for score in scores]
        if diagonal:
            weights = [jnp.where(t <= p, weight, 0.0) for weight in weights]
        d_weights = [mm(v_ref[column], do_ref[row]) for row, column in pairs]
        low_weights = [weight.astype(bf16) for weight in weights]
        d_scores = [(weight * d_weight).astype(bf16) for weight, d_weight in zip(weights, d_weights)]
        parts = [mm(do_ref[row, :HDIM], weight, NT) for (row, _), weight in zip(pairs, low_weights)]
        for (_, column), part in zip(pairs, parts):
            dv_ref[column] += part
        parts = [mm(kt_ref[column], d_score) for (_, column), d_score in zip(pairs, d_scores)]
        for (row, _), part in zip(pairs, parts):
            dq_ref[row] += part
        parts = [mm(q_ref[row, :80], d_score, NT) for (row, _), d_score in zip(pairs, d_scores)]
        for (_, column), part in zip(pairs, parts):
            dk_ref[column] += part

    def own_rows(step, carried):
        rows = [own_ref[step * UNROLL_BACK + i] for i in range(UNROLL_BACK)]
        together([(row, jnp.minimum(row, blocks - 1)) for row in rows], True)
        return carried

    def kept_pairs(step, carried):
        codes = [pairs_ref[step * UNROLL_BACK + i] for i in range(UNROLL_BACK)]
        together([(code >> 10, code & 1023) for code in codes], False)
        return carried

    lax.fori_loop(0, own_steps, own_rows, 0)
    lax.fori_loop(0, pair_steps, kept_pairs, 0)

    def finish(step, carried):
        next_k, next_v, sum_q, sum_k = carried
        block = blocks - 1 - step
        place, lanes = place_of(block, count), lanes_of(block, count)
        earlier = jnp.maximum(block - 1, 0)
        place_before, lanes_before = place_of(earlier, count), lanes_of(earlier, count)
        exists = jnp.where(block > 0, 1.0, 0.0)
        q_raw, k_raw, v_raw = (raw_ref[place, i, :, lanes].astype(f32) for i in range(3))
        k_step = shifted(k_raw, raw_ref[place_before, 1, :, lanes_before].astype(f32) * exists) - k_raw
        v_step = shifted(v_raw, raw_ref[place_before, 2, :, lanes_before].astype(f32) * exists) - v_raw
        rate_k = jax.nn.sigmoid(logit_ref[place, 1:2, lanes])
        rate_v = jax.nn.sigmoid(logit_ref[place, 2:3, lanes])
        dq, dk, dv = dq_ref[block], dk_ref[block], dv_ref[block]
        dq_raw, part_q = norm_back(q_raw, gain_q, dq[:HDIM] * SCORE)
        dk_mixed, part_k = norm_back(k_raw + rate_k * k_step, gain_k, dk[:HDIM] * LN2)
        send_k, send_v = rate_k * dk_mixed, rate_v * dv
        draw_ref[place, 0, :, lanes] = dq_raw.astype(bf16)
        draw_ref[place, 1, :, lanes] = (dk_mixed - send_k + shifted_back(send_k, next_k)).astype(bf16)
        draw_ref[place, 2, :, lanes] = (dv - send_v + shifted_back(send_v, next_v)).astype(bf16)
        dlogit_ref[place, 1:2, lanes] = (1.0 - rate_k) * jnp.sum(k_step * send_k, 0, keepdims=True)
        dlogit_ref[place, 2:3, lanes] = (1.0 - rate_v) * jnp.sum(v_step * send_v, 0, keepdims=True)
        cum_ref[pl.ds(place, 1), lanes] = dq[HDIM : HDIM + 1] - dk[HDIM + 3 : HDIM + 4]
        part_q = jnp.where(is_mine(device, slot, place, count), part_q, 0.0)
        return send_k, send_v, sum_q + part_q, sum_k + part_k

    zero = jnp.zeros((HDIM, BLK), f32)
    _, _, sum_q, sum_k = lax.fori_loop(0, blocks, finish, (zero, zero, zero, zero))
    dgain_ref[:, 0:1] = jnp.sum(sum_q, 1, keepdims=True)
    dgain_ref[:, 1:2] = jnp.sum(sum_k, 1, keepdims=True)
    d_log = running_sum(cum_ref[...], count, True)
    dlogit_ref[:, 0, :] = d_log * jax.nn.sigmoid(-(logit_ref[:, 0, :] + bias_ref[slot]))
    dlogit_ref[:, 3:, :] = jnp.zeros((count, 5, 2 * BLK), f32)


def attend_backward(device, skip, bias, raw, logits, gains, dmixed, mixed, q, k, kt, vt):
    count = raw.shape[0]
    blocks = 2 * count
    most = blocks * (blocks - 1) // 2 + UNROLL_BACK
    mode = buffers(count)
    by_slot = lambda *shape: pl.BlockSpec((None,) + shape, lambda s, *_: (s,) + (0,) * len(shape), pipeline_mode=mode)
    raw_spec = pl.BlockSpec((count, 3, None, HDIM, 2 * BLK), lambda s, *_: (0, 0, s, 0, 0), pipeline_mode=mode)
    place_spec = lambda rows: pl.BlockSpec((count, None, rows, 2 * BLK), lambda s, *_: (0, s, 0, 0), pipeline_mode=mode)
    return pl.pallas_call(
        functools.partial(backward_kernel, count),
        grid_spec=pltpu.PrefetchScalarGridSpec(
            num_scalar_prefetch=3,
            grid=(2,),
            in_specs=[
                raw_spec,
                place_spec(8),
                by_slot(HDIM, 2),
                place_spec(HDIM),
                by_slot(blocks, HDIM, BLK),
                by_slot(blocks + 1, 128, BLK),
                by_slot(blocks, BLK, 128),
                by_slot(blocks, 80, BLK),
                by_slot(blocks, 80, BLK),
            ],
            out_specs=[raw_spec, place_spec(8), by_slot(HDIM, 2)],
            scratch_shapes=[
                pltpu.VMEM((blocks + 1, 128, BLK), bf16),
                pltpu.VMEM((blocks, BLK, 128), bf16),
                pltpu.VMEM((count, 2 * BLK), f32),
                pltpu.VMEM((blocks + 1, 80, BLK), f32),
                pltpu.VMEM((blocks, 80, BLK), f32),
                pltpu.VMEM((blocks, HDIM, BLK), f32),
                pltpu.SMEM((most,), jnp.int32),
                pltpu.SMEM((blocks + UNROLL_BACK,), jnp.int32),
            ],
        ),
        out_shape=[
            jax.ShapeDtypeStruct(raw.shape, bf16),
            jax.ShapeDtypeStruct(logits.shape, f32),
            jax.ShapeDtypeStruct(gains.shape, f32),
        ],
        compiler_params=pltpu.CompilerParams(vmem_limit_bytes=60 * 2**20),
        name="attend_backward",
    )(device, skip, bias, raw, logits, gains, dmixed, mixed, q, k, kt, vt)


def holder(head, place, count):
    return (head * count + place) // HEADS


def greet(count):
    me = lax.axis_index("seq")
    barrier = pltpu.get_barrier_semaphore()
    for k in range(1, count):
        peer = lax.rem(me + k, count)
        pl.semaphore_signal(barrier, inc=1, device_id={"seq": peer}, device_id_type=MESH)
    pl.semaphore_wait(barrier, count - 1)
    return me


def far_first(count):
    return sorted(range(1, count), key=lambda k: -min(k, count - k))


def push(src, dst, send, recv, peer):
    return pltpu.make_async_remote_copy(
        src_ref=src, dst_ref=dst, send_sem=send, recv_sem=recv, device_id={"seq": peer}, device_id_type=MESH
    )


def heads_out_kernel(count, x_ref, logit_in, raw_ref, logit_ref, send, recv, local):
    me = greet(count)

    def copies(peer, source, k):
        head = first_head(peer, count)
        items = []
        for slot in range(2):
            items.append((is_mine(peer, slot, me, count), is_mine(me, slot, source, count),
                          push(x_ref.at[0, head + slot], raw_ref.at[me, 0, slot], send.at[k, slot], recv.at[k, slot], peer)))
        items.append((None, None, push(x_ref.at[pl.ds(1, 2), pl.ds(head, 2)], raw_ref.at[me, pl.ds(1, 2)], send.at[k, 2], recv.at[k, 2], peer)))
        items.append((None, None, push(logit_in.at[pl.ds(head, 2)], logit_ref.at[me], send.at[k, 3], recv.at[k, 3], peer)))
        return items

    every = []
    for k in far_first(count):
        items = copies(lax.rem(me + k, count), lax.rem(me + count - k, count), k)
        every.append(items)
        for out, _, copy in items:
            if out is None:
                copy.start()
            else:
                pl.when(out)(copy.start)
    head = first_head(me, count)
    own = [
        pltpu.make_async_copy(x_ref.at[:, pl.ds(head, 2)], raw_ref.at[me], local.at[0]),
        pltpu.make_async_copy(logit_in.at[pl.ds(head, 2)], logit_ref.at[me], local.at[1]),
    ]
    for copy in own:
        copy.start()
    for items in every:
        for out, into, copy in items:
            if out is None:
                copy.wait()
            else:
                pl.when(out)(copy.wait_send)
                pl.when(into)(copy.wait_recv)
    for copy in own:
        copy.wait()


def heads_out(qkv, logits, count):
    return pl.pallas_call(
        functools.partial(heads_out_kernel, count),
        out_shape=[
            jax.ShapeDtypeStruct((count, 3, 2, HDIM, 2 * BLK), bf16),
            jax.ShapeDtypeStruct((count, 2, 8, 2 * BLK), f32),
        ],
        in_specs=[ANY, ANY],
        out_specs=[ANY, ANY],
        scratch_shapes=[pltpu.SemaphoreType.DMA((count, 4)), pltpu.SemaphoreType.DMA((count, 4)), pltpu.SemaphoreType.DMA((2,))],
        compiler_params=pltpu.CompilerParams(collective_id=0, has_side_effects=True),
        name="heads_out",
    )(qkv, logits)


def mixed_back_kernel(count, x_ref, o_ref, send, recv, local):
    me = greet(count)
    first = first_head(me, count)
    started = []
    for k in far_first(count) + [0]:
        peer = lax.rem(me + k, count)
        for slot in range(2):
            mine = is_mine(me, slot, peer, count)
            src, dst = x_ref.at[slot, peer], o_ref.at[first + slot]
            if k:
                copy = push(src, dst, send.at[k, slot], recv.at[first + slot], peer)
            else:
                copy = pltpu.make_async_copy(src, dst, local.at[slot])
            started.append((mine, k, copy))
            pl.when(mine)(copy.start)
    for mine, k, copy in started:
        pl.when(mine)(copy.wait_send if k else copy.wait)
    for head in range(HEADS):
        source = holder(head, me, count)
        copy = push(x_ref.at[0, 0], o_ref.at[head], send.at[0, 0], recv.at[head], lax.rem(me + 1, count))
        pl.when(source != me)(copy.wait_recv)


def mixed_back(mixed, count):
    return pl.pallas_call(
        functools.partial(mixed_back_kernel, count),
        out_shape=jax.ShapeDtypeStruct((HEADS, HDIM, 2 * BLK), bf16),
        in_specs=[ANY],
        out_specs=ANY,
        scratch_shapes=[pltpu.SemaphoreType.DMA((count, 2)), pltpu.SemaphoreType.DMA((HEADS,)), pltpu.SemaphoreType.DMA((2,))],
        compiler_params=pltpu.CompilerParams(collective_id=1, has_side_effects=True),
        name="mixed_back",
    )(mixed)


TN = (((0,), (0,)), ((), ()))


def grads_out_kernel(count, x_ref, h1_ref, dgate_ref, h2_ref, dgu_ref, hidden_ref, dlow_ref, gated_ref, branch_ref,
                     o_ref, grads_ref, send, recv, local):
    me = greet(count)
    started = []
    for head in range(HEADS):
        peer = holder(head, me, count)
        slot = head - first_head(peer, count)
        away = peer != me
        there = jnp.where(away, peer, lax.rem(me + 1, count))
        copy = push(x_ref.at[head], o_ref.at[me, slot], send.at[head], recv.at[me, slot], there)
        own = pltpu.make_async_copy(x_ref.at[head], o_ref.at[me, slot], local.at[slot])
        pl.when(away)(copy.start)
        pl.when(peer == me)(own.start)
        started.append((away, peer == me, copy, own))

    def put(unit, part):
        grads_ref[pl.ds(unit, 16)] = part.astype(bf16).reshape(16, UNIT, 256)

    def gate_up(i, carried):
        right = dgu_ref[:, pl.ds(pl.multiple_of(i * 256, 256), 256)]
        for j in range(3):
            put(i * 48 + 16 * j, mm(h2_ref[:, 256 * j : 256 * j + 256], right, TN))
        return carried

    lax.fori_loop(0, 2 * FF // 256, gate_up, 0)

    def down(i, carried):
        left = hidden_ref[:, pl.ds(pl.multiple_of(i * 256, 256), 256)]
        for j in range(3):
            put(768 + 128 * j + 16 * i, mm(left, dlow_ref[:, 256 * j : 256 * j + 256], TN))
        return carried

    lax.fori_loop(0, FF // 256, down, 0)
    for i in range(3):
        for j in range(3):
            put(1152 + 48 * i + 16 * j, mm(gated_ref[256 * j : 256 * j + 256, :], branch_ref[:, 256 * i : 256 * i + 256]))
            put(1296 + 48 * i + 16 * j, lax.dot_general(
                h1_ref[:, 256 * j : 256 * j + 256], dgate_ref[256 * i : 256 * i + 256, :],
                (((0,), (1,)), ((), ())), preferred_element_type=f32))
    units = grads_ref.shape[0]
    if units > 1440:
        grads_ref[1440:] = jnp.zeros((units - 1440, UNIT, 256), bf16)

    for away, here, copy, own in started:
        pl.when(away)(copy.wait_send)
        pl.when(here)(own.wait)
    for k in range(1, count):
        source = lax.rem(me + k, count)
        for slot in range(2):
            copy = push(x_ref.at[0], o_ref.at[source, slot], send.at[0], recv.at[source, slot], source)
            pl.when(is_mine(me, slot, source, count))(copy.wait_recv)


def grads_out(count, units, d_mixed, *operands):
    vmem = pl.BlockSpec(memory_space=pltpu.VMEM)
    return pl.pallas_call(
        functools.partial(grads_out_kernel, count),
        out_shape=[
            jax.ShapeDtypeStruct((count, 2, HDIM, 2 * BLK), bf16),
            jax.ShapeDtypeStruct((units, UNIT, 256), bf16),
        ],
        in_specs=[ANY] + [vmem] * 8,
        out_specs=[ANY, vmem],
        scratch_shapes=[pltpu.SemaphoreType.DMA((HEADS,)), pltpu.SemaphoreType.DMA((count, 2)), pltpu.SemaphoreType.DMA((2,))],
        compiler_params=pltpu.CompilerParams(collective_id=2, has_side_effects=True, vmem_limit_bytes=60 * 2**20),
        name="grads_out",
    )(d_mixed, *operands)


def dot(a, b, i, j):
    return lax.dot_general(a, b, (((i,), (j,)), ((), ())), preferred_element_type=f32)


SMALL = 48
UNIT = 16
PIECE = 8


def group_bits(group_count, count):
    bits = [("group", 1 << i) for i in range(group_count.bit_length() - 1)]
    return bits, [("seq", 1 << i) for i in range(count.bit_length() - 1)]


def partner(bit):
    axis, step = bit
    here = lax.axis_index(axis)
    side = lax.rem(here // step, 2)
    return {axis: here + step - 2 * step * side}, side


def greet_all(bits, count):
    me = lax.axis_index("seq")
    others = [partner(bit)[0] for bit in bits if bit[0] != "seq"]
    others += [{"seq": lax.rem(me + k, count)} for k in range(1, count)]
    barrier = pltpu.get_barrier_semaphore()
    for there in others:
        pl.semaphore_signal(barrier, inc=1, device_id=there, device_id_type=MESH)
    pl.semaphore_wait(barrier, len(others))
    return me


def orders(near, far, seq):
    x, others = seq[0], seq[1:]
    z = others[0]
    rest = others[1:]
    return [
        [near, far, x, z] + rest,
        [near, x, far, z] + rest,
        [near, z, x, far] + rest,
        [near, far, z, x] + rest,
        [near, x, z] + rest + [far],
        [near, z, far] + rest + [x],
    ]


PARTS = 6


class Summing:
    def __init__(self, base, size, order, source, own, landing, result, send, recv, local):
        self.start, self.size, self.order, self.source, self.local = base, size, order, source, local
        self.own, self.landing, self.result, self.send, self.recv = own, landing, result, send, recv
        self.at, self.stage, self.copy, self.load = base, 0, None, None

    def give(self):
        there, side = partner(self.order[self.stage])
        half = self.size // 2
        self.keep = self.start + side * half
        held = self.own
        if self.stage == 0 and self.source is not None:
            held = self.source
            mine = pl.ds(self.keep, half)
            self.load = pltpu.make_async_copy(self.source.at[mine], self.own.at[mine], self.local)
            self.load.start()
        self.copy = pltpu.make_async_remote_copy(
            src_ref=held.at[pl.ds(self.start + (1 - side) * half, half)],
            dst_ref=self.landing.at[pl.ds(self.at, half)],
            send_sem=self.send.at[self.stage], recv_sem=self.recv.at[self.stage],
            device_id=there, device_id_type=MESH,
        )
        self.copy.start()

    def add(self):
        self.copy.wait()
        if self.load is not None:
            self.load.wait()
            self.load = None
        half = self.size // 2
        step = PIECE if half % PIECE == 0 else 1
        keep, at, own, landing = self.keep, self.at, self.own, self.landing

        def piece(i, carried):
            mine = pl.ds(keep + i * step, step)
            theirs = landing[pl.ds(at + i * step, step)].astype(f32)
            own[mine] = (own[mine].astype(f32) + theirs).astype(bf16)
            return carried

        lax.fori_loop(0, half // step, piece, 0)
        self.start, self.size, self.at, self.stage = keep, half, at + half, self.stage + 1

    def settle(self):
        copy = pltpu.make_async_copy(
            self.own.at[pl.ds(self.start, self.size)], self.result.at[pl.ds(self.start, self.size)], self.local
        )
        copy.start()
        copy.wait()
        self.left = len(self.order)

    def spread(self):
        self.left -= 1
        there, side = partner(self.order[self.left])
        part = self.result.at[pl.ds(self.start, self.size)]
        stage = 2 * len(self.order) - 1 - self.left
        self.copy = pltpu.make_async_remote_copy(
            src_ref=part, dst_ref=part, send_sem=self.send.at[stage], recv_sem=self.recv.at[stage],
            device_id=there, device_id_type=MESH,
        )
        self.copy.start()
        self.start, self.size = self.start - side * self.size, 2 * self.size

    def gathered(self):
        self.copy.wait()


def total(parts):
    return functools.reduce(jnp.add, parts)


def held_heads(count):
    first = [min(HEADS * d // count, HEADS - 2) for d in range(count)]
    return [
        [(d, h - first[d]) for d in range(h * count // HEADS, ((h + 1) * count - 1) // HEADS + 1)]
        for h in range(HEADS)
    ]


def padded(units, least):
    return -(-units // least) * least


def sums_of(units, least, sets, source, own, landing, result, send, recv, local):
    pieces, base, sums = units // least, 0, []
    for i, order in enumerate(orders(*sets)):
        size = least * ((pieces + PARTS - 1 - i) // PARTS)
        if not size:
            break
        sums.append(Summing(base, size, order, source, own, landing, result, send.at[i], recv.at[i], local.at[i]))
        base += size
    return sums


def step(sums, stages):
    for part in sums:
        if part.stage < stages:
            part.add()
            if part.stage < stages:
                part.give()
            else:
                part.settle()
                part.spread()
        else:
            part.gathered()
            if part.left > 0:
                part.spread()


def last_kernel(count, sets, draw_ref, dlogit_ref, early_ref, h_ref, dgate_ref, w_ref, wsmall_ref, x_ref, gain_ref,
                dresid_ref, extra_ref, late_out, early_out, dx_ref,
                proj_ref, logit_ref, part_ref, dsmall_ref, rows_ref, dn_ref, g_ref, land_ref, e_ref, eland_ref,
                send, recv, recv_q, recv_kv, local, gsend, grecv, gsem, esend, erecv, esem):
    near, far, seq = sets
    bits = [near, far] + seq
    stages, least = len(bits), 1 << len(bits)
    me = greet_all(bits, count)
    rows = h_ref.shape[0]
    early = sums_of(e_ref.shape[0], least, sets, early_ref, e_ref, eland_ref, early_out, esend, erecv, esem)
    for part in early:
        part.give()

    holders = held_heads(count)
    first = first_head(me, count)
    started = []
    for k in far_first(count) + [0]:
        peer = lax.rem(me + k, count)
        pairs = [(None, dlogit_ref.at[peer], logit_ref.at[me], recv.at[k])]
        for slot in range(2):
            head = first + slot
            target = proj_ref.at[pl.ds(pl.multiple_of(head * HDIM, HDIM), HDIM)]
            pairs.append((is_mine(me, slot, peer, count), draw_ref.at[peer, 0, slot], target, recv_q.at[head]))
            used = (head * count < HEADS * (me + 1)) & (head * count + count > HEADS * me)
            order = me - holder(head, 0, count)
            pairs.append((used, draw_ref.at[peer, pl.ds(1, 2), slot], part_ref.at[head, order], recv_kv.at[head, order]))
        for i, (mine, src, dst, sem) in enumerate(pairs):
            copy = push(src, dst, send.at[k, i], sem, peer) if k else pltpu.make_async_copy(src, dst, local.at[i])
            started.append((mine, k, copy))
            if mine is None:
                copy.start()
            else:
                pl.when(mine)(copy.start)

    step(early, stages)
    step(early, stages)

    for mine, k, copy in started:
        if mine is not None:
            pl.when(mine)(copy.wait_send if k else copy.wait)
        else:
            copy.wait()
    for head in range(HEADS):
        source = holder(head, me, count)
        copy = push(draw_ref.at[0, 0, 0], proj_ref.at[pl.ds(head * HDIM, HDIM)], send.at[0, 0], recv_q.at[head], lax.rem(me + 1, count))
        pl.when(source != me)(copy.wait_recv)
        for j, (d, s) in enumerate(holders[head]):
            copy = push(draw_ref.at[0, pl.ds(1, 2), 0], part_ref.at[head, j], send.at[0, 0], recv_kv.at[head, j], lax.rem(me + 1, count))
            pl.when(me != d)(copy.wait_recv)

    for head, held in enumerate(holders):
        for i in range(2):
            start = D * (1 + i) + head * HDIM
            if len(held) == 1:
                proj_ref[start : start + HDIM] = part_ref[head, 0, i]
            else:
                proj_ref[start : start + HDIM] = total([part_ref[head, j, i].astype(f32) for j in range(len(held))]).astype(bf16)
        dsmall_ref[8 * head : 8 * head + 8] = total([logit_ref[d, s] for d, s in held])
    proj_ref[3 * D :] = dgate_ref[...]

    def block(i, carried):
        grads = proj_ref[pl.ds(pl.multiple_of(i * 256, 256), 256)]
        for j in range(3):
            part = lax.dot_general(h_ref[:, 256 * j : 256 * j + 256], grads, (((0,), (1,)), ((), ())), preferred_element_type=f32)
            g_ref[pl.ds(i * (D // UNIT) + j * 16, 16)] = part.astype(bf16).reshape(16, UNIT, 256)
        return carried

    lax.fori_loop(0, 9, block, 0)
    low_small = dsmall_ref[...].astype(bf16)
    for i in range(3):
        cols = slice(256 * i, 256 * i + 256)
        part = mm(w_ref[cols, :], proj_ref[...]) + mm(wsmall_ref[cols, :], low_small)
        dn_ref[:, cols] = part.T
    small = mm(low_small, h_ref[...])
    for head in range(HEADS):
        rows_ref[3 * head : 3 * head + 3] = small[8 * head : 8 * head + 3]
    rows_ref[3 * HEADS :] = extra_ref[...]
    gain = gain_ref[...]
    dgain = jnp.zeros((1, D), f32)
    for i in range(rows // 128):
        here = slice(128 * i, 128 * i + 128)
        v, u = x_ref[here].astype(f32), dn_ref[here]
        scale = lax.rsqrt(jnp.mean(v * v, 1, keepdims=True) + EPS)
        hat, gu = v * scale, u * gain
        dx_ref[here] = dresid_ref[here] + scale * (gu - hat * jnp.mean(hat * gu, 1, keepdims=True))
        dgain = dgain + jnp.sum(hat * u, 0, keepdims=True)
    rows_ref[3 * HEADS : 3 * HEADS + 1] = dgain
    bias_rows = jnp.concatenate([dsmall_ref[8 * head : 8 * head + 1] for head in range(HEADS)], 0)
    bias_sum = jnp.sum(bias_rows, 1, keepdims=True)
    lane = lax.broadcasted_iota(jnp.int32, (HEADS, 128), 1)
    row = lax.broadcasted_iota(jnp.int32, (HEADS, 128), 0)
    rows_ref[3 * HEADS + 4 : 3 * HEADS + 5, 0:128] = jnp.sum(jnp.where(lane == row, bias_sum, 0.0), 0, keepdims=True)

    used = 9 * (D // UNIT)
    units = g_ref.shape[0]
    for i in range(3):
        g_ref[used + 3 * i : used + 3 * i + 3] = rows_ref[:, 256 * i : 256 * i + 256].astype(bf16).reshape(3, UNIT, 256)
    if units > used + 9:
        g_ref[used + 9 :] = jnp.zeros((units - used - 9, UNIT, 256), bf16)
    late = sums_of(units, least, sets, None, g_ref, land_ref, late_out, gsend, grecv, gsem)
    for part in late:
        part.give()
    step(early, stages)
    early_left = 2 * stages - 3
    for stage in range(2 * stages):
        step(late, stages)
        if stage < early_left:
            step(early, stages)


def last(count, sets, d_raw, d_logits, early, h, d_gate, w_attn, w_small, x, gain, d_resid, extra):
    stages = 2 + len(sets[2])
    units = padded(9 * (D // UNIT) + 9, 1 << stages)
    rows = h.shape[0]
    most = max(len(held) for held in held_heads(count))
    vmem = pl.BlockSpec(memory_space=pltpu.VMEM)
    dma = pltpu.SemaphoreType.DMA
    shape = (UNIT, 256)
    return pl.pallas_call(
        functools.partial(last_kernel, count, sets),
        out_shape=[
            jax.ShapeDtypeStruct((units,) + shape, bf16),
            jax.ShapeDtypeStruct(early.shape, bf16),
            jax.ShapeDtypeStruct((rows, D), f32),
        ],
        in_specs=[ANY] * 3 + [vmem] * 8,
        out_specs=[ANY, ANY, vmem],
        scratch_shapes=[
            pltpu.VMEM((4 * D, rows), bf16),
            pltpu.VMEM((count, 2, 8, rows), f32),
            pltpu.VMEM((HEADS, most, 2, HDIM, rows), bf16),
            pltpu.VMEM((8 * HEADS, rows), f32),
            pltpu.VMEM((SMALL, D), f32),
            pltpu.VMEM((rows, D), f32),
            pltpu.VMEM((units,) + shape, bf16),
            pltpu.VMEM((units,) + shape, bf16),
            pltpu.VMEM(early.shape, bf16),
            pltpu.VMEM(early.shape, bf16),
            dma((count, 5)), dma((count,)), dma((HEADS,)), dma((HEADS, most)), dma((5,)),
            dma((PARTS, 2 * stages)), dma((PARTS, 2 * stages)), dma((PARTS,)),
            dma((PARTS, 2 * stages)), dma((PARTS, 2 * stages)), dma((PARTS,)),
        ],
        compiler_params=pltpu.CompilerParams(collective_id=3, has_side_effects=True, vmem_limit_bytes=62 * 2**20),
        name="last",
    )(d_raw, d_logits, early, h, d_gate, w_attn, w_small, x, gain, d_resid, extra)


def unpack_kernel(parts, *refs):
    o_ref = refs[-1]
    at = 0
    for ref, blocks in zip(refs, parts):
        here = (pl.program_id(0) >= at) & (pl.program_id(0) < at + blocks)

        @pl.when(here)
        def _():
            o_ref[...] = ref[...].reshape(o_ref.shape).astype(f32)

        at += blocks


def unpack(rows, *parts):
    size = rows // UNIT
    specs, at = [], 0
    for _, first, blocks in parts:
        index = lambda i, at=at, first=first, blocks=blocks: (first + jnp.clip(i - at, 0, blocks - 1), 0, 0)
        specs.append(pl.BlockSpec((size, UNIT, 256), index))
        at += blocks
    return pl.pallas_call(
        functools.partial(unpack_kernel, [blocks for _, _, blocks in parts]),
        grid=(at,),
        in_specs=specs,
        out_specs=pl.BlockSpec((rows, 256), lambda i: (0, i)),
        out_shape=jax.ShapeDtypeStruct((rows, 256 * at), f32),
        compiler_params=pltpu.CompilerParams(vmem_limit_bytes=32 * 2**20),
        name="unpack",
    )(*[units for units, _, _ in parts])


def rms_scale(values, gains):
    inverse = lax.rsqrt(jnp.mean(values * values, axis=-1, keepdims=True) + EPS)
    return values * inverse * gains


def swiglu(gate_up):
    return jax.nn.silu(gate_up[:, :FF]) * gate_up[:, FF:]


def local(tokens, cotangent, skip_table, gain_attn, w_attn, w_heads, forget_bias, query_gain, key_gain,
          w_out, gain_ffn, w_gate_up, w_down):
    count = lax.axis_size("seq")
    me = lax.axis_index("seq")
    rows = tokens.shape[1]
    both = ("seq", "group")
    inputs = tokens[0].astype(f32)
    device = me.astype(jnp.int32)[None]
    head = first_head(me, count)
    skip = skip_table[0]
    gains = jnp.stack([query_gain.reshape(HEADS, HDIM), key_gain.reshape(HEADS, HDIM)], 2)
    gains = lax.dynamic_slice_in_dim(gains, head, 2, 0)
    bias = lax.dynamic_slice_in_dim(forget_bias, head, 2, 0)
    w_small = jnp.pad(w_heads.reshape(D, 3, HEADS).transpose(0, 2, 1), ((0, 0), (0, 0), (0, 5))).reshape(D, HEADS * 8)

    normed_attn, norm_back_attn = jax.vjp(rms_scale, inputs, gain_attn)
    h_first = normed_attn.astype(bf16)
    qkv = dot(w_attn[:, : 3 * D], h_first, 0, 1).astype(bf16).reshape(3, HEADS, HDIM, rows)
    gate_logit = dot(w_attn[:, 3 * D :], h_first, 0, 1)
    logits_here = dot(w_small, h_first, 0, 1).reshape(HEADS, 8, rows)

    raw, logits = heads_out(qkv, logits_here, count)
    mixed_low, mixed, q, k, kt, vt = attend_forward(device, skip, bias, raw, logits, gains)
    attended = mixed_back(mixed_low, count).reshape(D, rows).astype(f32)

    gate_open = jax.nn.sigmoid(gate_logit)
    gated = (gate_open * attended).astype(bf16)
    resid = inputs + dot(gated, w_out, 0, 0)
    normed_ffn, norm_back_ffn = jax.vjp(rms_scale, resid, gain_ffn)
    h_second = normed_ffn.astype(bf16)
    gate_up = dot(h_second, w_gate_up, 1, 0)
    hidden, hidden_back = jax.vjp(swiglu, gate_up)
    hidden_low = hidden.astype(bf16)
    output = resid + dot(hidden_low, w_down, 1, 0)
    d_low = cotangent[0]
    d_output = d_low.astype(f32)
    (d_gate_up,) = hidden_back(dot(d_low, w_down, 1, 1))
    d_gate_low = d_gate_up.astype(bf16)
    d_resid_norm, grad_gain_ffn = norm_back_ffn(dot(d_gate_low, w_gate_up, 1, 1))
    d_resid = d_output + d_resid_norm
    d_branch = d_resid.astype(bf16)
    d_gated = dot(w_out, d_branch, 1, 1)
    d_gate_logit = (d_gated * attended * gate_open * (1.0 - gate_open)).astype(bf16)
    d_mixed = (d_gated * gate_open).astype(bf16).reshape(HEADS, HDIM, rows)

    near_far, seq_bits = group_bits(lax.axis_size("group"), count)
    sets = (near_far[0], near_far[1], seq_bits)
    units = padded(1440, 1 << (2 + len(seq_bits)))
    d_mixed_all, early = grads_out(
        count, units, d_mixed, h_first, d_gate_logit, h_second, d_gate_low, hidden_low, d_low, gated, d_branch
    )
    d_raw, d_logits, d_gains = attend_backward(device, skip, bias, raw, logits, gains, d_mixed_all, mixed, q, k, kt, vt)

    placed = jnp.zeros((HEADS, HDIM, 2), f32)
    placed = lax.dynamic_update_slice(placed, d_gains, (head, 0, 0)).reshape(D, 2).T
    extra = jnp.concatenate([jnp.zeros((1, D), f32), grad_gain_ffn[None], placed, jnp.zeros((SMALL - 3 * HEADS - 4, D), f32)], 0)
    late, early, d_inputs = last(
        count, sets, d_raw, d_logits, early, h_first, d_gate_logit, w_attn, w_small, tokens[0], gain_attn[None], d_resid, extra
    )
    row = 3 * HEADS
    used = 9 * (D // UNIT)
    small = late[used : used + 9].reshape(3, SMALL, 256).transpose(1, 0, 2).reshape(SMALL, D).astype(f32)
    return (
        output[None].astype(bf16),
        d_inputs[None],
        small[row],
        unpack(D, (late, 0, 9), (early, 27, 3)),
        small[:row].reshape(HEADS, 3, D).transpose(2, 1, 0).reshape(D, row),
        small[row + 4, :HEADS],
        small[row + 2],
        small[row + 3],
        unpack(D, (early, 24, 3)),
        small[row + 1],
        unpack(D, (early, 0, 16)),
        unpack(FF, (early, 6, 3)),
    )


def solution(mesh):
    rows = P("group", "seq", None)
    return jax.shard_map(
        local,
        mesh=mesh,
        in_specs=(rows, rows, P("group", None, None)) + (P(),) * 10,
        out_specs=(rows, rows) + (P(),) * 10,
        check_vma=False,
    )
```

```python
import functools

import jax
import jax.numpy as jnp
from jax import lax
from jax.experimental import pallas as pl
from jax.experimental.pallas import tpu as pltpu
from jax.sharding import PartitionSpec as P

D, FF = 768, 2048
MESH = pl.DeviceIdType.MESH
ANY = pl.BlockSpec(memory_space=pl.ANY)

HEADS, HDIM, BLK = 12, 64, 256
EPS = 1e-06
LOG2E = 1.4426950408889634
LN2 = 0.6931471805599453
SCORE = HDIM ** -0.5
f32, bf16 = jnp.float32, jnp.bfloat16
UNROLL = 8
UNROLL_BACK = 4
NN = (((1,), (0,)), ((), ()))
NT = (((1,), (1,)), ((), ()))
TN = (((0,), (0,)), ((), ()))


def mm(a, b, dims=NN):
    return lax.dot_general(a, b, dims, preferred_element_type=f32)


def split3(v):
    hi = v.astype(bf16).astype(f32)
    rest = v - hi
    mid = rest.astype(bf16).astype(f32)
    return hi, mid, rest - mid


def place_of(block, count):
    return jnp.where(block < count, block, 2 * count - 1 - block)


def lanes_of(block, count):
    return pl.ds(pl.multiple_of(jnp.where(block < count, 0, BLK), BLK), BLK)


def first_head(device, count):
    return jnp.minimum(HEADS * device // count, HEADS - 2)


def is_mine(device, slot, place, count):
    chunk = (first_head(device, count) + slot) * count + place
    return (chunk >= HEADS * device) & (chunk < HEADS * device + HEADS)


def list_pairs(skip_ref, pairs_ref, own_ref, device, slot, count, unroll):
    spare = 2 * count

    def row(number, found):
        def column(other, found):
            pairs_ref[found] = number * 1024 + other
            return found + jnp.where(skip_ref[number, other] == 0, 1, 0)

        mine = is_mine(device, slot, place_of(number, count), count)
        own_ref[found[1]] = number
        below = lax.fori_loop(0, jnp.where(mine, number, 0), column, found[0])
        return below, found[1] + jnp.where(mine, 1, 0)

    below, own = lax.fori_loop(0, spare, row, (0, 0))
    for extra in range(unroll):
        pairs_ref[below + extra] = spare * 1024
        own_ref[own + extra] = spare
    return pl.cdiv(below, unroll), pl.cdiv(own, unroll)


def running_sum(values, count, reverse):
    t = lax.broadcasted_iota(jnp.int32, (BLK, BLK), 0)
    p = lax.broadcasted_iota(jnp.int32, (BLK, BLK), 1)
    ones = jnp.where(t >= p if reverse else t <= p, 1.0, 0.0).astype(bf16)
    halves = []
    for half in range(2):
        part = values[:, half * BLK : (half + 1) * BLK]
        halves.append(sum(mm(piece.astype(bf16), ones) for piece in split3(part)))
    edge = 0 if reverse else BLK - 1
    first, last = (jnp.broadcast_to(h[:, edge : edge + 1], (count, 128)) for h in halves)
    rows = lax.broadcasted_iota(jnp.int32, (count, 128), 0)

    def scan(total, down):
        own = total
        step = 1
        while step < count:
            moved = pltpu.roll(total, step if down else count - step, 0)
            total = total + jnp.where(rows >= step if down else rows < count - step, moved, 0.0)
            step *= 2
        return total - own

    if reverse:
        all_last = jnp.sum(last, axis=0, keepdims=True)
        offsets = scan(first, False) + all_last, scan(last, True)
    else:
        all_first = jnp.sum(first, axis=0, keepdims=True)
        offsets = scan(first, True), scan(last, False) + all_first
    return jnp.concatenate([halves[0] + offsets[0][:, :1], halves[1] + offsets[1][:, :1]], 1)


def shifted(current, before):
    lane = lax.broadcasted_iota(jnp.int32, current.shape, 1)
    return jnp.where(lane == 0, pltpu.roll(before, 1, 1), pltpu.roll(current, 1, 1))


def shifted_back(current, after):
    lane = lax.broadcasted_iota(jnp.int32, current.shape, 1)
    return jnp.where(lane == BLK - 1, pltpu.roll(after, BLK - 1, 1), pltpu.roll(current, BLK - 1, 1))


def stack_rows(top, rows, size):
    extra = size if top is None else size - top.shape[0]
    number = lax.broadcasted_iota(jnp.int32, (extra, BLK), 0)
    bottom = jnp.zeros((extra, BLK), f32)
    for i, r in enumerate(rows):
        bottom = jnp.where(number == i, r, bottom)
    return bottom if top is None else jnp.concatenate([top, bottom], 0)


def prepare_block(count, block, carried, raw_ref, logit_ref, gain_ref, cum_ref, q_ref, k_ref, kt_ref, vt_ref):
    place, lanes = place_of(block, count), lanes_of(block, count)
    q_raw, k_raw, v_raw = (raw_ref[place, i, :, lanes].astype(f32) for i in range(3))
    cum = cum_ref[pl.ds(place, 1), lanes]
    parts = split3(cum)
    one = jnp.ones_like(cum)
    query = q_raw * lax.rsqrt(jnp.mean(q_raw * q_raw, 0, keepdims=True) + EPS) * (gain_ref[:, 0:1] * (SCORE * LOG2E))
    q_ref[block] = stack_rows(query, (*parts, one, one, one), 128).astype(bf16)
    rate_k = jax.nn.sigmoid(logit_ref[place, 1:2, lanes])
    rate_v = jax.nn.sigmoid(logit_ref[place, 2:3, lanes])
    key = k_raw + rate_k * (shifted(k_raw, carried[0]) - k_raw)
    key = key * lax.rsqrt(jnp.mean(key * key, 0, keepdims=True) + EPS) * gain_ref[:, 1:2]
    value = v_raw + rate_v * (shifted(v_raw, carried[1]) - v_raw)
    k_ref[block] = stack_rows(key, (one, one, one, *(-c for c in parts)), 128).T.astype(bf16)
    kt_ref[block] = stack_rows(key, (one,), 80).astype(bf16)
    vt_ref[block] = stack_rows(value, (one, one, one), 80).astype(bf16)
    return k_raw, v_raw


def finish_block(count, block, acc_ref, cum_ref, mixed_full_ref, mixed_ref, q_ref):
    place, lanes = place_of(block, count), lanes_of(block, count)
    summed = acc_ref[block]
    norm = summed[HDIM : HDIM + 1]
    mixed = summed[:HDIM] * (1.0 / norm)
    mixed_full_ref[block] = mixed
    mixed_ref[place, :, lanes] = mixed.astype(bf16)
    parts = split3(cum_ref[pl.ds(place, 1), lanes] - jnp.log2(norm))
    one = jnp.ones_like(norm)
    q_ref[block, HDIM : HDIM + 16, :] = stack_rows(None, (*parts, one, one, one), 16).astype(bf16)


def log_forget_sums(logits, count):
    log_forget = jnp.minimum(logits, 0.0) - jnp.log1p(jnp.exp(-jnp.abs(logits)))
    return running_sum(log_forget, count, False) * LOG2E


def causal():
    return lax.broadcasted_iota(jnp.int32, (BLK, BLK), 0) <= lax.broadcasted_iota(jnp.int32, (BLK, BLK), 1)


def forward_kernel(count, device_ref, skip_ref, bias_ref, raw_ref, logit_ref, gain_ref,
                   mixed_ref, mixed_full_ref, q_ref, k_ref, kt_ref, vt_ref,
                   cum_ref, acc_ref, pairs_ref, own_ref):
    slot = pl.program_id(0)
    device = device_ref[0]
    blocks = 2 * count
    pair_steps, own_steps = list_pairs(skip_ref, pairs_ref, own_ref, device, slot, count, UNROLL)
    cum_ref[...] = log_forget_sums(logit_ref[:, 0, :] + bias_ref[slot], count)

    def prepare(block, carried):
        return prepare_block(count, block, carried, raw_ref, logit_ref, gain_ref, cum_ref, q_ref, k_ref, kt_ref, vt_ref)

    zero = jnp.zeros((HDIM, BLK), f32)
    lax.fori_loop(0, blocks, prepare, (zero, zero))
    q_ref[blocks] = jnp.zeros(q_ref.shape[1:], bf16)

    def together(pairs, diagonal):
        scores = [mm(k_ref[column], q_ref[row]) for row, column in pairs]
        weights = [jnp.exp2(score) for score in scores]
        if diagonal:
            weights = [jnp.where(causal(), weight, 0.0) for weight in weights]
        weights = [weight.astype(bf16) for weight in weights]
        parts = [mm(vt_ref[column], weight) for (row, column), weight in zip(pairs, weights)]
        for (row, column), part in zip(pairs, parts):
            acc_ref[row] = part if diagonal else acc_ref[row] + part

    def own_rows(step, carried):
        rows = [own_ref[step * UNROLL + i] for i in range(UNROLL)]
        together([(row, jnp.minimum(row, blocks - 1)) for row in rows], True)
        return carried

    def kept_pairs(step, carried):
        codes = [pairs_ref[step * UNROLL + i] for i in range(UNROLL)]
        together([(code >> 10, code & 1023) for code in codes], False)
        return carried

    lax.fori_loop(0, own_steps, own_rows, 0)
    lax.fori_loop(0, pair_steps, kept_pairs, 0)

    def finish(block, carried):
        finish_block(count, block, acc_ref, cum_ref, mixed_full_ref, mixed_ref, q_ref)
        return carried

    lax.fori_loop(0, blocks, finish, 0)


def own_places(device, slot, count):
    start = (first_head(device, count) + slot) * count
    low = jnp.clip(HEADS * device - start, 0, count)
    return low, jnp.clip(HEADS * device + HEADS - start, low, count)


def pairs_of_place(place, batch, size, count):
    found = []
    for i in range(size):
        number = batch * size + i
        lower = number < place
        found.append((jnp.where(lower, place, 2 * count - 1 - place), jnp.where(lower, number, number - place)))
    return found


def keep_factor(skip_ref, row, column):
    return jnp.where(skip_ref[row, column] == 0, 1.0, 0.0)


def buffers(count):
    return pl.Buffered(1 if count > 8 else 2)


def attend_forward(device, skip, bias, raw, logits, gains):
    count = raw.shape[0]
    blocks = 2 * count
    most = blocks * (blocks - 1) // 2 + UNROLL
    mode = buffers(count)
    by_slot = lambda *shape: pl.BlockSpec((None,) + shape, lambda s, *_: (s,) + (0,) * len(shape), pipeline_mode=mode)
    out = lambda shape, dtype: jax.ShapeDtypeStruct((2,) + shape, dtype)
    return pl.pallas_call(
        functools.partial(forward_kernel, count),
        grid_spec=pltpu.PrefetchScalarGridSpec(
            num_scalar_prefetch=3,
            grid=(2,),
            in_specs=[
                pl.BlockSpec((count, 3, None, HDIM, 2 * BLK), lambda s, *_: (0, 0, s, 0, 0), pipeline_mode=mode),
                pl.BlockSpec((count, None, 8, 2 * BLK), lambda s, *_: (0, s, 0, 0), pipeline_mode=mode),
                by_slot(HDIM, 2),
            ],
            out_specs=[
                by_slot(count, HDIM, 2 * BLK),
                by_slot(blocks, HDIM, BLK),
                by_slot(blocks + 1, 128, BLK),
                by_slot(blocks, BLK, 128),
                by_slot(blocks, 80, BLK),
                by_slot(blocks, 80, BLK),
            ],
            scratch_shapes=[
                pltpu.VMEM((count, 2 * BLK), f32),
                pltpu.VMEM((blocks + 1, 80, BLK), f32),
                pltpu.SMEM((most,), jnp.int32),
                pltpu.SMEM((blocks + UNROLL,), jnp.int32),
            ],
        ),
        out_shape=[
            out((count, HDIM, 2 * BLK), bf16),
            out((blocks, HDIM, BLK), f32),
            out((blocks + 1, 128, BLK), bf16),
            out((blocks, BLK, 128), bf16),
            out((blocks, 80, BLK), bf16),
            out((blocks, 80, BLK), bf16),
        ],
        compiler_params=pltpu.CompilerParams(vmem_limit_bytes=60 * 2**20),
        name="attend_forward",
    )(device, skip, bias, raw, logits, gains)


def norm_back(v, gain, u):
    scale = lax.rsqrt(jnp.mean(v * v, 0, keepdims=True) + EPS)
    hat = v * scale
    gu = gain * u
    return scale * (gu - hat * jnp.mean(hat * gu, 0, keepdims=True)), hat * u


def backward_kernel(count, device_ref, skip_ref, bias_ref, raw_ref, logit_ref, gain_ref, dmixed_ref, mixed_ref,
                    q_ref, k_ref, kt_ref, vt_ref, draw_ref, dlogit_ref, dgain_ref,
                    do_ref, v_ref, cum_ref, dq_ref, dk_ref, dv_ref, pairs_ref, own_ref):
    slot = pl.program_id(0)
    device = device_ref[0]
    blocks = 2 * count
    pair_steps, own_steps = list_pairs(skip_ref, pairs_ref, own_ref, device, slot, count, UNROLL_BACK)
    gain_q, gain_k = gain_ref[:, 0:1], gain_ref[:, 1:2]
    wide = jnp.zeros((128 - 80, BLK), f32)

    def prepare(block, carried):
        place, lanes = place_of(block, count), lanes_of(block, count)
        d_out = dmixed_ref[place, :, lanes].astype(f32)
        delta = jnp.sum(d_out * mixed_ref[block], 0, keepdims=True)
        do_ref[block] = stack_rows(d_out, [-d for d in split3(delta)], 128).astype(bf16)
        v_ref[block] = jnp.concatenate([vt_ref[block].astype(f32), wide], 0).T.astype(bf16)
        dq_ref[block] = jnp.zeros(dq_ref.shape[1:], f32)
        dk_ref[block] = jnp.zeros(dk_ref.shape[1:], f32)
        dv_ref[block] = jnp.zeros(dv_ref.shape[1:], f32)
        return carried

    lax.fori_loop(0, blocks, prepare, 0)
    do_ref[blocks] = jnp.zeros(do_ref.shape[1:], bf16)
    dq_ref[blocks] = jnp.zeros(dq_ref.shape[1:], f32)

    def together(pairs, diagonal):
        scores = [mm(k_ref[column], q_ref[row]) for row, column in pairs]
        weights = [jnp.exp2(score) for score in scores]
        if diagonal:
            weights = [jnp.where(causal(), weight, 0.0) for weight in weights]
        d_weights = [mm(v_ref[column], do_ref[row]) for row, column in pairs]
        low_weights = [weight.astype(bf16) for weight in weights]
        d_scores = [(weight * d_weight).astype(bf16) for weight, d_weight in zip(weights, d_weights)]
        parts = [mm(do_ref[row, :HDIM], weight, NT) for (row, _), weight in zip(pairs, low_weights)]
        for (_, column), part in zip(pairs, parts):
            dv_ref[column] += part
        parts = [mm(kt_ref[column], d_score) for (_, column), d_score in zip(pairs, d_scores)]
        for (row, _), part in zip(pairs, parts):
            dq_ref[row] += part
        parts = [mm(q_ref[row, :80], d_score, NT) for (row, _), d_score in zip(pairs, d_scores)]
        for (_, column), part in zip(pairs, parts):
            dk_ref[column] += part

    def own_rows(step, carried):
        rows = [own_ref[step * UNROLL_BACK + i] for i in range(UNROLL_BACK)]
        together([(row, jnp.minimum(row, blocks - 1)) for row in rows], True)
        return carried

    def kept_pairs(step, carried):
        codes = [pairs_ref[step * UNROLL_BACK + i] for i in range(UNROLL_BACK)]
        together([(code >> 10, code & 1023) for code in codes], False)
        return carried

    lax.fori_loop(0, own_steps, own_rows, 0)
    lax.fori_loop(0, pair_steps, kept_pairs, 0)

    def finish(step, carried):
        next_k, next_v, sum_q, sum_k = carried
        block = blocks - 1 - step
        place, lanes = place_of(block, count), lanes_of(block, count)
        earlier = jnp.maximum(block - 1, 0)
        place_before, lanes_before = place_of(earlier, count), lanes_of(earlier, count)
        exists = jnp.where(block > 0, 1.0, 0.0)
        q_raw, k_raw, v_raw = (raw_ref[place, i, :, lanes].astype(f32) for i in range(3))
        k_step = shifted(k_raw, raw_ref[place_before, 1, :, lanes_before].astype(f32) * exists) - k_raw
        v_step = shifted(v_raw, raw_ref[place_before, 2, :, lanes_before].astype(f32) * exists) - v_raw
        rate_k = jax.nn.sigmoid(logit_ref[place, 1:2, lanes])
        rate_v = jax.nn.sigmoid(logit_ref[place, 2:3, lanes])
        dq, dk, dv = dq_ref[block], dk_ref[block], dv_ref[block]
        dq_raw, part_q = norm_back(q_raw, gain_q, dq[:HDIM] * SCORE)
        dk_mixed, part_k = norm_back(k_raw + rate_k * k_step, gain_k, dk[:HDIM] * LN2)
        send_k, send_v = rate_k * dk_mixed, rate_v * dv
        draw_ref[place, 0, :, lanes] = dq_raw.astype(bf16)
        draw_ref[place, 1, :, lanes] = (dk_mixed - send_k + shifted_back(send_k, next_k)).astype(bf16)
        draw_ref[place, 2, :, lanes] = (dv - send_v + shifted_back(send_v, next_v)).astype(bf16)
        dlogit_ref[place, 1:2, lanes] = (1.0 - rate_k) * jnp.sum(k_step * send_k, 0, keepdims=True)
        dlogit_ref[place, 2:3, lanes] = (1.0 - rate_v) * jnp.sum(v_step * send_v, 0, keepdims=True)
        cum_ref[pl.ds(place, 1), lanes] = dq[HDIM : HDIM + 1] - dk[HDIM + 3 : HDIM + 4]
        part_q = jnp.where(is_mine(device, slot, place, count), part_q, 0.0)
        return send_k, send_v, sum_q + part_q, sum_k + part_k

    zero = jnp.zeros((HDIM, BLK), f32)
    _, _, sum_q, sum_k = lax.fori_loop(0, blocks, finish, (zero, zero, zero, zero))
    dgain_ref[:, 0:1] = jnp.sum(sum_q, 1, keepdims=True)
    dgain_ref[:, 1:2] = jnp.sum(sum_k, 1, keepdims=True)
    d_log = running_sum(cum_ref[...], count, True)
    dlogit_ref[:, 0, :] = d_log * jax.nn.sigmoid(-(logit_ref[:, 0, :] + bias_ref[slot]))
    dlogit_ref[:, 3:, :] = jnp.zeros((count, 5, 2 * BLK), f32)


def attend_backward(device, skip, bias, raw, logits, gains, dmixed, mixed, q, k, kt, vt):
    count = raw.shape[0]
    blocks = 2 * count
    most = blocks * (blocks - 1) // 2 + UNROLL_BACK
    mode = buffers(count)
    by_slot = lambda *shape: pl.BlockSpec((None,) + shape, lambda s, *_: (s,) + (0,) * len(shape), pipeline_mode=mode)
    raw_spec = pl.BlockSpec((count, 3, None, HDIM, 2 * BLK), lambda s, *_: (0, 0, s, 0, 0), pipeline_mode=mode)
    place_spec = lambda rows: pl.BlockSpec((count, None, rows, 2 * BLK), lambda s, *_: (0, s, 0, 0), pipeline_mode=mode)
    return pl.pallas_call(
        functools.partial(backward_kernel, count),
        grid_spec=pltpu.PrefetchScalarGridSpec(
            num_scalar_prefetch=3,
            grid=(2,),
            in_specs=[
                raw_spec,
                place_spec(8),
                by_slot(HDIM, 2),
                place_spec(HDIM),
                by_slot(blocks, HDIM, BLK),
                by_slot(blocks + 1, 128, BLK),
                by_slot(blocks, BLK, 128),
                by_slot(blocks, 80, BLK),
                by_slot(blocks, 80, BLK),
            ],
            out_specs=[raw_spec, place_spec(8), by_slot(HDIM, 2)],
            scratch_shapes=[
                pltpu.VMEM((blocks + 1, 128, BLK), bf16),
                pltpu.VMEM((blocks, BLK, 128), bf16),
                pltpu.VMEM((count, 2 * BLK), f32),
                pltpu.VMEM((blocks + 1, 80, BLK), f32),
                pltpu.VMEM((blocks, 80, BLK), f32),
                pltpu.VMEM((blocks, HDIM, BLK), f32),
                pltpu.SMEM((most,), jnp.int32),
                pltpu.SMEM((blocks + UNROLL_BACK,), jnp.int32),
            ],
        ),
        out_shape=[
            jax.ShapeDtypeStruct(raw.shape, bf16),
            jax.ShapeDtypeStruct(logits.shape, f32),
            jax.ShapeDtypeStruct(gains.shape, f32),
        ],
        compiler_params=pltpu.CompilerParams(vmem_limit_bytes=60 * 2**20),
        name="attend_backward",
    )(device, skip, bias, raw, logits, gains, dmixed, mixed, q, k, kt, vt)


def holder(head, place, count):
    return (head * count + place) // HEADS


def greet(count):
    me = lax.axis_index("seq")
    barrier = pltpu.get_barrier_semaphore()
    for k in range(1, count):
        peer = lax.rem(me + k, count)
        pl.semaphore_signal(barrier, inc=1, device_id={"seq": peer}, device_id_type=MESH)
    pl.semaphore_wait(barrier, count - 1)
    return me


def far_first(count):
    return sorted(range(1, count), key=lambda k: -min(k, count - k))


def push(src, dst, send, recv, peer):
    return pltpu.make_async_remote_copy(
        src_ref=src, dst_ref=dst, send_sem=send, recv_sem=recv, device_id={"seq": peer}, device_id_type=MESH
    )


def heads_out_kernel(count, x_ref, logit_in, raw_ref, logit_ref, send, recv, local):
    me = greet(count)

    def copies(peer, source, k):
        head = first_head(peer, count)
        items = []
        for slot in range(2):
            items.append((is_mine(peer, slot, me, count), is_mine(me, slot, source, count),
                          push(x_ref.at[0, head + slot], raw_ref.at[me, 0, slot], send.at[k, slot], recv.at[k, slot], peer)))
        items.append((None, None, push(x_ref.at[pl.ds(1, 2), pl.ds(head, 2)], raw_ref.at[me, pl.ds(1, 2)], send.at[k, 2], recv.at[k, 2], peer)))
        items.append((None, None, push(logit_in.at[pl.ds(head, 2)], logit_ref.at[me], send.at[k, 3], recv.at[k, 3], peer)))
        return items

    every = []
    for k in far_first(count):
        items = copies(lax.rem(me + k, count), lax.rem(me + count - k, count), k)
        every.append(items)
        for out, _, copy in items:
            if out is None:
                copy.start()
            else:
                pl.when(out)(copy.start)
    head = first_head(me, count)
    own = [
        pltpu.make_async_copy(x_ref.at[:, pl.ds(head, 2)], raw_ref.at[me], local.at[0]),
        pltpu.make_async_copy(logit_in.at[pl.ds(head, 2)], logit_ref.at[me], local.at[1]),
    ]
    for copy in own:
        copy.start()
    for items in every:
        for out, into, copy in items:
            if out is None:
                copy.wait()
            else:
                pl.when(out)(copy.wait_send)
                pl.when(into)(copy.wait_recv)
    for copy in own:
        copy.wait()


def heads_out(qkv, logits, count):
    return pl.pallas_call(
        functools.partial(heads_out_kernel, count),
        out_shape=[
            jax.ShapeDtypeStruct((count, 3, 2, HDIM, 2 * BLK), bf16),
            jax.ShapeDtypeStruct((count, 2, 8, 2 * BLK), f32),
        ],
        in_specs=[ANY, ANY],
        out_specs=[ANY, ANY],
        scratch_shapes=[pltpu.SemaphoreType.DMA((count, 4)), pltpu.SemaphoreType.DMA((count, 4)), pltpu.SemaphoreType.DMA((2,))],
        compiler_params=pltpu.CompilerParams(collective_id=0, has_side_effects=True),
        name="heads_out",
    )(qkv, logits)


def mixed_back_kernel(count, x_ref, o_ref, send, recv, local):
    me = greet(count)
    first = first_head(me, count)
    started = []
    for k in far_first(count) + [0]:
        peer = lax.rem(me + k, count)
        for slot in range(2):
            mine = is_mine(me, slot, peer, count)
            src, dst = x_ref.at[slot, peer], o_ref.at[first + slot]
            if k:
                copy = push(src, dst, send.at[k, slot], recv.at[first + slot], peer)
            else:
                copy = pltpu.make_async_copy(src, dst, local.at[slot])
            started.append((mine, k, copy))
            pl.when(mine)(copy.start)
    for mine, k, copy in started:
        pl.when(mine)(copy.wait_send if k else copy.wait)
    for head in range(HEADS):
        source = holder(head, me, count)
        copy = push(x_ref.at[0, 0], o_ref.at[head], send.at[0, 0], recv.at[head], lax.rem(me + 1, count))
        pl.when(source != me)(copy.wait_recv)


def mixed_back(mixed, count):
    return pl.pallas_call(
        functools.partial(mixed_back_kernel, count),
        out_shape=jax.ShapeDtypeStruct((HEADS, HDIM, 2 * BLK), bf16),
        in_specs=[ANY],
        out_specs=ANY,
        scratch_shapes=[pltpu.SemaphoreType.DMA((count, 2)), pltpu.SemaphoreType.DMA((HEADS,)), pltpu.SemaphoreType.DMA((2,))],
        compiler_params=pltpu.CompilerParams(collective_id=1, has_side_effects=True),
        name="mixed_back",
    )(mixed)


def grads_out_kernel(count, x_ref, h1_ref, dgate_ref, h2_ref, dgu_ref, hidden_ref, dlow_ref, gated_ref, branch_ref,
                     o_ref, grads_ref, send, recv, local):
    me = greet(count)
    started = []
    for head in range(HEADS):
        peer = holder(head, me, count)
        slot = head - first_head(peer, count)
        away = peer != me
        there = jnp.where(away, peer, lax.rem(me + 1, count))
        copy = push(x_ref.at[head], o_ref.at[me, slot], send.at[head], recv.at[me, slot], there)
        own = pltpu.make_async_copy(x_ref.at[head], o_ref.at[me, slot], local.at[slot])
        pl.when(away)(copy.start)
        pl.when(peer == me)(own.start)
        started.append((away, peer == me, copy, own))

    def put(unit, part):
        grads_ref[pl.ds(unit, 16)] = part.astype(bf16).reshape(16, UNIT, 256)

    def gate_up(i, carried):
        right = dgu_ref[:, pl.ds(pl.multiple_of(i * 256, 256), 256)]
        for j in range(3):
            put(i * 48 + 16 * j, mm(h2_ref[:, 256 * j : 256 * j + 256], right, TN))
        return carried

    lax.fori_loop(0, 2 * FF // 256, gate_up, 0)

    def down(i, carried):
        left = hidden_ref[:, pl.ds(pl.multiple_of(i * 256, 256), 256)]
        for j in range(3):
            put(768 + 128 * j + 16 * i, mm(left, dlow_ref[:, 256 * j : 256 * j + 256], TN))
        return carried

    lax.fori_loop(0, FF // 256, down, 0)
    for i in range(3):
        for j in range(3):
            put(1152 + 48 * i + 16 * j, mm(gated_ref[256 * j : 256 * j + 256, :], branch_ref[:, 256 * i : 256 * i + 256]))
            put(1296 + 48 * i + 16 * j, lax.dot_general(
                h1_ref[:, 256 * j : 256 * j + 256], dgate_ref[256 * i : 256 * i + 256, :],
                (((0,), (1,)), ((), ())), preferred_element_type=f32))
    units = grads_ref.shape[0]
    if units > 1440:
        grads_ref[1440:] = jnp.zeros((units - 1440, UNIT, 256), bf16)

    for away, here, copy, own in started:
        pl.when(away)(copy.wait_send)
        pl.when(here)(own.wait)
    for k in range(1, count):
        source = lax.rem(me + k, count)
        for slot in range(2):
            copy = push(x_ref.at[0], o_ref.at[source, slot], send.at[0], recv.at[source, slot], source)
            pl.when(is_mine(me, slot, source, count))(copy.wait_recv)


def grads_out(count, units, d_mixed, *operands):
    vmem = pl.BlockSpec(memory_space=pltpu.VMEM)
    return pl.pallas_call(
        functools.partial(grads_out_kernel, count),
        out_shape=[
            jax.ShapeDtypeStruct((count, 2, HDIM, 2 * BLK), bf16),
            jax.ShapeDtypeStruct((units, UNIT, 256), bf16),
        ],
        in_specs=[ANY] + [vmem] * 8,
        out_specs=[ANY, vmem],
        scratch_shapes=[pltpu.SemaphoreType.DMA((HEADS,)), pltpu.SemaphoreType.DMA((count, 2)), pltpu.SemaphoreType.DMA((2,))],
        compiler_params=pltpu.CompilerParams(collective_id=2, has_side_effects=True, vmem_limit_bytes=60 * 2**20),
        name="grads_out",
    )(d_mixed, *operands)


def dot(a, b, i, j):
    return lax.dot_general(a, b, (((i,), (j,)), ((), ())), preferred_element_type=f32)


def front_kernel(count, skip_ref, bias_ref, x_ref, w_ref, wsmall_ref, gain_ref, gains_ref,
                 h_ref, gate_ref, att_ref, raw_out, logit_out, full_out, q_out, k_out, kt_out, vt_out,
                 ht_ref, proj_ref, small_ref, raw_ref, logit_ref, mixed_ref, full_ref, q_ref, k_ref, kt_ref, vt_ref, cum_ref, acc_ref,
                 send, recv, own, back_send, back_recv, back_own, keep):
    me = lax.axis_index("seq")
    barrier = pltpu.get_barrier_semaphore()
    for k in range(1, count):
        pl.semaphore_signal(barrier, inc=1, device_id={"seq": lax.rem(me + k, count)}, device_id_type=MESH)
    blocks = 2 * count
    rows = x_ref.shape[0]
    for i in range(rows // 128):
        here = slice(128 * i, 128 * i + 128)
        v = x_ref[here].astype(f32)
        normed = v * lax.rsqrt(jnp.mean(v * v, 1, keepdims=True) + EPS) * gain_ref[...]
        h_ref[here] = normed.astype(bf16)
        ht_ref[:, here] = normed.T.astype(bf16)

    def project(i, carried):
        block = mm(w_ref[:, pl.ds(pl.multiple_of(256 * i, 256), 256)], ht_ref[...], TN)
        proj_ref[pl.ds(4 * i, 4)] = block.astype(bf16).reshape(4, HDIM, rows)
        return carried

    small_ref[...] = mm(wsmall_ref[...], ht_ref[...], TN).reshape(HEADS, 8, rows)
    lax.fori_loop(0, 9, project, 0)
    pl.semaphore_wait(barrier, count - 1)
    first = first_head(me, count)

    def out(slot, k, peer):
        head = first_head(peer, count) + slot
        sems = lambda i: (send.at[k, slot, i], recv.at[k, slot, i], peer)
        return [
            push(proj_ref.at[head], raw_ref.at[me, 0, slot], *sems(0)),
            push(proj_ref.at[HEADS + head], raw_ref.at[me, 1, slot], *sems(1)),
            push(proj_ref.at[2 * HEADS + head], raw_ref.at[me, 2, slot], *sems(2)),
            push(small_ref.at[head], logit_ref.at[me, slot], *sems(3)),
        ]

    def own_copies(slot):
        head = first + slot
        return [
            pltpu.make_async_copy(proj_ref.at[head], raw_ref.at[me, 0, slot], own.at[slot, 0]),
            pltpu.make_async_copy(proj_ref.at[HEADS + head], raw_ref.at[me, 1, slot], own.at[slot, 1]),
            pltpu.make_async_copy(proj_ref.at[2 * HEADS + head], raw_ref.at[me, 2, slot], own.at[slot, 2]),
            pltpu.make_async_copy(small_ref.at[head], logit_ref.at[me, slot], own.at[slot, 3]),
        ]

    for slot in range(2):
        for k in far_first(count):
            peer = lax.rem(me + k, count)
            copies = out(slot, k, peer)
            pl.when(is_mine(peer, slot, me, count))(copies[0].start)
            for copy in copies[1:]:
                copy.start()
        for copy in own_copies(slot):
            copy.start()

    def gate(i, carried):
        here = pl.ds(pl.multiple_of(256 * i, 256), 256)
        gate_ref[here] = mm(w_ref[:, pl.ds(pl.multiple_of(3 * D + 256 * i, 256), 256)], ht_ref[...], TN)
        return carried

    lax.fori_loop(0, 3, gate, 0)

    def saved(slot):
        return [
            pltpu.make_async_copy(src.at[slot], dst.at[slot], keep.at[slot, i])
            for i, (src, dst) in enumerate(
                ((full_ref, full_out), (q_ref, q_out), (k_ref, k_out), (kt_ref, kt_out), (vt_ref, vt_out)))
        ]

    def back(slot, k, peer):
        target = att_ref.at[pl.ds(pl.multiple_of((first + slot) * HDIM, HDIM), HDIM)]
        if k:
            return push(mixed_ref.at[slot, peer], target, back_send.at[k, slot], back_recv.at[first + slot], peer)
        return pltpu.make_async_copy(mixed_ref.at[slot, peer], target, back_own.at[slot])

    def one_slot(slot, carried):
        for copy in own_copies(slot):
            copy.wait()
        for k in far_first(count):
            source = lax.rem(me + count - k, count)
            copies = out(slot, k, source)
            pl.when(is_mine(me, slot, source, count))(copies[0].wait_recv)
            for copy in copies[1:]:
                copy.wait_recv()
        raws, logits, gains = raw_ref.at[:, :, slot], logit_ref.at[:, slot], gains_ref.at[slot]
        qs, ks, kts, vts = q_ref.at[slot], k_ref.at[slot], kt_ref.at[slot], vt_ref.at[slot]
        cum_ref[...] = log_forget_sums(logits[:, 0, :] + bias_ref[slot], count)

        def prepare(block, state):
            acc_ref[block] = jnp.zeros(acc_ref.shape[1:], f32)
            return prepare_block(count, block, state, raws, logits, gains, cum_ref, qs, ks, kts, vts)

        zero = jnp.zeros((HDIM, BLK), f32)
        lax.fori_loop(0, blocks, prepare, (zero, zero))
        qs[blocks] = jnp.zeros(q_ref.shape[2:], bf16)

        def batch(pairs, on_diagonal):
            weights = [jnp.exp2(mm(ks[column], qs[row])) for row, column in pairs]
            low = []
            for (row, column), weight, diagonal in zip(pairs, weights, on_diagonal):
                weight = jnp.where(causal(), weight, 0.0) if diagonal else weight * keep_factor(skip_ref, row, column)
                low.append(weight.astype(bf16))
            parts = [mm(vts[column], weight) for (_, column), weight in zip(pairs, low)]
            for (row, _), part in zip(pairs, parts):
                acc_ref[row] += part

        def one_place(place, state):
            number = blocks // UNROLL
            for i in range(number):
                pairs = pairs_of_place(place, i, UNROLL, count)
                diagonal = [False] * UNROLL
                if i == number - 1:
                    pairs.append((place, place))
                    diagonal[-1:] = [True, True]
                batch(pairs, diagonal)
            return state

        low, high = own_places(me, slot, count)
        lax.fori_loop(low, high, one_place, 0)

        def finish(block, state):
            finish_block(count, block, acc_ref, cum_ref, full_ref.at[slot], mixed_ref.at[slot], qs)
            return state

        lax.fori_loop(0, blocks, finish, 0)
        for k in far_first(count) + [0]:
            peer = lax.rem(me + k, count)
            pl.when(is_mine(me, slot, peer, count))(back(slot, k, peer).start)
        for copy in saved(slot):
            copy.start()
        return carried

    lax.fori_loop(0, 2, one_slot, 0)
    keep_raw = [
        pltpu.make_async_copy(raw_ref, raw_out, keep.at[0, 5]),
        pltpu.make_async_copy(logit_ref, logit_out, keep.at[1, 5]),
    ]
    for copy in keep_raw:
        copy.start()
    for slot in range(2):
        for k in far_first(count):
            peer = lax.rem(me + k, count)
            copies = out(slot, k, peer)
            pl.when(is_mine(peer, slot, me, count))(copies[0].wait_send)
            for copy in copies[1:]:
                copy.wait_send()
        for k in far_first(count) + [0]:
            peer = lax.rem(me + k, count)
            copy = back(slot, k, peer)
            pl.when(is_mine(me, slot, peer, count))(copy.wait_send if k else copy.wait)
    for head in range(HEADS):
        source = holder(head, me, count)
        copy = push(mixed_ref.at[0, 0], att_ref.at[pl.ds(head * HDIM, HDIM)], back_send.at[0, 0], back_recv.at[head], lax.rem(me + 1, count))
        pl.when(source != me)(copy.wait_recv)
    for slot in range(2):
        for copy in saved(slot):
            copy.wait()
    for copy in keep_raw:
        copy.wait()


def front(count, skip, bias, x, w_attn, w_small, gain, gains):
    rows = x.shape[0]
    blocks = 2 * count
    vmem = pl.BlockSpec(memory_space=pltpu.VMEM)
    smem = pl.BlockSpec(memory_space=pltpu.SMEM)
    dma = pltpu.SemaphoreType.DMA
    raw, logit = (count, 3, 2, HDIM, rows), (count, 2, 8, rows)
    state = [((2, blocks, HDIM, BLK), f32), ((2, blocks + 1, 128, BLK), bf16), ((2, blocks, BLK, 128), bf16),
             ((2, blocks, 80, BLK), bf16), ((2, blocks, 80, BLK), bf16)]
    return pl.pallas_call(
        functools.partial(front_kernel, count),
        out_shape=[jax.ShapeDtypeStruct(s, t) for s, t in [
            ((rows, D), bf16), ((D, rows), f32), ((D, rows), bf16), (raw, bf16), (logit, f32)] + state],
        in_specs=[smem, smem] + [vmem] * 5,
        out_specs=[vmem] * 3 + [ANY] * 7,
        scratch_shapes=[
            pltpu.VMEM((D, rows), bf16),
            pltpu.VMEM((3 * HEADS, HDIM, rows), bf16),
            pltpu.VMEM((HEADS, 8, rows), f32),
            pltpu.VMEM(raw, bf16),
            pltpu.VMEM(logit, f32),
            pltpu.VMEM((2, count, HDIM, rows), bf16),
        ] + [pltpu.VMEM(s, t) for s, t in state] + [
            pltpu.VMEM((count, rows), f32),
            pltpu.VMEM((blocks + 1, 80, BLK), f32),
            dma((count, 2, 4)), dma((count, 2, 4)), dma((2, 4)),
            dma((count, 2)), dma((HEADS,)), dma((2,)), dma((2, 6)),
        ],
        compiler_params=pltpu.CompilerParams(collective_id=0, has_side_effects=True, vmem_limit_bytes=60 * 2**20),
        name="front",
    )(skip, bias, x, w_attn, w_small, gain, gains)


SMALL = 48
UNIT = 16
PIECE = 8


def group_bits(group_count, count):
    bits = [("group", 1 << i) for i in range(group_count.bit_length() - 1)]
    return bits, [("seq", 1 << i) for i in range(count.bit_length() - 1)]


def partner(bit):
    axis, step = bit
    here = lax.axis_index(axis)
    side = lax.rem(here // step, 2)
    return {axis: here + step - 2 * step * side}, side


def greet_all(bits, count):
    me = lax.axis_index("seq")
    others = [partner(bit)[0] for bit in bits if bit[0] != "seq"]
    others += [{"seq": lax.rem(me + k, count)} for k in range(1, count)]
    barrier = pltpu.get_barrier_semaphore()
    for there in others:
        pl.semaphore_signal(barrier, inc=1, device_id=there, device_id_type=MESH)
    pl.semaphore_wait(barrier, len(others))
    return me


def orders(near, far, seq):
    x, others = seq[0], seq[1:]
    z = others[0]
    rest = others[1:]
    return [
        [near, far, x, z] + rest,
        [near, x, far, z] + rest,
        [near, z, x, far] + rest,
        [near, far, z, x] + rest,
        [near, x, z] + rest + [far],
        [near, z, far] + rest + [x],
    ]


PARTS = 6


class Summing:
    def __init__(self, base, size, order, source, own, landing, result, send, recv, local):
        self.start, self.size, self.order, self.source, self.local = base, size, order, source, local
        self.own, self.landing, self.result, self.send, self.recv = own, landing, result, send, recv
        self.at, self.stage, self.copy, self.load = base, 0, None, None

    def give(self):
        there, side = partner(self.order[self.stage])
        half = self.size // 2
        self.keep = self.start + side * half
        held = self.own
        if self.stage == 0 and self.source is not None:
            held = self.source
            mine = pl.ds(self.keep, half)
            self.load = pltpu.make_async_copy(self.source.at[mine], self.own.at[mine], self.local)
            self.load.start()
        self.copy = pltpu.make_async_remote_copy(
            src_ref=held.at[pl.ds(self.start + (1 - side) * half, half)],
            dst_ref=self.landing.at[pl.ds(self.at, half)],
            send_sem=self.send.at[self.stage], recv_sem=self.recv.at[self.stage],
            device_id=there, device_id_type=MESH,
        )
        self.copy.start()

    def add(self):
        self.copy.wait()
        if self.load is not None:
            self.load.wait()
            self.load = None
        half = self.size // 2
        step = PIECE if half % PIECE == 0 else 1
        keep, at, own, landing = self.keep, self.at, self.own, self.landing

        def piece(i, carried):
            mine = pl.ds(keep + i * step, step)
            theirs = landing[pl.ds(at + i * step, step)].astype(f32)
            own[mine] = (own[mine].astype(f32) + theirs).astype(bf16)
            return carried

        lax.fori_loop(0, half // step, piece, 0)
        self.start, self.size, self.at, self.stage = keep, half, at + half, self.stage + 1

    def settle(self):
        copy = pltpu.make_async_copy(
            self.own.at[pl.ds(self.start, self.size)], self.result.at[pl.ds(self.start, self.size)], self.local
        )
        copy.start()
        copy.wait()
        self.left = len(self.order)

    def spread(self):
        self.left -= 1
        there, side = partner(self.order[self.left])
        part = self.result.at[pl.ds(self.start, self.size)]
        stage = 2 * len(self.order) - 1 - self.left
        self.copy = pltpu.make_async_remote_copy(
            src_ref=part, dst_ref=part, send_sem=self.send.at[stage], recv_sem=self.recv.at[stage],
            device_id=there, device_id_type=MESH,
        )
        self.copy.start()
        self.start, self.size = self.start - side * self.size, 2 * self.size

    def gathered(self):
        self.copy.wait()


def total(parts):
    return functools.reduce(jnp.add, parts)


def held_heads(count):
    first = [min(HEADS * d // count, HEADS - 2) for d in range(count)]
    return [
        [(d, h - first[d]) for d in range(h * count // HEADS, ((h + 1) * count - 1) // HEADS + 1)]
        for h in range(HEADS)
    ]


def padded(units, least):
    return -(-units // least) * least


def sums_of(units, least, sets, source, own, landing, result, send, recv, local):
    pieces, base, sums = units // least, 0, []
    for i, order in enumerate(orders(*sets)):
        size = least * ((pieces + PARTS - 1 - i) // PARTS)
        if not size:
            break
        sums.append(Summing(base, size, order, source, own, landing, result, send.at[i], recv.at[i], local.at[i]))
        base += size
    return sums


def step(sums, stages):
    for part in sums:
        if part.stage < stages:
            part.add()
            if part.stage < stages:
                part.give()
            else:
                part.settle()
                part.spread()
        else:
            part.gathered()
            if part.left > 0:
                part.spread()


def last_kernel(count, sets, draw_ref, dlogit_ref, early_ref, h_ref, dgate_ref, w_ref, wsmall_ref, x_ref, gain_ref,
                dresid_ref, extra_ref, late_out, early_out, dx_ref,
                proj_ref, logit_ref, part_ref, dsmall_ref, rows_ref, dn_ref, g_ref, land_ref, e_ref, eland_ref,
                send, recv, recv_q, recv_kv, local, gsend, grecv, gsem, esend, erecv, esem):
    near, far, seq = sets
    bits = [near, far] + seq
    stages, least = len(bits), 1 << len(bits)
    me = greet_all(bits, count)
    rows = h_ref.shape[0]
    early = sums_of(e_ref.shape[0], least, sets, early_ref, e_ref, eland_ref, early_out, esend, erecv, esem)
    for part in early:
        part.give()

    holders = held_heads(count)
    first = first_head(me, count)
    started = []
    for k in far_first(count) + [0]:
        peer = lax.rem(me + k, count)
        pairs = [(None, dlogit_ref.at[peer], logit_ref.at[me], recv.at[k])]
        for slot in range(2):
            head = first + slot
            target = proj_ref.at[pl.ds(pl.multiple_of(head * HDIM, HDIM), HDIM)]
            pairs.append((is_mine(me, slot, peer, count), draw_ref.at[peer, 0, slot], target, recv_q.at[head]))
            used = (head * count < HEADS * (me + 1)) & (head * count + count > HEADS * me)
            order = me - holder(head, 0, count)
            pairs.append((used, draw_ref.at[peer, pl.ds(1, 2), slot], part_ref.at[head, order], recv_kv.at[head, order]))
        for i, (mine, src, dst, sem) in enumerate(pairs):
            copy = push(src, dst, send.at[k, i], sem, peer) if k else pltpu.make_async_copy(src, dst, local.at[i])
            started.append((mine, k, copy))
            if mine is None:
                copy.start()
            else:
                pl.when(mine)(copy.start)

    step(early, stages)
    step(early, stages)

    for mine, k, copy in started:
        if mine is not None:
            pl.when(mine)(copy.wait_send if k else copy.wait)
        else:
            copy.wait()
    for head in range(HEADS):
        source = holder(head, me, count)
        copy = push(draw_ref.at[0, 0, 0], proj_ref.at[pl.ds(head * HDIM, HDIM)], send.at[0, 0], recv_q.at[head], lax.rem(me + 1, count))
        pl.when(source != me)(copy.wait_recv)
        for j, (d, s) in enumerate(holders[head]):
            copy = push(draw_ref.at[0, pl.ds(1, 2), 0], part_ref.at[head, j], send.at[0, 0], recv_kv.at[head, j], lax.rem(me + 1, count))
            pl.when(me != d)(copy.wait_recv)

    for head, held in enumerate(holders):
        for i in range(2):
            start = D * (1 + i) + head * HDIM
            if len(held) == 1:
                proj_ref[start : start + HDIM] = part_ref[head, 0, i]
            else:
                proj_ref[start : start + HDIM] = total([part_ref[head, j, i].astype(f32) for j in range(len(held))]).astype(bf16)
        dsmall_ref[8 * head : 8 * head + 8] = total([logit_ref[d, s] for d, s in held])
    proj_ref[3 * D :] = dgate_ref[...]

    def block(i, carried):
        grads = proj_ref[pl.ds(pl.multiple_of(i * 256, 256), 256)]
        for j in range(3):
            part = lax.dot_general(h_ref[:, 256 * j : 256 * j + 256], grads, (((0,), (1,)), ((), ())), preferred_element_type=f32)
            g_ref[pl.ds(i * (D // UNIT) + j * 16, 16)] = part.astype(bf16).reshape(16, UNIT, 256)
        return carried

    lax.fori_loop(0, 9, block, 0)
    low_small = dsmall_ref[...].astype(bf16)
    for i in range(3):
        cols = slice(256 * i, 256 * i + 256)
        part = mm(w_ref[cols, :], proj_ref[...]) + mm(wsmall_ref[cols, :], low_small)
        dn_ref[:, cols] = part.T
    small = mm(low_small, h_ref[...])
    for head in range(HEADS):
        rows_ref[3 * head : 3 * head + 3] = small[8 * head : 8 * head + 3]
    rows_ref[3 * HEADS :] = extra_ref[...]
    gain = gain_ref[...]
    dgain = jnp.zeros((1, D), f32)
    for i in range(rows // 128):
        here = slice(128 * i, 128 * i + 128)
        v, u = x_ref[here].astype(f32), dn_ref[here]
        scale = lax.rsqrt(jnp.mean(v * v, 1, keepdims=True) + EPS)
        hat, gu = v * scale, u * gain
        dx_ref[here] = dresid_ref[here] + scale * (gu - hat * jnp.mean(hat * gu, 1, keepdims=True))
        dgain = dgain + jnp.sum(hat * u, 0, keepdims=True)
    rows_ref[3 * HEADS : 3 * HEADS + 1] = dgain
    bias_rows = jnp.concatenate([dsmall_ref[8 * head : 8 * head + 1] for head in range(HEADS)], 0)
    bias_sum = jnp.sum(bias_rows, 1, keepdims=True)
    lane = lax.broadcasted_iota(jnp.int32, (HEADS, 128), 1)
    row = lax.broadcasted_iota(jnp.int32, (HEADS, 128), 0)
    rows_ref[3 * HEADS + 4 : 3 * HEADS + 5, 0:128] = jnp.sum(jnp.where(lane == row, bias_sum, 0.0), 0, keepdims=True)

    used = 9 * (D // UNIT)
    units = g_ref.shape[0]
    for i in range(3):
        g_ref[used + 3 * i : used + 3 * i + 3] = rows_ref[:, 256 * i : 256 * i + 256].astype(bf16).reshape(3, UNIT, 256)
    if units > used + 9:
        g_ref[used + 9 :] = jnp.zeros((units - used - 9, UNIT, 256), bf16)
    late = sums_of(units, least, sets, None, g_ref, land_ref, late_out, gsend, grecv, gsem)
    for part in late:
        part.give()
    step(early, stages)
    early_left = 2 * stages - 3
    for stage in range(2 * stages):
        step(late, stages)
        if stage < early_left:
            step(early, stages)


def last(count, sets, d_raw, d_logits, early, h, d_gate, w_attn, w_small, x, gain, d_resid, extra):
    stages = 2 + len(sets[2])
    units = padded(9 * (D // UNIT) + 9, 1 << stages)
    rows = h.shape[0]
    most = max(len(held) for held in held_heads(count))
    vmem = pl.BlockSpec(memory_space=pltpu.VMEM)
    dma = pltpu.SemaphoreType.DMA
    shape = (UNIT, 256)
    return pl.pallas_call(
        functools.partial(last_kernel, count, sets),
        out_shape=[
            jax.ShapeDtypeStruct((units,) + shape, bf16),
            jax.ShapeDtypeStruct(early.shape, bf16),
            jax.ShapeDtypeStruct((rows, D), f32),
        ],
        in_specs=[ANY] * 3 + [vmem] * 8,
        out_specs=[ANY, ANY, vmem],
        scratch_shapes=[
            pltpu.VMEM((4 * D, rows), bf16),
            pltpu.VMEM((count, 2, 8, rows), f32),
            pltpu.VMEM((HEADS, most, 2, HDIM, rows), bf16),
            pltpu.VMEM((8 * HEADS, rows), f32),
            pltpu.VMEM((SMALL, D), f32),
            pltpu.VMEM((rows, D), f32),
            pltpu.VMEM((units,) + shape, bf16),
            pltpu.VMEM((units,) + shape, bf16),
            pltpu.VMEM(early.shape, bf16),
            pltpu.VMEM(early.shape, bf16),
            dma((count, 5)), dma((count,)), dma((HEADS,)), dma((HEADS, most)), dma((5,)),
            dma((PARTS, 2 * stages)), dma((PARTS, 2 * stages)), dma((PARTS,)),
            dma((PARTS, 2 * stages)), dma((PARTS, 2 * stages)), dma((PARTS,)),
        ],
        compiler_params=pltpu.CompilerParams(collective_id=3, has_side_effects=True, vmem_limit_bytes=62 * 2**20),
        name="last",
    )(d_raw, d_logits, early, h, d_gate, w_attn, w_small, x, gain, d_resid, extra)


def unpack_kernel(parts, *refs):
    o_ref = refs[-1]
    at = 0
    for ref, blocks in zip(refs, parts):
        here = (pl.program_id(0) >= at) & (pl.program_id(0) < at + blocks)

        @pl.when(here)
        def _():
            o_ref[...] = ref[...].reshape(o_ref.shape).astype(f32)

        at += blocks


def unpack(rows, *parts):
    size = rows // UNIT
    specs, at = [], 0
    for _, first, blocks in parts:
        index = lambda i, at=at, first=first, blocks=blocks: (first + jnp.clip(i - at, 0, blocks - 1), 0, 0)
        specs.append(pl.BlockSpec((size, UNIT, 256), index))
        at += blocks
    return pl.pallas_call(
        functools.partial(unpack_kernel, [blocks for _, _, blocks in parts]),
        grid=(at,),
        in_specs=specs,
        out_specs=pl.BlockSpec((rows, 256), lambda i: (0, i)),
        out_shape=jax.ShapeDtypeStruct((rows, 256 * at), f32),
        compiler_params=pltpu.CompilerParams(vmem_limit_bytes=32 * 2**20),
        name="unpack",
    )(*[units for units, _, _ in parts])


def rms_scale(values, gains):
    inverse = lax.rsqrt(jnp.mean(values * values, axis=-1, keepdims=True) + EPS)
    return values * inverse * gains


def swiglu(gate_up):
    return jax.nn.silu(gate_up[:, :FF]) * gate_up[:, FF:]


def local(tokens, cotangent, skip_table, gain_attn, w_attn, w_heads, forget_bias, query_gain, key_gain,
          w_out, gain_ffn, w_gate_up, w_down):
    count = lax.axis_size("seq")
    me = lax.axis_index("seq")
    rows = tokens.shape[1]
    both = ("seq", "group")
    inputs = tokens[0].astype(f32)
    device = me.astype(jnp.int32)[None]
    head = first_head(me, count)
    skip = skip_table[0]
    gains = jnp.stack([query_gain.reshape(HEADS, HDIM), key_gain.reshape(HEADS, HDIM)], 2)
    gains = lax.dynamic_slice_in_dim(gains, head, 2, 0)
    bias = lax.dynamic_slice_in_dim(forget_bias, head, 2, 0)
    w_small = jnp.pad(w_heads.reshape(D, 3, HEADS).transpose(0, 2, 1), ((0, 0), (0, 0), (0, 5))).reshape(D, HEADS * 8)

    if count <= 8:
        h_first, gate_logit, attended, raw, logits, mixed, q, k, kt, vt = front(
            count, skip, bias, tokens[0], w_attn, w_small, gain_attn[None], gains
        )
    else:
        h_first = rms_scale(inputs, gain_attn).astype(bf16)
        qkv = dot(w_attn[:, : 3 * D], h_first, 0, 1).astype(bf16).reshape(3, HEADS, HDIM, rows)
        gate_logit = dot(w_attn[:, 3 * D :], h_first, 0, 1)
        logits_here = dot(w_small, h_first, 0, 1).reshape(HEADS, 8, rows)
        raw, logits = heads_out(qkv, logits_here, count)
        mixed_low, mixed, q, k, kt, vt = attend_forward(device, skip, bias, raw, logits, gains)
        attended = mixed_back(mixed_low, count).reshape(D, rows)
    attended = attended.astype(f32)

    gate_open = jax.nn.sigmoid(gate_logit)
    gated = (gate_open * attended).astype(bf16)
    resid = inputs + dot(gated, w_out, 0, 0)
    normed_ffn, norm_back_ffn = jax.vjp(rms_scale, resid, gain_ffn)
    h_second = normed_ffn.astype(bf16)
    gate_up = dot(h_second, w_gate_up, 1, 0)
    hidden, hidden_back = jax.vjp(swiglu, gate_up)
    hidden_low = hidden.astype(bf16)
    output = resid + dot(hidden_low, w_down, 1, 0)
    d_low = cotangent[0]
    d_output = d_low.astype(f32)
    (d_gate_up,) = hidden_back(dot(d_low, w_down, 1, 1))
    d_gate_low = d_gate_up.astype(bf16)
    d_resid_norm, grad_gain_ffn = norm_back_ffn(dot(d_gate_low, w_gate_up, 1, 1))
    d_resid = d_output + d_resid_norm
    d_branch = d_resid.astype(bf16)
    d_gated = dot(w_out, d_branch, 1, 1)
    d_gate_logit = (d_gated * attended * gate_open * (1.0 - gate_open)).astype(bf16)
    d_mixed = (d_gated * gate_open).astype(bf16).reshape(HEADS, HDIM, rows)

    near_far, seq_bits = group_bits(lax.axis_size("group"), count)
    sets = (near_far[0], near_far[1], seq_bits)
    units = padded(1440, 1 << (2 + len(seq_bits)))
    d_mixed_all, early = grads_out(
        count, units, d_mixed, h_first, d_gate_logit, h_second, d_gate_low, hidden_low, d_low, gated, d_branch
    )
    d_raw, d_logits, d_gains = attend_backward(device, skip, bias, raw, logits, gains, d_mixed_all, mixed, q, k, kt, vt)

    placed = jnp.zeros((HEADS, HDIM, 2), f32)
    placed = lax.dynamic_update_slice(placed, d_gains, (head, 0, 0)).reshape(D, 2).T
    extra = jnp.concatenate([jnp.zeros((1, D), f32), grad_gain_ffn[None], placed, jnp.zeros((SMALL - 3 * HEADS - 4, D), f32)], 0)
    late, early, d_inputs = last(
        count, sets, d_raw, d_logits, early, h_first, d_gate_logit, w_attn, w_small, tokens[0], gain_attn[None], d_resid, extra
    )
    row = 3 * HEADS
    used = 9 * (D // UNIT)
    small = late[used : used + 9].reshape(3, SMALL, 256).transpose(1, 0, 2).reshape(SMALL, D).astype(f32)
    return (
        output[None].astype(bf16),
        d_inputs[None],
        small[row],
        unpack(D, (late, 0, 9), (early, 27, 3)),
        small[:row].reshape(HEADS, 3, D).transpose(2, 1, 0).reshape(D, row),
        small[row + 4, :HEADS],
        small[row + 2],
        small[row + 3],
        unpack(D, (early, 24, 3)),
        small[row + 1],
        unpack(D, (early, 0, 16)),
        unpack(FF, (early, 6, 3)),
    )


def solution(mesh):
    rows = P("group", "seq", None)
    return jax.shard_map(
        local,
        mesh=mesh,
        in_specs=(rows, rows, P("group", None, None)) + (P(),) * 10,
        out_specs=(rows, rows) + (P(),) * 10,
        check_vma=False,
    )
```

```python
import functools

import jax
import jax.numpy as jnp
from jax import lax
from jax.experimental import pallas as pl
from jax.experimental.pallas import tpu as pltpu
from jax.sharding import PartitionSpec as P

D, FF = 768, 2048
MESH = pl.DeviceIdType.MESH
ANY = pl.BlockSpec(memory_space=pl.ANY)

HEADS, HDIM, BLK = 12, 64, 256
EPS = 1e-06
LOG2E = 1.4426950408889634
LN2 = 0.6931471805599453
SCORE = HDIM ** -0.5
f32, bf16 = jnp.float32, jnp.bfloat16
UNROLL = 8
UNROLL_BACK = 4
NN = (((1,), (0,)), ((), ()))
NT = (((1,), (1,)), ((), ()))
TN = (((0,), (0,)), ((), ()))


def mm(a, b, dims=NN):
    return lax.dot_general(a, b, dims, preferred_element_type=f32)


def split3(v):
    hi = v.astype(bf16).astype(f32)
    rest = v - hi
    mid = rest.astype(bf16).astype(f32)
    return hi, mid, rest - mid


def place_of(block, count):
    return jnp.where(block < count, block, 2 * count - 1 - block)


def lanes_of(block, count):
    return pl.ds(pl.multiple_of(jnp.where(block < count, 0, BLK), BLK), BLK)


def first_head(device, count):
    return jnp.minimum(HEADS * device // count, HEADS - 2)


def is_mine(device, slot, place, count):
    chunk = (first_head(device, count) + slot) * count + place
    return (chunk >= HEADS * device) & (chunk < HEADS * device + HEADS)


def list_pairs(skip_ref, pairs_ref, own_ref, device, slot, count, unroll):
    spare = 2 * count

    def row(number, found):
        def column(other, found):
            pairs_ref[found] = number * 1024 + other
            return found + jnp.where(skip_ref[number, other] == 0, 1, 0)

        mine = is_mine(device, slot, place_of(number, count), count)
        own_ref[found[1]] = number
        below = lax.fori_loop(0, jnp.where(mine, number, 0), column, found[0])
        return below, found[1] + jnp.where(mine, 1, 0)

    below, own = lax.fori_loop(0, spare, row, (0, 0))
    for extra in range(unroll):
        pairs_ref[below + extra] = spare * 1024
        own_ref[own + extra] = spare
    return pl.cdiv(below, unroll), pl.cdiv(own, unroll)


def running_sum(values, count, reverse):
    t = lax.broadcasted_iota(jnp.int32, (BLK, BLK), 0)
    p = lax.broadcasted_iota(jnp.int32, (BLK, BLK), 1)
    ones = jnp.where(t >= p if reverse else t <= p, 1.0, 0.0).astype(bf16)
    halves = []
    for half in range(2):
        part = values[:, half * BLK : (half + 1) * BLK]
        halves.append(sum(mm(piece.astype(bf16), ones) for piece in split3(part)))
    edge = 0 if reverse else BLK - 1
    first, last = (jnp.broadcast_to(h[:, edge : edge + 1], (count, 128)) for h in halves)
    rows = lax.broadcasted_iota(jnp.int32, (count, 128), 0)

    def scan(total, down):
        own = total
        step = 1
        while step < count:
            moved = pltpu.roll(total, step if down else count - step, 0)
            total = total + jnp.where(rows >= step if down else rows < count - step, moved, 0.0)
            step *= 2
        return total - own

    if reverse:
        all_last = jnp.sum(last, axis=0, keepdims=True)
        offsets = scan(first, False) + all_last, scan(last, True)
    else:
        all_first = jnp.sum(first, axis=0, keepdims=True)
        offsets = scan(first, True), scan(last, False) + all_first
    return jnp.concatenate([halves[0] + offsets[0][:, :1], halves[1] + offsets[1][:, :1]], 1)


def shifted(current, before):
    lane = lax.broadcasted_iota(jnp.int32, current.shape, 1)
    return jnp.where(lane == 0, pltpu.roll(before, 1, 1), pltpu.roll(current, 1, 1))


def shifted_back(current, after):
    lane = lax.broadcasted_iota(jnp.int32, current.shape, 1)
    return jnp.where(lane == BLK - 1, pltpu.roll(after, BLK - 1, 1), pltpu.roll(current, BLK - 1, 1))


def stack_rows(top, rows, size):
    extra = size if top is None else size - top.shape[0]
    number = lax.broadcasted_iota(jnp.int32, (extra, BLK), 0)
    bottom = jnp.zeros((extra, BLK), f32)
    for i, r in enumerate(rows):
        bottom = jnp.where(number == i, r, bottom)
    return bottom if top is None else jnp.concatenate([top, bottom], 0)


def prepare_block(count, block, carried, raw_ref, logit_ref, gain_ref, cum_ref, q_ref, k_ref, kt_ref, vt_ref):
    place, lanes = place_of(block, count), lanes_of(block, count)
    q_raw, k_raw, v_raw = (raw_ref[place, i, :, lanes].astype(f32) for i in range(3))
    cum = cum_ref[pl.ds(place, 1), lanes]
    parts = split3(cum)
    one = jnp.ones_like(cum)
    query = q_raw * lax.rsqrt(jnp.mean(q_raw * q_raw, 0, keepdims=True) + EPS) * (gain_ref[:, 0:1] * (SCORE * LOG2E))
    q_ref[block] = stack_rows(query, (*parts, one, one, one), 128).astype(bf16)
    rate_k = jax.nn.sigmoid(logit_ref[place, 1:2, lanes])
    rate_v = jax.nn.sigmoid(logit_ref[place, 2:3, lanes])
    key = k_raw + rate_k * (shifted(k_raw, carried[0]) - k_raw)
    key = key * lax.rsqrt(jnp.mean(key * key, 0, keepdims=True) + EPS) * gain_ref[:, 1:2]
    value = v_raw + rate_v * (shifted(v_raw, carried[1]) - v_raw)
    k_ref[block] = stack_rows(key, (one, one, one, *(-c for c in parts)), 128).T.astype(bf16)
    kt_ref[block] = stack_rows(key, (one,), 80).astype(bf16)
    vt_ref[block] = stack_rows(value, (one, one, one), 80).astype(bf16)
    return k_raw, v_raw


def finish_block(count, block, acc_ref, cum_ref, mixed_full_ref, mixed_ref, q_ref):
    place, lanes = place_of(block, count), lanes_of(block, count)
    summed = acc_ref[block]
    norm = summed[HDIM : HDIM + 1]
    mixed = summed[:HDIM] * (1.0 / norm)
    mixed_full_ref[block] = mixed
    mixed_ref[place, :, lanes] = mixed.astype(bf16)
    parts = split3(cum_ref[pl.ds(place, 1), lanes] - jnp.log2(norm))
    one = jnp.ones_like(norm)
    q_ref[block, HDIM : HDIM + 16, :] = stack_rows(None, (*parts, one, one, one), 16).astype(bf16)


def log_forget_sums(logits, count):
    log_forget = jnp.minimum(logits, 0.0) - jnp.log1p(jnp.exp(-jnp.abs(logits)))
    return running_sum(log_forget, count, False) * LOG2E


def causal():
    return lax.broadcasted_iota(jnp.int32, (BLK, BLK), 0) <= lax.broadcasted_iota(jnp.int32, (BLK, BLK), 1)


def forward_kernel(count, device_ref, skip_ref, bias_ref, raw_ref, logit_ref, gain_ref,
                   mixed_ref, mixed_full_ref, q_ref, k_ref, kt_ref, vt_ref,
                   cum_ref, acc_ref, pairs_ref, own_ref):
    slot = pl.program_id(0)
    device = device_ref[0]
    blocks = 2 * count
    pair_steps, own_steps = list_pairs(skip_ref, pairs_ref, own_ref, device, slot, count, UNROLL)
    cum_ref[...] = log_forget_sums(logit_ref[:, 0, :] + bias_ref[slot], count)

    def prepare(block, carried):
        return prepare_block(count, block, carried, raw_ref, logit_ref, gain_ref, cum_ref, q_ref, k_ref, kt_ref, vt_ref)

    zero = jnp.zeros((HDIM, BLK), f32)
    lax.fori_loop(0, blocks, prepare, (zero, zero))
    q_ref[blocks] = jnp.zeros(q_ref.shape[1:], bf16)

    def together(pairs, diagonal):
        scores = [mm(k_ref[column], q_ref[row]) for row, column in pairs]
        weights = [jnp.exp2(score) for score in scores]
        if diagonal:
            weights = [jnp.where(causal(), weight, 0.0) for weight in weights]
        weights = [weight.astype(bf16) for weight in weights]
        parts = [mm(vt_ref[column], weight) for (row, column), weight in zip(pairs, weights)]
        for (row, column), part in zip(pairs, parts):
            acc_ref[row] = part if diagonal else acc_ref[row] + part

    def own_rows(step, carried):
        rows = [own_ref[step * UNROLL + i] for i in range(UNROLL)]
        together([(row, jnp.minimum(row, blocks - 1)) for row in rows], True)
        return carried

    def kept_pairs(step, carried):
        codes = [pairs_ref[step * UNROLL + i] for i in range(UNROLL)]
        together([(code >> 10, code & 1023) for code in codes], False)
        return carried

    lax.fori_loop(0, own_steps, own_rows, 0)
    lax.fori_loop(0, pair_steps, kept_pairs, 0)

    def finish(block, carried):
        finish_block(count, block, acc_ref, cum_ref, mixed_full_ref, mixed_ref, q_ref)
        return carried

    lax.fori_loop(0, blocks, finish, 0)


def own_places(device, slot, count):
    start = (first_head(device, count) + slot) * count
    low = jnp.clip(HEADS * device - start, 0, count)
    return low, jnp.clip(HEADS * device + HEADS - start, low, count)


def pairs_of_place(place, batch, size, count):
    found = []
    for i in range(size):
        number = batch * size + i
        lower = number < place
        found.append((jnp.where(lower, place, 2 * count - 1 - place), jnp.where(lower, number, number - place)))
    return found


def keep_factor(skip_ref, row, column):
    return jnp.where(skip_ref[row, column] == 0, 1.0, 0.0)


def buffers(count):
    return pl.Buffered(1 if count > 8 else 2)


def attend_forward(device, skip, bias, raw, logits, gains):
    count = raw.shape[0]
    blocks = 2 * count
    most = blocks * (blocks - 1) // 2 + UNROLL
    mode = buffers(count)
    by_slot = lambda *shape: pl.BlockSpec((None,) + shape, lambda s, *_: (s,) + (0,) * len(shape), pipeline_mode=mode)
    out = lambda shape, dtype: jax.ShapeDtypeStruct((2,) + shape, dtype)
    return pl.pallas_call(
        functools.partial(forward_kernel, count),
        grid_spec=pltpu.PrefetchScalarGridSpec(
            num_scalar_prefetch=3,
            grid=(2,),
            in_specs=[
                pl.BlockSpec((count, 3, None, HDIM, 2 * BLK), lambda s, *_: (0, 0, s, 0, 0), pipeline_mode=mode),
                pl.BlockSpec((count, None, 8, 2 * BLK), lambda s, *_: (0, s, 0, 0), pipeline_mode=mode),
                by_slot(HDIM, 2),
            ],
            out_specs=[
                by_slot(count, HDIM, 2 * BLK),
                by_slot(blocks, HDIM, BLK),
                by_slot(blocks + 1, 128, BLK),
                by_slot(blocks, BLK, 128),
                by_slot(blocks, 80, BLK),
                by_slot(blocks, 80, BLK),
            ],
            scratch_shapes=[
                pltpu.VMEM((count, 2 * BLK), f32),
                pltpu.VMEM((blocks + 1, 80, BLK), f32),
                pltpu.SMEM((most,), jnp.int32),
                pltpu.SMEM((blocks + UNROLL,), jnp.int32),
            ],
        ),
        out_shape=[
            out((count, HDIM, 2 * BLK), bf16),
            out((blocks, HDIM, BLK), f32),
            out((blocks + 1, 128, BLK), bf16),
            out((blocks, BLK, 128), bf16),
            out((blocks, 80, BLK), bf16),
            out((blocks, 80, BLK), bf16),
        ],
        compiler_params=pltpu.CompilerParams(vmem_limit_bytes=60 * 2**20),
        name="attend_forward",
    )(device, skip, bias, raw, logits, gains)


def norm_back(v, gain, u):
    scale = lax.rsqrt(jnp.mean(v * v, 0, keepdims=True) + EPS)
    hat = v * scale
    gu = gain * u
    return scale * (gu - hat * jnp.mean(hat * gu, 0, keepdims=True)), hat * u


def prepare_back(count, block, dmixed_ref, mixed_ref, vt_ref, do_ref, v_ref, dq_ref, dk_ref, dv_ref):
    place, lanes = place_of(block, count), lanes_of(block, count)
    d_out = dmixed_ref[place, :, lanes].astype(f32)
    delta = jnp.sum(d_out * mixed_ref[block], 0, keepdims=True)
    do_ref[block] = stack_rows(d_out, [-d for d in split3(delta)], 128).astype(bf16)
    wide = jnp.zeros((128 - 80, BLK), f32)
    v_ref[block] = jnp.concatenate([vt_ref[block].astype(f32), wide], 0).T.astype(bf16)
    dq_ref[block] = jnp.zeros(dq_ref.shape[1:], f32)
    dk_ref[block] = jnp.zeros(dk_ref.shape[1:], f32)
    dv_ref[block] = jnp.zeros(dv_ref.shape[1:], f32)


def batch_back(pairs, masks, q_ref, k_ref, kt_ref, v_ref, do_ref, dq_ref, dk_ref, dv_ref):
    weights = [jnp.exp2(mm(k_ref[column], q_ref[row])) for row, column in pairs]
    for i, mask in enumerate(masks):
        if mask is True:
            weights[i] = jnp.where(causal(), weights[i], 0.0)
        elif mask is not None:
            weights[i] = weights[i] * mask
    d_weights = [mm(v_ref[column], do_ref[row]) for row, column in pairs]
    low_weights = [weight.astype(bf16) for weight in weights]
    d_scores = [(weight * d_weight).astype(bf16) for weight, d_weight in zip(weights, d_weights)]
    parts = [mm(do_ref[row, :HDIM], weight, NT) for (row, _), weight in zip(pairs, low_weights)]
    for (_, column), part in zip(pairs, parts):
        dv_ref[column] += part
    parts = [mm(kt_ref[column], d_score) for (_, column), d_score in zip(pairs, d_scores)]
    for (row, _), part in zip(pairs, parts):
        dq_ref[row] += part
    parts = [mm(q_ref[row, :80], d_score, NT) for (row, _), d_score in zip(pairs, d_scores)]
    for (_, column), part in zip(pairs, parts):
        dk_ref[column] += part


def finish_back(count, block, carried, mine, raw_ref, logit_ref, gain_ref, dq_ref, dk_ref, dv_ref, draw_ref, dlogit_ref, cum_ref):
    next_k, next_v, sum_q, sum_k = carried
    place, lanes = place_of(block, count), lanes_of(block, count)
    earlier = jnp.maximum(block - 1, 0)
    place_before, lanes_before = place_of(earlier, count), lanes_of(earlier, count)
    exists = jnp.where(block > 0, 1.0, 0.0)
    q_raw, k_raw, v_raw = (raw_ref[place, i, :, lanes].astype(f32) for i in range(3))
    k_step = shifted(k_raw, raw_ref[place_before, 1, :, lanes_before].astype(f32) * exists) - k_raw
    v_step = shifted(v_raw, raw_ref[place_before, 2, :, lanes_before].astype(f32) * exists) - v_raw
    rate_k = jax.nn.sigmoid(logit_ref[place, 1:2, lanes])
    rate_v = jax.nn.sigmoid(logit_ref[place, 2:3, lanes])
    dq, dk, dv = dq_ref[block], dk_ref[block], dv_ref[block]
    dq_raw, part_q = norm_back(q_raw, gain_ref[:, 0:1], dq[:HDIM] * SCORE)
    dk_mixed, part_k = norm_back(k_raw + rate_k * k_step, gain_ref[:, 1:2], dk[:HDIM] * LN2)
    send_k, send_v = rate_k * dk_mixed, rate_v * dv
    draw_ref[place, 0, :, lanes] = dq_raw.astype(bf16)
    draw_ref[place, 1, :, lanes] = (dk_mixed - send_k + shifted_back(send_k, next_k)).astype(bf16)
    draw_ref[place, 2, :, lanes] = (dv - send_v + shifted_back(send_v, next_v)).astype(bf16)
    dlogit_ref[place, 1:2, lanes] = (1.0 - rate_k) * jnp.sum(k_step * send_k, 0, keepdims=True)
    dlogit_ref[place, 2:3, lanes] = (1.0 - rate_v) * jnp.sum(v_step * send_v, 0, keepdims=True)
    cum_ref[pl.ds(place, 1), lanes] = dq[HDIM : HDIM + 1] - dk[HDIM + 3 : HDIM + 4]
    return send_k, send_v, sum_q + jnp.where(mine, part_q, 0.0), sum_k + part_k


def forget_back(count, bias, logit_ref, cum_ref, dlogit_ref):
    d_log = running_sum(cum_ref[...], count, True)
    dlogit_ref[:, 0, :] = d_log * jax.nn.sigmoid(-(logit_ref[:, 0, :] + bias))
    dlogit_ref[:, 3:, :] = jnp.zeros((count, 5, 2 * BLK), f32)


def backward_kernel(count, device_ref, skip_ref, bias_ref, raw_ref, logit_ref, gain_ref, dmixed_ref, mixed_ref,
                    q_ref, k_ref, kt_ref, vt_ref, draw_ref, dlogit_ref, dgain_ref,
                    do_ref, v_ref, cum_ref, dq_ref, dk_ref, dv_ref, pairs_ref, own_ref):
    slot = pl.program_id(0)
    device = device_ref[0]
    blocks = 2 * count
    pair_steps, own_steps = list_pairs(skip_ref, pairs_ref, own_ref, device, slot, count, UNROLL_BACK)
    sums = (dq_ref, dk_ref, dv_ref)

    def prepare(block, carried):
        prepare_back(count, block, dmixed_ref, mixed_ref, vt_ref, do_ref, v_ref, *sums)
        return carried

    lax.fori_loop(0, blocks, prepare, 0)
    do_ref[blocks] = jnp.zeros(do_ref.shape[1:], bf16)
    dq_ref[blocks] = jnp.zeros(dq_ref.shape[1:], f32)

    def own_rows(step, carried):
        rows = [own_ref[step * UNROLL_BACK + i] for i in range(UNROLL_BACK)]
        pairs = [(row, jnp.minimum(row, blocks - 1)) for row in rows]
        batch_back(pairs, [True] * UNROLL_BACK, q_ref, k_ref, kt_ref, v_ref, do_ref, *sums)
        return carried

    def kept_pairs(step, carried):
        codes = [pairs_ref[step * UNROLL_BACK + i] for i in range(UNROLL_BACK)]
        pairs = [(code >> 10, code & 1023) for code in codes]
        batch_back(pairs, [None] * UNROLL_BACK, q_ref, k_ref, kt_ref, v_ref, do_ref, *sums)
        return carried

    lax.fori_loop(0, own_steps, own_rows, 0)
    lax.fori_loop(0, pair_steps, kept_pairs, 0)

    def finish(step, carried):
        block = blocks - 1 - step
        mine = is_mine(device, slot, place_of(block, count), count)
        return finish_back(count, block, carried, mine, raw_ref, logit_ref, gain_ref, *sums, draw_ref, dlogit_ref, cum_ref)

    zero = jnp.zeros((HDIM, BLK), f32)
    _, _, sum_q, sum_k = lax.fori_loop(0, blocks, finish, (zero, zero, zero, zero))
    dgain_ref[:, 0:1] = jnp.sum(sum_q, 1, keepdims=True)
    dgain_ref[:, 1:2] = jnp.sum(sum_k, 1, keepdims=True)
    forget_back(count, bias_ref[slot], logit_ref, cum_ref, dlogit_ref)


def attend_backward(device, skip, bias, raw, logits, gains, dmixed, mixed, q, k, kt, vt):
    count = raw.shape[0]
    blocks = 2 * count
    most = blocks * (blocks - 1) // 2 + UNROLL_BACK
    mode = buffers(count)
    by_slot = lambda *shape: pl.BlockSpec((None,) + shape, lambda s, *_: (s,) + (0,) * len(shape), pipeline_mode=mode)
    raw_spec = pl.BlockSpec((count, 3, None, HDIM, 2 * BLK), lambda s, *_: (0, 0, s, 0, 0), pipeline_mode=mode)
    place_spec = lambda rows: pl.BlockSpec((count, None, rows, 2 * BLK), lambda s, *_: (0, s, 0, 0), pipeline_mode=mode)
    return pl.pallas_call(
        functools.partial(backward_kernel, count),
        grid_spec=pltpu.PrefetchScalarGridSpec(
            num_scalar_prefetch=3,
            grid=(2,),
            in_specs=[
                raw_spec,
                place_spec(8),
                by_slot(HDIM, 2),
                place_spec(HDIM),
                by_slot(blocks, HDIM, BLK),
                by_slot(blocks + 1, 128, BLK),
                by_slot(blocks, BLK, 128),
                by_slot(blocks, 80, BLK),
                by_slot(blocks, 80, BLK),
            ],
            out_specs=[raw_spec, place_spec(8), by_slot(HDIM, 2)],
            scratch_shapes=[
                pltpu.VMEM((blocks + 1, 128, BLK), bf16),
                pltpu.VMEM((blocks, BLK, 128), bf16),
                pltpu.VMEM((count, 2 * BLK), f32),
                pltpu.VMEM((blocks + 1, 80, BLK), f32),
                pltpu.VMEM((blocks, 80, BLK), f32),
                pltpu.VMEM((blocks, HDIM, BLK), f32),
                pltpu.SMEM((most,), jnp.int32),
                pltpu.SMEM((blocks + UNROLL_BACK,), jnp.int32),
            ],
        ),
        out_shape=[
            jax.ShapeDtypeStruct(raw.shape, bf16),
            jax.ShapeDtypeStruct(logits.shape, f32),
            jax.ShapeDtypeStruct(gains.shape, f32),
        ],
        compiler_params=pltpu.CompilerParams(vmem_limit_bytes=60 * 2**20),
        name="attend_backward",
    )(device, skip, bias, raw, logits, gains, dmixed, mixed, q, k, kt, vt)


def holder(head, place, count):
    return (head * count + place) // HEADS


def greet(count):
    me = lax.axis_index("seq")
    barrier = pltpu.get_barrier_semaphore()
    for k in range(1, count):
        peer = lax.rem(me + k, count)
        pl.semaphore_signal(barrier, inc=1, device_id={"seq": peer}, device_id_type=MESH)
    pl.semaphore_wait(barrier, count - 1)
    return me


def far_first(count):
    return sorted(range(1, count), key=lambda k: -min(k, count - k))


def push(src, dst, send, recv, peer):
    return pltpu.make_async_remote_copy(
        src_ref=src, dst_ref=dst, send_sem=send, recv_sem=recv, device_id={"seq": peer}, device_id_type=MESH
    )


def heads_out_kernel(count, x_ref, logit_in, raw_ref, logit_ref, send, recv, local):
    me = greet(count)

    def copies(peer, source, k):
        head = first_head(peer, count)
        items = []
        for slot in range(2):
            items.append((is_mine(peer, slot, me, count), is_mine(me, slot, source, count),
                          push(x_ref.at[0, head + slot], raw_ref.at[me, 0, slot], send.at[k, slot], recv.at[k, slot], peer)))
        items.append((None, None, push(x_ref.at[pl.ds(1, 2), pl.ds(head, 2)], raw_ref.at[me, pl.ds(1, 2)], send.at[k, 2], recv.at[k, 2], peer)))
        items.append((None, None, push(logit_in.at[pl.ds(head, 2)], logit_ref.at[me], send.at[k, 3], recv.at[k, 3], peer)))
        return items

    every = []
    for k in far_first(count):
        items = copies(lax.rem(me + k, count), lax.rem(me + count - k, count), k)
        every.append(items)
        for out, _, copy in items:
            if out is None:
                copy.start()
            else:
                pl.when(out)(copy.start)
    head = first_head(me, count)
    own = [
        pltpu.make_async_copy(x_ref.at[:, pl.ds(head, 2)], raw_ref.at[me], local.at[0]),
        pltpu.make_async_copy(logit_in.at[pl.ds(head, 2)], logit_ref.at[me], local.at[1]),
    ]
    for copy in own:
        copy.start()
    for items in every:
        for out, into, copy in items:
            if out is None:
                copy.wait()
            else:
                pl.when(out)(copy.wait_send)
                pl.when(into)(copy.wait_recv)
    for copy in own:
        copy.wait()


def heads_out(qkv, logits, count):
    return pl.pallas_call(
        functools.partial(heads_out_kernel, count),
        out_shape=[
            jax.ShapeDtypeStruct((count, 3, 2, HDIM, 2 * BLK), bf16),
            jax.ShapeDtypeStruct((count, 2, 8, 2 * BLK), f32),
        ],
        in_specs=[ANY, ANY],
        out_specs=[ANY, ANY],
        scratch_shapes=[pltpu.SemaphoreType.DMA((count, 4)), pltpu.SemaphoreType.DMA((count, 4)), pltpu.SemaphoreType.DMA((2,))],
        compiler_params=pltpu.CompilerParams(collective_id=0, has_side_effects=True),
        name="heads_out",
    )(qkv, logits)


def mixed_back_kernel(count, x_ref, o_ref, send, recv, local):
    me = greet(count)
    first = first_head(me, count)
    started = []
    for k in far_first(count) + [0]:
        peer = lax.rem(me + k, count)
        for slot in range(2):
            mine = is_mine(me, slot, peer, count)
            src, dst = x_ref.at[slot, peer], o_ref.at[first + slot]
            if k:
                copy = push(src, dst, send.at[k, slot], recv.at[first + slot], peer)
            else:
                copy = pltpu.make_async_copy(src, dst, local.at[slot])
            started.append((mine, k, copy))
            pl.when(mine)(copy.start)
    for mine, k, copy in started:
        pl.when(mine)(copy.wait_send if k else copy.wait)
    for head in range(HEADS):
        source = holder(head, me, count)
        copy = push(x_ref.at[0, 0], o_ref.at[head], send.at[0, 0], recv.at[head], lax.rem(me + 1, count))
        pl.when(source != me)(copy.wait_recv)


def mixed_back(mixed, count):
    return pl.pallas_call(
        functools.partial(mixed_back_kernel, count),
        out_shape=jax.ShapeDtypeStruct((HEADS, HDIM, 2 * BLK), bf16),
        in_specs=[ANY],
        out_specs=ANY,
        scratch_shapes=[pltpu.SemaphoreType.DMA((count, 2)), pltpu.SemaphoreType.DMA((HEADS,)), pltpu.SemaphoreType.DMA((2,))],
        compiler_params=pltpu.CompilerParams(collective_id=1, has_side_effects=True),
        name="mixed_back",
    )(mixed)


def grads_out_kernel(count, x_ref, h1_ref, dgate_ref, h2_ref, dgu_ref, hidden_ref, dlow_ref, gated_ref, branch_ref,
                     o_ref, grads_ref, send, recv, local):
    me = greet(count)
    started = []
    for head in range(HEADS):
        peer = holder(head, me, count)
        slot = head - first_head(peer, count)
        away = peer != me
        there = jnp.where(away, peer, lax.rem(me + 1, count))
        copy = push(x_ref.at[head], o_ref.at[me, slot], send.at[head], recv.at[me, slot], there)
        own = pltpu.make_async_copy(x_ref.at[head], o_ref.at[me, slot], local.at[slot])
        pl.when(away)(copy.start)
        pl.when(peer == me)(own.start)
        started.append((away, peer == me, copy, own))

    def put(unit, part):
        grads_ref[pl.ds(unit, 16)] = part.astype(bf16).reshape(16, UNIT, 256)

    def gate_up(i, carried):
        right = dgu_ref[:, pl.ds(pl.multiple_of(i * 256, 256), 256)]
        for j in range(3):
            put(i * 48 + 16 * j, mm(h2_ref[:, 256 * j : 256 * j + 256], right, TN))
        return carried

    lax.fori_loop(0, 2 * FF // 256, gate_up, 0)

    def down(i, carried):
        left = hidden_ref[:, pl.ds(pl.multiple_of(i * 256, 256), 256)]
        for j in range(3):
            put(768 + 128 * j + 16 * i, mm(left, dlow_ref[:, 256 * j : 256 * j + 256], TN))
        return carried

    lax.fori_loop(0, FF // 256, down, 0)
    for i in range(3):
        for j in range(3):
            put(1152 + 48 * i + 16 * j, mm(gated_ref[256 * j : 256 * j + 256, :], branch_ref[:, 256 * i : 256 * i + 256]))
            put(1296 + 48 * i + 16 * j, lax.dot_general(
                h1_ref[:, 256 * j : 256 * j + 256], dgate_ref[256 * i : 256 * i + 256, :],
                (((0,), (1,)), ((), ())), preferred_element_type=f32))
    units = grads_ref.shape[0]
    if units > 1440:
        grads_ref[1440:] = jnp.zeros((units - 1440, UNIT, 256), bf16)

    for away, here, copy, own in started:
        pl.when(away)(copy.wait_send)
        pl.when(here)(own.wait)
    for k in range(1, count):
        source = lax.rem(me + k, count)
        for slot in range(2):
            copy = push(x_ref.at[0], o_ref.at[source, slot], send.at[0], recv.at[source, slot], source)
            pl.when(is_mine(me, slot, source, count))(copy.wait_recv)


def grads_out(count, units, d_mixed, *operands):
    vmem = pl.BlockSpec(memory_space=pltpu.VMEM)
    return pl.pallas_call(
        functools.partial(grads_out_kernel, count),
        out_shape=[
            jax.ShapeDtypeStruct((count, 2, HDIM, 2 * BLK), bf16),
            jax.ShapeDtypeStruct((units, UNIT, 256), bf16),
        ],
        in_specs=[ANY] + [vmem] * 8,
        out_specs=[ANY, vmem],
        scratch_shapes=[pltpu.SemaphoreType.DMA((HEADS,)), pltpu.SemaphoreType.DMA((count, 2)), pltpu.SemaphoreType.DMA((2,))],
        compiler_params=pltpu.CompilerParams(collective_id=2, has_side_effects=True, vmem_limit_bytes=60 * 2**20),
        name="grads_out",
    )(d_mixed, *operands)


def dot(a, b, i, j):
    return lax.dot_general(a, b, (((i,), (j,)), ((), ())), preferred_element_type=f32)


def front_kernel(count, skip_ref, bias_ref, x_ref, w_ref, wsmall_ref, gain_ref, gains_ref,
                 h_ref, gate_ref, att_ref, raw_out, logit_out, full_out, q_out, k_out, kt_out, vt_out,
                 ht_ref, proj_ref, small_ref, raw_ref, logit_ref, mixed_ref, full_ref, q_ref, k_ref, kt_ref, vt_ref, cum_ref, acc_ref,
                 send, recv, own, back_send, back_recv, back_own, keep):
    me = lax.axis_index("seq")
    barrier = pltpu.get_barrier_semaphore()
    for k in range(1, count):
        pl.semaphore_signal(barrier, inc=1, device_id={"seq": lax.rem(me + k, count)}, device_id_type=MESH)
    blocks = 2 * count
    rows = x_ref.shape[0]
    for i in range(rows // 128):
        here = slice(128 * i, 128 * i + 128)
        v = x_ref[here].astype(f32)
        normed = v * lax.rsqrt(jnp.mean(v * v, 1, keepdims=True) + EPS) * gain_ref[...]
        h_ref[here] = normed.astype(bf16)
        ht_ref[:, here] = normed.T.astype(bf16)

    def project(i, carried):
        block = mm(w_ref[:, pl.ds(pl.multiple_of(256 * i, 256), 256)], ht_ref[...], TN)
        proj_ref[pl.ds(4 * i, 4)] = block.astype(bf16).reshape(4, HDIM, rows)
        return carried

    small_ref[...] = mm(wsmall_ref[...], ht_ref[...], TN).reshape(HEADS, 8, rows)
    lax.fori_loop(0, 9, project, 0)
    pl.semaphore_wait(barrier, count - 1)
    first = first_head(me, count)

    def out(slot, k, peer):
        head = first_head(peer, count) + slot
        sems = lambda i: (send.at[k, slot, i], recv.at[k, slot, i], peer)
        return [
            push(proj_ref.at[head], raw_ref.at[me, 0, slot], *sems(0)),
            push(proj_ref.at[HEADS + head], raw_ref.at[me, 1, slot], *sems(1)),
            push(proj_ref.at[2 * HEADS + head], raw_ref.at[me, 2, slot], *sems(2)),
            push(small_ref.at[head], logit_ref.at[me, slot], *sems(3)),
        ]

    def own_copies(slot):
        head = first + slot
        return [
            pltpu.make_async_copy(proj_ref.at[head], raw_ref.at[me, 0, slot], own.at[slot, 0]),
            pltpu.make_async_copy(proj_ref.at[HEADS + head], raw_ref.at[me, 1, slot], own.at[slot, 1]),
            pltpu.make_async_copy(proj_ref.at[2 * HEADS + head], raw_ref.at[me, 2, slot], own.at[slot, 2]),
            pltpu.make_async_copy(small_ref.at[head], logit_ref.at[me, slot], own.at[slot, 3]),
        ]

    for slot in range(2):
        for k in far_first(count):
            peer = lax.rem(me + k, count)
            copies = out(slot, k, peer)
            pl.when(is_mine(peer, slot, me, count))(copies[0].start)
            for copy in copies[1:]:
                copy.start()
        for copy in own_copies(slot):
            copy.start()

    def gate(i, carried):
        here = pl.ds(pl.multiple_of(256 * i, 256), 256)
        gate_ref[here] = mm(w_ref[:, pl.ds(pl.multiple_of(3 * D + 256 * i, 256), 256)], ht_ref[...], TN)
        return carried

    lax.fori_loop(0, 3, gate, 0)

    def saved(slot):
        return [
            pltpu.make_async_copy(src.at[slot], dst.at[slot], keep.at[slot, i])
            for i, (src, dst) in enumerate(
                ((full_ref, full_out), (q_ref, q_out), (k_ref, k_out), (kt_ref, kt_out), (vt_ref, vt_out)))
        ]

    def back(slot, k, peer):
        target = att_ref.at[pl.ds(pl.multiple_of((first + slot) * HDIM, HDIM), HDIM)]
        if k:
            return push(mixed_ref.at[slot, peer], target, back_send.at[k, slot], back_recv.at[first + slot], peer)
        return pltpu.make_async_copy(mixed_ref.at[slot, peer], target, back_own.at[slot])

    def one_slot(slot, carried):
        for copy in own_copies(slot):
            copy.wait()
        for k in far_first(count):
            source = lax.rem(me + count - k, count)
            copies = out(slot, k, source)
            pl.when(is_mine(me, slot, source, count))(copies[0].wait_recv)
            for copy in copies[1:]:
                copy.wait_recv()
        raws, logits, gains = raw_ref.at[:, :, slot], logit_ref.at[:, slot], gains_ref.at[slot]
        qs, ks, kts, vts = q_ref.at[slot], k_ref.at[slot], kt_ref.at[slot], vt_ref.at[slot]
        cum_ref[...] = log_forget_sums(logits[:, 0, :] + bias_ref[slot], count)

        def prepare(block, state):
            acc_ref[block] = jnp.zeros(acc_ref.shape[1:], f32)
            return prepare_block(count, block, state, raws, logits, gains, cum_ref, qs, ks, kts, vts)

        zero = jnp.zeros((HDIM, BLK), f32)
        lax.fori_loop(0, blocks, prepare, (zero, zero))
        qs[blocks] = jnp.zeros(q_ref.shape[2:], bf16)

        def batch(pairs, on_diagonal):
            weights = [jnp.exp2(mm(ks[column], qs[row])) for row, column in pairs]
            low = []
            for (row, column), weight, diagonal in zip(pairs, weights, on_diagonal):
                weight = jnp.where(causal(), weight, 0.0) if diagonal else weight * keep_factor(skip_ref, row, column)
                low.append(weight.astype(bf16))
            parts = [mm(vts[column], weight) for (_, column), weight in zip(pairs, low)]
            for (row, _), part in zip(pairs, parts):
                acc_ref[row] += part

        def one_place(place, state):
            number = blocks // UNROLL
            for i in range(number):
                pairs = pairs_of_place(place, i, UNROLL, count)
                diagonal = [False] * UNROLL
                if i == number - 1:
                    pairs.append((place, place))
                    diagonal[-1:] = [True, True]
                batch(pairs, diagonal)
            return state

        low, high = own_places(me, slot, count)
        lax.fori_loop(low, high, one_place, 0)

        def finish(block, state):
            finish_block(count, block, acc_ref, cum_ref, full_ref.at[slot], mixed_ref.at[slot], qs)
            return state

        lax.fori_loop(0, blocks, finish, 0)
        for k in far_first(count) + [0]:
            peer = lax.rem(me + k, count)
            pl.when(is_mine(me, slot, peer, count))(back(slot, k, peer).start)
        for copy in saved(slot):
            copy.start()
        return carried

    lax.fori_loop(0, 2, one_slot, 0)
    keep_raw = [
        pltpu.make_async_copy(raw_ref, raw_out, keep.at[0, 5]),
        pltpu.make_async_copy(logit_ref, logit_out, keep.at[1, 5]),
    ]
    for copy in keep_raw:
        copy.start()
    for slot in range(2):
        for k in far_first(count):
            peer = lax.rem(me + k, count)
            copies = out(slot, k, peer)
            pl.when(is_mine(peer, slot, me, count))(copies[0].wait_send)
            for copy in copies[1:]:
                copy.wait_send()
        for k in far_first(count) + [0]:
            peer = lax.rem(me + k, count)
            copy = back(slot, k, peer)
            pl.when(is_mine(me, slot, peer, count))(copy.wait_send if k else copy.wait)
    for head in range(HEADS):
        source = holder(head, me, count)
        copy = push(mixed_ref.at[0, 0], att_ref.at[pl.ds(head * HDIM, HDIM)], back_send.at[0, 0], back_recv.at[head], lax.rem(me + 1, count))
        pl.when(source != me)(copy.wait_recv)
    for slot in range(2):
        for copy in saved(slot):
            copy.wait()
    for copy in keep_raw:
        copy.wait()


def front(count, skip, bias, x, w_attn, w_small, gain, gains):
    rows = x.shape[0]
    blocks = 2 * count
    vmem = pl.BlockSpec(memory_space=pltpu.VMEM)
    smem = pl.BlockSpec(memory_space=pltpu.SMEM)
    dma = pltpu.SemaphoreType.DMA
    raw, logit = (count, 3, 2, HDIM, rows), (count, 2, 8, rows)
    state = [((2, blocks, HDIM, BLK), f32), ((2, blocks + 1, 128, BLK), bf16), ((2, blocks, BLK, 128), bf16),
             ((2, blocks, 80, BLK), bf16), ((2, blocks, 80, BLK), bf16)]
    return pl.pallas_call(
        functools.partial(front_kernel, count),
        out_shape=[jax.ShapeDtypeStruct(s, t) for s, t in [
            ((rows, D), bf16), ((D, rows), f32), ((D, rows), bf16), (raw, bf16), (logit, f32)] + state],
        in_specs=[smem, smem] + [vmem] * 5,
        out_specs=[vmem] * 3 + [ANY] * 7,
        scratch_shapes=[
            pltpu.VMEM((D, rows), bf16),
            pltpu.VMEM((3 * HEADS, HDIM, rows), bf16),
            pltpu.VMEM((HEADS, 8, rows), f32),
            pltpu.VMEM(raw, bf16),
            pltpu.VMEM(logit, f32),
            pltpu.VMEM((2, count, HDIM, rows), bf16),
        ] + [pltpu.VMEM(s, t) for s, t in state] + [
            pltpu.VMEM((count, rows), f32),
            pltpu.VMEM((blocks + 1, 80, BLK), f32),
            dma((count, 2, 4)), dma((count, 2, 4)), dma((2, 4)),
            dma((count, 2)), dma((HEADS,)), dma((2,)), dma((2, 6)),
        ],
        compiler_params=pltpu.CompilerParams(collective_id=0, has_side_effects=True, vmem_limit_bytes=60 * 2**20),
        name="front",
    )(skip, bias, x, w_attn, w_small, gain, gains)


SMALL = 48
UNIT = 16
PIECE = 8


def group_bits(group_count, count):
    bits = [("group", 1 << i) for i in range(group_count.bit_length() - 1)]
    return bits, [("seq", 1 << i) for i in range(count.bit_length() - 1)]


def partner(bit):
    axis, step = bit
    here = lax.axis_index(axis)
    side = lax.rem(here // step, 2)
    return {axis: here + step - 2 * step * side}, side


def greet_all(bits, count):
    me = lax.axis_index("seq")
    others = [partner(bit)[0] for bit in bits if bit[0] != "seq"]
    others += [{"seq": lax.rem(me + k, count)} for k in range(1, count)]
    barrier = pltpu.get_barrier_semaphore()
    for there in others:
        pl.semaphore_signal(barrier, inc=1, device_id=there, device_id_type=MESH)
    pl.semaphore_wait(barrier, len(others))
    return me


def orders(near, far, seq, busy):
    x, z, rest = seq[0], seq[1], seq[2:]
    kinds = [
        [near, far, x, z] + rest,
        [near, x, far, z] + rest,
        [near, z, x, far] + rest,
        [near, z, far, x] + rest,
    ]
    return [kinds[i] for i in (EARLY_KINDS if busy else (0, 1, 2, 0, 1, 3))]


EARLY_KINDS = (0, 1, 2, 0, 1, 3)
PARTS = 6


class Summing:
    def __init__(self, base, size, order, source, own, landing, result, send, recv, local):
        self.start, self.size, self.order, self.source, self.local = base, size, order, source, local
        self.own, self.landing, self.result, self.send, self.recv = own, landing, result, send, recv
        self.base, self.at, self.stage, self.copy, self.load = base, base, 0, None, None
        self.off = 0

    def give(self):
        there, side = partner(self.order[self.stage])
        half = self.size // 2
        self.keep = self.start + side * half
        held = self.own
        if self.stage == 0 and self.source is not None:
            held = self.source
            self.load = pltpu.make_async_copy(
                self.source.at[pl.ds(self.keep, half)], self.own.at[pl.ds(self.base // 2, half)], self.local
            )
            self.load.start()
        self.copy = pltpu.make_async_remote_copy(
            src_ref=held.at[pl.ds(self.start + (1 - side) * half - self.off, half)],
            dst_ref=self.landing.at[pl.ds(self.at, half)],
            send_sem=self.send.at[self.stage], recv_sem=self.recv.at[self.stage],
            device_id=there, device_id_type=MESH,
        )
        self.copy.start()

    def add(self):
        self.copy.wait()
        if self.load is not None:
            self.load.wait()
            self.load = None
            self.off = self.keep - self.base // 2
        half = self.size // 2
        step = PIECE if half % PIECE == 0 else 1
        keep, at, own, landing = self.keep - self.off, self.at, self.own, self.landing

        def piece(i, carried):
            mine = pl.ds(keep + i * step, step)
            own[mine] = own[mine] + landing[pl.ds(at + i * step, step)]
            return carried

        lax.fori_loop(0, half // step, piece, 0)
        self.start, self.size, self.at, self.stage = self.keep, half, at + half, self.stage + 1

    def settle(self):
        copy = pltpu.make_async_copy(
            self.own.at[pl.ds(self.start - self.off, self.size)], self.result.at[pl.ds(self.start, self.size)], self.local
        )
        copy.start()
        copy.wait()
        self.left = len(self.order)

    def spread(self):
        self.left -= 1
        there, side = partner(self.order[self.left])
        part = self.result.at[pl.ds(self.start, self.size)]
        stage = 2 * len(self.order) - 1 - self.left
        self.copy = pltpu.make_async_remote_copy(
            src_ref=part, dst_ref=part, send_sem=self.send.at[stage], recv_sem=self.recv.at[stage],
            device_id=there, device_id_type=MESH,
        )
        self.copy.start()
        self.start, self.size = self.start - side * self.size, 2 * self.size

    def gathered(self):
        self.copy.wait()


def total(parts):
    return functools.reduce(jnp.add, parts)


def held_heads(count):
    first = [min(HEADS * d // count, HEADS - 2) for d in range(count)]
    return [
        [(d, h - first[d]) for d in range(h * count // HEADS, ((h + 1) * count - 1) // HEADS + 1)]
        for h in range(HEADS)
    ]


def padded(units, least):
    return -(-units // least) * least


def sums_of(units, least, sets, source, own, landing, result, send, recv, local):
    pieces, base, sums = units // least, 0, []
    for i, order in enumerate(orders(*sets, source is not None)):
        size = least * ((pieces + PARTS - 1 - i) // PARTS)
        if not size:
            break
        sums.append(Summing(base, size, order, source, own, landing, result, send.at[i], recv.at[i], local.at[i]))
        base += size
    return sums


def step(sums, stages):
    for part in sums:
        if part.stage < stages:
            part.add()
            if part.stage < stages:
                part.give()
            else:
                part.settle()
                part.spread()
        else:
            part.gathered()
            if part.left > 0:
                part.spread()


def put_together(holders, part_ref, logit_ref, proj_ref, dsmall_ref):
    for head, held in enumerate(holders):
        for i in range(2):
            start = D * (1 + i) + head * HDIM
            if len(held) == 1:
                proj_ref[start : start + HDIM] = part_ref[head, 0, i]
            else:
                proj_ref[start : start + HDIM] = total([part_ref[head, j, i].astype(f32) for j in range(len(held))]).astype(bf16)
        dsmall_ref[8 * head : 8 * head + 8] = total([logit_ref[d, s] for d, s in held])


def late_weights(h_ref, proj_ref, g_ref):
    def block(i, carried):
        grads = proj_ref[pl.ds(pl.multiple_of(i * 256, 256), 256)]
        for j in range(3):
            part = lax.dot_general(h_ref[:, 256 * j : 256 * j + 256], grads, (((0,), (1,)), ((), ())), preferred_element_type=f32)
            g_ref[pl.ds(i * (D // UNIT) + j * 16, 16)] = part.astype(bf16).reshape(16, UNIT, 256)
        return carried

    lax.fori_loop(0, 9, block, 0)


def late_rest(h_ref, proj_ref, w_ref, wsmall_ref, x_ref, gain_ref, dresid_ref, extra_ref, dsmall_ref, rows_ref, dx_ref, g_ref, gsum_ref=None):
    low_small = dsmall_ref[...].astype(bf16)
    for i in range(3):
        cols = slice(256 * i, 256 * i + 256)
        part = mm(w_ref[cols, :], proj_ref[...]) + mm(wsmall_ref[cols, :], low_small)
        dx_ref[:, cols] = part.T
    small = mm(low_small, h_ref[...])
    for head in range(HEADS):
        rows_ref[3 * head : 3 * head + 3] = small[8 * head : 8 * head + 3]
    rows_ref[3 * HEADS :] = extra_ref[...]
    if gsum_ref is not None:
        rows_ref[3 * HEADS + 2 : 3 * HEADS + 4] = gsum_ref[0:2]
    gain = gain_ref[...]
    dgain = jnp.zeros((1, D), f32)
    for i in range(h_ref.shape[0] // 128):
        here = slice(128 * i, 128 * i + 128)
        v, u = x_ref[here].astype(f32), dx_ref[here]
        scale = lax.rsqrt(jnp.mean(v * v, 1, keepdims=True) + EPS)
        hat, gu = v * scale, u * gain
        dx_ref[here] = dresid_ref[here] + scale * (gu - hat * jnp.mean(hat * gu, 1, keepdims=True))
        dgain = dgain + jnp.sum(hat * u, 0, keepdims=True)
    rows_ref[3 * HEADS : 3 * HEADS + 1] = dgain
    bias_rows = jnp.concatenate([dsmall_ref[8 * head : 8 * head + 1] for head in range(HEADS)], 0)
    bias_sum = jnp.sum(bias_rows, 1, keepdims=True)
    lane = lax.broadcasted_iota(jnp.int32, (HEADS, 128), 1)
    row = lax.broadcasted_iota(jnp.int32, (HEADS, 128), 0)
    rows_ref[3 * HEADS + 4 : 3 * HEADS + 5, 0:128] = jnp.sum(jnp.where(lane == row, bias_sum, 0.0), 0, keepdims=True)

    used = 9 * (D // UNIT)
    units = g_ref.shape[0]
    for i in range(3):
        g_ref[used + 3 * i : used + 3 * i + 3] = rows_ref[:, 256 * i : 256 * i + 256].astype(bf16).reshape(3, UNIT, 256)
    if units > used + 9:
        g_ref[used + 9 :] = jnp.zeros((units - used - 9, UNIT, 256), bf16)


def give_late(sums, rest, early, stages):
    units = 9 * (D // UNIT)
    ahead = [part for part in sums if part.start + part.size <= units]
    for part in ahead:
        part.give()
    rest()
    for part in sums[len(ahead):]:
        part.give()
    step(early, stages)


def last_kernel(count, sets, draw_ref, dlogit_ref, early_ref, h_ref, dgate_ref, w_ref, wsmall_ref, x_ref, gain_ref,
                dresid_ref, extra_ref, late_out, early_out, dx_ref,
                proj_ref, logit_ref, part_ref, dsmall_ref, rows_ref, g_ref, land_ref, e_ref, eland_ref,
                send, recv, recv_q, recv_kv, local, gsend, grecv, gsem, esend, erecv, esem):
    near, far, seq = sets
    bits = [near, far] + seq
    stages, least = len(bits), 1 << len(bits)
    me = greet_all(bits, count)
    early = sums_of(early_ref.shape[0], least, sets, early_ref, e_ref, eland_ref, early_out, esend, erecv, esem)
    for part in early:
        part.give()

    holders = held_heads(count)
    first = first_head(me, count)
    started = []
    for k in far_first(count) + [0]:
        peer = lax.rem(me + k, count)
        pairs = [(None, dlogit_ref.at[peer], logit_ref.at[me], recv.at[k])]
        for slot in range(2):
            head = first + slot
            target = proj_ref.at[pl.ds(pl.multiple_of(head * HDIM, HDIM), HDIM)]
            pairs.append((is_mine(me, slot, peer, count), draw_ref.at[peer, 0, slot], target, recv_q.at[head]))
            used = (head * count < HEADS * (me + 1)) & (head * count + count > HEADS * me)
            order = me - holder(head, 0, count)
            pairs.append((used, draw_ref.at[peer, pl.ds(1, 2), slot], part_ref.at[head, order], recv_kv.at[head, order]))
        for i, (mine, src, dst, sem) in enumerate(pairs):
            copy = push(src, dst, send.at[k, i], sem, peer) if k else pltpu.make_async_copy(src, dst, local.at[i])
            started.append((mine, k, copy))
            if mine is None:
                copy.start()
            else:
                pl.when(mine)(copy.start)

    step(early, stages)
    step(early, stages)

    for mine, k, copy in started:
        if mine is not None:
            pl.when(mine)(copy.wait_send if k else copy.wait)
        else:
            copy.wait()
    for head in range(HEADS):
        source = holder(head, me, count)
        copy = push(draw_ref.at[0, 0, 0], proj_ref.at[pl.ds(head * HDIM, HDIM)], send.at[0, 0], recv_q.at[head], lax.rem(me + 1, count))
        pl.when(source != me)(copy.wait_recv)
        for j, (d, s) in enumerate(holders[head]):
            copy = push(draw_ref.at[0, pl.ds(1, 2), 0], part_ref.at[head, j], send.at[0, 0], recv_kv.at[head, j], lax.rem(me + 1, count))
            pl.when(me != d)(copy.wait_recv)

    put_together(holders, part_ref, logit_ref, proj_ref, dsmall_ref)
    proj_ref[3 * D :] = dgate_ref[...]

    late_weights(h_ref, proj_ref, g_ref)
    late = sums_of(g_ref.shape[0], least, sets, None, g_ref, land_ref, late_out, gsend, grecv, gsem)

    def rest():
        late_rest(h_ref, proj_ref, w_ref, wsmall_ref, x_ref, gain_ref, dresid_ref, extra_ref, dsmall_ref, rows_ref, dx_ref, g_ref)

    give_late(late, rest, early, stages)
    early_left = 2 * stages - 3
    for stage in range(2 * stages):
        step(late, stages)
        if stage < early_left:
            step(early, stages)


def last(count, sets, d_raw, d_logits, early, h, d_gate, w_attn, w_small, x, gain, d_resid, extra):
    stages = 2 + len(sets[2])
    units = padded(9 * (D // UNIT) + 9, 1 << stages)
    rows = h.shape[0]
    most = max(len(held) for held in held_heads(count))
    vmem = pl.BlockSpec(memory_space=pltpu.VMEM)
    dma = pltpu.SemaphoreType.DMA
    shape = (UNIT, 256)
    return pl.pallas_call(
        functools.partial(last_kernel, count, sets),
        out_shape=[
            jax.ShapeDtypeStruct((units,) + shape, bf16),
            jax.ShapeDtypeStruct(early.shape, bf16),
            jax.ShapeDtypeStruct((rows, D), f32),
        ],
        in_specs=[ANY] * 3 + [vmem] * 8,
        out_specs=[ANY, ANY, vmem],
        scratch_shapes=[
            pltpu.VMEM((4 * D, rows), bf16),
            pltpu.VMEM((count, 2, 8, rows), f32),
            pltpu.VMEM((HEADS, most, 2, HDIM, rows), bf16),
            pltpu.VMEM((8 * HEADS, rows), f32),
            pltpu.VMEM((SMALL, D), f32),
            pltpu.VMEM((units,) + shape, bf16),
            pltpu.VMEM((units,) + shape, bf16),
            pltpu.VMEM((early.shape[0] // 2,) + shape, bf16),
            pltpu.VMEM(early.shape, bf16),
            dma((count, 5)), dma((count,)), dma((HEADS,)), dma((HEADS, most)), dma((5,)),
            dma((PARTS, 2 * stages)), dma((PARTS, 2 * stages)), dma((PARTS,)),
            dma((PARTS, 2 * stages)), dma((PARTS, 2 * stages)), dma((PARTS,)),
        ],
        compiler_params=pltpu.CompilerParams(collective_id=3, has_side_effects=True, vmem_limit_bytes=62 * 2**20),
        name="last",
    )(d_raw, d_logits, early, h, d_gate, w_attn, w_small, x, gain, d_resid, extra)


def unpack_kernel(parts, *refs):
    o_ref = refs[-1]
    at = 0
    for ref, blocks in zip(refs, parts):
        here = (pl.program_id(0) >= at) & (pl.program_id(0) < at + blocks)

        @pl.when(here)
        def _():
            o_ref[...] = ref[...].reshape(o_ref.shape).astype(f32)

        at += blocks


def unpack(rows, *parts):
    size = rows // UNIT
    specs, at = [], 0
    for _, first, blocks in parts:
        index = lambda i, at=at, first=first, blocks=blocks: (first + jnp.clip(i - at, 0, blocks - 1), 0, 0)
        specs.append(pl.BlockSpec((size, UNIT, 256), index))
        at += blocks
    return pl.pallas_call(
        functools.partial(unpack_kernel, [blocks for _, _, blocks in parts]),
        grid=(at,),
        in_specs=specs,
        out_specs=pl.BlockSpec((rows, 256), lambda i: (0, i)),
        out_shape=jax.ShapeDtypeStruct((rows, 256 * at), f32),
        compiler_params=pltpu.CompilerParams(vmem_limit_bytes=32 * 2**20),
        name="unpack",
    )(*[units for units, _, _ in parts])


def back_kernel(count, sets, skip_ref, bias_ref, dmixed_ref, logits_ref, gains_ref, wsmall_ref, gain_ref, extra_ref,
                raw_in, full_in, q_in, k_in, kt_in, vt_in, early_ref, h_in, dgate_in, w_in, x_in, dresid_in,
                late_out, early_out, dx_ref,
                raw_ref, full_ref, q_ref, k_ref, kt_ref, vt_ref, do_ref, v_ref, cum_ref, dq_ref, dk_ref, dv_ref,
                draw_ref, dlogit_ref, gsum_ref,
                proj_ref, logit_ref, part_ref, dsmall_ref, rows_ref, h_ref, w_ref, x_ref, dresid_ref,
                g_ref, land_ref, e_ref, eland_ref,
                load, send, recv, recv_q, recv_kv, own, gsend, grecv, gsem, esend, erecv, esem):
    near, far, seq = sets
    bits = [near, far] + seq
    stages, least = len(bits), 1 << len(bits)
    blocks = 2 * count
    sums = (dq_ref, dk_ref, dv_ref)

    def state(slot):
        pairs = ((full_in, full_ref), (q_in, q_ref), (k_in, k_ref), (kt_in, kt_ref), (vt_in, vt_ref))
        return [pltpu.make_async_copy(src.at[slot], dst, load.at[i]) for i, (src, dst) in enumerate(pairs)]

    other = [
        pltpu.make_async_copy(src, dst, load.at[5 + i])
        for i, (src, dst) in enumerate((
            (raw_in, raw_ref), (h_in, h_ref), (dgate_in, proj_ref.at[pl.ds(3 * D, D)]), (w_in, w_ref), (x_in, x_ref), (dresid_in, dresid_ref)))
    ]
    for copy in state(0) + other:
        copy.start()
    me = greet_all(bits, count)
    first = first_head(me, count)
    holders = held_heads(count)
    early = sums_of(early_ref.shape[0], least, sets, early_ref, e_ref, eland_ref, early_out, esend, erecv, esem)
    for part in early:
        part.give()
    gsum_ref[...] = jnp.zeros(gsum_ref.shape, f32)

    def sends(slot, k):
        peer = lax.rem(me + k, count)
        head = first + slot
        order = me - holder(head, 0, count)
        used = (head * count < HEADS * (me + 1)) & (head * count + count > HEADS * me)
        target = proj_ref.at[pl.ds(pl.multiple_of(head * HDIM, HDIM), HDIM)]
        items = [
            (None, dlogit_ref.at[peer, slot], logit_ref.at[me, slot], recv.at[k, slot]),
            (is_mine(me, slot, peer, count), draw_ref.at[peer, 0, slot], target, recv_q.at[head]),
            (used, draw_ref.at[peer, pl.ds(1, 2), slot], part_ref.at[head, order], recv_kv.at[head, order]),
        ]
        return [
            (mine, push(src, dst, send.at[k, slot, i], sem, peer) if k else pltpu.make_async_copy(src, dst, own.at[slot, i]))
            for i, (mine, src, dst, sem) in enumerate(items)
        ]

    for slot in range(2):
        for copy in state(slot):
            copy.wait()

        def prepare(block, carried):
            prepare_back(count, block, dmixed_ref.at[:, slot], full_ref, vt_ref, do_ref, v_ref, *sums)
            return carried

        lax.fori_loop(0, blocks, prepare, 0)
        step(early, stages)

        def one_place(place, carried):
            for i in range(blocks // UNROLL_BACK):
                pairs = pairs_of_place(place, i, UNROLL_BACK, count)
                masks = [keep_factor(skip_ref, row, column) for row, column in pairs]
                if (i + 1) * UNROLL_BACK == blocks:
                    pairs.append((place, place))
                    masks[-1:] = [True, True]
                batch_back(pairs, masks, q_ref, k_ref, kt_ref, v_ref, do_ref, *sums)
            return carried

        low, high = own_places(me, slot, count)
        middle = (low + high) // 2
        if slot == 0:
            lax.fori_loop(low, high, one_place, 0)
        else:
            lax.fori_loop(low, middle, one_place, 0)
            step(early, stages)
            lax.fori_loop(middle, high, one_place, 0)
        step(early, stages)
        if slot == 0:
            for copy in state(1):
                copy.start()
            other[0].wait()
        raws, logits, gains = raw_ref.at[:, :, slot], logits_ref.at[:, slot], gains_ref.at[slot]
        draws, dlogits = draw_ref.at[:, :, slot], dlogit_ref.at[:, slot]

        def finish(number, carried):
            block = blocks - 1 - number
            mine = is_mine(me, slot, place_of(block, count), count)
            return finish_back(count, block, carried, mine, raws, logits, gains, *sums, draws, dlogits, cum_ref)

        zero = jnp.zeros((HDIM, BLK), f32)
        _, _, sum_q, sum_k = lax.fori_loop(0, blocks, finish, (zero, zero, zero, zero))
        lane = lax.broadcasted_iota(jnp.int32, (HDIM, D), 1)
        channel = lax.broadcasted_iota(jnp.int32, (HDIM, D), 0)
        here = lane == channel + (first + slot) * HDIM
        for i, column in enumerate((sum_q, sum_k)):
            placed = jnp.where(here, jnp.sum(column, 1, keepdims=True), 0.0)
            gsum_ref[i : i + 1] += jnp.sum(placed, 0, keepdims=True)
        forget_back(count, bias_ref[slot], logits, cum_ref, dlogits)
        for k in far_first(count) + [0]:
            for mine, copy in sends(slot, k):
                if mine is None:
                    copy.start()
                else:
                    pl.when(mine)(copy.start)
        step(early, stages)

    for _ in range(LATER):
        step(early, stages)
    for copy in other[1:]:
        copy.wait()
    for slot in range(2):
        for k in far_first(count) + [0]:
            for mine, copy in sends(slot, k):
                if mine is None:
                    copy.wait()
                else:
                    pl.when(mine)(copy.wait_send if k else copy.wait)
    for head in range(HEADS):
        source = holder(head, me, count)
        next_one = lax.rem(me + 1, count)
        copy = push(draw_ref.at[0, 0, 0], proj_ref.at[pl.ds(head * HDIM, HDIM)], send.at[0, 0, 0], recv_q.at[head], next_one)
        pl.when(source != me)(copy.wait_recv)
        for j, (d, s) in enumerate(holders[head]):
            copy = push(draw_ref.at[0, pl.ds(1, 2), 0], part_ref.at[head, j], send.at[0, 0, 0], recv_kv.at[head, j], next_one)
            pl.when(me != d)(copy.wait_recv)

    put_together(holders, part_ref, logit_ref, proj_ref, dsmall_ref)
    late_weights(h_ref, proj_ref, g_ref)
    late = sums_of(g_ref.shape[0], least, sets, None, g_ref, land_ref, late_out, gsend, grecv, gsem)

    def rest():
        late_rest(h_ref, proj_ref, w_ref, wsmall_ref, x_ref, gain_ref, dresid_ref, extra_ref, dsmall_ref, rows_ref, dx_ref, g_ref, gsum_ref)

    give_late(late, rest, early, stages)
    early_left = 2 * stages - 8 - LATER
    for stage in range(2 * stages):
        step(late, stages)
        if stage < early_left:
            step(early, stages)


LATER = 1


def back(count, sets, skip, bias, d_mixed, logits, gains, w_small, gain, extra, raw, full, q, k, kt, vt, early, h, d_gate, w_attn, x, d_resid):
    stages = 2 + len(sets[2])
    units = padded(9 * (D // UNIT) + 9, 1 << stages)
    rows = h.shape[0]
    blocks = 2 * count
    most = max(len(held) for held in held_heads(count))
    vmem = pl.BlockSpec(memory_space=pltpu.VMEM)
    smem = pl.BlockSpec(memory_space=pltpu.SMEM)
    dma = pltpu.SemaphoreType.DMA
    shape = (UNIT, 256)
    held = lambda array: pltpu.VMEM(array.shape[1:], array.dtype)
    return pl.pallas_call(
        functools.partial(back_kernel, count, sets),
        out_shape=[
            jax.ShapeDtypeStruct((units,) + shape, bf16),
            jax.ShapeDtypeStruct(early.shape, bf16),
            jax.ShapeDtypeStruct((rows, D), f32),
        ],
        in_specs=[smem, smem] + [vmem] * 6 + [ANY] * 12,
        out_specs=[ANY, ANY, vmem],
        scratch_shapes=[
            pltpu.VMEM(raw.shape, bf16), held(full), held(q), held(k), held(kt), held(vt),
            pltpu.VMEM((blocks + 1, 128, BLK), bf16),
            pltpu.VMEM((blocks, BLK, 128), bf16),
            pltpu.VMEM((count, rows), f32),
            pltpu.VMEM((blocks + 1, 80, BLK), f32),
            pltpu.VMEM((blocks, 80, BLK), f32),
            pltpu.VMEM((blocks, HDIM, BLK), f32),
            pltpu.VMEM(raw.shape, bf16),
            pltpu.VMEM(logits.shape, f32),
            pltpu.VMEM((8, D), f32),
            pltpu.VMEM((4 * D, rows), bf16),
            pltpu.VMEM((count, 2, 8, rows), f32),
            pltpu.VMEM((HEADS, most, 2, HDIM, rows), bf16),
            pltpu.VMEM((8 * HEADS, rows), f32),
            pltpu.VMEM((SMALL, D), f32),
            pltpu.VMEM(h.shape, bf16),
            pltpu.VMEM(w_attn.shape, bf16),
            pltpu.VMEM(x.shape, bf16),
            pltpu.VMEM(d_resid.shape, f32),
            pltpu.VMEM((units,) + shape, bf16),
            pltpu.VMEM((units,) + shape, bf16),
            pltpu.VMEM((early.shape[0] // 2,) + shape, bf16),
            pltpu.VMEM(early.shape, bf16),
            dma((11,)), dma((count, 2, 3)), dma((count, 2)), dma((HEADS,)), dma((HEADS, most)), dma((2, 3)),
            dma((PARTS, 2 * stages)), dma((PARTS, 2 * stages)), dma((PARTS,)),
            dma((PARTS, 2 * stages)), dma((PARTS, 2 * stages)), dma((PARTS,)),
        ],
        compiler_params=pltpu.CompilerParams(collective_id=4, has_side_effects=True, vmem_limit_bytes=63 * 2**20),
        name="back",
    )(skip, bias, d_mixed, logits, gains, w_small, gain, extra, raw, full, q, k, kt, vt, early, h, d_gate, w_attn, x, d_resid)


def rms_scale(values, gains):
    inverse = lax.rsqrt(jnp.mean(values * values, axis=-1, keepdims=True) + EPS)
    return values * inverse * gains


def swiglu(gate_up):
    return jax.nn.silu(gate_up[:, :FF]) * gate_up[:, FF:]


def local(tokens, cotangent, skip_table, gain_attn, w_attn, w_heads, forget_bias, query_gain, key_gain,
          w_out, gain_ffn, w_gate_up, w_down):
    count = lax.axis_size("seq")
    me = lax.axis_index("seq")
    rows = tokens.shape[1]
    both = ("seq", "group")
    inputs = tokens[0].astype(f32)
    device = me.astype(jnp.int32)[None]
    head = first_head(me, count)
    skip = skip_table[0]
    gains = jnp.stack([query_gain.reshape(HEADS, HDIM), key_gain.reshape(HEADS, HDIM)], 2)
    gains = lax.dynamic_slice_in_dim(gains, head, 2, 0)
    bias = lax.dynamic_slice_in_dim(forget_bias, head, 2, 0)
    w_small = jnp.pad(w_heads.reshape(D, 3, HEADS).transpose(0, 2, 1), ((0, 0), (0, 0), (0, 5))).reshape(D, HEADS * 8)

    if count <= 8:
        h_first, gate_logit, attended, raw, logits, mixed, q, k, kt, vt = front(
            count, skip, bias, tokens[0], w_attn, w_small, gain_attn[None], gains
        )
    else:
        h_first = rms_scale(inputs, gain_attn).astype(bf16)
        qkv = dot(w_attn[:, : 3 * D], h_first, 0, 1).astype(bf16).reshape(3, HEADS, HDIM, rows)
        gate_logit = dot(w_attn[:, 3 * D :], h_first, 0, 1)
        logits_here = dot(w_small, h_first, 0, 1).reshape(HEADS, 8, rows)
        raw, logits = heads_out(qkv, logits_here, count)
        mixed_low, mixed, q, k, kt, vt = attend_forward(device, skip, bias, raw, logits, gains)
        attended = mixed_back(mixed_low, count).reshape(D, rows)
    attended = attended.astype(f32)

    gate_open = jax.nn.sigmoid(gate_logit)
    gated = (gate_open * attended).astype(bf16)
    resid = inputs + dot(gated, w_out, 0, 0)
    normed_ffn, norm_back_ffn = jax.vjp(rms_scale, resid, gain_ffn)
    h_second = normed_ffn.astype(bf16)
    gate_up = dot(h_second, w_gate_up, 1, 0)
    hidden, hidden_back = jax.vjp(swiglu, gate_up)
    hidden_low = hidden.astype(bf16)
    output = resid + dot(hidden_low, w_down, 1, 0)
    d_low = cotangent[0]
    d_output = d_low.astype(f32)
    (d_gate_up,) = hidden_back(dot(d_low, w_down, 1, 1))
    d_gate_low = d_gate_up.astype(bf16)
    d_resid_norm, grad_gain_ffn = norm_back_ffn(dot(d_gate_low, w_gate_up, 1, 1))
    d_resid = d_output + d_resid_norm
    d_branch = d_resid.astype(bf16)
    d_gated = dot(w_out, d_branch, 1, 1)
    d_gate_logit = (d_gated * attended * gate_open * (1.0 - gate_open)).astype(bf16)
    d_mixed = (d_gated * gate_open).astype(bf16).reshape(HEADS, HDIM, rows)

    near_far, seq_bits = group_bits(lax.axis_size("group"), count)
    sets = (near_far[0], near_far[1], seq_bits)
    units = padded(1440, 1 << (2 + len(seq_bits)))
    d_mixed_all, early = grads_out(
        count, units, d_mixed, h_first, d_gate_logit, h_second, d_gate_low, hidden_low, d_low, gated, d_branch
    )
    zeros = lambda n: jnp.zeros((n, D), f32)
    if count <= 8:
        extra = jnp.concatenate([zeros(1), grad_gain_ffn[None], zeros(SMALL - 3 * HEADS - 2)], 0)
        late, early, d_inputs = back(
            count, sets, skip, bias, d_mixed_all, logits, gains, w_small, gain_attn[None], extra,
            raw, mixed, q, k, kt, vt, early, h_first, d_gate_logit, w_attn, tokens[0], d_resid,
        )
    else:
        d_raw, d_logits, d_gains = attend_backward(device, skip, bias, raw, logits, gains, d_mixed_all, mixed, q, k, kt, vt)
        placed = lax.dynamic_update_slice(jnp.zeros((HEADS, HDIM, 2), f32), d_gains, (head, 0, 0)).reshape(D, 2).T
        extra = jnp.concatenate([zeros(1), grad_gain_ffn[None], placed, zeros(SMALL - 3 * HEADS - 4)], 0)
        late, early, d_inputs = last(
            count, sets, d_raw, d_logits, early, h_first, d_gate_logit, w_attn, w_small, tokens[0], gain_attn[None], d_resid, extra
        )
    row = 3 * HEADS
    used = 9 * (D // UNIT)
    small = late[used : used + 9].reshape(3, SMALL, 256).transpose(1, 0, 2).reshape(SMALL, D).astype(f32)
    return (
        output[None].astype(bf16),
        d_inputs[None],
        small[row],
        unpack(D, (late, 0, 9), (early, 27, 3)),
        small[:row].reshape(HEADS, 3, D).transpose(2, 1, 0).reshape(D, row),
        small[row + 4, :HEADS],
        small[row + 2],
        small[row + 3],
        unpack(D, (early, 24, 3)),
        small[row + 1],
        unpack(D, (early, 0, 16)),
        unpack(FF, (early, 6, 3)),
    )


def solution(mesh):
    rows = P("group", "seq", None)
    return jax.shard_map(
        local,
        mesh=mesh,
        in_specs=(rows, rows, P("group", None, None)) + (P(),) * 10,
        out_specs=(rows, rows) + (P(),) * 10,
        check_vma=False,
    )
```

```python
import functools

import jax
import jax.numpy as jnp
from jax import lax
from jax.experimental import pallas as pl
from jax.experimental.pallas import tpu as pltpu
from jax.sharding import PartitionSpec as P

D, FF = 768, 2048
MESH = pl.DeviceIdType.MESH
ANY = pl.BlockSpec(memory_space=pl.ANY)

HEADS, HDIM, BLK = 12, 64, 256
EPS = 1e-06
LOG2E = 1.4426950408889634
LN2 = 0.6931471805599453
SCORE = HDIM ** -0.5
f32, bf16 = jnp.float32, jnp.bfloat16
UNROLL = 8
UNROLL_BACK = 4
NN = (((1,), (0,)), ((), ()))
NT = (((1,), (1,)), ((), ()))
TN = (((0,), (0,)), ((), ()))


def mm(a, b, dims=NN):
    return lax.dot_general(a, b, dims, preferred_element_type=f32)


def split3(v):
    hi = v.astype(bf16).astype(f32)
    rest = v - hi
    mid = rest.astype(bf16).astype(f32)
    return hi, mid, rest - mid


def place_of(block, count):
    return jnp.where(block < count, block, 2 * count - 1 - block)


def lanes_of(block, count):
    return pl.ds(pl.multiple_of(jnp.where(block < count, 0, BLK), BLK), BLK)


def first_head(device, count):
    return jnp.minimum(HEADS * device // count, HEADS - 2)


def is_mine(device, slot, place, count):
    chunk = (first_head(device, count) + slot) * count + place
    return (chunk >= HEADS * device) & (chunk < HEADS * device + HEADS)


def list_pairs(skip_ref, pairs_ref, own_ref, device, slot, count, unroll):
    spare = 2 * count

    def row(number, found):
        def column(other, found):
            pairs_ref[found] = number * 1024 + other
            return found + jnp.where(skip_ref[number, other] == 0, 1, 0)

        mine = is_mine(device, slot, place_of(number, count), count)
        own_ref[found[1]] = number
        below = lax.fori_loop(0, jnp.where(mine, number, 0), column, found[0])
        return below, found[1] + jnp.where(mine, 1, 0)

    below, own = lax.fori_loop(0, spare, row, (0, 0))
    for extra in range(unroll):
        pairs_ref[below + extra] = spare * 1024
        own_ref[own + extra] = spare
    return pl.cdiv(below, unroll), pl.cdiv(own, unroll)


def running_sum(values, count, reverse):
    t = lax.broadcasted_iota(jnp.int32, (BLK, BLK), 0)
    p = lax.broadcasted_iota(jnp.int32, (BLK, BLK), 1)
    ones = jnp.where(t >= p if reverse else t <= p, 1.0, 0.0).astype(bf16)
    halves = []
    for half in range(2):
        part = values[:, half * BLK : (half + 1) * BLK]
        halves.append(sum(mm(piece.astype(bf16), ones) for piece in split3(part)))
    edge = 0 if reverse else BLK - 1
    first, last = (jnp.broadcast_to(h[:, edge : edge + 1], (count, 128)) for h in halves)
    rows = lax.broadcasted_iota(jnp.int32, (count, 128), 0)

    def scan(total, down):
        own = total
        step = 1
        while step < count:
            moved = pltpu.roll(total, step if down else count - step, 0)
            total = total + jnp.where(rows >= step if down else rows < count - step, moved, 0.0)
            step *= 2
        return total - own

    if reverse:
        all_last = jnp.sum(last, axis=0, keepdims=True)
        offsets = scan(first, False) + all_last, scan(last, True)
    else:
        all_first = jnp.sum(first, axis=0, keepdims=True)
        offsets = scan(first, True), scan(last, False) + all_first
    return jnp.concatenate([halves[0] + offsets[0][:, :1], halves[1] + offsets[1][:, :1]], 1)


def shifted(current, before):
    lane = lax.broadcasted_iota(jnp.int32, current.shape, 1)
    return jnp.where(lane == 0, pltpu.roll(before, 1, 1), pltpu.roll(current, 1, 1))


def shifted_back(current, after):
    lane = lax.broadcasted_iota(jnp.int32, current.shape, 1)
    return jnp.where(lane == BLK - 1, pltpu.roll(after, BLK - 1, 1), pltpu.roll(current, BLK - 1, 1))


def stack_rows(top, rows, size):
    extra = size if top is None else size - top.shape[0]
    number = lax.broadcasted_iota(jnp.int32, (extra, BLK), 0)
    bottom = jnp.zeros((extra, BLK), f32)
    for i, r in enumerate(rows):
        bottom = jnp.where(number == i, r, bottom)
    return bottom if top is None else jnp.concatenate([top, bottom], 0)


def prepare_block(count, block, carried, raw_ref, logit_ref, gain_ref, cum_ref, q_ref, k_ref, kt_ref, vt_ref):
    place, lanes = place_of(block, count), lanes_of(block, count)
    q_raw, k_raw, v_raw = (raw_ref[place, i, :, lanes].astype(f32) for i in range(3))
    cum = cum_ref[pl.ds(place, 1), lanes]
    parts = split3(cum)
    one = jnp.ones_like(cum)
    query = q_raw * lax.rsqrt(jnp.mean(q_raw * q_raw, 0, keepdims=True) + EPS) * (gain_ref[:, 1:2] * (SCORE * LOG2E))
    q_ref[block] = stack_rows(query, (*parts, one, one, one), 128).astype(bf16)
    rate_k = jax.nn.sigmoid(logit_ref[place, 1:2, lanes])
    rate_v = jax.nn.sigmoid(logit_ref[place, 2:3, lanes])
    key = k_raw + rate_k * (shifted(k_raw, carried[0]) - k_raw)
    key = key * lax.rsqrt(jnp.mean(key * key, 0, keepdims=True) + EPS) * gain_ref[:, 2:3]
    value = v_raw + rate_v * (shifted(v_raw, carried[1]) - v_raw)
    k_ref[block] = stack_rows(key, (one, one, one, *(-c for c in parts)), 128).T.astype(bf16)
    kt_ref[block] = stack_rows(key, (one,), 80).astype(bf16)
    vt_ref[block] = stack_rows(value, (one, one, one), 80).astype(bf16)
    return k_raw, v_raw


def finish_block(count, block, acc_ref, cum_ref, mixed_full_ref, mixed_ref, q_ref):
    place, lanes = place_of(block, count), lanes_of(block, count)
    summed = acc_ref[block]
    norm = summed[HDIM : HDIM + 1]
    mixed = summed[:HDIM] * (1.0 / norm)
    mixed_full_ref[block] = mixed
    mixed_ref[place, :, lanes] = mixed.astype(bf16)
    parts = split3(cum_ref[pl.ds(place, 1), lanes] - jnp.log2(norm))
    one = jnp.ones_like(norm)
    q_ref[block, HDIM : HDIM + 16, :] = stack_rows(None, (*parts, one, one, one), 16).astype(bf16)


def log_forget_sums(logits, count):
    log_forget = jnp.minimum(logits, 0.0) - jnp.log1p(jnp.exp(-jnp.abs(logits)))
    return running_sum(log_forget, count, False) * LOG2E


def causal():
    return lax.broadcasted_iota(jnp.int32, (BLK, BLK), 0) <= lax.broadcasted_iota(jnp.int32, (BLK, BLK), 1)


def forward_kernel(count, device_ref, skip_ref, bias_ref, raw_ref, logit_ref, gain_ref,
                   mixed_ref, mixed_full_ref, q_ref, k_ref, kt_ref, vt_ref,
                   cum_ref, acc_ref, pairs_ref, own_ref):
    slot = pl.program_id(0)
    device = device_ref[0]
    blocks = 2 * count
    pair_steps, own_steps = list_pairs(skip_ref, pairs_ref, own_ref, device, slot, count, UNROLL)
    cum_ref[...] = log_forget_sums(logit_ref[:, 0, :] + bias_ref[slot], count)

    def prepare(block, carried):
        return prepare_block(count, block, carried, raw_ref, logit_ref, gain_ref, cum_ref, q_ref, k_ref, kt_ref, vt_ref)

    zero = jnp.zeros((HDIM, BLK), f32)
    lax.fori_loop(0, blocks, prepare, (zero, zero))
    q_ref[blocks] = jnp.zeros(q_ref.shape[1:], bf16)

    def together(pairs, diagonal):
        scores = [mm(k_ref[column], q_ref[row]) for row, column in pairs]
        weights = [jnp.exp2(score) for score in scores]
        if diagonal:
            weights = [jnp.where(causal(), weight, 0.0) for weight in weights]
        weights = [weight.astype(bf16) for weight in weights]
        parts = [mm(vt_ref[column], weight) for (row, column), weight in zip(pairs, weights)]
        for (row, column), part in zip(pairs, parts):
            acc_ref[row] = part if diagonal else acc_ref[row] + part

    def own_rows(step, carried):
        rows = [own_ref[step * UNROLL + i] for i in range(UNROLL)]
        together([(row, jnp.minimum(row, blocks - 1)) for row in rows], True)
        return carried

    def kept_pairs(step, carried):
        codes = [pairs_ref[step * UNROLL + i] for i in range(UNROLL)]
        together([(code >> 10, code & 1023) for code in codes], False)
        return carried

    lax.fori_loop(0, own_steps, own_rows, 0)
    lax.fori_loop(0, pair_steps, kept_pairs, 0)

    def finish(block, carried):
        finish_block(count, block, acc_ref, cum_ref, mixed_full_ref, mixed_ref, q_ref)
        return carried

    lax.fori_loop(0, blocks, finish, 0)


def own_places(device, slot, count):
    start = (first_head(device, count) + slot) * count
    low = jnp.clip(HEADS * device - start, 0, count)
    return low, jnp.clip(HEADS * device + HEADS - start, low, count)


def pairs_of_place(place, batch, size, count):
    found = []
    for i in range(size):
        number = batch * size + i
        lower = number < place
        found.append((jnp.where(lower, place, 2 * count - 1 - place), jnp.where(lower, number, number - place)))
    return found


def keep_factor(skip_ref, row, column):
    return jnp.where(skip_ref[row, column] == 0, 1.0, 0.0)


def buffers(count):
    return pl.Buffered(1 if count > 8 else 2)


def attend_forward(device, skip, bias, raw, logits, gains):
    count = raw.shape[0]
    blocks = 2 * count
    most = blocks * (blocks - 1) // 2 + UNROLL
    mode = buffers(count)
    by_slot = lambda *shape: pl.BlockSpec((None,) + shape, lambda s, *_: (s,) + (0,) * len(shape), pipeline_mode=mode)
    out = lambda shape, dtype: jax.ShapeDtypeStruct((2,) + shape, dtype)
    return pl.pallas_call(
        functools.partial(forward_kernel, count),
        grid_spec=pltpu.PrefetchScalarGridSpec(
            num_scalar_prefetch=3,
            grid=(2,),
            in_specs=[
                pl.BlockSpec((count, 3, None, HDIM, 2 * BLK), lambda s, *_: (0, 0, s, 0, 0), pipeline_mode=mode),
                pl.BlockSpec((count, None, 8, 2 * BLK), lambda s, *_: (0, s, 0, 0), pipeline_mode=mode),
                by_slot(HDIM, 8),
            ],
            out_specs=[
                by_slot(count, HDIM, 2 * BLK),
                by_slot(blocks, HDIM, BLK),
                by_slot(blocks + 1, 128, BLK),
                by_slot(blocks, BLK, 128),
                by_slot(blocks, 80, BLK),
                by_slot(blocks, 80, BLK),
            ],
            scratch_shapes=[
                pltpu.VMEM((count, 2 * BLK), f32),
                pltpu.VMEM((blocks + 1, 80, BLK), f32),
                pltpu.SMEM((most,), jnp.int32),
                pltpu.SMEM((blocks + UNROLL,), jnp.int32),
            ],
        ),
        out_shape=[
            out((count, HDIM, 2 * BLK), bf16),
            out((blocks, HDIM, BLK), f32),
            out((blocks + 1, 128, BLK), bf16),
            out((blocks, BLK, 128), bf16),
            out((blocks, 80, BLK), bf16),
            out((blocks, 80, BLK), bf16),
        ],
        compiler_params=pltpu.CompilerParams(vmem_limit_bytes=60 * 2**20),
        name="attend_forward",
    )(device, skip, bias, raw, logits, gains)


def norm_back(v, gain, u):
    scale = lax.rsqrt(jnp.mean(v * v, 0, keepdims=True) + EPS)
    hat = v * scale
    gu = gain * u
    return scale * (gu - hat * jnp.mean(hat * gu, 0, keepdims=True)), hat * u


def prepare_back(count, block, dmixed_ref, mixed_ref, vt_ref, do_ref, v_ref, dq_ref, dk_ref, dv_ref):
    place, lanes = place_of(block, count), lanes_of(block, count)
    d_out = dmixed_ref[place, :, lanes].astype(f32)
    delta = jnp.sum(d_out * mixed_ref[block], 0, keepdims=True)
    do_ref[block] = stack_rows(d_out, [-d for d in split3(delta)], 128).astype(bf16)
    wide = jnp.zeros((128 - 80, BLK), f32)
    v_ref[block] = jnp.concatenate([vt_ref[block].astype(f32), wide], 0).T.astype(bf16)
    dq_ref[block] = jnp.zeros(dq_ref.shape[1:], f32)
    dk_ref[block] = jnp.zeros(dk_ref.shape[1:], f32)
    dv_ref[block] = jnp.zeros(dv_ref.shape[1:], f32)


def batch_back(pairs, masks, q_ref, k_ref, kt_ref, v_ref, do_ref, dq_ref, dk_ref, dv_ref):
    weights = [jnp.exp2(mm(k_ref[column], q_ref[row])) for row, column in pairs]
    for i, mask in enumerate(masks):
        if mask is True:
            weights[i] = jnp.where(causal(), weights[i], 0.0)
        elif mask is not None:
            weights[i] = weights[i] * mask
    d_weights = [mm(v_ref[column], do_ref[row]) for row, column in pairs]
    low_weights = [weight.astype(bf16) for weight in weights]
    d_scores = [(weight * d_weight).astype(bf16) for weight, d_weight in zip(weights, d_weights)]
    parts = [mm(do_ref[row, :HDIM], weight, NT) for (row, _), weight in zip(pairs, low_weights)]
    for (_, column), part in zip(pairs, parts):
        dv_ref[column] += part
    parts = [mm(kt_ref[column], d_score) for (_, column), d_score in zip(pairs, d_scores)]
    for (row, _), part in zip(pairs, parts):
        dq_ref[row] += part
    parts = [mm(q_ref[row, :80], d_score, NT) for (row, _), d_score in zip(pairs, d_scores)]
    for (_, column), part in zip(pairs, parts):
        dk_ref[column] += part


def finish_back(count, block, carried, mine, raw_ref, logit_ref, gain_ref, dq_ref, dk_ref, dv_ref, draw_ref, dlogit_ref, cum_ref):
    next_k, next_v, sum_q, sum_k = carried
    place, lanes = place_of(block, count), lanes_of(block, count)
    earlier = jnp.maximum(block - 1, 0)
    place_before, lanes_before = place_of(earlier, count), lanes_of(earlier, count)
    exists = jnp.where(block > 0, 1.0, 0.0)
    q_raw, k_raw, v_raw = (raw_ref[place, i, :, lanes].astype(f32) for i in range(3))
    k_step = shifted(k_raw, raw_ref[place_before, 1, :, lanes_before].astype(f32) * exists) - k_raw
    v_step = shifted(v_raw, raw_ref[place_before, 2, :, lanes_before].astype(f32) * exists) - v_raw
    rate_k = jax.nn.sigmoid(logit_ref[place, 1:2, lanes])
    rate_v = jax.nn.sigmoid(logit_ref[place, 2:3, lanes])
    dq, dk, dv = dq_ref[block], dk_ref[block], dv_ref[block]
    dq_raw, part_q = norm_back(q_raw, gain_ref[:, 1:2], dq[:HDIM] * SCORE)
    dk_mixed, part_k = norm_back(k_raw + rate_k * k_step, gain_ref[:, 2:3], dk[:HDIM] * LN2)
    send_k, send_v = rate_k * dk_mixed, rate_v * dv
    draw_ref[place, 0, :, lanes] = dq_raw.astype(bf16)
    draw_ref[place, 1, :, lanes] = (dk_mixed - send_k + shifted_back(send_k, next_k)).astype(bf16)
    draw_ref[place, 2, :, lanes] = (dv - send_v + shifted_back(send_v, next_v)).astype(bf16)
    dlogit_ref[place, 1:2, lanes] = (1.0 - rate_k) * jnp.sum(k_step * send_k, 0, keepdims=True)
    dlogit_ref[place, 2:3, lanes] = (1.0 - rate_v) * jnp.sum(v_step * send_v, 0, keepdims=True)
    cum_ref[pl.ds(place, 1), lanes] = dq[HDIM : HDIM + 1] - dk[HDIM + 3 : HDIM + 4]
    return send_k, send_v, sum_q + jnp.where(mine, part_q, 0.0), sum_k + part_k


def forget_back(count, bias, logit_ref, cum_ref, dlogit_ref):
    d_log = running_sum(cum_ref[...], count, True)
    dlogit_ref[:, 0, :] = d_log * jax.nn.sigmoid(-(logit_ref[:, 0, :] + bias))
    dlogit_ref[:, 3:, :] = jnp.zeros((count, 5, 2 * BLK), f32)


def backward_kernel(count, device_ref, skip_ref, bias_ref, raw_ref, logit_ref, gain_ref, dmixed_ref, mixed_ref,
                    q_ref, k_ref, kt_ref, vt_ref, draw_ref, dlogit_ref, dgain_ref,
                    do_ref, v_ref, cum_ref, dq_ref, dk_ref, dv_ref, pairs_ref, own_ref):
    slot = pl.program_id(0)
    device = device_ref[0]
    blocks = 2 * count
    pair_steps, own_steps = list_pairs(skip_ref, pairs_ref, own_ref, device, slot, count, UNROLL_BACK)
    sums = (dq_ref, dk_ref, dv_ref)

    def prepare(block, carried):
        prepare_back(count, block, dmixed_ref, mixed_ref, vt_ref, do_ref, v_ref, *sums)
        return carried

    lax.fori_loop(0, blocks, prepare, 0)
    do_ref[blocks] = jnp.zeros(do_ref.shape[1:], bf16)
    dq_ref[blocks] = jnp.zeros(dq_ref.shape[1:], f32)

    def own_rows(step, carried):
        rows = [own_ref[step * UNROLL_BACK + i] for i in range(UNROLL_BACK)]
        pairs = [(row, jnp.minimum(row, blocks - 1)) for row in rows]
        batch_back(pairs, [True] * UNROLL_BACK, q_ref, k_ref, kt_ref, v_ref, do_ref, *sums)
        return carried

    def kept_pairs(step, carried):
        codes = [pairs_ref[step * UNROLL_BACK + i] for i in range(UNROLL_BACK)]
        pairs = [(code >> 10, code & 1023) for code in codes]
        batch_back(pairs, [None] * UNROLL_BACK, q_ref, k_ref, kt_ref, v_ref, do_ref, *sums)
        return carried

    lax.fori_loop(0, own_steps, own_rows, 0)
    lax.fori_loop(0, pair_steps, kept_pairs, 0)

    def finish(step, carried):
        block = blocks - 1 - step
        mine = is_mine(device, slot, place_of(block, count), count)
        return finish_back(count, block, carried, mine, raw_ref, logit_ref, gain_ref, *sums, draw_ref, dlogit_ref, cum_ref)

    zero = jnp.zeros((HDIM, BLK), f32)
    _, _, sum_q, sum_k = lax.fori_loop(0, blocks, finish, (zero, zero, zero, zero))
    dgain_ref[:, 1:2] = jnp.sum(sum_q, 1, keepdims=True)
    dgain_ref[:, 2:3] = jnp.sum(sum_k, 1, keepdims=True)
    forget_back(count, bias_ref[slot], logit_ref, cum_ref, dlogit_ref)


def attend_backward(device, skip, bias, raw, logits, gains, dmixed, mixed, q, k, kt, vt):
    count = raw.shape[0]
    blocks = 2 * count
    most = blocks * (blocks - 1) // 2 + UNROLL_BACK
    mode = buffers(count)
    by_slot = lambda *shape: pl.BlockSpec((None,) + shape, lambda s, *_: (s,) + (0,) * len(shape), pipeline_mode=mode)
    raw_spec = pl.BlockSpec((count, 3, None, HDIM, 2 * BLK), lambda s, *_: (0, 0, s, 0, 0), pipeline_mode=mode)
    place_spec = lambda rows: pl.BlockSpec((count, None, rows, 2 * BLK), lambda s, *_: (0, s, 0, 0), pipeline_mode=mode)
    return pl.pallas_call(
        functools.partial(backward_kernel, count),
        grid_spec=pltpu.PrefetchScalarGridSpec(
            num_scalar_prefetch=3,
            grid=(2,),
            in_specs=[
                raw_spec,
                place_spec(8),
                by_slot(HDIM, 8),
                place_spec(HDIM),
                by_slot(blocks, HDIM, BLK),
                by_slot(blocks + 1, 128, BLK),
                by_slot(blocks, BLK, 128),
                by_slot(blocks, 80, BLK),
                by_slot(blocks, 80, BLK),
            ],
            out_specs=[raw_spec, place_spec(8), by_slot(HDIM, 8)],
            scratch_shapes=[
                pltpu.VMEM((blocks + 1, 128, BLK), bf16),
                pltpu.VMEM((blocks, BLK, 128), bf16),
                pltpu.VMEM((count, 2 * BLK), f32),
                pltpu.VMEM((blocks + 1, 80, BLK), f32),
                pltpu.VMEM((blocks, 80, BLK), f32),
                pltpu.VMEM((blocks, HDIM, BLK), f32),
                pltpu.SMEM((most,), jnp.int32),
                pltpu.SMEM((blocks + UNROLL_BACK,), jnp.int32),
            ],
        ),
        out_shape=[
            jax.ShapeDtypeStruct(raw.shape, bf16),
            jax.ShapeDtypeStruct(logits.shape, f32),
            jax.ShapeDtypeStruct(gains.shape, f32),
        ],
        compiler_params=pltpu.CompilerParams(vmem_limit_bytes=60 * 2**20),
        name="attend_backward",
    )(device, skip, bias, raw, logits, gains, dmixed, mixed, q, k, kt, vt)


def holder(head, place, count):
    return (head * count + place) // HEADS


def greet(count):
    me = lax.axis_index("seq")
    barrier = pltpu.get_barrier_semaphore()
    for k in range(1, count):
        peer = lax.rem(me + k, count)
        pl.semaphore_signal(barrier, inc=1, device_id={"seq": peer}, device_id_type=MESH)
    pl.semaphore_wait(barrier, count - 1)
    return me


def far_first(count):
    return sorted(range(1, count), key=lambda k: -min(k, count - k))


def push(src, dst, send, recv, peer):
    return pltpu.make_async_remote_copy(
        src_ref=src, dst_ref=dst, send_sem=send, recv_sem=recv, device_id={"seq": peer}, device_id_type=MESH
    )


def heads_out_kernel(count, x_ref, logit_in, raw_ref, logit_ref, send, recv, local):
    me = greet(count)

    def copies(peer, source, k):
        head = first_head(peer, count)
        items = []
        for slot in range(2):
            items.append((is_mine(peer, slot, me, count), is_mine(me, slot, source, count),
                          push(x_ref.at[0, head + slot], raw_ref.at[me, 0, slot], send.at[k, slot], recv.at[k, slot], peer)))
        items.append((None, None, push(x_ref.at[pl.ds(1, 2), pl.ds(head, 2)], raw_ref.at[me, pl.ds(1, 2)], send.at[k, 2], recv.at[k, 2], peer)))
        items.append((None, None, push(logit_in.at[pl.ds(head, 2)], logit_ref.at[me], send.at[k, 3], recv.at[k, 3], peer)))
        return items

    every = []
    for k in far_first(count):
        items = copies(lax.rem(me + k, count), lax.rem(me + count - k, count), k)
        every.append(items)
        for out, _, copy in items:
            if out is None:
                copy.start()
            else:
                pl.when(out)(copy.start)
    head = first_head(me, count)
    own = [
        pltpu.make_async_copy(x_ref.at[:, pl.ds(head, 2)], raw_ref.at[me], local.at[0]),
        pltpu.make_async_copy(logit_in.at[pl.ds(head, 2)], logit_ref.at[me], local.at[1]),
    ]
    for copy in own:
        copy.start()
    for items in every:
        for out, into, copy in items:
            if out is None:
                copy.wait()
            else:
                pl.when(out)(copy.wait_send)
                pl.when(into)(copy.wait_recv)
    for copy in own:
        copy.wait()


def heads_out(qkv, logits, count):
    return pl.pallas_call(
        functools.partial(heads_out_kernel, count),
        out_shape=[
            jax.ShapeDtypeStruct((count, 3, 2, HDIM, 2 * BLK), bf16),
            jax.ShapeDtypeStruct((count, 2, 8, 2 * BLK), f32),
        ],
        in_specs=[ANY, ANY],
        out_specs=[ANY, ANY],
        scratch_shapes=[pltpu.SemaphoreType.DMA((count, 4)), pltpu.SemaphoreType.DMA((count, 4)), pltpu.SemaphoreType.DMA((2,))],
        compiler_params=pltpu.CompilerParams(collective_id=0, has_side_effects=True),
        name="heads_out",
    )(qkv, logits)


def mixed_back_kernel(count, x_ref, o_ref, send, recv, local):
    me = greet(count)
    first = first_head(me, count)
    started = []
    for k in far_first(count) + [0]:
        peer = lax.rem(me + k, count)
        for slot in range(2):
            mine = is_mine(me, slot, peer, count)
            src, dst = x_ref.at[slot, peer], o_ref.at[first + slot]
            if k:
                copy = push(src, dst, send.at[k, slot], recv.at[first + slot], peer)
            else:
                copy = pltpu.make_async_copy(src, dst, local.at[slot])
            started.append((mine, k, copy))
            pl.when(mine)(copy.start)
    for mine, k, copy in started:
        pl.when(mine)(copy.wait_send if k else copy.wait)
    for head in range(HEADS):
        source = holder(head, me, count)
        copy = push(x_ref.at[0, 0], o_ref.at[head], send.at[0, 0], recv.at[head], lax.rem(me + 1, count))
        pl.when(source != me)(copy.wait_recv)


def mixed_back(mixed, count):
    return pl.pallas_call(
        functools.partial(mixed_back_kernel, count),
        out_shape=jax.ShapeDtypeStruct((HEADS, HDIM, 2 * BLK), bf16),
        in_specs=[ANY],
        out_specs=ANY,
        scratch_shapes=[pltpu.SemaphoreType.DMA((count, 2)), pltpu.SemaphoreType.DMA((HEADS,)), pltpu.SemaphoreType.DMA((2,))],
        compiler_params=pltpu.CompilerParams(collective_id=1, has_side_effects=True),
        name="mixed_back",
    )(mixed)


def grads_out_kernel(count, x_ref, h1_ref, dgate_ref, h2_ref, dgu_ref, hidden_ref, dlow_ref, gated_ref, branch_ref,
                     o_ref, grads_ref, send, recv, local):
    me = greet(count)
    started = []
    for head in range(HEADS):
        peer = holder(head, me, count)
        slot = head - first_head(peer, count)
        away = peer != me
        there = jnp.where(away, peer, lax.rem(me + 1, count))
        copy = push(x_ref.at[head], o_ref.at[me, slot], send.at[head], recv.at[me, slot], there)
        own = pltpu.make_async_copy(x_ref.at[head], o_ref.at[me, slot], local.at[slot])
        pl.when(away)(copy.start)
        pl.when(peer == me)(own.start)
        started.append((away, peer == me, copy, own))

    def put(unit, part):
        grads_ref[pl.ds(unit, 16)] = part.astype(bf16).reshape(16, UNIT, 256)

    def gate_up(i, carried):
        right = dgu_ref[:, pl.ds(pl.multiple_of(i * 256, 256), 256)]
        for j in range(3):
            put(i * 48 + 16 * j, mm(h2_ref[:, 256 * j : 256 * j + 256], right, TN))
        return carried

    lax.fori_loop(0, 2 * FF // 256, gate_up, 0)

    def down(i, carried):
        left = hidden_ref[:, pl.ds(pl.multiple_of(i * 256, 256), 256)]
        for j in range(3):
            put(768 + 128 * j + 16 * i, mm(left, dlow_ref[:, 256 * j : 256 * j + 256], TN))
        return carried

    lax.fori_loop(0, FF // 256, down, 0)
    for i in range(3):
        for j in range(3):
            put(1152 + 48 * i + 16 * j, mm(gated_ref[256 * j : 256 * j + 256, :], branch_ref[:, 256 * i : 256 * i + 256]))
            put(1296 + 48 * i + 16 * j, lax.dot_general(
                h1_ref[:, 256 * j : 256 * j + 256], dgate_ref[256 * i : 256 * i + 256, :],
                (((0,), (1,)), ((), ())), preferred_element_type=f32))
    units = grads_ref.shape[0]
    if units > 1440:
        grads_ref[1440:] = jnp.zeros((units - 1440, UNIT, 256), bf16)

    for away, here, copy, own in started:
        pl.when(away)(copy.wait_send)
        pl.when(here)(own.wait)
    for k in range(1, count):
        source = lax.rem(me + k, count)
        for slot in range(2):
            copy = push(x_ref.at[0], o_ref.at[source, slot], send.at[0], recv.at[source, slot], source)
            pl.when(is_mine(me, slot, source, count))(copy.wait_recv)


def grads_out(count, units, d_mixed, *operands):
    vmem = pl.BlockSpec(memory_space=pltpu.VMEM)
    return pl.pallas_call(
        functools.partial(grads_out_kernel, count),
        out_shape=[
            jax.ShapeDtypeStruct((count, 2, HDIM, 2 * BLK), bf16),
            jax.ShapeDtypeStruct((units, UNIT, 256), bf16),
        ],
        in_specs=[ANY] + [vmem] * 8,
        out_specs=[ANY, vmem],
        scratch_shapes=[pltpu.SemaphoreType.DMA((HEADS,)), pltpu.SemaphoreType.DMA((count, 2)), pltpu.SemaphoreType.DMA((2,))],
        compiler_params=pltpu.CompilerParams(collective_id=2, has_side_effects=True, vmem_limit_bytes=60 * 2**20),
        name="grads_out",
    )(d_mixed, *operands)


def dot(a, b, i, j):
    return lax.dot_general(a, b, (((i,), (j,)), ((), ())), preferred_element_type=f32)


def front_kernel(count, skip_ref, bias_ref, x_ref, w_ref, wsmall_ref, gain_ref,
                 h_ref, gate_ref, att_ref, raw_out, logit_out, full_out, q_out, k_out, kt_out, vt_out,
                 ht_ref, proj_ref, small_ref, raw_ref, logit_ref, mixed_ref, full_ref, q_ref, k_ref, kt_ref, vt_ref, cum_ref, acc_ref, gains_ref,
                 send, recv, own, back_send, back_recv, back_own, keep):
    me = lax.axis_index("seq")
    barrier = pltpu.get_barrier_semaphore()
    for k in range(1, count):
        pl.semaphore_signal(barrier, inc=1, device_id={"seq": lax.rem(me + k, count)}, device_id_type=MESH)
    blocks = 2 * count
    rows = x_ref.shape[0]
    for i in range(rows // 128):
        here = slice(128 * i, 128 * i + 128)
        v = x_ref[here].astype(f32)
        normed = v * lax.rsqrt(jnp.mean(v * v, 1, keepdims=True) + EPS) * gain_ref[0:1]
        h_ref[here] = normed.astype(bf16)
        ht_ref[:, here] = normed.T.astype(bf16)

    def project(i, carried):
        block = mm(w_ref[:, pl.ds(pl.multiple_of(256 * i, 256), 256)], ht_ref[...], TN)
        proj_ref[pl.ds(4 * i, 4)] = block.astype(bf16).reshape(4, HDIM, rows)
        return carried

    gains_ref[...] = gain_ref[...].T
    small = mm(wsmall_ref[...], ht_ref[...], TN)
    for head in range(HEADS):
        ordered = [small[HEADS * i + head : HEADS * i + head + 1] for i in range(3)]
        small_ref[head] = jnp.concatenate(ordered + [jnp.zeros((5, rows), f32)], 0)
    lax.fori_loop(0, 9, project, 0)
    pl.semaphore_wait(barrier, count - 1)
    first = first_head(me, count)

    def out(slot, k, peer):
        head = first_head(peer, count) + slot
        sems = lambda i: (send.at[k, slot, i], recv.at[k, slot, i], peer)
        return [
            push(proj_ref.at[head], raw_ref.at[me, 0, slot], *sems(0)),
            push(proj_ref.at[HEADS + head], raw_ref.at[me, 1, slot], *sems(1)),
            push(proj_ref.at[2 * HEADS + head], raw_ref.at[me, 2, slot], *sems(2)),
            push(small_ref.at[head], logit_ref.at[me, slot], *sems(3)),
        ]

    def own_copies(slot):
        head = first + slot
        return [
            pltpu.make_async_copy(proj_ref.at[head], raw_ref.at[me, 0, slot], own.at[slot, 0]),
            pltpu.make_async_copy(proj_ref.at[HEADS + head], raw_ref.at[me, 1, slot], own.at[slot, 1]),
            pltpu.make_async_copy(proj_ref.at[2 * HEADS + head], raw_ref.at[me, 2, slot], own.at[slot, 2]),
            pltpu.make_async_copy(small_ref.at[head], logit_ref.at[me, slot], own.at[slot, 3]),
        ]

    for slot in range(2):
        for k in far_first(count):
            peer = lax.rem(me + k, count)
            copies = out(slot, k, peer)
            pl.when(is_mine(peer, slot, me, count))(copies[0].start)
            for copy in copies[1:]:
                copy.start()
        for copy in own_copies(slot):
            copy.start()

    def gate(i, carried):
        here = pl.ds(pl.multiple_of(256 * i, 256), 256)
        gate_ref[here] = mm(w_ref[:, pl.ds(pl.multiple_of(3 * D + 256 * i, 256), 256)], ht_ref[...], TN)
        return carried

    lax.fori_loop(0, 3, gate, 0)

    def saved(slot):
        return [
            pltpu.make_async_copy(src.at[slot], dst.at[slot], keep.at[slot, i])
            for i, (src, dst) in enumerate(
                ((full_ref, full_out), (q_ref, q_out), (k_ref, k_out), (kt_ref, kt_out), (vt_ref, vt_out)))
        ]

    def back(slot, k, peer):
        target = att_ref.at[pl.ds(pl.multiple_of((first + slot) * HDIM, HDIM), HDIM)]
        if k:
            return push(mixed_ref.at[slot, peer], target, back_send.at[k, slot], back_recv.at[first + slot], peer)
        return pltpu.make_async_copy(mixed_ref.at[slot, peer], target, back_own.at[slot])

    def one_slot(slot, carried):
        for copy in own_copies(slot):
            copy.wait()
        for k in far_first(count):
            source = lax.rem(me + count - k, count)
            copies = out(slot, k, source)
            pl.when(is_mine(me, slot, source, count))(copies[0].wait_recv)
            for copy in copies[1:]:
                copy.wait_recv()
        head = first + slot
        raws, logits = raw_ref.at[:, :, slot], logit_ref.at[:, slot]
        gains = gains_ref.at[pl.ds(pl.multiple_of(head * HDIM, HDIM), HDIM)]
        qs, ks, kts, vts = q_ref.at[slot], k_ref.at[slot], kt_ref.at[slot], vt_ref.at[slot]
        cum_ref[...] = log_forget_sums(logits[:, 0, :] + bias_ref[head], count)

        def prepare(block, state):
            acc_ref[block] = jnp.zeros(acc_ref.shape[1:], f32)
            return prepare_block(count, block, state, raws, logits, gains, cum_ref, qs, ks, kts, vts)

        zero = jnp.zeros((HDIM, BLK), f32)
        lax.fori_loop(0, blocks, prepare, (zero, zero))
        qs[blocks] = jnp.zeros(q_ref.shape[2:], bf16)

        def batch(pairs, on_diagonal):
            weights = [jnp.exp2(mm(ks[column], qs[row])) for row, column in pairs]
            low = []
            for (row, column), weight, diagonal in zip(pairs, weights, on_diagonal):
                weight = jnp.where(causal(), weight, 0.0) if diagonal else weight * keep_factor(skip_ref, row, column)
                low.append(weight.astype(bf16))
            parts = [mm(vts[column], weight) for (_, column), weight in zip(pairs, low)]
            for (row, _), part in zip(pairs, parts):
                acc_ref[row] += part

        def one_place(place, state):
            number = blocks // UNROLL
            for i in range(number):
                pairs = pairs_of_place(place, i, UNROLL, count)
                diagonal = [False] * UNROLL
                if i == number - 1:
                    pairs.append((place, place))
                    diagonal[-1:] = [True, True]
                batch(pairs, diagonal)
            return state

        low, high = own_places(me, slot, count)
        lax.fori_loop(low, high, one_place, 0)

        def finish(block, state):
            finish_block(count, block, acc_ref, cum_ref, full_ref.at[slot], mixed_ref.at[slot], qs)
            return state

        lax.fori_loop(0, blocks, finish, 0)
        for k in far_first(count) + [0]:
            peer = lax.rem(me + k, count)
            pl.when(is_mine(me, slot, peer, count))(back(slot, k, peer).start)
        for copy in saved(slot):
            copy.start()
        return carried

    lax.fori_loop(0, 2, one_slot, 0)
    keep_raw = [
        pltpu.make_async_copy(raw_ref, raw_out, keep.at[0, 5]),
        pltpu.make_async_copy(logit_ref, logit_out, keep.at[1, 5]),
    ]
    for copy in keep_raw:
        copy.start()
    for slot in range(2):
        for k in far_first(count):
            peer = lax.rem(me + k, count)
            copies = out(slot, k, peer)
            pl.when(is_mine(peer, slot, me, count))(copies[0].wait_send)
            for copy in copies[1:]:
                copy.wait_send()
        for k in far_first(count) + [0]:
            peer = lax.rem(me + k, count)
            copy = back(slot, k, peer)
            pl.when(is_mine(me, slot, peer, count))(copy.wait_send if k else copy.wait)
    for head in range(HEADS):
        source = holder(head, me, count)
        copy = push(mixed_ref.at[0, 0], att_ref.at[pl.ds(head * HDIM, HDIM)], back_send.at[0, 0], back_recv.at[head], lax.rem(me + 1, count))
        pl.when(source != me)(copy.wait_recv)
    for slot in range(2):
        for copy in saved(slot):
            copy.wait()
    for copy in keep_raw:
        copy.wait()


def front(count, skip, bias, x, w_attn, w_small, gains):
    rows = x.shape[0]
    blocks = 2 * count
    vmem = pl.BlockSpec(memory_space=pltpu.VMEM)
    smem = pl.BlockSpec(memory_space=pltpu.SMEM)
    dma = pltpu.SemaphoreType.DMA
    raw, logit = (count, 3, 2, HDIM, rows), (count, 2, 8, rows)
    state = [((2, blocks, HDIM, BLK), f32), ((2, blocks + 1, 128, BLK), bf16), ((2, blocks, BLK, 128), bf16),
             ((2, blocks, 80, BLK), bf16), ((2, blocks, 80, BLK), bf16)]
    return pl.pallas_call(
        functools.partial(front_kernel, count),
        out_shape=[jax.ShapeDtypeStruct(s, t) for s, t in [
            ((rows, D), bf16), ((D, rows), f32), ((D, rows), bf16), (raw, bf16), (logit, f32)] + state],
        in_specs=[smem, smem] + [vmem] * 4,
        out_specs=[vmem] * 3 + [ANY] * 7,
        scratch_shapes=[
            pltpu.VMEM((D, rows), bf16),
            pltpu.VMEM((3 * HEADS, HDIM, rows), bf16),
            pltpu.VMEM((HEADS, 8, rows), f32),
            pltpu.VMEM(raw, bf16),
            pltpu.VMEM(logit, f32),
            pltpu.VMEM((2, count, HDIM, rows), bf16),
        ] + [pltpu.VMEM(s, t) for s, t in state] + [
            pltpu.VMEM((count, rows), f32),
            pltpu.VMEM((blocks + 1, 80, BLK), f32),
            pltpu.VMEM((D, 8), f32),
            dma((count, 2, 4)), dma((count, 2, 4)), dma((2, 4)),
            dma((count, 2)), dma((HEADS,)), dma((2,)), dma((2, 6)),
        ],
        compiler_params=pltpu.CompilerParams(collective_id=0, has_side_effects=True, vmem_limit_bytes=60 * 2**20),
        name="front",
    )(skip, bias, x, w_attn, w_small, gains)


SMALL = 48
UNIT = 16
PIECE = 8


def group_bits(group_count, count):
    bits = [("group", 1 << i) for i in range(group_count.bit_length() - 1)]
    return bits, [("seq", 1 << i) for i in range(count.bit_length() - 1)]


def partner(bit):
    axis, step = bit
    here = lax.axis_index(axis)
    side = lax.rem(here // step, 2)
    return {axis: here + step - 2 * step * side}, side


def greet_all(bits, count):
    me = lax.axis_index("seq")
    others = [partner(bit)[0] for bit in bits if bit[0] != "seq"]
    others += [{"seq": lax.rem(me + k, count)} for k in range(1, count)]
    barrier = pltpu.get_barrier_semaphore()
    for there in others:
        pl.semaphore_signal(barrier, inc=1, device_id=there, device_id_type=MESH)
    pl.semaphore_wait(barrier, len(others))
    return me


def orders(near, far, seq, busy):
    x, z, rest = seq[0], seq[1], seq[2:]
    kinds = [
        [near, far, x, z] + rest,
        [near, x, far, z] + rest,
        [near, z, x, far] + rest,
        [near, z, far, x] + rest,
    ]
    return [kinds[i] for i in (EARLY_KINDS if busy else (0, 1, 2, 0, 1, 3))]


EARLY_KINDS = (0, 1, 2, 0, 1, 3)
PARTS = 6


class Summing:
    def __init__(self, base, size, order, source, own, landing, result, send, recv, local):
        self.start, self.size, self.order, self.source, self.local = base, size, order, source, local
        self.own, self.landing, self.result, self.send, self.recv = own, landing, result, send, recv
        self.base, self.at, self.stage, self.copy, self.load = base, base, 0, None, None
        self.off = 0

    def give(self):
        there, side = partner(self.order[self.stage])
        half = self.size // 2
        self.keep = self.start + side * half
        held = self.own
        if self.stage == 0 and self.source is not None:
            held = self.source
            self.load = pltpu.make_async_copy(
                self.source.at[pl.ds(self.keep, half)], self.own.at[pl.ds(self.base // 2, half)], self.local
            )
            self.load.start()
        self.copy = pltpu.make_async_remote_copy(
            src_ref=held.at[pl.ds(self.start + (1 - side) * half - self.off, half)],
            dst_ref=self.landing.at[pl.ds(self.at, half)],
            send_sem=self.send.at[self.stage], recv_sem=self.recv.at[self.stage],
            device_id=there, device_id_type=MESH,
        )
        self.copy.start()

    def add(self):
        self.copy.wait()
        if self.load is not None:
            self.load.wait()
            self.load = None
            self.off = self.keep - self.base // 2
        half = self.size // 2
        step = PIECE if half % PIECE == 0 else 1
        keep, at, own, landing = self.keep - self.off, self.at, self.own, self.landing

        def piece(i, carried):
            mine = pl.ds(keep + i * step, step)
            own[mine] = own[mine] + landing[pl.ds(at + i * step, step)]
            return carried

        lax.fori_loop(0, half // step, piece, 0)
        self.start, self.size, self.at, self.stage = self.keep, half, at + half, self.stage + 1

    def settle(self):
        copy = pltpu.make_async_copy(
            self.own.at[pl.ds(self.start - self.off, self.size)], self.result.at[pl.ds(self.start, self.size)], self.local
        )
        copy.start()
        copy.wait()
        self.left = len(self.order)

    def spread(self):
        self.left -= 1
        there, side = partner(self.order[self.left])
        part = self.result.at[pl.ds(self.start, self.size)]
        stage = 2 * len(self.order) - 1 - self.left
        self.copy = pltpu.make_async_remote_copy(
            src_ref=part, dst_ref=part, send_sem=self.send.at[stage], recv_sem=self.recv.at[stage],
            device_id=there, device_id_type=MESH,
        )
        self.copy.start()
        self.start, self.size = self.start - side * self.size, 2 * self.size

    def gathered(self):
        self.copy.wait()


def total(parts):
    return functools.reduce(jnp.add, parts)


def held_heads(count):
    first = [min(HEADS * d // count, HEADS - 2) for d in range(count)]
    return [
        [(d, h - first[d]) for d in range(h * count // HEADS, ((h + 1) * count - 1) // HEADS + 1)]
        for h in range(HEADS)
    ]


def padded(units, least):
    return -(-units // least) * least


def sums_of(units, least, sets, source, own, landing, result, send, recv, local):
    pieces, base, sums = units // least, 0, []
    for i, order in enumerate(orders(*sets, source is not None)):
        size = least * ((pieces + PARTS - 1 - i) // PARTS)
        if not size:
            break
        sums.append(Summing(base, size, order, source, own, landing, result, send.at[i], recv.at[i], local.at[i]))
        base += size
    return sums


def step(sums, stages):
    for part in sums:
        if part.stage < stages:
            part.add()
            if part.stage < stages:
                part.give()
            else:
                part.settle()
                part.spread()
        else:
            part.gathered()
            if part.left > 0:
                part.spread()


def put_together(holders, part_ref, logit_ref, proj_ref, dsmall_ref):
    for head, held in enumerate(holders):
        for i in range(2):
            start = D * (1 + i) + head * HDIM
            if len(held) == 1:
                proj_ref[start : start + HDIM] = part_ref[head, 0, i]
            else:
                proj_ref[start : start + HDIM] = total([part_ref[head, j, i].astype(f32) for j in range(len(held))]).astype(bf16)
        dsmall_ref[8 * head : 8 * head + 8] = total([logit_ref[d, s] for d, s in held])


def late_weights(h_ref, proj_ref, g_ref):
    def block(i, carried):
        grads = proj_ref[pl.ds(pl.multiple_of(i * 256, 256), 256)]
        for j in range(3):
            part = lax.dot_general(h_ref[:, 256 * j : 256 * j + 256], grads, (((0,), (1,)), ((), ())), preferred_element_type=f32)
            g_ref[pl.ds(i * (D // UNIT) + j * 16, 16)] = part.astype(bf16).reshape(16, UNIT, 256)
        return carried

    lax.fori_loop(0, 9, block, 0)


def late_rest(h_ref, proj_ref, w_ref, wsmall_ref, x_ref, gain_ref, dresid_ref, extra_ref, dsmall_ref, rows_ref, small_ref, dx_ref, g_ref, gsum_ref=None):
    ordered = [dsmall_ref[8 * head + i : 8 * head + i + 1] for i in range(3) for head in range(HEADS)]
    low_small = jnp.concatenate(ordered + [jnp.zeros((SMALL - 3 * HEADS, ordered[0].shape[1]), f32)], 0).astype(bf16)
    for i in range(3):
        cols = slice(256 * i, 256 * i + 256)
        part = mm(w_ref[cols, :], proj_ref[...]) + mm(wsmall_ref[cols, :], low_small)
        dx_ref[:, cols] = part.T
    rows_ref[...] = mm(low_small, h_ref[...])
    small_ref[...] = extra_ref[...]
    if gsum_ref is not None:
        small_ref[2:4] = gsum_ref[0:2]
    gain = gain_ref[0:1]
    dgain = jnp.zeros((1, D), f32)
    for i in range(h_ref.shape[0] // 128):
        here = slice(128 * i, 128 * i + 128)
        v, u = x_ref[here].astype(f32), dx_ref[here]
        scale = lax.rsqrt(jnp.mean(v * v, 1, keepdims=True) + EPS)
        hat, gu = v * scale, u * gain
        dx_ref[here] = dresid_ref[here] + scale * (gu - hat * jnp.mean(hat * gu, 1, keepdims=True))
        dgain = dgain + jnp.sum(hat * u, 0, keepdims=True)
    small_ref[0:1] = dgain
    bias_rows = jnp.concatenate([dsmall_ref[8 * head : 8 * head + 1] for head in range(HEADS)], 0)
    bias_sum = jnp.sum(bias_rows, 1, keepdims=True)
    lane = lax.broadcasted_iota(jnp.int32, (HEADS, 128), 1)
    row = lax.broadcasted_iota(jnp.int32, (HEADS, 128), 0)
    small_ref[4:5, 0:128] = jnp.sum(jnp.where(lane == row, bias_sum, 0.0), 0, keepdims=True)

    used = 9 * (D // UNIT)
    units = g_ref.shape[0]
    for i in range(3):
        g_ref[used + 3 * i : used + 3 * i + 3] = rows_ref[:, 256 * i : 256 * i + 256].astype(bf16).reshape(3, UNIT, 256)
    if units > used + 9:
        g_ref[used + 9 :] = jnp.zeros((units - used - 9, UNIT, 256), bf16)


class Doubling:
    def __init__(self, bits, own, landing, send, recv):
        self.bits, self.own, self.landing, self.send, self.recv = bits, own, landing, send, recv
        self.at = 0

    def give(self):
        there, _ = partner(self.bits[self.at])
        self.copy = pltpu.make_async_remote_copy(
            src_ref=self.own, dst_ref=self.landing.at[self.at], send_sem=self.send.at[self.at], recv_sem=self.recv.at[self.at],
            device_id=there, device_id_type=MESH,
        )
        self.copy.start()

    def add(self):
        self.copy.wait()
        self.own[...] += self.landing[self.at]
        self.at += 1


def finish_late(late, early, early_left, stages, small, small_out):
    for stage in range(2 * stages):
        if stage < stages:
            small.give()
        step(late, stages)
        if stage < early_left:
            step(early, stages)
        if stage < stages:
            small.add()
    small_out[...] = small.own[...]


def give_late(sums, rest, early, stages):
    units = 9 * (D // UNIT)
    ahead = [part for part in sums if part.start + part.size <= units]
    for part in ahead:
        part.give()
    rest()
    for part in sums[len(ahead):]:
        part.give()
    step(early, stages)


def last_kernel(count, sets, draw_ref, dlogit_ref, early_ref, h_ref, dgate_ref, w_ref, wsmall_ref, x_ref, gain_ref,
                dresid_ref, extra_ref, late_out, early_out, dx_ref, small_out,
                proj_ref, logit_ref, part_ref, dsmall_ref, rows_ref, small_ref, small_land, ssend, srecv, g_ref, land_ref, e_ref, eland_ref,
                send, recv, recv_q, recv_kv, local, gsend, grecv, gsem, esend, erecv, esem):
    near, far, seq = sets
    bits = [near, far] + seq
    stages, least = len(bits), 1 << len(bits)
    me = greet_all(bits, count)
    early = sums_of(early_ref.shape[0], least, sets, early_ref, e_ref, eland_ref, early_out, esend, erecv, esem)
    for part in early:
        part.give()

    holders = held_heads(count)
    first = first_head(me, count)
    started = []
    for k in far_first(count) + [0]:
        peer = lax.rem(me + k, count)
        pairs = [(None, dlogit_ref.at[peer], logit_ref.at[me], recv.at[k])]
        for slot in range(2):
            head = first + slot
            target = proj_ref.at[pl.ds(pl.multiple_of(head * HDIM, HDIM), HDIM)]
            pairs.append((is_mine(me, slot, peer, count), draw_ref.at[peer, 0, slot], target, recv_q.at[head]))
            used = (head * count < HEADS * (me + 1)) & (head * count + count > HEADS * me)
            order = me - holder(head, 0, count)
            pairs.append((used, draw_ref.at[peer, pl.ds(1, 2), slot], part_ref.at[head, order], recv_kv.at[head, order]))
        for i, (mine, src, dst, sem) in enumerate(pairs):
            copy = push(src, dst, send.at[k, i], sem, peer) if k else pltpu.make_async_copy(src, dst, local.at[i])
            started.append((mine, k, copy))
            if mine is None:
                copy.start()
            else:
                pl.when(mine)(copy.start)

    step(early, stages)
    step(early, stages)

    for mine, k, copy in started:
        if mine is not None:
            pl.when(mine)(copy.wait_send if k else copy.wait)
        else:
            copy.wait()
    for head in range(HEADS):
        source = holder(head, me, count)
        copy = push(draw_ref.at[0, 0, 0], proj_ref.at[pl.ds(head * HDIM, HDIM)], send.at[0, 0], recv_q.at[head], lax.rem(me + 1, count))
        pl.when(source != me)(copy.wait_recv)
        for j, (d, s) in enumerate(holders[head]):
            copy = push(draw_ref.at[0, pl.ds(1, 2), 0], part_ref.at[head, j], send.at[0, 0], recv_kv.at[head, j], lax.rem(me + 1, count))
            pl.when(me != d)(copy.wait_recv)

    put_together(holders, part_ref, logit_ref, proj_ref, dsmall_ref)
    proj_ref[3 * D :] = dgate_ref[...]

    late_weights(h_ref, proj_ref, g_ref)
    late = sums_of(g_ref.shape[0], least, sets, None, g_ref, land_ref, late_out, gsend, grecv, gsem)

    def rest():
        late_rest(h_ref, proj_ref, w_ref, wsmall_ref, x_ref, gain_ref, dresid_ref, extra_ref, dsmall_ref, rows_ref, small_ref, dx_ref, g_ref)

    give_late(late, rest, early, stages)
    finish_late(late, early, 2 * stages - 3, stages, Doubling(bits, small_ref, small_land, ssend, srecv), small_out)


def last(count, sets, d_raw, d_logits, early, h, d_gate, w_attn, w_small, x, gain, d_resid, extra):
    stages = 2 + len(sets[2])
    units = padded(9 * (D // UNIT) + 9, 1 << stages)
    rows = h.shape[0]
    most = max(len(held) for held in held_heads(count))
    vmem = pl.BlockSpec(memory_space=pltpu.VMEM)
    dma = pltpu.SemaphoreType.DMA
    shape = (UNIT, 256)
    return pl.pallas_call(
        functools.partial(last_kernel, count, sets),
        out_shape=[
            jax.ShapeDtypeStruct((units,) + shape, bf16),
            jax.ShapeDtypeStruct(early.shape, bf16),
            jax.ShapeDtypeStruct((rows, D), f32),
            jax.ShapeDtypeStruct((8, D), f32),
        ],
        in_specs=[ANY] * 3 + [vmem] * 8,
        out_specs=[ANY, ANY, vmem, vmem],
        scratch_shapes=[
            pltpu.VMEM((4 * D, rows), bf16),
            pltpu.VMEM((count, 2, 8, rows), f32),
            pltpu.VMEM((HEADS, most, 2, HDIM, rows), bf16),
            pltpu.VMEM((8 * HEADS, rows), f32),
            pltpu.VMEM((SMALL, D), f32),
            pltpu.VMEM((8, D), f32),
            pltpu.VMEM((stages, 8, D), f32),
            dma((stages,)), dma((stages,)),
            pltpu.VMEM((units,) + shape, bf16),
            pltpu.VMEM((units,) + shape, bf16),
            pltpu.VMEM((early.shape[0] // 2,) + shape, bf16),
            pltpu.VMEM(early.shape, bf16),
            dma((count, 5)), dma((count,)), dma((HEADS,)), dma((HEADS, most)), dma((5,)),
            dma((PARTS, 2 * stages)), dma((PARTS, 2 * stages)), dma((PARTS,)),
            dma((PARTS, 2 * stages)), dma((PARTS, 2 * stages)), dma((PARTS,)),
        ],
        compiler_params=pltpu.CompilerParams(collective_id=3, has_side_effects=True, vmem_limit_bytes=62 * 2**20),
        name="last",
    )(d_raw, d_logits, early, h, d_gate, w_attn, w_small, x, gain, d_resid, extra)


def unpack_kernel(parts, *refs):
    o_ref = refs[-1]
    width = refs[0].shape[0] // (o_ref.shape[0] // UNIT)
    at = 0
    for ref, blocks in zip(refs, parts):

        @pl.when((pl.program_id(0) >= at) & (pl.program_id(0) < at + blocks))
        def _(ref=ref):
            for i in range(width):
                size = o_ref.shape[0] // UNIT
                block = ref[size * i : size * i + size].reshape(o_ref.shape[0], 256)
                o_ref[:, 256 * i : 256 * i + 256] = block.astype(f32)

        at += blocks


def unpack(rows, width, *parts):
    size = rows // UNIT
    specs, at = [], 0
    for _, first, blocks in parts:
        first, blocks = first // width, blocks // width
        index = lambda i, at=at, first=first, blocks=blocks: (first + jnp.clip(i - at, 0, blocks - 1), 0, 0)
        specs.append(pl.BlockSpec((size * width, UNIT, 256), index))
        at += blocks
    return pl.pallas_call(
        functools.partial(unpack_kernel, [blocks // width for _, _, blocks in parts]),
        grid=(at,),
        in_specs=specs,
        out_specs=pl.BlockSpec((rows, 256 * width), lambda i: (0, i)),
        out_shape=jax.ShapeDtypeStruct((rows, 256 * at * width), f32),
        compiler_params=pltpu.CompilerParams(vmem_limit_bytes=62 * 2**20),
        name="unpack",
    )(*[units for units, _, _ in parts])


def back_kernel(count, sets, skip_ref, bias_ref, dmixed_ref, logits_ref, wsmall_ref, gain_ref, extra_ref,
                raw_in, full_in, q_in, k_in, kt_in, vt_in, early_ref, h_in, dgate_in, w_in, x_in, dresid_in,
                late_out, early_out, dx_ref, small_out,
                raw_ref, full_ref, q_ref, k_ref, kt_ref, vt_ref, do_ref, v_ref, cum_ref, dq_ref, dk_ref, dv_ref,
                dlogit_ref, gsum_ref, gains_ref,
                proj_ref, logit_ref, part_ref, dsmall_ref, rows_ref, small_ref, small_land, ssend, srecv, h_ref, w_ref, x_ref, dresid_ref,
                g_ref, land_ref, e_ref, eland_ref,
                load, send, recv, recv_q, recv_kv, own, gsend, grecv, gsem, esend, erecv, esem):
    near, far, seq = sets
    bits = [near, far] + seq
    stages, least = len(bits), 1 << len(bits)
    blocks = 2 * count
    draw_ref = raw_ref
    sums = (dq_ref, dk_ref, dv_ref)

    def state(slot):
        pairs = ((full_in, full_ref), (q_in, q_ref), (k_in, k_ref), (kt_in, kt_ref), (vt_in, vt_ref))
        return [pltpu.make_async_copy(src.at[slot], dst, load.at[i]) for i, (src, dst) in enumerate(pairs)]

    other = [
        pltpu.make_async_copy(src, dst, load.at[5 + i])
        for i, (src, dst) in enumerate((
            (raw_in, raw_ref), (h_in, h_ref), (dgate_in, proj_ref.at[pl.ds(3 * D, D)]), (w_in, w_ref), (x_in, x_ref), (dresid_in, dresid_ref)))
    ]
    for copy in state(0) + other:
        copy.start()
    me = greet_all(bits, count)
    first = first_head(me, count)
    holders = held_heads(count)
    early = sums_of(early_ref.shape[0], least, sets, early_ref, e_ref, eland_ref, early_out, esend, erecv, esem)
    for part in early:
        part.give()
    gsum_ref[...] = jnp.zeros(gsum_ref.shape, f32)
    gains_ref[...] = gain_ref[...].T

    def sends(slot, k):
        peer = lax.rem(me + k, count)
        head = first + slot
        order = me - holder(head, 0, count)
        used = (head * count < HEADS * (me + 1)) & (head * count + count > HEADS * me)
        target = proj_ref.at[pl.ds(pl.multiple_of(head * HDIM, HDIM), HDIM)]
        items = [
            (None, dlogit_ref.at[peer, slot], logit_ref.at[me, slot], recv.at[k, slot]),
            (is_mine(me, slot, peer, count), draw_ref.at[peer, 0, slot], target, recv_q.at[head]),
            (used, draw_ref.at[peer, pl.ds(1, 2), slot], part_ref.at[head, order], recv_kv.at[head, order]),
        ]
        return [
            (mine, push(src, dst, send.at[k, slot, i], sem, peer) if k else pltpu.make_async_copy(src, dst, own.at[slot, i]))
            for i, (mine, src, dst, sem) in enumerate(items)
        ]

    for slot in range(2):
        for copy in state(slot):
            copy.wait()

        def prepare(block, carried):
            prepare_back(count, block, dmixed_ref.at[:, slot], full_ref, vt_ref, do_ref, v_ref, *sums)
            return carried

        lax.fori_loop(0, blocks, prepare, 0)
        step(early, stages)

        def one_place(place, carried):
            for i in range(blocks // UNROLL_BACK):
                pairs = pairs_of_place(place, i, UNROLL_BACK, count)
                masks = [keep_factor(skip_ref, row, column) for row, column in pairs]
                if (i + 1) * UNROLL_BACK == blocks:
                    pairs.append((place, place))
                    masks[-1:] = [True, True]
                batch_back(pairs, masks, q_ref, k_ref, kt_ref, v_ref, do_ref, *sums)
            return carried

        low, high = own_places(me, slot, count)
        middle = (low + high) // 2
        if slot == 0:
            lax.fori_loop(low, high, one_place, 0)
        else:
            lax.fori_loop(low, middle, one_place, 0)
            step(early, stages)
            lax.fori_loop(middle, high, one_place, 0)
        step(early, stages)
        if slot == 0:
            for copy in state(1):
                copy.start()
            other[0].wait()
        raws, logits = raw_ref.at[:, :, slot], logits_ref.at[:, slot]
        gains = gains_ref.at[pl.ds(pl.multiple_of((first + slot) * HDIM, HDIM), HDIM)]
        draws, dlogits = draw_ref.at[:, :, slot], dlogit_ref.at[:, slot]

        def finish(number, carried):
            block = blocks - 1 - number
            mine = is_mine(me, slot, place_of(block, count), count)
            return finish_back(count, block, carried, mine, raws, logits, gains, *sums, draws, dlogits, cum_ref)

        zero = jnp.zeros((HDIM, BLK), f32)
        _, _, sum_q, sum_k = lax.fori_loop(0, blocks, finish, (zero, zero, zero, zero))
        lane = lax.broadcasted_iota(jnp.int32, (HDIM, D), 1)
        channel = lax.broadcasted_iota(jnp.int32, (HDIM, D), 0)
        here = lane == channel + (first + slot) * HDIM
        for i, column in enumerate((sum_q, sum_k)):
            placed = jnp.where(here, jnp.sum(column, 1, keepdims=True), 0.0)
            gsum_ref[i : i + 1] += jnp.sum(placed, 0, keepdims=True)
        forget_back(count, bias_ref[first + slot], logits, cum_ref, dlogits)
        for k in far_first(count) + [0]:
            for mine, copy in sends(slot, k):
                if mine is None:
                    copy.start()
                else:
                    pl.when(mine)(copy.start)
        step(early, stages)

    for _ in range(LATER):
        step(early, stages)
    for copy in other[1:]:
        copy.wait()
    for slot in range(2):
        for k in far_first(count) + [0]:
            for mine, copy in sends(slot, k):
                if mine is None:
                    copy.wait()
                else:
                    pl.when(mine)(copy.wait_send if k else copy.wait)
    for head in range(HEADS):
        source = holder(head, me, count)
        next_one = lax.rem(me + 1, count)
        copy = push(draw_ref.at[0, 0, 0], proj_ref.at[pl.ds(head * HDIM, HDIM)], send.at[0, 0, 0], recv_q.at[head], next_one)
        pl.when(source != me)(copy.wait_recv)
        for j, (d, s) in enumerate(holders[head]):
            copy = push(draw_ref.at[0, pl.ds(1, 2), 0], part_ref.at[head, j], send.at[0, 0, 0], recv_kv.at[head, j], next_one)
            pl.when(me != d)(copy.wait_recv)

    put_together(holders, part_ref, logit_ref, proj_ref, dsmall_ref)
    late_weights(h_ref, proj_ref, g_ref)
    late = sums_of(g_ref.shape[0], least, sets, None, g_ref, land_ref, late_out, gsend, grecv, gsem)

    def rest():
        late_rest(h_ref, proj_ref, w_ref, wsmall_ref, x_ref, gain_ref, dresid_ref, extra_ref, dsmall_ref, rows_ref, small_ref, dx_ref, g_ref, gsum_ref)

    give_late(late, rest, early, stages)
    finish_late(late, early, 2 * stages - 8 - LATER, stages, Doubling(bits, small_ref, small_land, ssend, srecv), small_out)


LATER = 1


def back(count, sets, skip, bias, d_mixed, logits, w_small, gains, extra, raw, full, q, k, kt, vt, early, h, d_gate, w_attn, x, d_resid):
    stages = 2 + len(sets[2])
    units = padded(9 * (D // UNIT) + 9, 1 << stages)
    rows = h.shape[0]
    blocks = 2 * count
    most = max(len(held) for held in held_heads(count))
    vmem = pl.BlockSpec(memory_space=pltpu.VMEM)
    smem = pl.BlockSpec(memory_space=pltpu.SMEM)
    dma = pltpu.SemaphoreType.DMA
    shape = (UNIT, 256)
    held = lambda array: pltpu.VMEM(array.shape[1:], array.dtype)
    return pl.pallas_call(
        functools.partial(back_kernel, count, sets),
        out_shape=[
            jax.ShapeDtypeStruct((units,) + shape, bf16),
            jax.ShapeDtypeStruct(early.shape, bf16),
            jax.ShapeDtypeStruct((rows, D), f32),
            jax.ShapeDtypeStruct((8, D), f32),
        ],
        in_specs=[smem, smem] + [vmem] * 5 + [ANY] * 12,
        out_specs=[ANY, ANY, vmem, vmem],
        scratch_shapes=[
            pltpu.VMEM(raw.shape, bf16), held(full), held(q), held(k), held(kt), held(vt),
            pltpu.VMEM((blocks + 1, 128, BLK), bf16),
            pltpu.VMEM((blocks, BLK, 128), bf16),
            pltpu.VMEM((count, rows), f32),
            pltpu.VMEM((blocks + 1, 80, BLK), f32),
            pltpu.VMEM((blocks, 80, BLK), f32),
            pltpu.VMEM((blocks, HDIM, BLK), f32),
            pltpu.VMEM(logits.shape, f32),
            pltpu.VMEM((8, D), f32),
            pltpu.VMEM((D, 8), f32),
            pltpu.VMEM((4 * D, rows), bf16),
            pltpu.VMEM((count, 2, 8, rows), f32),
            pltpu.VMEM((HEADS, most, 2, HDIM, rows), bf16),
            pltpu.VMEM((8 * HEADS, rows), f32),
            pltpu.VMEM((SMALL, D), f32),
            pltpu.VMEM((8, D), f32),
            pltpu.VMEM((stages, 8, D), f32),
            dma((stages,)), dma((stages,)),
            pltpu.VMEM(h.shape, bf16),
            pltpu.VMEM(w_attn.shape, bf16),
            pltpu.VMEM(x.shape, bf16),
            pltpu.VMEM(d_resid.shape, f32),
            pltpu.VMEM((units,) + shape, bf16),
            pltpu.VMEM((units,) + shape, bf16),
            pltpu.VMEM((early.shape[0] // 2,) + shape, bf16),
            pltpu.VMEM(early.shape, bf16),
            dma((11,)), dma((count, 2, 3)), dma((count, 2)), dma((HEADS,)), dma((HEADS, most)), dma((2, 3)),
            dma((PARTS, 2 * stages)), dma((PARTS, 2 * stages)), dma((PARTS,)),
            dma((PARTS, 2 * stages)), dma((PARTS, 2 * stages)), dma((PARTS,)),
        ],
        compiler_params=pltpu.CompilerParams(collective_id=4, has_side_effects=True, vmem_limit_bytes=63 * 2**20),
        name="back",
    )(skip, bias, d_mixed, logits, w_small, gains, extra, raw, full, q, k, kt, vt, early, h, d_gate, w_attn, x, d_resid)


def rms_scale(values, gains):
    inverse = lax.rsqrt(jnp.mean(values * values, axis=-1, keepdims=True) + EPS)
    return values * inverse * gains


def swiglu(gate_up):
    return jax.nn.silu(gate_up[:, :FF]) * gate_up[:, FF:]


def local(tokens, cotangent, skip_table, gain_attn, w_attn, w_heads, forget_bias, query_gain, key_gain,
          w_out, gain_ffn, w_gate_up, w_down):
    count = lax.axis_size("seq")
    me = lax.axis_index("seq")
    rows = tokens.shape[1]
    both = ("seq", "group")
    inputs = tokens[0].astype(f32)
    device = me.astype(jnp.int32)[None]
    head = first_head(me, count)
    skip = skip_table[0]
    all_gains = jnp.concatenate([jnp.stack([gain_attn, query_gain, key_gain]), jnp.zeros((5, D), f32)], 0)
    if count <= 8:
        h_first, gate_logit, attended, raw, logits, mixed, q, k, kt, vt = front(
            count, skip, forget_bias, tokens[0], w_attn, w_heads, all_gains
        )
    else:
        gains = lax.dynamic_slice_in_dim(all_gains.T.reshape(HEADS, HDIM, 8), head, 2, 0)
        bias = lax.dynamic_slice_in_dim(forget_bias, head, 2, 0)
        w_small = jnp.pad(w_heads.reshape(D, 3, HEADS).transpose(0, 2, 1), ((0, 0), (0, 0), (0, 5))).reshape(D, HEADS * 8)
        h_first = rms_scale(inputs, gain_attn).astype(bf16)
        qkv = dot(w_attn[:, : 3 * D], h_first, 0, 1).astype(bf16).reshape(3, HEADS, HDIM, rows)
        gate_logit = dot(w_attn[:, 3 * D :], h_first, 0, 1)
        logits_here = dot(w_small, h_first, 0, 1).reshape(HEADS, 8, rows)
        raw, logits = heads_out(qkv, logits_here, count)
        mixed_low, mixed, q, k, kt, vt = attend_forward(device, skip, bias, raw, logits, gains)
        attended = mixed_back(mixed_low, count).reshape(D, rows)
    attended = attended.astype(f32)

    gate_open = jax.nn.sigmoid(gate_logit)
    gated = (gate_open * attended).astype(bf16)
    resid = inputs + dot(gated, w_out, 0, 0)
    normed_ffn, norm_back_ffn = jax.vjp(rms_scale, resid, gain_ffn)
    h_second = normed_ffn.astype(bf16)
    gate_up = dot(h_second, w_gate_up, 1, 0)
    hidden, hidden_back = jax.vjp(swiglu, gate_up)
    hidden_low = hidden.astype(bf16)
    output = resid + dot(hidden_low, w_down, 1, 0)
    d_low = cotangent[0]
    d_output = d_low.astype(f32)
    (d_gate_up,) = hidden_back(dot(d_low, w_down, 1, 1))
    d_gate_low = d_gate_up.astype(bf16)
    d_resid_norm, grad_gain_ffn = norm_back_ffn(dot(d_gate_low, w_gate_up, 1, 1))
    d_resid = d_output + d_resid_norm
    d_branch = d_resid.astype(bf16)
    d_gated = dot(w_out, d_branch, 1, 1)
    d_gate_logit = (d_gated * attended * gate_open * (1.0 - gate_open)).astype(bf16)
    d_mixed = (d_gated * gate_open).astype(bf16).reshape(HEADS, HDIM, rows)

    near_far, seq_bits = group_bits(lax.axis_size("group"), count)
    sets = (near_far[0], near_far[1], seq_bits)
    units = padded(1440, 1 << (2 + len(seq_bits)))
    d_mixed_all, early = grads_out(
        count, units, d_mixed, h_first, d_gate_logit, h_second, d_gate_low, hidden_low, d_low, gated, d_branch
    )
    zeros = lambda n: jnp.zeros((n, D), f32)
    if count <= 8:
        extra = jnp.concatenate([zeros(1), grad_gain_ffn[None], zeros(6)], 0)
        late, early, d_inputs, small = back(
            count, sets, skip, forget_bias, d_mixed_all, logits, jnp.pad(w_heads, ((0, 0), (0, SMALL - 3 * HEADS))), all_gains, extra,
            raw, mixed, q, k, kt, vt, early, h_first, d_gate_logit, w_attn, tokens[0], d_resid,
        )
    else:
        d_raw, d_logits, d_gains = attend_backward(device, skip, bias, raw, logits, gains, d_mixed_all, mixed, q, k, kt, vt)
        placed = lax.dynamic_update_slice(jnp.zeros((HEADS, HDIM, 2), f32), d_gains[..., 1:3], (head, 0, 0)).reshape(D, 2).T
        extra = jnp.concatenate([zeros(1), grad_gain_ffn[None], placed, zeros(4)], 0)
        late, early, d_inputs, small = last(
            count, sets, d_raw, d_logits, early, h_first, d_gate_logit, w_attn,
            jnp.pad(w_heads, ((0, 0), (0, SMALL - 3 * HEADS))), tokens[0], gain_attn[None], d_resid, extra
        )
    row = 3 * HEADS
    used = 9 * (D // UNIT)
    heads_rows = late[used : used + 9].reshape(3, SMALL, 256).transpose(1, 0, 2).reshape(SMALL, D).astype(f32)
    return (
        output[None].astype(bf16),
        d_inputs[None],
        small[0],
        unpack(D, 3, (late, 0, 9), (early, 27, 3)),
        heads_rows[:row].T,
        small[4, :HEADS],
        small[2],
        small[3],
        unpack(D, 1, (early, 24, 3)),
        small[1],
        unpack(D, 2, (early, 0, 16)),
        unpack(FF, 1, (early, 6, 3)),
    )


def solution(mesh):
    rows = P("group", "seq", None)
    return jax.shard_map(
        local,
        mesh=mesh,
        in_specs=(rows, rows, P("group", None, None)) + (P(),) * 10,
        out_specs=(rows, rows) + (P(),) * 10,
        check_vma=False,
    )
```

```python
import functools

import jax
import jax.numpy as jnp
from jax import lax
from jax.experimental import pallas as pl
from jax.experimental.pallas import tpu as pltpu
from jax.sharding import PartitionSpec as P

D, FF = 768, 2048
MESH = pl.DeviceIdType.MESH
ANY = pl.BlockSpec(memory_space=pl.ANY)

HEADS, HDIM, BLK = 12, 64, 256
EPS = 1e-06
LOG2E = 1.4426950408889634
LN2 = 0.6931471805599453
SCORE = HDIM ** -0.5
f32, bf16 = jnp.float32, jnp.bfloat16
UNROLL = 8
UNROLL_BACK = 4
NN = (((1,), (0,)), ((), ()))
NT = (((1,), (1,)), ((), ()))
TN = (((0,), (0,)), ((), ()))


def mm(a, b, dims=NN):
    return lax.dot_general(a, b, dims, preferred_element_type=f32)


def split3(v):
    hi = v.astype(bf16).astype(f32)
    rest = v - hi
    mid = rest.astype(bf16).astype(f32)
    return hi, mid, rest - mid


def place_of(block, count):
    return jnp.where(block < count, block, 2 * count - 1 - block)


def lanes_of(block, count):
    return pl.ds(pl.multiple_of(jnp.where(block < count, 0, BLK), BLK), BLK)


def first_head(device, count):
    return jnp.minimum(HEADS * device // count, HEADS - 2)


def is_mine(device, slot, place, count):
    chunk = (first_head(device, count) + slot) * count + place
    return (chunk >= HEADS * device) & (chunk < HEADS * device + HEADS)


def list_pairs(skip_ref, pairs_ref, own_ref, device, slot, count, unroll):
    spare = 2 * count

    def row(number, found):
        def column(other, found):
            pairs_ref[found] = number * 1024 + other
            return found + jnp.where(skip_ref[number, other] == 0, 1, 0)

        mine = is_mine(device, slot, place_of(number, count), count)
        own_ref[found[1]] = number
        below = lax.fori_loop(0, jnp.where(mine, number, 0), column, found[0])
        return below, found[1] + jnp.where(mine, 1, 0)

    below, own = lax.fori_loop(0, spare, row, (0, 0))
    for extra in range(unroll):
        pairs_ref[below + extra] = spare * 1024
        own_ref[own + extra] = spare
    return pl.cdiv(below, unroll), pl.cdiv(own, unroll)


def running_sum(values, count, reverse):
    t = lax.broadcasted_iota(jnp.int32, (BLK, BLK), 0)
    p = lax.broadcasted_iota(jnp.int32, (BLK, BLK), 1)
    ones = jnp.where(t >= p if reverse else t <= p, 1.0, 0.0).astype(bf16)
    halves = []
    for half in range(2):
        part = values[:, half * BLK : (half + 1) * BLK]
        halves.append(sum(mm(piece.astype(bf16), ones) for piece in split3(part)))
    edge = 0 if reverse else BLK - 1
    first, last = (jnp.broadcast_to(h[:, edge : edge + 1], (count, 128)) for h in halves)
    rows = lax.broadcasted_iota(jnp.int32, (count, 128), 0)

    def scan(total, down):
        own = total
        step = 1
        while step < count:
            moved = pltpu.roll(total, step if down else count - step, 0)
            total = total + jnp.where(rows >= step if down else rows < count - step, moved, 0.0)
            step *= 2
        return total - own

    if reverse:
        all_last = jnp.sum(last, axis=0, keepdims=True)
        offsets = scan(first, False) + all_last, scan(last, True)
    else:
        all_first = jnp.sum(first, axis=0, keepdims=True)
        offsets = scan(first, True), scan(last, False) + all_first
    return jnp.concatenate([halves[0] + offsets[0][:, :1], halves[1] + offsets[1][:, :1]], 1)


def shifted(current, before):
    lane = lax.broadcasted_iota(jnp.int32, current.shape, 1)
    return jnp.where(lane == 0, pltpu.roll(before, 1, 1), pltpu.roll(current, 1, 1))


def shifted_back(current, after):
    lane = lax.broadcasted_iota(jnp.int32, current.shape, 1)
    return jnp.where(lane == BLK - 1, pltpu.roll(after, BLK - 1, 1), pltpu.roll(current, BLK - 1, 1))


def stack_rows(top, rows, size):
    extra = size if top is None else size - top.shape[0]
    number = lax.broadcasted_iota(jnp.int32, (extra, BLK), 0)
    bottom = jnp.zeros((extra, BLK), f32)
    for i, r in enumerate(rows):
        bottom = jnp.where(number == i, r, bottom)
    return bottom if top is None else jnp.concatenate([top, bottom], 0)


def prepare_block(count, block, carried, raw_ref, logit_ref, gain_ref, cum_ref, q_ref, k_ref, kt_ref, vt_ref):
    place, lanes = place_of(block, count), lanes_of(block, count)
    q_raw, k_raw, v_raw = (raw_ref[place, i, :, lanes].astype(f32) for i in range(3))
    cum = cum_ref[pl.ds(place, 1), lanes]
    parts = split3(cum)
    one = jnp.ones_like(cum)
    query = q_raw * lax.rsqrt(jnp.mean(q_raw * q_raw, 0, keepdims=True) + EPS) * (gain_ref[:, 1:2] * (SCORE * LOG2E))
    q_ref[block] = stack_rows(query, (*parts, one, one, one), 128).astype(bf16)
    rate_k = jax.nn.sigmoid(logit_ref[place, 1:2, lanes])
    rate_v = jax.nn.sigmoid(logit_ref[place, 2:3, lanes])
    key = k_raw + rate_k * (shifted(k_raw, carried[0]) - k_raw)
    key = key * lax.rsqrt(jnp.mean(key * key, 0, keepdims=True) + EPS) * gain_ref[:, 2:3]
    value = v_raw + rate_v * (shifted(v_raw, carried[1]) - v_raw)
    k_ref[block] = stack_rows(key, (one, one, one, *(-c for c in parts)), 128).T.astype(bf16)
    kt_ref[block] = stack_rows(key, (one,), 80).astype(bf16)
    vt_ref[block] = stack_rows(value, (one, one, one), 80).astype(bf16)
    return k_raw, v_raw


def finish_block(count, block, acc_ref, cum_ref, mixed_full_ref, mixed_ref, q_ref):
    place, lanes = place_of(block, count), lanes_of(block, count)
    summed = acc_ref[block]
    norm = summed[HDIM : HDIM + 1]
    mixed = summed[:HDIM] * (1.0 / norm)
    mixed_full_ref[block] = mixed
    mixed_ref[place, :, lanes] = mixed.astype(bf16)
    parts = split3(cum_ref[pl.ds(place, 1), lanes] - jnp.log2(norm))
    one = jnp.ones_like(norm)
    q_ref[block, HDIM : HDIM + 16, :] = stack_rows(None, (*parts, one, one, one), 16).astype(bf16)


def log_forget_sums(logits, count):
    log_forget = jnp.minimum(logits, 0.0) - jnp.log1p(jnp.exp(-jnp.abs(logits)))
    return running_sum(log_forget, count, False) * LOG2E


def causal():
    return lax.broadcasted_iota(jnp.int32, (BLK, BLK), 0) <= lax.broadcasted_iota(jnp.int32, (BLK, BLK), 1)


def forward_kernel(count, device_ref, skip_ref, bias_ref, raw_ref, logit_ref, gain_ref,
                   mixed_ref, mixed_full_ref, q_ref, k_ref, kt_ref, vt_ref,
                   cum_ref, acc_ref, pairs_ref, own_ref):
    slot = pl.program_id(0)
    device = device_ref[0]
    blocks = 2 * count
    pair_steps, own_steps = list_pairs(skip_ref, pairs_ref, own_ref, device, slot, count, UNROLL)
    cum_ref[...] = log_forget_sums(logit_ref[:, 0, :] + bias_ref[slot], count)

    def prepare(block, carried):
        return prepare_block(count, block, carried, raw_ref, logit_ref, gain_ref, cum_ref, q_ref, k_ref, kt_ref, vt_ref)

    zero = jnp.zeros((HDIM, BLK), f32)
    lax.fori_loop(0, blocks, prepare, (zero, zero))
    q_ref[blocks] = jnp.zeros(q_ref.shape[1:], bf16)

    def together(pairs, diagonal):
        scores = [mm(k_ref[column], q_ref[row]) for row, column in pairs]
        weights = [jnp.exp2(score) for score in scores]
        if diagonal:
            weights = [jnp.where(causal(), weight, 0.0) for weight in weights]
        weights = [weight.astype(bf16) for weight in weights]
        parts = [mm(vt_ref[column], weight) for (row, column), weight in zip(pairs, weights)]
        for (row, column), part in zip(pairs, parts):
            acc_ref[row] = part if diagonal else acc_ref[row] + part

    def own_rows(step, carried):
        rows = [own_ref[step * UNROLL + i] for i in range(UNROLL)]
        together([(row, jnp.minimum(row, blocks - 1)) for row in rows], True)
        return carried

    def kept_pairs(step, carried):
        codes = [pairs_ref[step * UNROLL + i] for i in range(UNROLL)]
        together([(code >> 10, code & 1023) for code in codes], False)
        return carried

    lax.fori_loop(0, own_steps, own_rows, 0)
    lax.fori_loop(0, pair_steps, kept_pairs, 0)

    def finish(block, carried):
        finish_block(count, block, acc_ref, cum_ref, mixed_full_ref, mixed_ref, q_ref)
        return carried

    lax.fori_loop(0, blocks, finish, 0)


def own_places(device, slot, count):
    start = (first_head(device, count) + slot) * count
    low = jnp.clip(HEADS * device - start, 0, count)
    return low, jnp.clip(HEADS * device + HEADS - start, low, count)


def slot_at(device, phase, count):
    low, high = own_places(device, 0, count)
    later, end = own_places(device, 1, count)
    swap = jnp.where(end - later > high - low, 1, 0)
    return phase + swap - 2 * phase * swap


def pairs_of_place(place, batch, size, count):
    found = []
    for i in range(size):
        number = batch * size + i
        lower = number < place
        found.append((jnp.where(lower, place, 2 * count - 1 - place), jnp.where(lower, number, number - place)))
    return found


def keep_factor(skip_ref, row, column):
    return jnp.where(skip_ref[row, column] == 0, 1.0, 0.0)


def buffers(count):
    return pl.Buffered(1 if count > 8 else 2)


def attend_forward(device, skip, bias, raw, logits, gains):
    count = raw.shape[0]
    blocks = 2 * count
    most = blocks * (blocks - 1) // 2 + UNROLL
    mode = buffers(count)
    by_slot = lambda *shape: pl.BlockSpec((None,) + shape, lambda s, *_: (s,) + (0,) * len(shape), pipeline_mode=mode)
    out = lambda shape, dtype: jax.ShapeDtypeStruct((2,) + shape, dtype)
    return pl.pallas_call(
        functools.partial(forward_kernel, count),
        grid_spec=pltpu.PrefetchScalarGridSpec(
            num_scalar_prefetch=3,
            grid=(2,),
            in_specs=[
                pl.BlockSpec((count, 3, None, HDIM, 2 * BLK), lambda s, *_: (0, 0, s, 0, 0), pipeline_mode=mode),
                pl.BlockSpec((count, None, 8, 2 * BLK), lambda s, *_: (0, s, 0, 0), pipeline_mode=mode),
                by_slot(HDIM, 8),
            ],
            out_specs=[
                by_slot(count, HDIM, 2 * BLK),
                by_slot(blocks, HDIM, BLK),
                by_slot(blocks + 1, 128, BLK),
                by_slot(blocks, BLK, 128),
                by_slot(blocks, 80, BLK),
                by_slot(blocks, 80, BLK),
            ],
            scratch_shapes=[
                pltpu.VMEM((count, 2 * BLK), f32),
                pltpu.VMEM((blocks + 1, 80, BLK), f32),
                pltpu.SMEM((most,), jnp.int32),
                pltpu.SMEM((blocks + UNROLL,), jnp.int32),
            ],
        ),
        out_shape=[
            out((count, HDIM, 2 * BLK), bf16),
            out((blocks, HDIM, BLK), f32),
            out((blocks + 1, 128, BLK), bf16),
            out((blocks, BLK, 128), bf16),
            out((blocks, 80, BLK), bf16),
            out((blocks, 80, BLK), bf16),
        ],
        compiler_params=pltpu.CompilerParams(vmem_limit_bytes=60 * 2**20),
        name="attend_forward",
    )(device, skip, bias, raw, logits, gains)


def norm_back(v, gain, u):
    scale = lax.rsqrt(jnp.mean(v * v, 0, keepdims=True) + EPS)
    hat = v * scale
    gu = gain * u
    return scale * (gu - hat * jnp.mean(hat * gu, 0, keepdims=True)), hat * u


def prepare_back(count, block, dmixed_ref, mixed_ref, vt_ref, do_ref, v_ref, dq_ref, dk_ref, dv_ref):
    place, lanes = place_of(block, count), lanes_of(block, count)
    d_out = dmixed_ref[place, :, lanes].astype(f32)
    delta = jnp.sum(d_out * mixed_ref[block], 0, keepdims=True)
    do_ref[block] = stack_rows(d_out, [-d for d in split3(delta)], 128).astype(bf16)
    wide = jnp.zeros((128 - 80, BLK), f32)
    v_ref[block] = jnp.concatenate([vt_ref[block].astype(f32), wide], 0).T.astype(bf16)
    dq_ref[block] = jnp.zeros(dq_ref.shape[1:], f32)
    dk_ref[block] = jnp.zeros(dk_ref.shape[1:], f32)
    dv_ref[block] = jnp.zeros(dv_ref.shape[1:], f32)


def batch_back(pairs, masks, q_ref, k_ref, kt_ref, v_ref, do_ref, dq_ref, dk_ref, dv_ref):
    weights = [jnp.exp2(mm(k_ref[column], q_ref[row])) for row, column in pairs]
    for i, mask in enumerate(masks):
        if mask is True:
            weights[i] = jnp.where(causal(), weights[i], 0.0)
        elif mask is not None:
            weights[i] = weights[i] * mask
    d_weights = [mm(v_ref[column], do_ref[row]) for row, column in pairs]
    low_weights = [weight.astype(bf16) for weight in weights]
    d_scores = [(weight * d_weight).astype(bf16) for weight, d_weight in zip(weights, d_weights)]
    parts = [mm(do_ref[row, :HDIM], weight, NT) for (row, _), weight in zip(pairs, low_weights)]
    for (_, column), part in zip(pairs, parts):
        dv_ref[column] += part
    parts = [mm(kt_ref[column], d_score) for (_, column), d_score in zip(pairs, d_scores)]
    for (row, _), part in zip(pairs, parts):
        dq_ref[row] += part
    parts = [mm(q_ref[row, :80], d_score, NT) for (row, _), d_score in zip(pairs, d_scores)]
    for (_, column), part in zip(pairs, parts):
        dk_ref[column] += part


def finish_back(count, block, carried, mine, raw_ref, logit_ref, gain_ref, dq_ref, dk_ref, dv_ref, draw_ref, dlogit_ref, cum_ref):
    next_k, next_v, sum_q, sum_k = carried
    place, lanes = place_of(block, count), lanes_of(block, count)
    earlier = jnp.maximum(block - 1, 0)
    place_before, lanes_before = place_of(earlier, count), lanes_of(earlier, count)
    exists = jnp.where(block > 0, 1.0, 0.0)
    q_raw, k_raw, v_raw = (raw_ref[place, i, :, lanes].astype(f32) for i in range(3))
    k_step = shifted(k_raw, raw_ref[place_before, 1, :, lanes_before].astype(f32) * exists) - k_raw
    v_step = shifted(v_raw, raw_ref[place_before, 2, :, lanes_before].astype(f32) * exists) - v_raw
    rate_k = jax.nn.sigmoid(logit_ref[place, 1:2, lanes])
    rate_v = jax.nn.sigmoid(logit_ref[place, 2:3, lanes])
    dq, dk, dv = dq_ref[block], dk_ref[block], dv_ref[block]
    dq_raw, part_q = norm_back(q_raw, gain_ref[:, 1:2], dq[:HDIM] * SCORE)
    dk_mixed, part_k = norm_back(k_raw + rate_k * k_step, gain_ref[:, 2:3], dk[:HDIM] * LN2)
    send_k, send_v = rate_k * dk_mixed, rate_v * dv
    draw_ref[place, 0, :, lanes] = dq_raw.astype(bf16)
    draw_ref[place, 1, :, lanes] = (dk_mixed - send_k + shifted_back(send_k, next_k)).astype(bf16)
    draw_ref[place, 2, :, lanes] = (dv - send_v + shifted_back(send_v, next_v)).astype(bf16)
    dlogit_ref[place, 1:2, lanes] = (1.0 - rate_k) * jnp.sum(k_step * send_k, 0, keepdims=True)
    dlogit_ref[place, 2:3, lanes] = (1.0 - rate_v) * jnp.sum(v_step * send_v, 0, keepdims=True)
    cum_ref[pl.ds(place, 1), lanes] = dq[HDIM : HDIM + 1] - dk[HDIM + 3 : HDIM + 4]
    return send_k, send_v, sum_q + jnp.where(mine, part_q, 0.0), sum_k + part_k


def forget_back(count, bias, logit_ref, cum_ref, dlogit_ref):
    d_log = running_sum(cum_ref[...], count, True)
    dlogit_ref[:, 0, :] = d_log * jax.nn.sigmoid(-(logit_ref[:, 0, :] + bias))
    dlogit_ref[:, 3:, :] = jnp.zeros((count, 5, 2 * BLK), f32)


def backward_kernel(count, device_ref, skip_ref, bias_ref, raw_ref, logit_ref, gain_ref, dmixed_ref, mixed_ref,
                    q_ref, k_ref, kt_ref, vt_ref, draw_ref, dlogit_ref, dgain_ref,
                    do_ref, v_ref, cum_ref, dq_ref, dk_ref, dv_ref, pairs_ref, own_ref):
    slot = pl.program_id(0)
    device = device_ref[0]
    blocks = 2 * count
    pair_steps, own_steps = list_pairs(skip_ref, pairs_ref, own_ref, device, slot, count, UNROLL_BACK)
    sums = (dq_ref, dk_ref, dv_ref)

    def prepare(block, carried):
        prepare_back(count, block, dmixed_ref, mixed_ref, vt_ref, do_ref, v_ref, *sums)
        return carried

    lax.fori_loop(0, blocks, prepare, 0)
    do_ref[blocks] = jnp.zeros(do_ref.shape[1:], bf16)
    dq_ref[blocks] = jnp.zeros(dq_ref.shape[1:], f32)

    def own_rows(step, carried):
        rows = [own_ref[step * UNROLL_BACK + i] for i in range(UNROLL_BACK)]
        pairs = [(row, jnp.minimum(row, blocks - 1)) for row in rows]
        batch_back(pairs, [True] * UNROLL_BACK, q_ref, k_ref, kt_ref, v_ref, do_ref, *sums)
        return carried

    def kept_pairs(step, carried):
        codes = [pairs_ref[step * UNROLL_BACK + i] for i in range(UNROLL_BACK)]
        pairs = [(code >> 10, code & 1023) for code in codes]
        batch_back(pairs, [None] * UNROLL_BACK, q_ref, k_ref, kt_ref, v_ref, do_ref, *sums)
        return carried

    lax.fori_loop(0, own_steps, own_rows, 0)
    lax.fori_loop(0, pair_steps, kept_pairs, 0)

    def finish(step, carried):
        block = blocks - 1 - step
        mine = is_mine(device, slot, place_of(block, count), count)
        return finish_back(count, block, carried, mine, raw_ref, logit_ref, gain_ref, *sums, draw_ref, dlogit_ref, cum_ref)

    zero = jnp.zeros((HDIM, BLK), f32)
    _, _, sum_q, sum_k = lax.fori_loop(0, blocks, finish, (zero, zero, zero, zero))
    dgain_ref[:, 1:2] = jnp.sum(sum_q, 1, keepdims=True)
    dgain_ref[:, 2:3] = jnp.sum(sum_k, 1, keepdims=True)
    forget_back(count, bias_ref[slot], logit_ref, cum_ref, dlogit_ref)


def attend_backward(device, skip, bias, raw, logits, gains, dmixed, mixed, q, k, kt, vt):
    count = raw.shape[0]
    blocks = 2 * count
    most = blocks * (blocks - 1) // 2 + UNROLL_BACK
    mode = buffers(count)
    by_slot = lambda *shape: pl.BlockSpec((None,) + shape, lambda s, *_: (s,) + (0,) * len(shape), pipeline_mode=mode)
    raw_spec = pl.BlockSpec((count, 3, None, HDIM, 2 * BLK), lambda s, *_: (0, 0, s, 0, 0), pipeline_mode=mode)
    place_spec = lambda rows: pl.BlockSpec((count, None, rows, 2 * BLK), lambda s, *_: (0, s, 0, 0), pipeline_mode=mode)
    return pl.pallas_call(
        functools.partial(backward_kernel, count),
        grid_spec=pltpu.PrefetchScalarGridSpec(
            num_scalar_prefetch=3,
            grid=(2,),
            in_specs=[
                raw_spec,
                place_spec(8),
                by_slot(HDIM, 8),
                place_spec(HDIM),
                by_slot(blocks, HDIM, BLK),
                by_slot(blocks + 1, 128, BLK),
                by_slot(blocks, BLK, 128),
                by_slot(blocks, 80, BLK),
                by_slot(blocks, 80, BLK),
            ],
            out_specs=[raw_spec, place_spec(8), by_slot(HDIM, 8)],
            scratch_shapes=[
                pltpu.VMEM((blocks + 1, 128, BLK), bf16),
                pltpu.VMEM((blocks, BLK, 128), bf16),
                pltpu.VMEM((count, 2 * BLK), f32),
                pltpu.VMEM((blocks + 1, 80, BLK), f32),
                pltpu.VMEM((blocks, 80, BLK), f32),
                pltpu.VMEM((blocks, HDIM, BLK), f32),
                pltpu.SMEM((most,), jnp.int32),
                pltpu.SMEM((blocks + UNROLL_BACK,), jnp.int32),
            ],
        ),
        out_shape=[
            jax.ShapeDtypeStruct(raw.shape, bf16),
            jax.ShapeDtypeStruct(logits.shape, f32),
            jax.ShapeDtypeStruct(gains.shape, f32),
        ],
        compiler_params=pltpu.CompilerParams(vmem_limit_bytes=60 * 2**20),
        name="attend_backward",
    )(device, skip, bias, raw, logits, gains, dmixed, mixed, q, k, kt, vt)


def holder(head, place, count):
    return (head * count + place) // HEADS


def greet(count):
    me = lax.axis_index("seq")
    barrier = pltpu.get_barrier_semaphore()
    for k in range(1, count):
        peer = lax.rem(me + k, count)
        pl.semaphore_signal(barrier, inc=1, device_id={"seq": peer}, device_id_type=MESH)
    pl.semaphore_wait(barrier, count - 1)
    return me


def far_first(count):
    return sorted(range(1, count), key=lambda k: -min(k, count - k))


def push(src, dst, send, recv, peer):
    return pltpu.make_async_remote_copy(
        src_ref=src, dst_ref=dst, send_sem=send, recv_sem=recv, device_id={"seq": peer}, device_id_type=MESH
    )


def heads_out_kernel(count, x_ref, logit_in, raw_ref, logit_ref, send, recv, local):
    me = greet(count)

    def copies(peer, source, k):
        head = first_head(peer, count)
        items = []
        for slot in range(2):
            items.append((is_mine(peer, slot, me, count), is_mine(me, slot, source, count),
                          push(x_ref.at[0, head + slot], raw_ref.at[me, 0, slot], send.at[k, slot], recv.at[k, slot], peer)))
        items.append((None, None, push(x_ref.at[pl.ds(1, 2), pl.ds(head, 2)], raw_ref.at[me, pl.ds(1, 2)], send.at[k, 2], recv.at[k, 2], peer)))
        items.append((None, None, push(logit_in.at[pl.ds(head, 2)], logit_ref.at[me], send.at[k, 3], recv.at[k, 3], peer)))
        return items

    every = []
    for k in far_first(count):
        items = copies(lax.rem(me + k, count), lax.rem(me + count - k, count), k)
        every.append(items)
        for out, _, copy in items:
            if out is None:
                copy.start()
            else:
                pl.when(out)(copy.start)
    head = first_head(me, count)
    own = [
        pltpu.make_async_copy(x_ref.at[:, pl.ds(head, 2)], raw_ref.at[me], local.at[0]),
        pltpu.make_async_copy(logit_in.at[pl.ds(head, 2)], logit_ref.at[me], local.at[1]),
    ]
    for copy in own:
        copy.start()
    for items in every:
        for out, into, copy in items:
            if out is None:
                copy.wait()
            else:
                pl.when(out)(copy.wait_send)
                pl.when(into)(copy.wait_recv)
    for copy in own:
        copy.wait()


def heads_out(qkv, logits, count):
    return pl.pallas_call(
        functools.partial(heads_out_kernel, count),
        out_shape=[
            jax.ShapeDtypeStruct((count, 3, 2, HDIM, 2 * BLK), bf16),
            jax.ShapeDtypeStruct((count, 2, 8, 2 * BLK), f32),
        ],
        in_specs=[ANY, ANY],
        out_specs=[ANY, ANY],
        scratch_shapes=[pltpu.SemaphoreType.DMA((count, 4)), pltpu.SemaphoreType.DMA((count, 4)), pltpu.SemaphoreType.DMA((2,))],
        compiler_params=pltpu.CompilerParams(collective_id=0, has_side_effects=True),
        name="heads_out",
    )(qkv, logits)


def mixed_back_kernel(count, x_ref, o_ref, send, recv, local):
    me = greet(count)
    first = first_head(me, count)
    started = []
    for k in far_first(count) + [0]:
        peer = lax.rem(me + k, count)
        for slot in range(2):
            mine = is_mine(me, slot, peer, count)
            src, dst = x_ref.at[slot, peer], o_ref.at[first + slot]
            if k:
                copy = push(src, dst, send.at[k, slot], recv.at[first + slot], peer)
            else:
                copy = pltpu.make_async_copy(src, dst, local.at[slot])
            started.append((mine, k, copy))
            pl.when(mine)(copy.start)
    for mine, k, copy in started:
        pl.when(mine)(copy.wait_send if k else copy.wait)
    for head in range(HEADS):
        source = holder(head, me, count)
        copy = push(x_ref.at[0, 0], o_ref.at[head], send.at[0, 0], recv.at[head], lax.rem(me + 1, count))
        pl.when(source != me)(copy.wait_recv)


def mixed_back(mixed, count):
    return pl.pallas_call(
        functools.partial(mixed_back_kernel, count),
        out_shape=jax.ShapeDtypeStruct((HEADS, HDIM, 2 * BLK), bf16),
        in_specs=[ANY],
        out_specs=ANY,
        scratch_shapes=[pltpu.SemaphoreType.DMA((count, 2)), pltpu.SemaphoreType.DMA((HEADS,)), pltpu.SemaphoreType.DMA((2,))],
        compiler_params=pltpu.CompilerParams(collective_id=1, has_side_effects=True),
        name="mixed_back",
    )(mixed)


def grads_out_kernel(count, x_ref, h1_ref, dgate_ref, h2_ref, dgu_ref, hidden_ref, dlow_ref, gated_ref, branch_ref,
                     o_ref, grads_ref, send, recv, local):
    me = greet(count)
    started = []
    for head in range(HEADS):
        peer = holder(head, me, count)
        slot = head - first_head(peer, count)
        away = peer != me
        there = jnp.where(away, peer, lax.rem(me + 1, count))
        copy = push(x_ref.at[head], o_ref.at[me, slot], send.at[head], recv.at[me, slot], there)
        own = pltpu.make_async_copy(x_ref.at[head], o_ref.at[me, slot], local.at[slot])
        pl.when(away)(copy.start)
        pl.when(peer == me)(own.start)
        started.append((away, peer == me, copy, own))

    def put(unit, part):
        grads_ref[pl.ds(unit, 16)] = part.astype(bf16).reshape(16, UNIT, 256)

    def gate_up(i, carried):
        right = dgu_ref[:, pl.ds(pl.multiple_of(i * 256, 256), 256)]
        for j in range(3):
            put(i * 48 + 16 * j, mm(h2_ref[:, 256 * j : 256 * j + 256], right, TN))
        return carried

    lax.fori_loop(0, 2 * FF // 256, gate_up, 0)

    def down(i, carried):
        left = hidden_ref[:, pl.ds(pl.multiple_of(i * 256, 256), 256)]
        for j in range(3):
            put(768 + 128 * j + 16 * i, mm(left, dlow_ref[:, 256 * j : 256 * j + 256], TN))
        return carried

    lax.fori_loop(0, FF // 256, down, 0)
    for i in range(3):
        for j in range(3):
            put(1152 + 48 * i + 16 * j, mm(gated_ref[256 * j : 256 * j + 256, :], branch_ref[:, 256 * i : 256 * i + 256]))
            put(1296 + 48 * i + 16 * j, lax.dot_general(
                h1_ref[:, 256 * j : 256 * j + 256], dgate_ref[256 * i : 256 * i + 256, :],
                (((0,), (1,)), ((), ())), preferred_element_type=f32))
    units = grads_ref.shape[0]
    if units > 1440:
        grads_ref[1440:] = jnp.zeros((units - 1440, UNIT, 256), bf16)

    for away, here, copy, own in started:
        pl.when(away)(copy.wait_send)
        pl.when(here)(own.wait)
    for k in range(1, count):
        source = lax.rem(me + k, count)
        for slot in range(2):
            copy = push(x_ref.at[0], o_ref.at[source, slot], send.at[0], recv.at[source, slot], source)
            pl.when(is_mine(me, slot, source, count))(copy.wait_recv)


def grads_out(count, units, d_mixed, *operands):
    vmem = pl.BlockSpec(memory_space=pltpu.VMEM)
    return pl.pallas_call(
        functools.partial(grads_out_kernel, count),
        out_shape=[
            jax.ShapeDtypeStruct((count, 2, HDIM, 2 * BLK), bf16),
            jax.ShapeDtypeStruct((units, UNIT, 256), bf16),
        ],
        in_specs=[ANY] + [vmem] * 8,
        out_specs=[ANY, vmem],
        scratch_shapes=[pltpu.SemaphoreType.DMA((HEADS,)), pltpu.SemaphoreType.DMA((count, 2)), pltpu.SemaphoreType.DMA((2,))],
        compiler_params=pltpu.CompilerParams(collective_id=2, has_side_effects=True, vmem_limit_bytes=60 * 2**20),
        name="grads_out",
    )(d_mixed, *operands)


def dot(a, b, i, j):
    return lax.dot_general(a, b, (((i,), (j,)), ((), ())), preferred_element_type=f32)


def front_kernel(count, skip_ref, bias_ref, x_ref, w_ref, wsmall_ref, gain_ref,
                 h_ref, gate_ref, att_ref, raw_out, logit_out, full_out, q_out, k_out, kt_out, vt_out,
                 ht_ref, proj_ref, small_ref, raw_ref, logit_ref, mixed_ref, full_ref, q_ref, k_ref, kt_ref, vt_ref, cum_ref, acc_ref, gains_ref,
                 send, recv, own, back_send, back_recv, back_own, keep):
    me = lax.axis_index("seq")
    barrier = pltpu.get_barrier_semaphore()
    for k in range(1, count):
        pl.semaphore_signal(barrier, inc=1, device_id={"seq": lax.rem(me + k, count)}, device_id_type=MESH)
    blocks = 2 * count
    rows = x_ref.shape[0]
    for i in range(rows // 128):
        here = slice(128 * i, 128 * i + 128)
        v = x_ref[here].astype(f32)
        normed = v * lax.rsqrt(jnp.mean(v * v, 1, keepdims=True) + EPS) * gain_ref[0:1]
        h_ref[here] = normed.astype(bf16)
        ht_ref[:, here] = normed.T.astype(bf16)

    def project(i, carried):
        block = mm(w_ref[:, pl.ds(pl.multiple_of(256 * i, 256), 256)], ht_ref[...], TN)
        proj_ref[pl.ds(4 * i, 4)] = block.astype(bf16).reshape(4, HDIM, rows)
        return carried

    gains_ref[...] = gain_ref[...].T
    small = mm(wsmall_ref[...], ht_ref[...], TN)
    for head in range(HEADS):
        ordered = [small[HEADS * i + head : HEADS * i + head + 1] for i in range(3)]
        small_ref[head] = jnp.concatenate(ordered + [jnp.zeros((5, rows), f32)], 0)
    lax.fori_loop(0, 9, project, 0)
    pl.semaphore_wait(barrier, count - 1)
    first = first_head(me, count)

    def out(slot, k, peer):
        head = first_head(peer, count) + slot
        sems = lambda i: (send.at[k, slot, i], recv.at[k, slot, i], peer)
        return [
            push(proj_ref.at[head], raw_ref.at[me, 0, slot], *sems(0)),
            push(proj_ref.at[HEADS + head], raw_ref.at[me, 1, slot], *sems(1)),
            push(proj_ref.at[2 * HEADS + head], raw_ref.at[me, 2, slot], *sems(2)),
            push(small_ref.at[head], logit_ref.at[me, slot], *sems(3)),
        ]

    def own_copies(slot):
        head = first + slot
        return [
            pltpu.make_async_copy(proj_ref.at[head], raw_ref.at[me, 0, slot], own.at[slot, 0]),
            pltpu.make_async_copy(proj_ref.at[HEADS + head], raw_ref.at[me, 1, slot], own.at[slot, 1]),
            pltpu.make_async_copy(proj_ref.at[2 * HEADS + head], raw_ref.at[me, 2, slot], own.at[slot, 2]),
            pltpu.make_async_copy(small_ref.at[head], logit_ref.at[me, slot], own.at[slot, 3]),
        ]

    for phase in range(2):
        for k in far_first(count):
            peer = lax.rem(me + k, count)
            slot = slot_at(peer, phase, count)
            copies = out(slot, k, peer)
            pl.when(is_mine(peer, slot, me, count))(copies[0].start)
            for copy in copies[1:]:
                copy.start()
        for copy in own_copies(slot_at(me, phase, count)):
            copy.start()

    def gate(i, carried):
        here = pl.ds(pl.multiple_of(256 * i, 256), 256)
        gate_ref[here] = mm(w_ref[:, pl.ds(pl.multiple_of(3 * D + 256 * i, 256), 256)], ht_ref[...], TN)
        return carried

    lax.fori_loop(0, 3, gate, 0)

    def saved(slot):
        return [
            pltpu.make_async_copy(src.at[slot], dst.at[slot], keep.at[slot, i])
            for i, (src, dst) in enumerate(
                ((full_ref, full_out), (q_ref, q_out), (k_ref, k_out), (kt_ref, kt_out), (vt_ref, vt_out)))
        ]

    def back(slot, k, peer):
        target = att_ref.at[pl.ds(pl.multiple_of((first + slot) * HDIM, HDIM), HDIM)]
        if k:
            return push(mixed_ref.at[slot, peer], target, back_send.at[k, slot], back_recv.at[first + slot], peer)
        return pltpu.make_async_copy(mixed_ref.at[slot, peer], target, back_own.at[slot])

    def one_slot(phase, carried):
        slot = slot_at(me, phase, count)
        for copy in own_copies(slot):
            copy.wait()
        for k in far_first(count):
            source = lax.rem(me + count - k, count)
            copies = out(slot, k, source)
            pl.when(is_mine(me, slot, source, count))(copies[0].wait_recv)
            for copy in copies[1:]:
                copy.wait_recv()
        head = first + slot
        raws, logits = raw_ref.at[:, :, slot], logit_ref.at[:, slot]
        gains = gains_ref.at[pl.ds(pl.multiple_of(head * HDIM, HDIM), HDIM)]
        qs, ks, kts, vts = q_ref.at[slot], k_ref.at[slot], kt_ref.at[slot], vt_ref.at[slot]
        cum_ref[...] = log_forget_sums(logits[:, 0, :] + bias_ref[head], count)

        def prepare(block, state):
            acc_ref[block] = jnp.zeros(acc_ref.shape[1:], f32)
            return prepare_block(count, block, state, raws, logits, gains, cum_ref, qs, ks, kts, vts)

        zero = jnp.zeros((HDIM, BLK), f32)
        lax.fori_loop(0, blocks, prepare, (zero, zero))
        qs[blocks] = jnp.zeros(q_ref.shape[2:], bf16)

        def batch(pairs, on_diagonal):
            weights = [jnp.exp2(mm(ks[column], qs[row])) for row, column in pairs]
            low = []
            for (row, column), weight, diagonal in zip(pairs, weights, on_diagonal):
                weight = jnp.where(causal(), weight, 0.0) if diagonal else weight * keep_factor(skip_ref, row, column)
                low.append(weight.astype(bf16))
            parts = [mm(vts[column], weight) for (_, column), weight in zip(pairs, low)]
            for (row, _), part in zip(pairs, parts):
                acc_ref[row] += part

        def one_place(place, state):
            number = blocks // UNROLL
            for i in range(number):
                pairs = pairs_of_place(place, i, UNROLL, count)
                diagonal = [False] * UNROLL
                if i == number - 1:
                    pairs.append((place, place))
                    diagonal[-1:] = [True, True]
                batch(pairs, diagonal)
            return state

        low, high = own_places(me, slot, count)
        lax.fori_loop(low, high, one_place, 0)

        def finish(block, state):
            finish_block(count, block, acc_ref, cum_ref, full_ref.at[slot], mixed_ref.at[slot], qs)
            return state

        lax.fori_loop(0, blocks, finish, 0)
        for k in far_first(count) + [0]:
            peer = lax.rem(me + k, count)
            pl.when(is_mine(me, slot, peer, count))(back(slot, k, peer).start)
        for copy in saved(slot):
            copy.start()
        return carried

    lax.fori_loop(0, 2, one_slot, 0)
    keep_raw = [
        pltpu.make_async_copy(raw_ref, raw_out, keep.at[0, 5]),
        pltpu.make_async_copy(logit_ref, logit_out, keep.at[1, 5]),
    ]
    for copy in keep_raw:
        copy.start()
    for slot in range(2):
        for k in far_first(count):
            peer = lax.rem(me + k, count)
            copies = out(slot, k, peer)
            pl.when(is_mine(peer, slot, me, count))(copies[0].wait_send)
            for copy in copies[1:]:
                copy.wait_send()
        for k in far_first(count) + [0]:
            peer = lax.rem(me + k, count)
            copy = back(slot, k, peer)
            pl.when(is_mine(me, slot, peer, count))(copy.wait_send if k else copy.wait)
    for head in range(HEADS):
        source = holder(head, me, count)
        copy = push(mixed_ref.at[0, 0], att_ref.at[pl.ds(head * HDIM, HDIM)], back_send.at[0, 0], back_recv.at[head], lax.rem(me + 1, count))
        pl.when(source != me)(copy.wait_recv)
    for slot in range(2):
        for copy in saved(slot):
            copy.wait()
    for copy in keep_raw:
        copy.wait()


def front(count, skip, bias, x, w_attn, w_small, gains):
    rows = x.shape[0]
    blocks = 2 * count
    vmem = pl.BlockSpec(memory_space=pltpu.VMEM)
    smem = pl.BlockSpec(memory_space=pltpu.SMEM)
    dma = pltpu.SemaphoreType.DMA
    raw, logit = (count, 3, 2, HDIM, rows), (count, 2, 8, rows)
    state = [((2, blocks, HDIM, BLK), f32), ((2, blocks + 1, 128, BLK), bf16), ((2, blocks, BLK, 128), bf16),
             ((2, blocks, 80, BLK), bf16), ((2, blocks, 80, BLK), bf16)]
    return pl.pallas_call(
        functools.partial(front_kernel, count),
        out_shape=[jax.ShapeDtypeStruct(s, t) for s, t in [
            ((rows, D), bf16), ((D, rows), f32), ((D, rows), bf16), (raw, bf16), (logit, f32)] + state],
        in_specs=[smem, smem] + [vmem] * 4,
        out_specs=[vmem] * 3 + [ANY] * 7,
        scratch_shapes=[
            pltpu.VMEM((D, rows), bf16),
            pltpu.VMEM((3 * HEADS, HDIM, rows), bf16),
            pltpu.VMEM((HEADS, 8, rows), f32),
            pltpu.VMEM(raw, bf16),
            pltpu.VMEM(logit, f32),
            pltpu.VMEM((2, count, HDIM, rows), bf16),
        ] + [pltpu.VMEM(s, t) for s, t in state] + [
            pltpu.VMEM((count, rows), f32),
            pltpu.VMEM((blocks + 1, 80, BLK), f32),
            pltpu.VMEM((D, 8), f32),
            dma((count, 2, 4)), dma((count, 2, 4)), dma((2, 4)),
            dma((count, 2)), dma((HEADS,)), dma((2,)), dma((2, 6)),
        ],
        compiler_params=pltpu.CompilerParams(collective_id=0, has_side_effects=True, vmem_limit_bytes=60 * 2**20),
        name="front",
    )(skip, bias, x, w_attn, w_small, gains)


SMALL = 48
UNIT = 16
PIECE = 8


def group_bits(group_count, count):
    bits = [("group", 1 << i) for i in range(group_count.bit_length() - 1)]
    return bits, [("seq", 1 << i) for i in range(count.bit_length() - 1)]


def partner(bit):
    axis, step = bit
    here = lax.axis_index(axis)
    side = lax.rem(here // step, 2)
    return {axis: here + step - 2 * step * side}, side


def greet_all(bits, count):
    me = lax.axis_index("seq")
    others = [partner(bit)[0] for bit in bits if bit[0] != "seq"]
    others += [{"seq": lax.rem(me + k, count)} for k in range(1, count)]
    barrier = pltpu.get_barrier_semaphore()
    for there in others:
        pl.semaphore_signal(barrier, inc=1, device_id=there, device_id_type=MESH)
    pl.semaphore_wait(barrier, len(others))
    return me


def orders(near, far, seq, busy):
    x, z, rest = seq[0], seq[1], seq[2:]
    kinds = [
        [near, far, x, z] + rest,
        [near, x, far, z] + rest,
        [near, z, x, far] + rest,
        [near, z, far, x] + rest,
    ]
    return [kinds[i] for i in (EARLY_KINDS if busy else (0, 1, 2, 0, 1, 3))]


EARLY_KINDS = (0, 1, 2, 0, 1, 3)
PARTS = 6


class Summing:
    def __init__(self, base, size, order, source, own, landing, result, send, recv, local):
        self.start, self.size, self.order, self.source, self.local = base, size, order, source, local
        self.own, self.landing, self.result, self.send, self.recv = own, landing, result, send, recv
        self.base, self.at, self.stage, self.copy, self.load = base, base, 0, None, None
        self.off = 0

    def give(self):
        there, side = partner(self.order[self.stage])
        half = self.size // 2
        self.keep = self.start + side * half
        held = self.own
        if self.stage == 0 and self.source is not None:
            held = self.source
            self.load = pltpu.make_async_copy(
                self.source.at[pl.ds(self.keep, half)], self.own.at[pl.ds(self.base // 2, half)], self.local
            )
            self.load.start()
        self.copy = pltpu.make_async_remote_copy(
            src_ref=held.at[pl.ds(self.start + (1 - side) * half - self.off, half)],
            dst_ref=self.landing.at[pl.ds(self.at, half)],
            send_sem=self.send.at[self.stage], recv_sem=self.recv.at[self.stage],
            device_id=there, device_id_type=MESH,
        )
        self.copy.start()

    def add(self):
        self.copy.wait()
        if self.load is not None:
            self.load.wait()
            self.load = None
            self.off = self.keep - self.base // 2
        half = self.size // 2
        step = PIECE if half % PIECE == 0 else 1
        keep, at, own, landing = self.keep - self.off, self.at, self.own, self.landing

        def piece(i, carried):
            mine = pl.ds(keep + i * step, step)
            own[mine] = own[mine] + landing[pl.ds(at + i * step, step)]
            return carried

        lax.fori_loop(0, half // step, piece, 0)
        self.start, self.size, self.at, self.stage = self.keep, half, at + half, self.stage + 1

    def settle(self):
        copy = pltpu.make_async_copy(
            self.own.at[pl.ds(self.start - self.off, self.size)], self.result.at[pl.ds(self.start, self.size)], self.local
        )
        copy.start()
        copy.wait()
        self.left = len(self.order)

    def spread(self):
        self.left -= 1
        there, side = partner(self.order[self.left])
        part = self.result.at[pl.ds(self.start, self.size)]
        stage = 2 * len(self.order) - 1 - self.left
        self.copy = pltpu.make_async_remote_copy(
            src_ref=part, dst_ref=part, send_sem=self.send.at[stage], recv_sem=self.recv.at[stage],
            device_id=there, device_id_type=MESH,
        )
        self.copy.start()
        self.start, self.size = self.start - side * self.size, 2 * self.size

    def gathered(self):
        self.copy.wait()


def total(parts):
    return functools.reduce(jnp.add, parts)


def held_heads(count):
    first = [min(HEADS * d // count, HEADS - 2) for d in range(count)]
    return [
        [(d, h - first[d]) for d in range(h * count // HEADS, ((h + 1) * count - 1) // HEADS + 1)]
        for h in range(HEADS)
    ]


def padded(units, least):
    return -(-units // least) * least


def sums_of(units, least, sets, source, own, landing, result, send, recv, local):
    pieces, base, sums = units // least, 0, []
    for i, order in enumerate(orders(*sets, source is not None)):
        size = least * ((pieces + PARTS - 1 - i) // PARTS)
        if not size:
            break
        sums.append(Summing(base, size, order, source, own, landing, result, send.at[i], recv.at[i], local.at[i]))
        base += size
    return sums


def step(sums, stages):
    for part in sums:
        if part.stage < stages:
            part.add()
            if part.stage < stages:
                part.give()
            else:
                part.settle()
                part.spread()
        else:
            part.gathered()
            if part.left > 0:
                part.spread()


def put_together(holders, part_ref, logit_ref, proj_ref, dsmall_ref):
    for head, held in enumerate(holders):
        for i in range(2):
            start = D * (1 + i) + head * HDIM
            if len(held) == 1:
                proj_ref[start : start + HDIM] = part_ref[head, 0, i]
            else:
                proj_ref[start : start + HDIM] = total([part_ref[head, j, i].astype(f32) for j in range(len(held))]).astype(bf16)
        dsmall_ref[8 * head : 8 * head + 8] = total([logit_ref[d, s] for d, s in held])


def late_weights(h_ref, proj_ref, g_ref):
    def block(i, carried):
        grads = proj_ref[pl.ds(pl.multiple_of(i * 256, 256), 256)]
        for j in range(3):
            part = lax.dot_general(h_ref[:, 256 * j : 256 * j + 256], grads, (((0,), (1,)), ((), ())), preferred_element_type=f32)
            g_ref[pl.ds(i * (D // UNIT) + j * 16, 16)] = part.astype(bf16).reshape(16, UNIT, 256)
        return carried

    lax.fori_loop(0, 9, block, 0)


def late_rest(h_ref, proj_ref, w_ref, wsmall_ref, x_ref, gain_ref, dresid_ref, extra_ref, dsmall_ref, rows_ref, small_ref, dx_ref, g_ref, gsum_ref=None):
    ordered = [dsmall_ref[8 * head + i : 8 * head + i + 1] for i in range(3) for head in range(HEADS)]
    low_small = jnp.concatenate(ordered + [jnp.zeros((SMALL - 3 * HEADS, ordered[0].shape[1]), f32)], 0).astype(bf16)
    for i in range(3):
        cols = slice(256 * i, 256 * i + 256)
        part = mm(w_ref[cols, :], proj_ref[...]) + mm(wsmall_ref[cols, :], low_small)
        dx_ref[:, cols] = part.T
    rows_ref[...] = mm(low_small, h_ref[...])
    small_ref[...] = extra_ref[...]
    if gsum_ref is not None:
        small_ref[2:4] = gsum_ref[0:2]
    gain = gain_ref[0:1]
    dgain = jnp.zeros((1, D), f32)
    for i in range(h_ref.shape[0] // 128):
        here = slice(128 * i, 128 * i + 128)
        v, u = x_ref[here].astype(f32), dx_ref[here]
        scale = lax.rsqrt(jnp.mean(v * v, 1, keepdims=True) + EPS)
        hat, gu = v * scale, u * gain
        dx_ref[here] = dresid_ref[here] + scale * (gu - hat * jnp.mean(hat * gu, 1, keepdims=True))
        dgain = dgain + jnp.sum(hat * u, 0, keepdims=True)
    small_ref[0:1] = dgain
    bias_rows = jnp.concatenate([dsmall_ref[8 * head : 8 * head + 1] for head in range(HEADS)], 0)
    bias_sum = jnp.sum(bias_rows, 1, keepdims=True)
    lane = lax.broadcasted_iota(jnp.int32, (HEADS, 128), 1)
    row = lax.broadcasted_iota(jnp.int32, (HEADS, 128), 0)
    small_ref[4:5, 0:128] = jnp.sum(jnp.where(lane == row, bias_sum, 0.0), 0, keepdims=True)

    used = 9 * (D // UNIT)
    units = g_ref.shape[0]
    for i in range(3):
        g_ref[used + 3 * i : used + 3 * i + 3] = rows_ref[:, 256 * i : 256 * i + 256].astype(bf16).reshape(3, UNIT, 256)
    if units > used + 9:
        g_ref[used + 9 :] = jnp.zeros((units - used - 9, UNIT, 256), bf16)


class Doubling:
    def __init__(self, bits, own, landing, send, recv):
        self.bits, self.own, self.landing, self.send, self.recv = bits, own, landing, send, recv
        self.at = 0

    def give(self):
        there, _ = partner(self.bits[self.at])
        self.copy = pltpu.make_async_remote_copy(
            src_ref=self.own, dst_ref=self.landing.at[self.at], send_sem=self.send.at[self.at], recv_sem=self.recv.at[self.at],
            device_id=there, device_id_type=MESH,
        )
        self.copy.start()

    def add(self):
        self.copy.wait()
        self.own[...] += self.landing[self.at]
        self.at += 1


def finish_late(late, early, early_left, stages, small, small_out):
    for stage in range(2 * stages):
        if stage < stages:
            small.give()
        step(late, stages)
        if stage < early_left:
            step(early, stages)
        if stage < stages:
            small.add()
    small_out[...] = small.own[...]


def give_late(sums, rest, early, stages):
    units = 9 * (D // UNIT)
    ahead = [part for part in sums if part.start + part.size <= units]
    for part in ahead:
        part.give()
    rest()
    for part in sums[len(ahead):]:
        part.give()
    step(early, stages)


def last_kernel(count, sets, draw_ref, dlogit_ref, early_ref, h_ref, dgate_ref, w_ref, wsmall_ref, x_ref, gain_ref,
                dresid_ref, extra_ref, late_out, early_out, dx_ref, small_out,
                proj_ref, logit_ref, part_ref, dsmall_ref, rows_ref, small_ref, small_land, ssend, srecv, g_ref, land_ref, e_ref, eland_ref,
                send, recv, recv_q, recv_kv, local, gsend, grecv, gsem, esend, erecv, esem):
    near, far, seq = sets
    bits = [near, far] + seq
    stages, least = len(bits), 1 << len(bits)
    me = greet_all(bits, count)
    early = sums_of(early_ref.shape[0], least, sets, early_ref, e_ref, eland_ref, early_out, esend, erecv, esem)
    for part in early:
        part.give()

    holders = held_heads(count)
    first = first_head(me, count)
    started = []
    for k in far_first(count) + [0]:
        peer = lax.rem(me + k, count)
        pairs = [(None, dlogit_ref.at[peer], logit_ref.at[me], recv.at[k])]
        for slot in range(2):
            head = first + slot
            target = proj_ref.at[pl.ds(pl.multiple_of(head * HDIM, HDIM), HDIM)]
            pairs.append((is_mine(me, slot, peer, count), draw_ref.at[peer, 0, slot], target, recv_q.at[head]))
            used = (head * count < HEADS * (me + 1)) & (head * count + count > HEADS * me)
            order = me - holder(head, 0, count)
            pairs.append((used, draw_ref.at[peer, pl.ds(1, 2), slot], part_ref.at[head, order], recv_kv.at[head, order]))
        for i, (mine, src, dst, sem) in enumerate(pairs):
            copy = push(src, dst, send.at[k, i], sem, peer) if k else pltpu.make_async_copy(src, dst, local.at[i])
            started.append((mine, k, copy))
            if mine is None:
                copy.start()
            else:
                pl.when(mine)(copy.start)

    step(early, stages)
    step(early, stages)

    for mine, k, copy in started:
        if mine is not None:
            pl.when(mine)(copy.wait_send if k else copy.wait)
        else:
            copy.wait()
    for head in range(HEADS):
        source = holder(head, me, count)
        copy = push(draw_ref.at[0, 0, 0], proj_ref.at[pl.ds(head * HDIM, HDIM)], send.at[0, 0], recv_q.at[head], lax.rem(me + 1, count))
        pl.when(source != me)(copy.wait_recv)
        for j, (d, s) in enumerate(holders[head]):
            copy = push(draw_ref.at[0, pl.ds(1, 2), 0], part_ref.at[head, j], send.at[0, 0], recv_kv.at[head, j], lax.rem(me + 1, count))
            pl.when(me != d)(copy.wait_recv)

    put_together(holders, part_ref, logit_ref, proj_ref, dsmall_ref)
    proj_ref[3 * D :] = dgate_ref[...]

    late_weights(h_ref, proj_ref, g_ref)
    late = sums_of(g_ref.shape[0], least, sets, None, g_ref, land_ref, late_out, gsend, grecv, gsem)

    def rest():
        late_rest(h_ref, proj_ref, w_ref, wsmall_ref, x_ref, gain_ref, dresid_ref, extra_ref, dsmall_ref, rows_ref, small_ref, dx_ref, g_ref)

    give_late(late, rest, early, stages)
    finish_late(late, early, 2 * stages - 3, stages, Doubling(bits, small_ref, small_land, ssend, srecv), small_out)


def last(count, sets, d_raw, d_logits, early, h, d_gate, w_attn, w_small, x, gain, d_resid, extra):
    stages = 2 + len(sets[2])
    units = padded(9 * (D // UNIT) + 9, 1 << stages)
    rows = h.shape[0]
    most = max(len(held) for held in held_heads(count))
    vmem = pl.BlockSpec(memory_space=pltpu.VMEM)
    dma = pltpu.SemaphoreType.DMA
    shape = (UNIT, 256)
    return pl.pallas_call(
        functools.partial(last_kernel, count, sets),
        out_shape=[
            jax.ShapeDtypeStruct((units,) + shape, bf16),
            jax.ShapeDtypeStruct(early.shape, bf16),
            jax.ShapeDtypeStruct((rows, D), f32),
            jax.ShapeDtypeStruct((8, D), f32),
        ],
        in_specs=[ANY] * 3 + [vmem] * 8,
        out_specs=[ANY, ANY, vmem, vmem],
        scratch_shapes=[
            pltpu.VMEM((4 * D, rows), bf16),
            pltpu.VMEM((count, 2, 8, rows), f32),
            pltpu.VMEM((HEADS, most, 2, HDIM, rows), bf16),
            pltpu.VMEM((8 * HEADS, rows), f32),
            pltpu.VMEM((SMALL, D), f32),
            pltpu.VMEM((8, D), f32),
            pltpu.VMEM((stages, 8, D), f32),
            dma((stages,)), dma((stages,)),
            pltpu.VMEM((units,) + shape, bf16),
            pltpu.VMEM((units,) + shape, bf16),
            pltpu.VMEM((early.shape[0] // 2,) + shape, bf16),
            pltpu.VMEM(early.shape, bf16),
            dma((count, 5)), dma((count,)), dma((HEADS,)), dma((HEADS, most)), dma((5,)),
            dma((PARTS, 2 * stages)), dma((PARTS, 2 * stages)), dma((PARTS,)),
            dma((PARTS, 2 * stages)), dma((PARTS, 2 * stages)), dma((PARTS,)),
        ],
        compiler_params=pltpu.CompilerParams(collective_id=3, has_side_effects=True, vmem_limit_bytes=62 * 2**20),
        name="last",
    )(d_raw, d_logits, early, h, d_gate, w_attn, w_small, x, gain, d_resid, extra)


def unpack_kernel(parts, *refs):
    o_ref = refs[-1]
    width = refs[0].shape[0] // (o_ref.shape[0] // UNIT)
    at = 0
    for ref, blocks in zip(refs, parts):

        @pl.when((pl.program_id(0) >= at) & (pl.program_id(0) < at + blocks))
        def _(ref=ref):
            for i in range(width):
                size = o_ref.shape[0] // UNIT
                block = ref[size * i : size * i + size].reshape(o_ref.shape[0], 256)
                o_ref[:, 256 * i : 256 * i + 256] = block.astype(f32)

        at += blocks


def unpack(rows, width, *parts):
    size = rows // UNIT
    specs, at = [], 0
    for _, first, blocks in parts:
        first, blocks = first // width, blocks // width
        index = lambda i, at=at, first=first, blocks=blocks: (first + jnp.clip(i - at, 0, blocks - 1), 0, 0)
        specs.append(pl.BlockSpec((size * width, UNIT, 256), index))
        at += blocks
    return pl.pallas_call(
        functools.partial(unpack_kernel, [blocks // width for _, _, blocks in parts]),
        grid=(at,),
        in_specs=specs,
        out_specs=pl.BlockSpec((rows, 256 * width), lambda i: (0, i)),
        out_shape=jax.ShapeDtypeStruct((rows, 256 * at * width), f32),
        compiler_params=pltpu.CompilerParams(vmem_limit_bytes=62 * 2**20),
        name="unpack",
    )(*[units for units, _, _ in parts])


def back_kernel(count, sets, skip_ref, bias_ref, dmixed_ref, logits_ref, wsmall_ref, gain_ref, extra_ref,
                raw_in, full_in, q_in, k_in, kt_in, vt_in, early_ref, h_in, dgate_in, w_in, x_in, dresid_in,
                late_out, early_out, dx_ref, small_out,
                raw_ref, full_ref, q_ref, k_ref, kt_ref, vt_ref, do_ref, v_ref, cum_ref, dq_ref, dk_ref, dv_ref,
                dlogit_ref, gsum_ref, gains_ref,
                proj_ref, logit_ref, part_ref, dsmall_ref, rows_ref, small_ref, small_land, ssend, srecv, h_ref, w_ref, x_ref, dresid_ref,
                g_ref, land_ref, e_ref, eland_ref,
                load, send, recv, recv_q, recv_kv, own, gsend, grecv, gsem, esend, erecv, esem):
    near, far, seq = sets
    bits = [near, far] + seq
    stages, least = len(bits), 1 << len(bits)
    blocks = 2 * count
    draw_ref = raw_ref
    sums = (dq_ref, dk_ref, dv_ref)

    def state(slot):
        pairs = ((full_in, full_ref), (q_in, q_ref), (k_in, k_ref), (kt_in, kt_ref), (vt_in, vt_ref))
        return [pltpu.make_async_copy(src.at[slot], dst, load.at[i]) for i, (src, dst) in enumerate(pairs)]

    other = [
        pltpu.make_async_copy(src, dst, load.at[5 + i])
        for i, (src, dst) in enumerate((
            (raw_in, raw_ref), (h_in, h_ref), (dgate_in, proj_ref.at[pl.ds(3 * D, D)]), (w_in, w_ref), (x_in, x_ref), (dresid_in, dresid_ref)))
    ]
    me = lax.axis_index("seq")
    for copy in state(slot_at(me, 0, count)) + other:
        copy.start()
    greet_all(bits, count)
    first = first_head(me, count)
    holders = held_heads(count)
    early = sums_of(early_ref.shape[0], least, sets, early_ref, e_ref, eland_ref, early_out, esend, erecv, esem)
    for part in early:
        part.give()
    gsum_ref[...] = jnp.zeros(gsum_ref.shape, f32)
    gains_ref[...] = gain_ref[...].T

    def sends(slot, k):
        peer = lax.rem(me + k, count)
        head = first + slot
        order = me - holder(head, 0, count)
        used = (head * count < HEADS * (me + 1)) & (head * count + count > HEADS * me)
        target = proj_ref.at[pl.ds(pl.multiple_of(head * HDIM, HDIM), HDIM)]
        items = [
            (None, dlogit_ref.at[peer, slot], logit_ref.at[me, slot], recv.at[k, slot]),
            (is_mine(me, slot, peer, count), draw_ref.at[peer, 0, slot], target, recv_q.at[head]),
            (used, draw_ref.at[peer, pl.ds(1, 2), slot], part_ref.at[head, order], recv_kv.at[head, order]),
        ]
        return [
            (mine, push(src, dst, send.at[k, slot, i], sem, peer) if k else pltpu.make_async_copy(src, dst, own.at[slot, i]))
            for i, (mine, src, dst, sem) in enumerate(items)
        ]

    for phase in range(2):
        slot = slot_at(me, phase, count)
        for copy in state(slot):
            copy.wait()

        def prepare(block, carried):
            prepare_back(count, block, dmixed_ref.at[:, slot], full_ref, vt_ref, do_ref, v_ref, *sums)
            return carried

        lax.fori_loop(0, blocks, prepare, 0)
        step(early, stages)

        def one_place(place, carried):
            for i in range(blocks // UNROLL_BACK):
                pairs = pairs_of_place(place, i, UNROLL_BACK, count)
                masks = [keep_factor(skip_ref, row, column) for row, column in pairs]
                if (i + 1) * UNROLL_BACK == blocks:
                    pairs.append((place, place))
                    masks[-1:] = [True, True]
                batch_back(pairs, masks, q_ref, k_ref, kt_ref, v_ref, do_ref, *sums)
            return carried

        low, high = own_places(me, slot, count)
        middle = (low + high) // 2
        if phase == 0:
            lax.fori_loop(low, high, one_place, 0)
        else:
            lax.fori_loop(low, middle, one_place, 0)
            step(early, stages)
            lax.fori_loop(middle, high, one_place, 0)
        step(early, stages)
        if phase == 0:
            for copy in state(slot_at(me, 1, count)):
                copy.start()
            other[0].wait()
        raws, logits = raw_ref.at[:, :, slot], logits_ref.at[:, slot]
        gains = gains_ref.at[pl.ds(pl.multiple_of((first + slot) * HDIM, HDIM), HDIM)]
        draws, dlogits = draw_ref.at[:, :, slot], dlogit_ref.at[:, slot]

        def finish(number, carried):
            block = blocks - 1 - number
            mine = is_mine(me, slot, place_of(block, count), count)
            return finish_back(count, block, carried, mine, raws, logits, gains, *sums, draws, dlogits, cum_ref)

        zero = jnp.zeros((HDIM, BLK), f32)
        _, _, sum_q, sum_k = lax.fori_loop(0, blocks, finish, (zero, zero, zero, zero))
        lane = lax.broadcasted_iota(jnp.int32, (HDIM, D), 1)
        channel = lax.broadcasted_iota(jnp.int32, (HDIM, D), 0)
        here = lane == channel + (first + slot) * HDIM
        for i, column in enumerate((sum_q, sum_k)):
            placed = jnp.where(here, jnp.sum(column, 1, keepdims=True), 0.0)
            gsum_ref[i : i + 1] += jnp.sum(placed, 0, keepdims=True)
        forget_back(count, bias_ref[first + slot], logits, cum_ref, dlogits)
        for k in far_first(count) + [0]:
            for mine, copy in sends(slot, k):
                if mine is None:
                    copy.start()
                else:
                    pl.when(mine)(copy.start)
        step(early, stages)

    for _ in range(LATER):
        step(early, stages)
    for copy in other[1:]:
        copy.wait()
    for slot in range(2):
        for k in far_first(count) + [0]:
            for mine, copy in sends(slot, k):
                if mine is None:
                    copy.wait()
                else:
                    pl.when(mine)(copy.wait_send if k else copy.wait)
    for head in range(HEADS):
        source = holder(head, me, count)
        next_one = lax.rem(me + 1, count)
        copy = push(draw_ref.at[0, 0, 0], proj_ref.at[pl.ds(head * HDIM, HDIM)], send.at[0, 0, 0], recv_q.at[head], next_one)
        pl.when(source != me)(copy.wait_recv)
        for j, (d, s) in enumerate(holders[head]):
            copy = push(draw_ref.at[0, pl.ds(1, 2), 0], part_ref.at[head, j], send.at[0, 0, 0], recv_kv.at[head, j], next_one)
            pl.when(me != d)(copy.wait_recv)

    put_together(holders, part_ref, logit_ref, proj_ref, dsmall_ref)
    late_weights(h_ref, proj_ref, g_ref)
    late = sums_of(g_ref.shape[0], least, sets, None, g_ref, land_ref, late_out, gsend, grecv, gsem)

    def rest():
        late_rest(h_ref, proj_ref, w_ref, wsmall_ref, x_ref, gain_ref, dresid_ref, extra_ref, dsmall_ref, rows_ref, small_ref, dx_ref, g_ref, gsum_ref)

    give_late(late, rest, early, stages)
    finish_late(late, early, 2 * stages - 8 - LATER, stages, Doubling(bits, small_ref, small_land, ssend, srecv), small_out)


LATER = 1


def back(count, sets, skip, bias, d_mixed, logits, w_small, gains, extra, raw, full, q, k, kt, vt, early, h, d_gate, w_attn, x, d_resid):
    stages = 2 + len(sets[2])
    units = padded(9 * (D // UNIT) + 9, 1 << stages)
    rows = h.shape[0]
    blocks = 2 * count
    most = max(len(held) for held in held_heads(count))
    vmem = pl.BlockSpec(memory_space=pltpu.VMEM)
    smem = pl.BlockSpec(memory_space=pltpu.SMEM)
    dma = pltpu.SemaphoreType.DMA
    shape = (UNIT, 256)
    held = lambda array: pltpu.VMEM(array.shape[1:], array.dtype)
    return pl.pallas_call(
        functools.partial(back_kernel, count, sets),
        out_shape=[
            jax.ShapeDtypeStruct((units,) + shape, bf16),
            jax.ShapeDtypeStruct(early.shape, bf16),
            jax.ShapeDtypeStruct((rows, D), f32),
            jax.ShapeDtypeStruct((8, D), f32),
        ],
        in_specs=[smem, smem] + [vmem] * 5 + [ANY] * 12,
        out_specs=[ANY, ANY, vmem, vmem],
        scratch_shapes=[
            pltpu.VMEM(raw.shape, bf16), held(full), held(q), held(k), held(kt), held(vt),
            pltpu.VMEM((blocks + 1, 128, BLK), bf16),
            pltpu.VMEM((blocks, BLK, 128), bf16),
            pltpu.VMEM((count, rows), f32),
            pltpu.VMEM((blocks + 1, 80, BLK), f32),
            pltpu.VMEM((blocks, 80, BLK), f32),
            pltpu.VMEM((blocks, HDIM, BLK), f32),
            pltpu.VMEM(logits.shape, f32),
            pltpu.VMEM((8, D), f32),
            pltpu.VMEM((D, 8), f32),
            pltpu.VMEM((4 * D, rows), bf16),
            pltpu.VMEM((count, 2, 8, rows), f32),
            pltpu.VMEM((HEADS, most, 2, HDIM, rows), bf16),
            pltpu.VMEM((8 * HEADS, rows), f32),
            pltpu.VMEM((SMALL, D), f32),
            pltpu.VMEM((8, D), f32),
            pltpu.VMEM((stages, 8, D), f32),
            dma((stages,)), dma((stages,)),
            pltpu.VMEM(h.shape, bf16),
            pltpu.VMEM(w_attn.shape, bf16),
            pltpu.VMEM(x.shape, bf16),
            pltpu.VMEM(d_resid.shape, f32),
            pltpu.VMEM((units,) + shape, bf16),
            pltpu.VMEM((units,) + shape, bf16),
            pltpu.VMEM((early.shape[0] // 2,) + shape, bf16),
            pltpu.VMEM(early.shape, bf16),
            dma((11,)), dma((count, 2, 3)), dma((count, 2)), dma((HEADS,)), dma((HEADS, most)), dma((2, 3)),
            dma((PARTS, 2 * stages)), dma((PARTS, 2 * stages)), dma((PARTS,)),
            dma((PARTS, 2 * stages)), dma((PARTS, 2 * stages)), dma((PARTS,)),
        ],
        compiler_params=pltpu.CompilerParams(collective_id=4, has_side_effects=True, vmem_limit_bytes=63 * 2**20),
        name="back",
    )(skip, bias, d_mixed, logits, w_small, gains, extra, raw, full, q, k, kt, vt, early, h, d_gate, w_attn, x, d_resid)


def rms_scale(values, gains):
    inverse = lax.rsqrt(jnp.mean(values * values, axis=-1, keepdims=True) + EPS)
    return values * inverse * gains


def swiglu(gate_up):
    return jax.nn.silu(gate_up[:, :FF]) * gate_up[:, FF:]


def local(tokens, cotangent, skip_table, gain_attn, w_attn, w_heads, forget_bias, query_gain, key_gain,
          w_out, gain_ffn, w_gate_up, w_down):
    count = lax.axis_size("seq")
    me = lax.axis_index("seq")
    rows = tokens.shape[1]
    both = ("seq", "group")
    inputs = tokens[0].astype(f32)
    device = me.astype(jnp.int32)[None]
    head = first_head(me, count)
    skip = skip_table[0]
    all_gains = jnp.concatenate([jnp.stack([gain_attn, query_gain, key_gain]), jnp.zeros((5, D), f32)], 0)
    if count <= 8:
        h_first, gate_logit, attended, raw, logits, mixed, q, k, kt, vt = front(
            count, skip, forget_bias, tokens[0], w_attn, w_heads, all_gains
        )
    else:
        gains = lax.dynamic_slice_in_dim(all_gains.T.reshape(HEADS, HDIM, 8), head, 2, 0)
        bias = lax.dynamic_slice_in_dim(forget_bias, head, 2, 0)
        w_small = jnp.pad(w_heads.reshape(D, 3, HEADS).transpose(0, 2, 1), ((0, 0), (0, 0), (0, 5))).reshape(D, HEADS * 8)
        h_first = rms_scale(inputs, gain_attn).astype(bf16)
        qkv = dot(w_attn[:, : 3 * D], h_first, 0, 1).astype(bf16).reshape(3, HEADS, HDIM, rows)
        gate_logit = dot(w_attn[:, 3 * D :], h_first, 0, 1)
        logits_here = dot(w_small, h_first, 0, 1).reshape(HEADS, 8, rows)
        raw, logits = heads_out(qkv, logits_here, count)
        mixed_low, mixed, q, k, kt, vt = attend_forward(device, skip, bias, raw, logits, gains)
        attended = mixed_back(mixed_low, count).reshape(D, rows)
    attended = attended.astype(f32)

    gate_open = jax.nn.sigmoid(gate_logit)
    gated = (gate_open * attended).astype(bf16)
    resid = inputs + dot(gated, w_out, 0, 0)
    normed_ffn, norm_back_ffn = jax.vjp(rms_scale, resid, gain_ffn)
    h_second = normed_ffn.astype(bf16)
    gate_up = dot(h_second, w_gate_up, 1, 0)
    hidden, hidden_back = jax.vjp(swiglu, gate_up)
    hidden_low = hidden.astype(bf16)
    output = resid + dot(hidden_low, w_down, 1, 0)
    d_low = cotangent[0]
    d_output = d_low.astype(f32)
    (d_gate_up,) = hidden_back(dot(d_low, w_down, 1, 1))
    d_gate_low = d_gate_up.astype(bf16)
    d_resid_norm, grad_gain_ffn = norm_back_ffn(dot(d_gate_low, w_gate_up, 1, 1))
    d_resid = d_output + d_resid_norm
    d_branch = d_resid.astype(bf16)
    d_gated = dot(w_out, d_branch, 1, 1)
    d_gate_logit = (d_gated * attended * gate_open * (1.0 - gate_open)).astype(bf16)
    d_mixed = (d_gated * gate_open).astype(bf16).reshape(HEADS, HDIM, rows)

    near_far, seq_bits = group_bits(lax.axis_size("group"), count)
    sets = (near_far[0], near_far[1], seq_bits)
    units = padded(1440, 1 << (2 + len(seq_bits)))
    d_mixed_all, early = grads_out(
        count, units, d_mixed, h_first, d_gate_logit, h_second, d_gate_low, hidden_low, d_low, gated, d_branch
    )
    zeros = lambda n: jnp.zeros((n, D), f32)
    if count <= 8:
        extra = jnp.concatenate([zeros(1), grad_gain_ffn[None], zeros(6)], 0)
        late, early, d_inputs, small = back(
            count, sets, skip, forget_bias, d_mixed_all, logits, jnp.pad(w_heads, ((0, 0), (0, SMALL - 3 * HEADS))), all_gains, extra,
            raw, mixed, q, k, kt, vt, early, h_first, d_gate_logit, w_attn, tokens[0], d_resid,
        )
    else:
        d_raw, d_logits, d_gains = attend_backward(device, skip, bias, raw, logits, gains, d_mixed_all, mixed, q, k, kt, vt)
        placed = lax.dynamic_update_slice(jnp.zeros((HEADS, HDIM, 2), f32), d_gains[..., 1:3], (head, 0, 0)).reshape(D, 2).T
        extra = jnp.concatenate([zeros(1), grad_gain_ffn[None], placed, zeros(4)], 0)
        late, early, d_inputs, small = last(
            count, sets, d_raw, d_logits, early, h_first, d_gate_logit, w_attn,
            jnp.pad(w_heads, ((0, 0), (0, SMALL - 3 * HEADS))), tokens[0], gain_attn[None], d_resid, extra
        )
    row = 3 * HEADS
    used = 9 * (D // UNIT)
    heads_rows = late[used : used + 9].reshape(3, SMALL, 256).transpose(1, 0, 2).reshape(SMALL, D).astype(f32)
    return (
        output[None].astype(bf16),
        d_inputs[None],
        small[0],
        unpack(D, 3, (late, 0, 9), (early, 27, 3)),
        heads_rows[:row].T,
        small[4, :HEADS],
        small[2],
        small[3],
        unpack(D, 1, (early, 24, 3)),
        small[1],
        unpack(D, 2, (early, 0, 16)),
        unpack(FF, 1, (early, 6, 3)),
    )


def solution(mesh):
    rows = P("group", "seq", None)
    return jax.shard_map(
        local,
        mesh=mesh,
        in_specs=(rows, rows, P("group", None, None)) + (P(),) * 10,
        out_specs=(rows, rows) + (P(),) * 10,
        check_vma=False,
    )
```

```python
import functools

import jax
import jax.numpy as jnp
from jax import lax
from jax.experimental import pallas as pl
from jax.experimental.pallas import tpu as pltpu
from jax.sharding import PartitionSpec as P

D, FF = 768, 2048
MESH = pl.DeviceIdType.MESH
ANY = pl.BlockSpec(memory_space=pl.ANY)

HEADS, HDIM, BLK = 12, 64, 256
EPS = 1e-06
LOG2E = 1.4426950408889634
LN2 = 0.6931471805599453
SCORE = HDIM ** -0.5
f32, bf16 = jnp.float32, jnp.bfloat16
UNROLL = 8
UNROLL_BACK = 4
NN = (((1,), (0,)), ((), ()))
NT = (((1,), (1,)), ((), ()))
TN = (((0,), (0,)), ((), ()))


def mm(a, b, dims=NN):
    return lax.dot_general(a, b, dims, preferred_element_type=f32)


def split3(v):
    hi = v.astype(bf16).astype(f32)
    rest = v - hi
    mid = rest.astype(bf16).astype(f32)
    return hi, mid, rest - mid


def place_of(block, count):
    return jnp.where(block < count, block, 2 * count - 1 - block)


def lanes_of(block, count):
    return pl.ds(pl.multiple_of(jnp.where(block < count, 0, BLK), BLK), BLK)


def first_head(device, count):
    return jnp.minimum(HEADS * device // count, HEADS - 2)


def is_mine(device, slot, place, count):
    chunk = (first_head(device, count) + slot) * count + place
    return (chunk >= HEADS * device) & (chunk < HEADS * device + HEADS)


def list_pairs(skip_ref, pairs_ref, own_ref, device, slot, count, unroll):
    spare = 2 * count

    def row(number, found):
        def column(other, found):
            pairs_ref[found] = number * 1024 + other
            return found + jnp.where(skip_ref[number, other] == 0, 1, 0)

        mine = is_mine(device, slot, place_of(number, count), count)
        own_ref[found[1]] = number
        below = lax.fori_loop(0, jnp.where(mine, number, 0), column, found[0])
        return below, found[1] + jnp.where(mine, 1, 0)

    below, own = lax.fori_loop(0, spare, row, (0, 0))
    for extra in range(unroll):
        pairs_ref[below + extra] = spare * 1024
        own_ref[own + extra] = spare
    return pl.cdiv(below, unroll), pl.cdiv(own, unroll)


def running_sum(values, count, reverse):
    t = lax.broadcasted_iota(jnp.int32, (BLK, BLK), 0)
    p = lax.broadcasted_iota(jnp.int32, (BLK, BLK), 1)
    ones = jnp.where(t >= p if reverse else t <= p, 1.0, 0.0).astype(bf16)
    halves = []
    for half in range(2):
        part = values[:, half * BLK : (half + 1) * BLK]
        halves.append(sum(mm(piece.astype(bf16), ones) for piece in split3(part)))
    edge = 0 if reverse else BLK - 1
    first, last = (jnp.broadcast_to(h[:, edge : edge + 1], (count, 128)) for h in halves)
    rows = lax.broadcasted_iota(jnp.int32, (count, 128), 0)

    def scan(total, down):
        own = total
        step = 1
        while step < count:
            moved = pltpu.roll(total, step if down else count - step, 0)
            total = total + jnp.where(rows >= step if down else rows < count - step, moved, 0.0)
            step *= 2
        return total - own

    if reverse:
        all_last = jnp.sum(last, axis=0, keepdims=True)
        offsets = scan(first, False) + all_last, scan(last, True)
    else:
        all_first = jnp.sum(first, axis=0, keepdims=True)
        offsets = scan(first, True), scan(last, False) + all_first
    return jnp.concatenate([halves[0] + offsets[0][:, :1], halves[1] + offsets[1][:, :1]], 1)


def shifted(current, before):
    lane = lax.broadcasted_iota(jnp.int32, current.shape, 1)
    return jnp.where(lane == 0, pltpu.roll(before, 1, 1), pltpu.roll(current, 1, 1))


def shifted_back(current, after):
    lane = lax.broadcasted_iota(jnp.int32, current.shape, 1)
    return jnp.where(lane == BLK - 1, pltpu.roll(after, BLK - 1, 1), pltpu.roll(current, BLK - 1, 1))


def stack_rows(top, rows, size):
    extra = size if top is None else size - top.shape[0]
    number = lax.broadcasted_iota(jnp.int32, (extra, BLK), 0)
    bottom = jnp.zeros((extra, BLK), f32)
    for i, r in enumerate(rows):
        bottom = jnp.where(number == i, r, bottom)
    return bottom if top is None else jnp.concatenate([top, bottom], 0)


def prepare_block(count, block, carried, raw_ref, logit_ref, gain_ref, cum_ref, q_ref, k_ref, kt_ref, vt_ref):
    place, lanes = place_of(block, count), lanes_of(block, count)
    q_raw, k_raw, v_raw = (raw_ref[place, i, :, lanes].astype(f32) for i in range(3))
    cum = cum_ref[pl.ds(place, 1), lanes]
    parts = split3(cum)
    one = jnp.ones_like(cum)
    query = q_raw * lax.rsqrt(jnp.mean(q_raw * q_raw, 0, keepdims=True) + EPS) * (gain_ref[:, 1:2] * (SCORE * LOG2E))
    q_ref[block] = stack_rows(query, (*parts, one, one, one), 128).astype(bf16)
    rate_k = jax.nn.sigmoid(logit_ref[place, 1:2, lanes])
    rate_v = jax.nn.sigmoid(logit_ref[place, 2:3, lanes])
    key = k_raw + rate_k * (shifted(k_raw, carried[0]) - k_raw)
    key = key * lax.rsqrt(jnp.mean(key * key, 0, keepdims=True) + EPS) * gain_ref[:, 2:3]
    value = v_raw + rate_v * (shifted(v_raw, carried[1]) - v_raw)
    k_ref[block] = stack_rows(key, (one, one, one, *(-c for c in parts)), 128).T.astype(bf16)
    kt_ref[block] = stack_rows(key, (one,), 80).astype(bf16)
    vt_ref[block] = stack_rows(value, (one, one, one), 80).astype(bf16)
    return k_raw, v_raw


def finish_block(count, block, acc_ref, cum_ref, mixed_full_ref, mixed_ref, q_ref):
    place, lanes = place_of(block, count), lanes_of(block, count)
    summed = acc_ref[block]
    norm = summed[HDIM : HDIM + 1]
    mixed = summed[:HDIM] * (1.0 / norm)
    mixed_full_ref[block] = mixed
    mixed_ref[place, :, lanes] = mixed.astype(bf16)
    parts = split3(cum_ref[pl.ds(place, 1), lanes] - jnp.log2(norm))
    one = jnp.ones_like(norm)
    q_ref[block, HDIM : HDIM + 16, :] = stack_rows(None, (*parts, one, one, one), 16).astype(bf16)


def log_forget_sums(logits, count):
    log_forget = jnp.minimum(logits, 0.0) - jnp.log1p(jnp.exp(-jnp.abs(logits)))
    return running_sum(log_forget, count, False) * LOG2E


def causal():
    return lax.broadcasted_iota(jnp.int32, (BLK, BLK), 0) <= lax.broadcasted_iota(jnp.int32, (BLK, BLK), 1)


def forward_kernel(count, device_ref, skip_ref, bias_ref, raw_ref, logit_ref, gain_ref,
                   mixed_ref, mixed_full_ref, q_ref, k_ref, kt_ref, vt_ref,
                   cum_ref, acc_ref, pairs_ref, own_ref):
    slot = pl.program_id(0)
    device = device_ref[0]
    blocks = 2 * count
    pair_steps, own_steps = list_pairs(skip_ref, pairs_ref, own_ref, device, slot, count, UNROLL)
    cum_ref[...] = log_forget_sums(logit_ref[:, 0, :] + bias_ref[slot], count)

    def prepare(block, carried):
        return prepare_block(count, block, carried, raw_ref, logit_ref, gain_ref, cum_ref, q_ref, k_ref, kt_ref, vt_ref)

    zero = jnp.zeros((HDIM, BLK), f32)
    lax.fori_loop(0, blocks, prepare, (zero, zero))
    q_ref[blocks] = jnp.zeros(q_ref.shape[1:], bf16)

    def together(pairs, diagonal):
        scores = [mm(k_ref[column], q_ref[row]) for row, column in pairs]
        weights = [jnp.exp2(score) for score in scores]
        if diagonal:
            weights = [jnp.where(causal(), weight, 0.0) for weight in weights]
        weights = [weight.astype(bf16) for weight in weights]
        parts = [mm(vt_ref[column], weight) for (row, column), weight in zip(pairs, weights)]
        for (row, column), part in zip(pairs, parts):
            acc_ref[row] = part if diagonal else acc_ref[row] + part

    def own_rows(step, carried):
        rows = [own_ref[step * UNROLL + i] for i in range(UNROLL)]
        together([(row, jnp.minimum(row, blocks - 1)) for row in rows], True)
        return carried

    def kept_pairs(step, carried):
        codes = [pairs_ref[step * UNROLL + i] for i in range(UNROLL)]
        together([(code >> 10, code & 1023) for code in codes], False)
        return carried

    lax.fori_loop(0, own_steps, own_rows, 0)
    lax.fori_loop(0, pair_steps, kept_pairs, 0)

    def finish(block, carried):
        finish_block(count, block, acc_ref, cum_ref, mixed_full_ref, mixed_ref, q_ref)
        return carried

    lax.fori_loop(0, blocks, finish, 0)


def own_places(device, slot, count):
    start = (first_head(device, count) + slot) * count
    low = jnp.clip(HEADS * device - start, 0, count)
    return low, jnp.clip(HEADS * device + HEADS - start, low, count)


def slot_at(device, phase, count):
    low, high = own_places(device, 0, count)
    later, end = own_places(device, 1, count)
    swap = jnp.where(end - later > high - low, 1, 0)
    return phase + swap - 2 * phase * swap


def pairs_of_place(place, batch, size, count):
    found = []
    for i in range(size):
        number = batch * size + i
        lower = number < place
        found.append((jnp.where(lower, place, 2 * count - 1 - place), jnp.where(lower, number, number - place)))
    return found


def keep_factor(skip_ref, row, column):
    return jnp.where(skip_ref[row, column] == 0, 1.0, 0.0)


def buffers(count):
    return pl.Buffered(1 if count > 8 else 2)


def attend_forward(device, skip, bias, raw, logits, gains):
    count = raw.shape[0]
    blocks = 2 * count
    most = blocks * (blocks - 1) // 2 + UNROLL
    mode = buffers(count)
    by_slot = lambda *shape: pl.BlockSpec((None,) + shape, lambda s, *_: (s,) + (0,) * len(shape), pipeline_mode=mode)
    out = lambda shape, dtype: jax.ShapeDtypeStruct((2,) + shape, dtype)
    return pl.pallas_call(
        functools.partial(forward_kernel, count),
        grid_spec=pltpu.PrefetchScalarGridSpec(
            num_scalar_prefetch=3,
            grid=(2,),
            in_specs=[
                pl.BlockSpec((count, 3, None, HDIM, 2 * BLK), lambda s, *_: (0, 0, s, 0, 0), pipeline_mode=mode),
                pl.BlockSpec((count, None, 8, 2 * BLK), lambda s, *_: (0, s, 0, 0), pipeline_mode=mode),
                by_slot(HDIM, 8),
            ],
            out_specs=[
                by_slot(count, HDIM, 2 * BLK),
                by_slot(blocks, HDIM, BLK),
                by_slot(blocks + 1, 128, BLK),
                by_slot(blocks, BLK, 128),
                by_slot(blocks, 80, BLK),
                by_slot(blocks, 80, BLK),
            ],
            scratch_shapes=[
                pltpu.VMEM((count, 2 * BLK), f32),
                pltpu.VMEM((blocks + 1, 80, BLK), f32),
                pltpu.SMEM((most,), jnp.int32),
                pltpu.SMEM((blocks + UNROLL,), jnp.int32),
            ],
        ),
        out_shape=[
            out((count, HDIM, 2 * BLK), bf16),
            out((blocks, HDIM, BLK), f32),
            out((blocks + 1, 128, BLK), bf16),
            out((blocks, BLK, 128), bf16),
            out((blocks, 80, BLK), bf16),
            out((blocks, 80, BLK), bf16),
        ],
        compiler_params=pltpu.CompilerParams(vmem_limit_bytes=60 * 2**20),
        name="attend_forward",
    )(device, skip, bias, raw, logits, gains)


def norm_back(v, gain, u):
    scale = lax.rsqrt(jnp.mean(v * v, 0, keepdims=True) + EPS)
    hat = v * scale
    gu = gain * u
    return scale * (gu - hat * jnp.mean(hat * gu, 0, keepdims=True)), hat * u


def prepare_back(count, block, dmixed_ref, mixed_ref, vt_ref, do_ref, v_ref, dq_ref, dk_ref, dv_ref):
    place, lanes = place_of(block, count), lanes_of(block, count)
    d_out = dmixed_ref[place, :, lanes].astype(f32)
    delta = jnp.sum(d_out * mixed_ref[block], 0, keepdims=True)
    do_ref[block] = stack_rows(d_out, [-d for d in split3(delta)], 128).astype(bf16)
    wide = jnp.zeros((128 - 80, BLK), f32)
    v_ref[block] = jnp.concatenate([vt_ref[block].astype(f32), wide], 0).T.astype(bf16)
    dq_ref[block] = jnp.zeros(dq_ref.shape[1:], f32)
    dk_ref[block] = jnp.zeros(dk_ref.shape[1:], f32)
    dv_ref[block] = jnp.zeros(dv_ref.shape[1:], f32)


def batch_back(pairs, masks, q_ref, k_ref, kt_ref, v_ref, do_ref, dq_ref, dk_ref, dv_ref):
    weights = [jnp.exp2(mm(k_ref[column], q_ref[row])) for row, column in pairs]
    for i, mask in enumerate(masks):
        if mask is True:
            weights[i] = jnp.where(causal(), weights[i], 0.0)
        elif mask is not None:
            weights[i] = weights[i] * mask
    d_weights = [mm(v_ref[column], do_ref[row]) for row, column in pairs]
    low_weights = [weight.astype(bf16) for weight in weights]
    d_scores = [(weight * d_weight).astype(bf16) for weight, d_weight in zip(weights, d_weights)]
    parts = [mm(do_ref[row, :HDIM], weight, NT) for (row, _), weight in zip(pairs, low_weights)]
    for (_, column), part in zip(pairs, parts):
        dv_ref[column] += part
    parts = [mm(kt_ref[column], d_score) for (_, column), d_score in zip(pairs, d_scores)]
    for (row, _), part in zip(pairs, parts):
        dq_ref[row] += part
    parts = [mm(q_ref[row, :80], d_score, NT) for (row, _), d_score in zip(pairs, d_scores)]
    for (_, column), part in zip(pairs, parts):
        dk_ref[column] += part


def finish_back(count, block, carried, mine, raw_ref, logit_ref, gain_ref, dq_ref, dk_ref, dv_ref, draw_ref, dlogit_ref, cum_ref):
    next_k, next_v, sum_q, sum_k = carried
    place, lanes = place_of(block, count), lanes_of(block, count)
    earlier = jnp.maximum(block - 1, 0)
    place_before, lanes_before = place_of(earlier, count), lanes_of(earlier, count)
    exists = jnp.where(block > 0, 1.0, 0.0)
    q_raw, k_raw, v_raw = (raw_ref[place, i, :, lanes].astype(f32) for i in range(3))
    k_step = shifted(k_raw, raw_ref[place_before, 1, :, lanes_before].astype(f32) * exists) - k_raw
    v_step = shifted(v_raw, raw_ref[place_before, 2, :, lanes_before].astype(f32) * exists) - v_raw
    rate_k = jax.nn.sigmoid(logit_ref[place, 1:2, lanes])
    rate_v = jax.nn.sigmoid(logit_ref[place, 2:3, lanes])
    dq, dk, dv = dq_ref[block], dk_ref[block], dv_ref[block]
    dq_raw, part_q = norm_back(q_raw, gain_ref[:, 1:2], dq[:HDIM] * SCORE)
    dk_mixed, part_k = norm_back(k_raw + rate_k * k_step, gain_ref[:, 2:3], dk[:HDIM] * LN2)
    send_k, send_v = rate_k * dk_mixed, rate_v * dv
    draw_ref[place, 0, :, lanes] = dq_raw.astype(bf16)
    draw_ref[place, 1, :, lanes] = (dk_mixed - send_k + shifted_back(send_k, next_k)).astype(bf16)
    draw_ref[place, 2, :, lanes] = (dv - send_v + shifted_back(send_v, next_v)).astype(bf16)
    dlogit_ref[place, 1:2, lanes] = (1.0 - rate_k) * jnp.sum(k_step * send_k, 0, keepdims=True)
    dlogit_ref[place, 2:3, lanes] = (1.0 - rate_v) * jnp.sum(v_step * send_v, 0, keepdims=True)
    cum_ref[pl.ds(place, 1), lanes] = dq[HDIM : HDIM + 1] - dk[HDIM + 3 : HDIM + 4]
    return send_k, send_v, sum_q + jnp.where(mine, part_q, 0.0), sum_k + part_k


def forget_back(count, bias, logit_ref, cum_ref, dlogit_ref):
    d_log = running_sum(cum_ref[...], count, True)
    dlogit_ref[:, 0, :] = d_log * jax.nn.sigmoid(-(logit_ref[:, 0, :] + bias))
    dlogit_ref[:, 3:, :] = jnp.zeros((count, 5, 2 * BLK), f32)


def backward_kernel(count, device_ref, skip_ref, bias_ref, raw_ref, logit_ref, gain_ref, dmixed_ref, mixed_ref,
                    q_ref, k_ref, kt_ref, vt_ref, draw_ref, dlogit_ref, dgain_ref,
                    do_ref, v_ref, cum_ref, dq_ref, dk_ref, dv_ref, pairs_ref, own_ref):
    slot = pl.program_id(0)
    device = device_ref[0]
    blocks = 2 * count
    pair_steps, own_steps = list_pairs(skip_ref, pairs_ref, own_ref, device, slot, count, UNROLL_BACK)
    sums = (dq_ref, dk_ref, dv_ref)

    def prepare(block, carried):
        prepare_back(count, block, dmixed_ref, mixed_ref, vt_ref, do_ref, v_ref, *sums)
        return carried

    lax.fori_loop(0, blocks, prepare, 0)
    do_ref[blocks] = jnp.zeros(do_ref.shape[1:], bf16)
    dq_ref[blocks] = jnp.zeros(dq_ref.shape[1:], f32)

    def own_rows(step, carried):
        rows = [own_ref[step * UNROLL_BACK + i] for i in range(UNROLL_BACK)]
        pairs = [(row, jnp.minimum(row, blocks - 1)) for row in rows]
        batch_back(pairs, [True] * UNROLL_BACK, q_ref, k_ref, kt_ref, v_ref, do_ref, *sums)
        return carried

    def kept_pairs(step, carried):
        codes = [pairs_ref[step * UNROLL_BACK + i] for i in range(UNROLL_BACK)]
        pairs = [(code >> 10, code & 1023) for code in codes]
        batch_back(pairs, [None] * UNROLL_BACK, q_ref, k_ref, kt_ref, v_ref, do_ref, *sums)
        return carried

    lax.fori_loop(0, own_steps, own_rows, 0)
    lax.fori_loop(0, pair_steps, kept_pairs, 0)

    def finish(step, carried):
        block = blocks - 1 - step
        mine = is_mine(device, slot, place_of(block, count), count)
        return finish_back(count, block, carried, mine, raw_ref, logit_ref, gain_ref, *sums, draw_ref, dlogit_ref, cum_ref)

    zero = jnp.zeros((HDIM, BLK), f32)
    _, _, sum_q, sum_k = lax.fori_loop(0, blocks, finish, (zero, zero, zero, zero))
    dgain_ref[:, 1:2] = jnp.sum(sum_q, 1, keepdims=True)
    dgain_ref[:, 2:3] = jnp.sum(sum_k, 1, keepdims=True)
    forget_back(count, bias_ref[slot], logit_ref, cum_ref, dlogit_ref)


def attend_backward(device, skip, bias, raw, logits, gains, dmixed, mixed, q, k, kt, vt):
    count = raw.shape[0]
    blocks = 2 * count
    most = blocks * (blocks - 1) // 2 + UNROLL_BACK
    mode = buffers(count)
    by_slot = lambda *shape: pl.BlockSpec((None,) + shape, lambda s, *_: (s,) + (0,) * len(shape), pipeline_mode=mode)
    raw_spec = pl.BlockSpec((count, 3, None, HDIM, 2 * BLK), lambda s, *_: (0, 0, s, 0, 0), pipeline_mode=mode)
    place_spec = lambda rows: pl.BlockSpec((count, None, rows, 2 * BLK), lambda s, *_: (0, s, 0, 0), pipeline_mode=mode)
    return pl.pallas_call(
        functools.partial(backward_kernel, count),
        grid_spec=pltpu.PrefetchScalarGridSpec(
            num_scalar_prefetch=3,
            grid=(2,),
            in_specs=[
                raw_spec,
                place_spec(8),
                by_slot(HDIM, 8),
                place_spec(HDIM),
                by_slot(blocks, HDIM, BLK),
                by_slot(blocks + 1, 128, BLK),
                by_slot(blocks, BLK, 128),
                by_slot(blocks, 80, BLK),
                by_slot(blocks, 80, BLK),
            ],
            out_specs=[raw_spec, place_spec(8), by_slot(HDIM, 8)],
            scratch_shapes=[
                pltpu.VMEM((blocks + 1, 128, BLK), bf16),
                pltpu.VMEM((blocks, BLK, 128), bf16),
                pltpu.VMEM((count, 2 * BLK), f32),
                pltpu.VMEM((blocks + 1, 80, BLK), f32),
                pltpu.VMEM((blocks, 80, BLK), f32),
                pltpu.VMEM((blocks, HDIM, BLK), f32),
                pltpu.SMEM((most,), jnp.int32),
                pltpu.SMEM((blocks + UNROLL_BACK,), jnp.int32),
            ],
        ),
        out_shape=[
            jax.ShapeDtypeStruct(raw.shape, bf16),
            jax.ShapeDtypeStruct(logits.shape, f32),
            jax.ShapeDtypeStruct(gains.shape, f32),
        ],
        compiler_params=pltpu.CompilerParams(vmem_limit_bytes=60 * 2**20),
        name="attend_backward",
    )(device, skip, bias, raw, logits, gains, dmixed, mixed, q, k, kt, vt)


def holder(head, place, count):
    return (head * count + place) // HEADS


def greet(count):
    me = lax.axis_index("seq")
    barrier = pltpu.get_barrier_semaphore()
    for k in range(1, count):
        peer = lax.rem(me + k, count)
        pl.semaphore_signal(barrier, inc=1, device_id={"seq": peer}, device_id_type=MESH)
    pl.semaphore_wait(barrier, count - 1)
    return me


def far_first(count):
    return sorted(range(1, count), key=lambda k: -min(k, count - k))


def push(src, dst, send, recv, peer):
    return pltpu.make_async_remote_copy(
        src_ref=src, dst_ref=dst, send_sem=send, recv_sem=recv, device_id={"seq": peer}, device_id_type=MESH
    )


def heads_out_kernel(count, x_ref, logit_in, raw_ref, logit_ref, send, recv, local):
    me = greet(count)

    def copies(peer, source, k):
        head = first_head(peer, count)
        items = []
        for slot in range(2):
            items.append((is_mine(peer, slot, me, count), is_mine(me, slot, source, count),
                          push(x_ref.at[0, head + slot], raw_ref.at[me, 0, slot], send.at[k, slot], recv.at[k, slot], peer)))
        items.append((None, None, push(x_ref.at[pl.ds(1, 2), pl.ds(head, 2)], raw_ref.at[me, pl.ds(1, 2)], send.at[k, 2], recv.at[k, 2], peer)))
        items.append((None, None, push(logit_in.at[pl.ds(head, 2)], logit_ref.at[me], send.at[k, 3], recv.at[k, 3], peer)))
        return items

    every = []
    for k in far_first(count):
        items = copies(lax.rem(me + k, count), lax.rem(me + count - k, count), k)
        every.append(items)
        for out, _, copy in items:
            if out is None:
                copy.start()
            else:
                pl.when(out)(copy.start)
    head = first_head(me, count)
    own = [
        pltpu.make_async_copy(x_ref.at[:, pl.ds(head, 2)], raw_ref.at[me], local.at[0]),
        pltpu.make_async_copy(logit_in.at[pl.ds(head, 2)], logit_ref.at[me], local.at[1]),
    ]
    for copy in own:
        copy.start()
    for items in every:
        for out, into, copy in items:
            if out is None:
                copy.wait()
            else:
                pl.when(out)(copy.wait_send)
                pl.when(into)(copy.wait_recv)
    for copy in own:
        copy.wait()


def heads_out(qkv, logits, count):
    return pl.pallas_call(
        functools.partial(heads_out_kernel, count),
        out_shape=[
            jax.ShapeDtypeStruct((count, 3, 2, HDIM, 2 * BLK), bf16),
            jax.ShapeDtypeStruct((count, 2, 8, 2 * BLK), f32),
        ],
        in_specs=[ANY, ANY],
        out_specs=[ANY, ANY],
        scratch_shapes=[pltpu.SemaphoreType.DMA((count, 4)), pltpu.SemaphoreType.DMA((count, 4)), pltpu.SemaphoreType.DMA((2,))],
        compiler_params=pltpu.CompilerParams(collective_id=0, has_side_effects=True),
        name="heads_out",
    )(qkv, logits)


def mixed_back_kernel(count, x_ref, o_ref, send, recv, local):
    me = greet(count)
    first = first_head(me, count)
    started = []
    for k in far_first(count) + [0]:
        peer = lax.rem(me + k, count)
        for slot in range(2):
            mine = is_mine(me, slot, peer, count)
            src, dst = x_ref.at[slot, peer], o_ref.at[first + slot]
            if k:
                copy = push(src, dst, send.at[k, slot], recv.at[first + slot], peer)
            else:
                copy = pltpu.make_async_copy(src, dst, local.at[slot])
            started.append((mine, k, copy))
            pl.when(mine)(copy.start)
    for mine, k, copy in started:
        pl.when(mine)(copy.wait_send if k else copy.wait)
    for head in range(HEADS):
        source = holder(head, me, count)
        copy = push(x_ref.at[0, 0], o_ref.at[head], send.at[0, 0], recv.at[head], lax.rem(me + 1, count))
        pl.when(source != me)(copy.wait_recv)


def mixed_back(mixed, count):
    return pl.pallas_call(
        functools.partial(mixed_back_kernel, count),
        out_shape=jax.ShapeDtypeStruct((HEADS, HDIM, 2 * BLK), bf16),
        in_specs=[ANY],
        out_specs=ANY,
        scratch_shapes=[pltpu.SemaphoreType.DMA((count, 2)), pltpu.SemaphoreType.DMA((HEADS,)), pltpu.SemaphoreType.DMA((2,))],
        compiler_params=pltpu.CompilerParams(collective_id=1, has_side_effects=True),
        name="mixed_back",
    )(mixed)


def grads_out_kernel(count, x_ref, h1_ref, dgate_ref, h2_ref, dgu_ref, hidden_ref, dlow_ref, gated_ref, branch_ref,
                     o_ref, grads_ref, send, recv, local):
    me = greet(count)
    started = []
    for head in range(HEADS):
        peer = holder(head, me, count)
        slot = head - first_head(peer, count)
        away = peer != me
        there = jnp.where(away, peer, lax.rem(me + 1, count))
        copy = push(x_ref.at[head], o_ref.at[me, slot], send.at[head], recv.at[me, slot], there)
        own = pltpu.make_async_copy(x_ref.at[head], o_ref.at[me, slot], local.at[slot])
        pl.when(away)(copy.start)
        pl.when(peer == me)(own.start)
        started.append((away, peer == me, copy, own))

    def put(unit, part):
        grads_ref[pl.ds(unit, 16)] = part.astype(bf16).reshape(16, UNIT, 256)

    def gate_up(i, carried):
        right = dgu_ref[:, pl.ds(pl.multiple_of(i * 256, 256), 256)]
        for j in range(3):
            put(i * 48 + 16 * j, mm(h2_ref[:, 256 * j : 256 * j + 256], right, TN))
        return carried

    lax.fori_loop(0, 2 * FF // 256, gate_up, 0)

    def down(i, carried):
        left = hidden_ref[:, pl.ds(pl.multiple_of(i * 256, 256), 256)]
        for j in range(3):
            put(768 + 128 * j + 16 * i, mm(left, dlow_ref[:, 256 * j : 256 * j + 256], TN))
        return carried

    lax.fori_loop(0, FF // 256, down, 0)
    for i in range(3):
        for j in range(3):
            put(1152 + 48 * i + 16 * j, mm(gated_ref[256 * j : 256 * j + 256, :], branch_ref[:, 256 * i : 256 * i + 256]))
            put(1296 + 48 * i + 16 * j, lax.dot_general(
                h1_ref[:, 256 * j : 256 * j + 256], dgate_ref[256 * i : 256 * i + 256, :],
                (((0,), (1,)), ((), ())), preferred_element_type=f32))
    units = grads_ref.shape[0]
    if units > 1440:
        grads_ref[1440:] = jnp.zeros((units - 1440, UNIT, 256), bf16)

    for away, here, copy, own in started:
        pl.when(away)(copy.wait_send)
        pl.when(here)(own.wait)
    for k in range(1, count):
        source = lax.rem(me + k, count)
        for slot in range(2):
            copy = push(x_ref.at[0], o_ref.at[source, slot], send.at[0], recv.at[source, slot], source)
            pl.when(is_mine(me, slot, source, count))(copy.wait_recv)


def grads_out(count, units, d_mixed, *operands):
    vmem = pl.BlockSpec(memory_space=pltpu.VMEM)
    return pl.pallas_call(
        functools.partial(grads_out_kernel, count),
        out_shape=[
            jax.ShapeDtypeStruct((count, 2, HDIM, 2 * BLK), bf16),
            jax.ShapeDtypeStruct((units, UNIT, 256), bf16),
        ],
        in_specs=[ANY] + [vmem] * 8,
        out_specs=[ANY, vmem],
        scratch_shapes=[pltpu.SemaphoreType.DMA((HEADS,)), pltpu.SemaphoreType.DMA((count, 2)), pltpu.SemaphoreType.DMA((2,))],
        compiler_params=pltpu.CompilerParams(collective_id=2, has_side_effects=True, vmem_limit_bytes=60 * 2**20),
        name="grads_out",
    )(d_mixed, *operands)


def dot(a, b, i, j):
    return lax.dot_general(a, b, (((i,), (j,)), ((), ())), preferred_element_type=f32)


def front_kernel(count, skip_ref, bias_ref, x_ref, w_ref, wsmall_ref, gain_ref,
                 h_ref, gate_ref, att_ref, raw_out, logit_out, full_out, q_out, k_out, kt_out, vt_out,
                 ht_ref, proj_ref, small_ref, raw_ref, logit_ref, mixed_ref, full_ref, q_ref, k_ref, kt_ref, vt_ref, cum_ref, acc_ref, gains_ref,
                 send, recv, own, back_send, back_recv, back_own, keep):
    me = lax.axis_index("seq")
    barrier = pltpu.get_barrier_semaphore()
    for k in range(1, count):
        pl.semaphore_signal(barrier, inc=1, device_id={"seq": lax.rem(me + k, count)}, device_id_type=MESH)
    blocks = 2 * count
    rows = x_ref.shape[0]
    for i in range(rows // 128):
        here = slice(128 * i, 128 * i + 128)
        v = x_ref[here].astype(f32)
        normed = v * lax.rsqrt(jnp.mean(v * v, 1, keepdims=True) + EPS) * gain_ref[0:1]
        h_ref[here] = normed.astype(bf16)
        ht_ref[:, here] = normed.T.astype(bf16)

    def project(i, carried):
        block = mm(w_ref[:, pl.ds(pl.multiple_of(256 * i, 256), 256)], ht_ref[...], TN)
        proj_ref[pl.ds(4 * i, 4)] = block.astype(bf16).reshape(4, HDIM, rows)
        return carried

    gains_ref[...] = gain_ref[...].T
    small = mm(wsmall_ref[...], ht_ref[...], TN)
    for head in range(HEADS):
        ordered = [small[HEADS * i + head : HEADS * i + head + 1] for i in range(3)]
        small_ref[head] = jnp.concatenate(ordered + [jnp.zeros((5, rows), f32)], 0)
    lax.fori_loop(0, 9, project, 0)
    pl.semaphore_wait(barrier, count - 1)
    first = first_head(me, count)

    def out(slot, k, peer):
        head = first_head(peer, count) + slot
        sems = lambda i: (send.at[k, slot, i], recv.at[k, slot, i], peer)
        return [
            push(proj_ref.at[head], raw_ref.at[me, 0, slot], *sems(0)),
            push(proj_ref.at[HEADS + head], raw_ref.at[me, 1, slot], *sems(1)),
            push(proj_ref.at[2 * HEADS + head], raw_ref.at[me, 2, slot], *sems(2)),
            push(small_ref.at[head], logit_ref.at[me, slot], *sems(3)),
        ]

    def own_copies(slot):
        head = first + slot
        return [
            pltpu.make_async_copy(proj_ref.at[head], raw_ref.at[me, 0, slot], own.at[slot, 0]),
            pltpu.make_async_copy(proj_ref.at[HEADS + head], raw_ref.at[me, 1, slot], own.at[slot, 1]),
            pltpu.make_async_copy(proj_ref.at[2 * HEADS + head], raw_ref.at[me, 2, slot], own.at[slot, 2]),
            pltpu.make_async_copy(small_ref.at[head], logit_ref.at[me, slot], own.at[slot, 3]),
        ]

    for phase in range(2):
        for k in far_first(count):
            peer = lax.rem(me + k, count)
            slot = slot_at(peer, phase, count)
            copies = out(slot, k, peer)
            pl.when(is_mine(peer, slot, me, count))(copies[0].start)
            for copy in copies[1:]:
                copy.start()
        for copy in own_copies(slot_at(me, phase, count)):
            copy.start()

    def gate(i, carried):
        here = pl.ds(pl.multiple_of(256 * i, 256), 256)
        gate_ref[here] = mm(w_ref[:, pl.ds(pl.multiple_of(3 * D + 256 * i, 256), 256)], ht_ref[...], TN)
        return carried

    lax.fori_loop(0, 3, gate, 0)

    def saved(slot):
        return [
            pltpu.make_async_copy(src.at[slot], dst.at[slot], keep.at[slot, i])
            for i, (src, dst) in enumerate(
                ((full_ref, full_out), (q_ref, q_out), (k_ref, k_out), (kt_ref, kt_out), (vt_ref, vt_out)))
        ]

    def back(slot, k, peer):
        target = att_ref.at[pl.ds(pl.multiple_of((first + slot) * HDIM, HDIM), HDIM)]
        if k:
            return push(mixed_ref.at[slot, peer], target, back_send.at[k, slot], back_recv.at[first + slot], peer)
        return pltpu.make_async_copy(mixed_ref.at[slot, peer], target, back_own.at[slot])

    def one_slot(phase, carried):
        slot = slot_at(me, phase, count)
        for copy in own_copies(slot):
            copy.wait()
        for k in far_first(count):
            source = lax.rem(me + count - k, count)
            copies = out(slot, k, source)
            pl.when(is_mine(me, slot, source, count))(copies[0].wait_recv)
            for copy in copies[1:]:
                copy.wait_recv()
        head = first + slot
        raws, logits = raw_ref.at[:, :, slot], logit_ref.at[:, slot]
        gains = gains_ref.at[pl.ds(pl.multiple_of(head * HDIM, HDIM), HDIM)]
        qs, ks, kts, vts = q_ref.at[slot], k_ref.at[slot], kt_ref.at[slot], vt_ref.at[slot]
        cum_ref[...] = log_forget_sums(logits[:, 0, :] + bias_ref[head], count)

        def prepare(block, state):
            acc_ref[block] = jnp.zeros(acc_ref.shape[1:], f32)
            return prepare_block(count, block, state, raws, logits, gains, cum_ref, qs, ks, kts, vts)

        zero = jnp.zeros((HDIM, BLK), f32)
        lax.fori_loop(0, blocks, prepare, (zero, zero))
        qs[blocks] = jnp.zeros(q_ref.shape[2:], bf16)

        def batch(pairs, on_diagonal):
            weights = [jnp.exp2(mm(ks[column], qs[row])) for row, column in pairs]
            low = []
            for (row, column), weight, diagonal in zip(pairs, weights, on_diagonal):
                weight = jnp.where(causal(), weight, 0.0) if diagonal else weight * keep_factor(skip_ref, row, column)
                low.append(weight.astype(bf16))
            parts = [mm(vts[column], weight) for (_, column), weight in zip(pairs, low)]
            for (row, _), part in zip(pairs, parts):
                acc_ref[row] += part

        def one_place(place, state):
            number = blocks // UNROLL
            for i in range(number):
                pairs = pairs_of_place(place, i, UNROLL, count)
                diagonal = [False] * UNROLL
                if i == number - 1:
                    pairs.append((place, place))
                    diagonal[-1:] = [True, True]
                batch(pairs, diagonal)
            return state

        low, high = own_places(me, slot, count)
        lax.fori_loop(low, high, one_place, 0)

        def finish(block, state):
            finish_block(count, block, acc_ref, cum_ref, full_ref.at[slot], mixed_ref.at[slot], qs)
            return state

        lax.fori_loop(0, blocks, finish, 0)
        for k in far_first(count) + [0]:
            peer = lax.rem(me + k, count)
            pl.when(is_mine(me, slot, peer, count))(back(slot, k, peer).start)
        for copy in saved(slot):
            copy.start()
        return carried

    lax.fori_loop(0, 2, one_slot, 0)
    keep_raw = [
        pltpu.make_async_copy(raw_ref, raw_out, keep.at[0, 5]),
        pltpu.make_async_copy(logit_ref, logit_out, keep.at[1, 5]),
    ]
    for copy in keep_raw:
        copy.start()
    for slot in range(2):
        for k in far_first(count):
            peer = lax.rem(me + k, count)
            copies = out(slot, k, peer)
            pl.when(is_mine(peer, slot, me, count))(copies[0].wait_send)
            for copy in copies[1:]:
                copy.wait_send()
        for k in far_first(count) + [0]:
            peer = lax.rem(me + k, count)
            copy = back(slot, k, peer)
            pl.when(is_mine(me, slot, peer, count))(copy.wait_send if k else copy.wait)
    for head in range(HEADS):
        source = holder(head, me, count)
        copy = push(mixed_ref.at[0, 0], att_ref.at[pl.ds(head * HDIM, HDIM)], back_send.at[0, 0], back_recv.at[head], lax.rem(me + 1, count))
        pl.when(source != me)(copy.wait_recv)
    for slot in range(2):
        for copy in saved(slot):
            copy.wait()
    for copy in keep_raw:
        copy.wait()


def front(count, skip, bias, x, w_attn, w_small, gains):
    rows = x.shape[0]
    blocks = 2 * count
    vmem = pl.BlockSpec(memory_space=pltpu.VMEM)
    smem = pl.BlockSpec(memory_space=pltpu.SMEM)
    dma = pltpu.SemaphoreType.DMA
    raw, logit = (count, 3, 2, HDIM, rows), (count, 2, 8, rows)
    state = [((2, blocks, HDIM, BLK), f32), ((2, blocks + 1, 128, BLK), bf16), ((2, blocks, BLK, 128), bf16),
             ((2, blocks, 80, BLK), bf16), ((2, blocks, 80, BLK), bf16)]
    return pl.pallas_call(
        functools.partial(front_kernel, count),
        out_shape=[jax.ShapeDtypeStruct(s, t) for s, t in [
            ((rows, D), bf16), ((D, rows), f32), ((D, rows), bf16), (raw, bf16), (logit, f32)] + state],
        in_specs=[smem, smem] + [vmem] * 4,
        out_specs=[vmem] * 3 + [ANY] * 7,
        scratch_shapes=[
            pltpu.VMEM((D, rows), bf16),
            pltpu.VMEM((3 * HEADS, HDIM, rows), bf16),
            pltpu.VMEM((HEADS, 8, rows), f32),
            pltpu.VMEM(raw, bf16),
            pltpu.VMEM(logit, f32),
            pltpu.VMEM((2, count, HDIM, rows), bf16),
        ] + [pltpu.VMEM(s, t) for s, t in state] + [
            pltpu.VMEM((count, rows), f32),
            pltpu.VMEM((blocks + 1, 80, BLK), f32),
            pltpu.VMEM((D, 8), f32),
            dma((count, 2, 4)), dma((count, 2, 4)), dma((2, 4)),
            dma((count, 2)), dma((HEADS,)), dma((2,)), dma((2, 6)),
        ],
        compiler_params=pltpu.CompilerParams(collective_id=0, has_side_effects=True, vmem_limit_bytes=60 * 2**20),
        name="front",
    )(skip, bias, x, w_attn, w_small, gains)


SMALL = 48
UNIT = 16
PIECE = 8


def group_bits(group_count, count):
    bits = [("group", 1 << i) for i in range(group_count.bit_length() - 1)]
    return bits, [("seq", 1 << i) for i in range(count.bit_length() - 1)]


def partner(bit):
    axis, step = bit
    here = lax.axis_index(axis)
    side = lax.rem(here // step, 2)
    return {axis: here + step - 2 * step * side}, side


def greet_all(bits, count):
    me = lax.axis_index("seq")
    others = [partner(bit)[0] for bit in bits if bit[0] != "seq"]
    others += [{"seq": lax.rem(me + k, count)} for k in range(1, count)]
    barrier = pltpu.get_barrier_semaphore()
    for there in others:
        pl.semaphore_signal(barrier, inc=1, device_id=there, device_id_type=MESH)
    pl.semaphore_wait(barrier, len(others))
    return me


def orders(near, far, seq, busy):
    x, z, rest = seq[0], seq[1], seq[2:]
    kinds = [
        [near, far, x, z] + rest,
        [near, x, far, z] + rest,
        [near, z, x, far] + rest,
        [near, z, far, x] + rest,
    ]
    return [kinds[i] for i in (EARLY_KINDS if busy else (0, 1, 2, 0, 1, 3))]


EARLY_KINDS = (0, 1, 3, 0, 1, 2)
PARTS = 6


class Summing:
    def __init__(self, base, size, order, source, own, landing, result, send, recv, local):
        self.start, self.size, self.order, self.source, self.local = base, size, order, source, local
        self.own, self.landing, self.result, self.send, self.recv = own, landing, result, send, recv
        self.base, self.at, self.stage, self.copy, self.load = base, base, 0, None, None
        self.off = 0

    def give(self):
        there, side = partner(self.order[self.stage])
        half = self.size // 2
        self.keep = self.start + side * half
        held = self.own
        if self.stage == 0 and self.source is not None:
            held = self.source
            self.load = pltpu.make_async_copy(
                self.source.at[pl.ds(self.keep, half)], self.own.at[pl.ds(self.base // 2, half)], self.local
            )
            self.load.start()
        self.copy = pltpu.make_async_remote_copy(
            src_ref=held.at[pl.ds(self.start + (1 - side) * half - self.off, half)],
            dst_ref=self.landing.at[pl.ds(self.at, half)],
            send_sem=self.send.at[self.stage], recv_sem=self.recv.at[self.stage],
            device_id=there, device_id_type=MESH,
        )
        self.copy.start()

    def add(self):
        self.copy.wait()
        if self.load is not None:
            self.load.wait()
            self.load = None
            self.off = self.keep - self.base // 2
        half = self.size // 2
        step = PIECE if half % PIECE == 0 else 1
        keep, at, own, landing = self.keep - self.off, self.at, self.own, self.landing

        def piece(i, carried):
            mine = pl.ds(keep + i * step, step)
            own[mine] = own[mine] + landing[pl.ds(at + i * step, step)]
            return carried

        lax.fori_loop(0, half // step, piece, 0)
        self.start, self.size, self.at, self.stage = self.keep, half, at + half, self.stage + 1

    def settle(self):
        copy = pltpu.make_async_copy(
            self.own.at[pl.ds(self.start - self.off, self.size)], self.result.at[pl.ds(self.start, self.size)], self.local
        )
        copy.start()
        copy.wait()
        self.left = len(self.order)

    def spread(self):
        self.left -= 1
        there, side = partner(self.order[self.left])
        part = self.result.at[pl.ds(self.start, self.size)]
        stage = 2 * len(self.order) - 1 - self.left
        self.copy = pltpu.make_async_remote_copy(
            src_ref=part, dst_ref=part, send_sem=self.send.at[stage], recv_sem=self.recv.at[stage],
            device_id=there, device_id_type=MESH,
        )
        self.copy.start()
        self.start, self.size = self.start - side * self.size, 2 * self.size

    def gathered(self):
        self.copy.wait()


def total(parts):
    return functools.reduce(jnp.add, parts)


def held_heads(count):
    first = [min(HEADS * d // count, HEADS - 2) for d in range(count)]
    return [
        [(d, h - first[d]) for d in range(h * count // HEADS, ((h + 1) * count - 1) // HEADS + 1)]
        for h in range(HEADS)
    ]


def padded(units, least):
    return -(-units // least) * least


def sums_of(units, least, sets, source, own, landing, result, send, recv, local):
    pieces, base, sums = units // least, 0, []
    for i, order in enumerate(orders(*sets, source is not None)):
        size = least * ((pieces + PARTS - 1 - i) // PARTS)
        if not size:
            break
        sums.append(Summing(base, size, order, source, own, landing, result, send.at[i], recv.at[i], local.at[i]))
        base += size
    return sums


def step(sums, stages):
    for part in sums:
        if part.stage < stages:
            part.add()
            if part.stage < stages:
                part.give()
            else:
                part.settle()
                part.spread()
        else:
            part.gathered()
            if part.left > 0:
                part.spread()


def put_together(holders, part_ref, logit_ref, proj_ref, dsmall_ref):
    for head, held in enumerate(holders):
        for i in range(2):
            start = D * (1 + i) + head * HDIM
            if len(held) == 1:
                proj_ref[start : start + HDIM] = part_ref[head, 0, i]
            else:
                proj_ref[start : start + HDIM] = total([part_ref[head, j, i].astype(f32) for j in range(len(held))]).astype(bf16)
        dsmall_ref[8 * head : 8 * head + 8] = total([logit_ref[d, s] for d, s in held])


def late_weights(h_ref, proj_ref, g_ref, low, high):
    def block(i, carried):
        grads = proj_ref[pl.ds(pl.multiple_of(i * 256, 256), 256)]
        for j in range(3):
            part = lax.dot_general(h_ref[:, 256 * j : 256 * j + 256], grads, (((0,), (1,)), ((), ())), preferred_element_type=f32)
            g_ref[pl.ds(i * (D // UNIT) + j * 16, 16)] = part.astype(bf16).reshape(16, UNIT, 256)
        return carried

    lax.fori_loop(low, high, block, 0)


def late_rest(h_ref, proj_ref, w_ref, wsmall_ref, x_ref, gain_ref, dresid_ref, extra_ref, dsmall_ref, rows_ref, small_ref, dx_ref, g_ref, gsum_ref=None):
    ordered = [dsmall_ref[8 * head + i : 8 * head + i + 1] for i in range(3) for head in range(HEADS)]
    low_small = jnp.concatenate(ordered + [jnp.zeros((SMALL - 3 * HEADS, ordered[0].shape[1]), f32)], 0).astype(bf16)
    for i in range(3):
        cols = slice(256 * i, 256 * i + 256)
        part = mm(w_ref[cols, :], proj_ref[...]) + mm(wsmall_ref[cols, :], low_small)
        dx_ref[:, cols] = part.T
    rows_ref[...] = mm(low_small, h_ref[...])
    small_ref[...] = extra_ref[...]
    if gsum_ref is not None:
        small_ref[2:4] = gsum_ref[0:2]
    gain = gain_ref[0:1]
    dgain = jnp.zeros((1, D), f32)
    for i in range(h_ref.shape[0] // 128):
        here = slice(128 * i, 128 * i + 128)
        v, u = x_ref[here].astype(f32), dx_ref[here]
        scale = lax.rsqrt(jnp.mean(v * v, 1, keepdims=True) + EPS)
        hat, gu = v * scale, u * gain
        dx_ref[here] = dresid_ref[here] + scale * (gu - hat * jnp.mean(hat * gu, 1, keepdims=True))
        dgain = dgain + jnp.sum(hat * u, 0, keepdims=True)
    small_ref[0:1] = dgain
    bias_rows = jnp.concatenate([dsmall_ref[8 * head : 8 * head + 1] for head in range(HEADS)], 0)
    bias_sum = jnp.sum(bias_rows, 1, keepdims=True)
    lane = lax.broadcasted_iota(jnp.int32, (HEADS, 128), 1)
    row = lax.broadcasted_iota(jnp.int32, (HEADS, 128), 0)
    small_ref[4:5, 0:128] = jnp.sum(jnp.where(lane == row, bias_sum, 0.0), 0, keepdims=True)

    used = 9 * (D // UNIT)
    units = g_ref.shape[0]
    for i in range(3):
        g_ref[used + 3 * i : used + 3 * i + 3] = rows_ref[:, 256 * i : 256 * i + 256].astype(bf16).reshape(3, UNIT, 256)
    if units > used + 9:
        g_ref[used + 9 :] = jnp.zeros((units - used - 9, UNIT, 256), bf16)


class Doubling:
    def __init__(self, bits, own, landing, send, recv):
        self.bits, self.own, self.landing, self.send, self.recv = bits, own, landing, send, recv
        self.at = 0

    def give(self):
        there, _ = partner(self.bits[self.at])
        self.copy = pltpu.make_async_remote_copy(
            src_ref=self.own, dst_ref=self.landing.at[self.at], send_sem=self.send.at[self.at], recv_sem=self.recv.at[self.at],
            device_id=there, device_id_type=MESH,
        )
        self.copy.start()

    def add(self):
        self.copy.wait()
        self.own[...] += self.landing[self.at]
        self.at += 1


def finish_late(late, early, early_left, stages, small, small_out):
    for stage in range(2 * stages):
        if stage < stages:
            small.give()
        step(late, stages)
        if stage < early_left:
            step(early, stages)
        if stage < stages:
            small.add()
    small_out[...] = small.own[...]


def give_late(sums, weights, rest, early, stages):
    block, blocks, given = D // UNIT, 9, 0
    ahead = [part for part in sums if part.start + part.size <= blocks * block]
    for part in ahead:
        needed = -(-(part.start + part.size) // block)
        weights(given, needed)
        given = needed
        part.give()
    weights(given, blocks)
    rest()
    for part in sums[len(ahead):]:
        part.give()
    step(early, stages)


def last_kernel(count, sets, draw_ref, dlogit_ref, early_ref, h_ref, dgate_ref, w_ref, wsmall_ref, x_ref, gain_ref,
                dresid_ref, extra_ref, late_out, early_out, dx_ref, small_out,
                proj_ref, logit_ref, part_ref, dsmall_ref, rows_ref, small_ref, small_land, ssend, srecv, g_ref, land_ref, e_ref, eland_ref,
                send, recv, recv_q, recv_kv, local, gsend, grecv, gsem, esend, erecv, esem):
    near, far, seq = sets
    bits = [near, far] + seq
    stages, least = len(bits), 1 << len(bits)
    me = greet_all(bits, count)
    early = sums_of(early_ref.shape[0], least, sets, early_ref, e_ref, eland_ref, early_out, esend, erecv, esem)
    for part in early:
        part.give()

    holders = held_heads(count)
    first = first_head(me, count)
    started = []
    for k in far_first(count) + [0]:
        peer = lax.rem(me + k, count)
        pairs = [(None, dlogit_ref.at[peer], logit_ref.at[me], recv.at[k])]
        for slot in range(2):
            head = first + slot
            target = proj_ref.at[pl.ds(pl.multiple_of(head * HDIM, HDIM), HDIM)]
            pairs.append((is_mine(me, slot, peer, count), draw_ref.at[peer, 0, slot], target, recv_q.at[head]))
            used = (head * count < HEADS * (me + 1)) & (head * count + count > HEADS * me)
            order = me - holder(head, 0, count)
            pairs.append((used, draw_ref.at[peer, pl.ds(1, 2), slot], part_ref.at[head, order], recv_kv.at[head, order]))
        for i, (mine, src, dst, sem) in enumerate(pairs):
            copy = push(src, dst, send.at[k, i], sem, peer) if k else pltpu.make_async_copy(src, dst, local.at[i])
            started.append((mine, k, copy))
            if mine is None:
                copy.start()
            else:
                pl.when(mine)(copy.start)

    step(early, stages)
    step(early, stages)

    for mine, k, copy in started:
        if mine is not None:
            pl.when(mine)(copy.wait_send if k else copy.wait)
        else:
            copy.wait()
    for head in range(HEADS):
        source = holder(head, me, count)
        copy = push(draw_ref.at[0, 0, 0], proj_ref.at[pl.ds(head * HDIM, HDIM)], send.at[0, 0], recv_q.at[head], lax.rem(me + 1, count))
        pl.when(source != me)(copy.wait_recv)
        for j, (d, s) in enumerate(holders[head]):
            copy = push(draw_ref.at[0, pl.ds(1, 2), 0], part_ref.at[head, j], send.at[0, 0], recv_kv.at[head, j], lax.rem(me + 1, count))
            pl.when(me != d)(copy.wait_recv)

    put_together(holders, part_ref, logit_ref, proj_ref, dsmall_ref)
    proj_ref[3 * D :] = dgate_ref[...]

    late = sums_of(g_ref.shape[0], least, sets, None, g_ref, land_ref, late_out, gsend, grecv, gsem)

    def rest():
        late_rest(h_ref, proj_ref, w_ref, wsmall_ref, x_ref, gain_ref, dresid_ref, extra_ref, dsmall_ref, rows_ref, small_ref, dx_ref, g_ref)

    give_late(late, functools.partial(late_weights, h_ref, proj_ref, g_ref), rest, early, stages)
    finish_late(late, early, 2 * stages - 3, stages, Doubling(bits, small_ref, small_land, ssend, srecv), small_out)


def last(count, sets, d_raw, d_logits, early, h, d_gate, w_attn, w_small, x, gain, d_resid, extra):
    stages = 2 + len(sets[2])
    units = padded(9 * (D // UNIT) + 9, 1 << stages)
    rows = h.shape[0]
    most = max(len(held) for held in held_heads(count))
    vmem = pl.BlockSpec(memory_space=pltpu.VMEM)
    dma = pltpu.SemaphoreType.DMA
    shape = (UNIT, 256)
    return pl.pallas_call(
        functools.partial(last_kernel, count, sets),
        out_shape=[
            jax.ShapeDtypeStruct((units,) + shape, bf16),
            jax.ShapeDtypeStruct(early.shape, bf16),
            jax.ShapeDtypeStruct((rows, D), f32),
            jax.ShapeDtypeStruct((8, D), f32),
        ],
        in_specs=[ANY] * 3 + [vmem] * 8,
        out_specs=[ANY, ANY, vmem, vmem],
        scratch_shapes=[
            pltpu.VMEM((4 * D, rows), bf16),
            pltpu.VMEM((count, 2, 8, rows), f32),
            pltpu.VMEM((HEADS, most, 2, HDIM, rows), bf16),
            pltpu.VMEM((8 * HEADS, rows), f32),
            pltpu.VMEM((SMALL, D), f32),
            pltpu.VMEM((8, D), f32),
            pltpu.VMEM((stages, 8, D), f32),
            dma((stages,)), dma((stages,)),
            pltpu.VMEM((units,) + shape, bf16),
            pltpu.VMEM((units,) + shape, bf16),
            pltpu.VMEM((early.shape[0] // 2,) + shape, bf16),
            pltpu.VMEM(early.shape, bf16),
            dma((count, 5)), dma((count,)), dma((HEADS,)), dma((HEADS, most)), dma((5,)),
            dma((PARTS, 2 * stages)), dma((PARTS, 2 * stages)), dma((PARTS,)),
            dma((PARTS, 2 * stages)), dma((PARTS, 2 * stages)), dma((PARTS,)),
        ],
        compiler_params=pltpu.CompilerParams(collective_id=3, has_side_effects=True, vmem_limit_bytes=62 * 2**20),
        name="last",
    )(d_raw, d_logits, early, h, d_gate, w_attn, w_small, x, gain, d_resid, extra)


def unpack_kernel(parts, *refs):
    o_ref = refs[-1]
    width = refs[0].shape[0] // (o_ref.shape[0] // UNIT)
    at = 0
    for ref, blocks in zip(refs, parts):

        @pl.when((pl.program_id(0) >= at) & (pl.program_id(0) < at + blocks))
        def _(ref=ref):
            for i in range(width):
                size = o_ref.shape[0] // UNIT
                block = ref[size * i : size * i + size].reshape(o_ref.shape[0], 256)
                o_ref[:, 256 * i : 256 * i + 256] = block.astype(f32)

        at += blocks


def unpack(rows, width, *parts):
    size = rows // UNIT
    specs, at = [], 0
    for _, first, blocks in parts:
        first, blocks = first // width, blocks // width
        index = lambda i, at=at, first=first, blocks=blocks: (first + jnp.clip(i - at, 0, blocks - 1), 0, 0)
        specs.append(pl.BlockSpec((size * width, UNIT, 256), index))
        at += blocks
    return pl.pallas_call(
        functools.partial(unpack_kernel, [blocks // width for _, _, blocks in parts]),
        grid=(at,),
        in_specs=specs,
        out_specs=pl.BlockSpec((rows, 256 * width), lambda i: (0, i)),
        out_shape=jax.ShapeDtypeStruct((rows, 256 * at * width), f32),
        compiler_params=pltpu.CompilerParams(vmem_limit_bytes=62 * 2**20),
        name="unpack",
    )(*[units for units, _, _ in parts])


def back_kernel(count, sets, skip_ref, bias_ref, dmixed_ref, logits_ref, wsmall_ref, gain_ref, extra_ref,
                raw_in, full_in, q_in, k_in, kt_in, vt_in, early_ref, h_in, dgate_in, w_in, x_in, dresid_in,
                late_out, early_out, dx_ref, small_out,
                raw_ref, full_ref, q_ref, k_ref, kt_ref, vt_ref, do_ref, v_ref, cum_ref, dq_ref, dk_ref, dv_ref,
                dlogit_ref, gsum_ref, gains_ref,
                proj_ref, logit_ref, part_ref, dsmall_ref, rows_ref, small_ref, small_land, ssend, srecv, h_ref, w_ref, x_ref, dresid_ref,
                g_ref, land_ref, e_ref, eland_ref,
                load, send, recv, recv_q, recv_kv, own, gsend, grecv, gsem, esend, erecv, esem):
    near, far, seq = sets
    bits = [near, far] + seq
    stages, least = len(bits), 1 << len(bits)
    blocks = 2 * count
    draw_ref = raw_ref
    sums = (dq_ref, dk_ref, dv_ref)

    def state(slot):
        pairs = ((full_in, full_ref), (q_in, q_ref), (k_in, k_ref), (kt_in, kt_ref), (vt_in, vt_ref))
        return [pltpu.make_async_copy(src.at[slot], dst, load.at[i]) for i, (src, dst) in enumerate(pairs)]

    other = [
        pltpu.make_async_copy(src, dst, load.at[5 + i])
        for i, (src, dst) in enumerate((
            (raw_in, raw_ref), (h_in, h_ref), (dgate_in, proj_ref.at[pl.ds(3 * D, D)]), (w_in, w_ref), (x_in, x_ref), (dresid_in, dresid_ref)))
    ]
    me = lax.axis_index("seq")
    for copy in state(slot_at(me, 0, count)) + other:
        copy.start()
    greet_all(bits, count)
    first = first_head(me, count)
    holders = held_heads(count)
    early = sums_of(early_ref.shape[0], least, sets, early_ref, e_ref, eland_ref, early_out, esend, erecv, esem)
    for part in early:
        part.give()
    gsum_ref[...] = jnp.zeros(gsum_ref.shape, f32)
    gains_ref[...] = gain_ref[...].T

    def sends(slot, k):
        peer = lax.rem(me + k, count)
        head = first + slot
        order = me - holder(head, 0, count)
        used = (head * count < HEADS * (me + 1)) & (head * count + count > HEADS * me)
        target = proj_ref.at[pl.ds(pl.multiple_of(head * HDIM, HDIM), HDIM)]
        items = [
            (None, dlogit_ref.at[peer, slot], logit_ref.at[me, slot], recv.at[k, slot]),
            (is_mine(me, slot, peer, count), draw_ref.at[peer, 0, slot], target, recv_q.at[head]),
            (used, draw_ref.at[peer, pl.ds(1, 2), slot], part_ref.at[head, order], recv_kv.at[head, order]),
        ]
        return [
            (mine, push(src, dst, send.at[k, slot, i], sem, peer) if k else pltpu.make_async_copy(src, dst, own.at[slot, i]))
            for i, (mine, src, dst, sem) in enumerate(items)
        ]

    for phase in range(2):
        slot = slot_at(me, phase, count)
        for copy in state(slot):
            copy.wait()

        def prepare(block, carried):
            prepare_back(count, block, dmixed_ref.at[:, slot], full_ref, vt_ref, do_ref, v_ref, *sums)
            return carried

        lax.fori_loop(0, blocks, prepare, 0)
        step(early, stages)

        def one_place(place, carried):
            for i in range(blocks // UNROLL_BACK):
                pairs = pairs_of_place(place, i, UNROLL_BACK, count)
                masks = [keep_factor(skip_ref, row, column) for row, column in pairs]
                if (i + 1) * UNROLL_BACK == blocks:
                    pairs.append((place, place))
                    masks[-1:] = [True, True]
                batch_back(pairs, masks, q_ref, k_ref, kt_ref, v_ref, do_ref, *sums)
            return carried

        low, high = own_places(me, slot, count)
        middle = (low + high) // 2
        if phase == 0:
            lax.fori_loop(low, high, one_place, 0)
        else:
            lax.fori_loop(low, middle, one_place, 0)
            step(early, stages)
            lax.fori_loop(middle, high, one_place, 0)
        step(early, stages)
        if phase == 0:
            for copy in state(slot_at(me, 1, count)):
                copy.start()
            other[0].wait()
        raws, logits = raw_ref.at[:, :, slot], logits_ref.at[:, slot]
        gains = gains_ref.at[pl.ds(pl.multiple_of((first + slot) * HDIM, HDIM), HDIM)]
        draws, dlogits = draw_ref.at[:, :, slot], dlogit_ref.at[:, slot]

        def finish(number, carried):
            block = blocks - 1 - number
            mine = is_mine(me, slot, place_of(block, count), count)
            return finish_back(count, block, carried, mine, raws, logits, gains, *sums, draws, dlogits, cum_ref)

        zero = jnp.zeros((HDIM, BLK), f32)
        _, _, sum_q, sum_k = lax.fori_loop(0, blocks, finish, (zero, zero, zero, zero))
        lane = lax.broadcasted_iota(jnp.int32, (HDIM, D), 1)
        channel = lax.broadcasted_iota(jnp.int32, (HDIM, D), 0)
        here = lane == channel + (first + slot) * HDIM
        for i, column in enumerate((sum_q, sum_k)):
            placed = jnp.where(here, jnp.sum(column, 1, keepdims=True), 0.0)
            gsum_ref[i : i + 1] += jnp.sum(placed, 0, keepdims=True)
        forget_back(count, bias_ref[first + slot], logits, cum_ref, dlogits)
        for k in far_first(count) + [0]:
            for mine, copy in sends(slot, k):
                if mine is None:
                    copy.start()
                else:
                    pl.when(mine)(copy.start)
        step(early, stages)

    for _ in range(LATER):
        step(early, stages)
    for copy in other[1:]:
        copy.wait()
    for slot in range(2):
        for k in far_first(count) + [0]:
            for mine, copy in sends(slot, k):
                if mine is None:
                    copy.wait()
                else:
                    pl.when(mine)(copy.wait_send if k else copy.wait)
    for head in range(HEADS):
        source = holder(head, me, count)
        next_one = lax.rem(me + 1, count)
        copy = push(draw_ref.at[0, 0, 0], proj_ref.at[pl.ds(head * HDIM, HDIM)], send.at[0, 0, 0], recv_q.at[head], next_one)
        pl.when(source != me)(copy.wait_recv)
        for j, (d, s) in enumerate(holders[head]):
            copy = push(draw_ref.at[0, pl.ds(1, 2), 0], part_ref.at[head, j], send.at[0, 0, 0], recv_kv.at[head, j], next_one)
            pl.when(me != d)(copy.wait_recv)

    put_together(holders, part_ref, logit_ref, proj_ref, dsmall_ref)
    late = sums_of(g_ref.shape[0], least, sets, None, g_ref, land_ref, late_out, gsend, grecv, gsem)

    def rest():
        late_rest(h_ref, proj_ref, w_ref, wsmall_ref, x_ref, gain_ref, dresid_ref, extra_ref, dsmall_ref, rows_ref, small_ref, dx_ref, g_ref, gsum_ref)

    give_late(late, functools.partial(late_weights, h_ref, proj_ref, g_ref), rest, early, stages)
    finish_late(late, early, 2 * stages - 8 - LATER, stages, Doubling(bits, small_ref, small_land, ssend, srecv), small_out)


LATER = 1


def back(count, sets, skip, bias, d_mixed, logits, w_small, gains, extra, raw, full, q, k, kt, vt, early, h, d_gate, w_attn, x, d_resid):
    stages = 2 + len(sets[2])
    units = padded(9 * (D // UNIT) + 9, 1 << stages)
    rows = h.shape[0]
    blocks = 2 * count
    most = max(len(held) for held in held_heads(count))
    vmem = pl.BlockSpec(memory_space=pltpu.VMEM)
    smem = pl.BlockSpec(memory_space=pltpu.SMEM)
    dma = pltpu.SemaphoreType.DMA
    shape = (UNIT, 256)
    held = lambda array: pltpu.VMEM(array.shape[1:], array.dtype)
    return pl.pallas_call(
        functools.partial(back_kernel, count, sets),
        out_shape=[
            jax.ShapeDtypeStruct((units,) + shape, bf16),
            jax.ShapeDtypeStruct(early.shape, bf16),
            jax.ShapeDtypeStruct((rows, D), f32),
            jax.ShapeDtypeStruct((8, D), f32),
        ],
        in_specs=[smem, smem] + [vmem] * 5 + [ANY] * 12,
        out_specs=[ANY, ANY, vmem, vmem],
        scratch_shapes=[
            pltpu.VMEM(raw.shape, bf16), held(full), held(q), held(k), held(kt), held(vt),
            pltpu.VMEM((blocks + 1, 128, BLK), bf16),
            pltpu.VMEM((blocks, BLK, 128), bf16),
            pltpu.VMEM((count, rows), f32),
            pltpu.VMEM((blocks + 1, 80, BLK), f32),
            pltpu.VMEM((blocks, 80, BLK), f32),
            pltpu.VMEM((blocks, HDIM, BLK), f32),
            pltpu.VMEM(logits.shape, f32),
            pltpu.VMEM((8, D), f32),
            pltpu.VMEM((D, 8), f32),
            pltpu.VMEM((4 * D, rows), bf16),
            pltpu.VMEM((count, 2, 8, rows), f32),
            pltpu.VMEM((HEADS, most, 2, HDIM, rows), bf16),
            pltpu.VMEM((8 * HEADS, rows), f32),
            pltpu.VMEM((SMALL, D), f32),
            pltpu.VMEM((8, D), f32),
            pltpu.VMEM((stages, 8, D), f32),
            dma((stages,)), dma((stages,)),
            pltpu.VMEM(h.shape, bf16),
            pltpu.VMEM(w_attn.shape, bf16),
            pltpu.VMEM(x.shape, bf16),
            pltpu.VMEM(d_resid.shape, f32),
            pltpu.VMEM((units,) + shape, bf16),
            pltpu.VMEM((units,) + shape, bf16),
            pltpu.VMEM((early.shape[0] // 2,) + shape, bf16),
            pltpu.VMEM(early.shape, bf16),
            dma((11,)), dma((count, 2, 3)), dma((count, 2)), dma((HEADS,)), dma((HEADS, most)), dma((2, 3)),
            dma((PARTS, 2 * stages)), dma((PARTS, 2 * stages)), dma((PARTS,)),
            dma((PARTS, 2 * stages)), dma((PARTS, 2 * stages)), dma((PARTS,)),
        ],
        compiler_params=pltpu.CompilerParams(collective_id=4, has_side_effects=True, vmem_limit_bytes=63 * 2**20),
        name="back",
    )(skip, bias, d_mixed, logits, w_small, gains, extra, raw, full, q, k, kt, vt, early, h, d_gate, w_attn, x, d_resid)


def rms_scale(values, gains):
    inverse = lax.rsqrt(jnp.mean(values * values, axis=-1, keepdims=True) + EPS)
    return values * inverse * gains


def swiglu(gate_up):
    return jax.nn.silu(gate_up[:, :FF]) * gate_up[:, FF:]


def local(tokens, cotangent, skip_table, gain_attn, w_attn, w_heads, forget_bias, query_gain, key_gain,
          w_out, gain_ffn, w_gate_up, w_down):
    count = lax.axis_size("seq")
    me = lax.axis_index("seq")
    rows = tokens.shape[1]
    both = ("seq", "group")
    inputs = tokens[0].astype(f32)
    device = me.astype(jnp.int32)[None]
    head = first_head(me, count)
    skip = skip_table[0]
    all_gains = jnp.concatenate([jnp.stack([gain_attn, query_gain, key_gain]), jnp.zeros((5, D), f32)], 0)
    if count <= 8:
        h_first, gate_logit, attended, raw, logits, mixed, q, k, kt, vt = front(
            count, skip, forget_bias, tokens[0], w_attn, w_heads, all_gains
        )
    else:
        gains = lax.dynamic_slice_in_dim(all_gains.T.reshape(HEADS, HDIM, 8), head, 2, 0)
        bias = lax.dynamic_slice_in_dim(forget_bias, head, 2, 0)
        w_small = jnp.pad(w_heads.reshape(D, 3, HEADS).transpose(0, 2, 1), ((0, 0), (0, 0), (0, 5))).reshape(D, HEADS * 8)
        h_first = rms_scale(inputs, gain_attn).astype(bf16)
        qkv = dot(w_attn[:, : 3 * D], h_first, 0, 1).astype(bf16).reshape(3, HEADS, HDIM, rows)
        gate_logit = dot(w_attn[:, 3 * D :], h_first, 0, 1)
        logits_here = dot(w_small, h_first, 0, 1).reshape(HEADS, 8, rows)
        raw, logits = heads_out(qkv, logits_here, count)
        mixed_low, mixed, q, k, kt, vt = attend_forward(device, skip, bias, raw, logits, gains)
        attended = mixed_back(mixed_low, count).reshape(D, rows)
    attended = attended.astype(f32)

    gate_open = jax.nn.sigmoid(gate_logit)
    gated = (gate_open * attended).astype(bf16)
    resid = inputs + dot(gated, w_out, 0, 0)
    normed_ffn, norm_back_ffn = jax.vjp(rms_scale, resid, gain_ffn)
    h_second = normed_ffn.astype(bf16)
    gate_up = dot(h_second, w_gate_up, 1, 0)
    hidden, hidden_back = jax.vjp(swiglu, gate_up)
    hidden_low = hidden.astype(bf16)
    output = resid + dot(hidden_low, w_down, 1, 0)
    d_low = cotangent[0]
    d_output = d_low.astype(f32)
    (d_gate_up,) = hidden_back(dot(d_low, w_down, 1, 1))
    d_gate_low = d_gate_up.astype(bf16)
    d_resid_norm, grad_gain_ffn = norm_back_ffn(dot(d_gate_low, w_gate_up, 1, 1))
    d_resid = d_output + d_resid_norm
    d_branch = d_resid.astype(bf16)
    d_gated = dot(w_out, d_branch, 1, 1)
    d_gate_logit = (d_gated * attended * gate_open * (1.0 - gate_open)).astype(bf16)
    d_mixed = (d_gated * gate_open).astype(bf16).reshape(HEADS, HDIM, rows)

    near_far, seq_bits = group_bits(lax.axis_size("group"), count)
    sets = (near_far[0], near_far[1], seq_bits)
    units = padded(1440, 1 << (2 + len(seq_bits)))
    d_mixed_all, early = grads_out(
        count, units, d_mixed, h_first, d_gate_logit, h_second, d_gate_low, hidden_low, d_low, gated, d_branch
    )
    zeros = lambda n: jnp.zeros((n, D), f32)
    if count <= 8:
        extra = jnp.concatenate([zeros(1), grad_gain_ffn[None], zeros(6)], 0)
        late, early, d_inputs, small = back(
            count, sets, skip, forget_bias, d_mixed_all, logits, jnp.pad(w_heads, ((0, 0), (0, SMALL - 3 * HEADS))), all_gains, extra,
            raw, mixed, q, k, kt, vt, early, h_first, d_gate_logit, w_attn, tokens[0], d_resid,
        )
    else:
        d_raw, d_logits, d_gains = attend_backward(device, skip, bias, raw, logits, gains, d_mixed_all, mixed, q, k, kt, vt)
        placed = lax.dynamic_update_slice(jnp.zeros((HEADS, HDIM, 2), f32), d_gains[..., 1:3], (head, 0, 0)).reshape(D, 2).T
        extra = jnp.concatenate([zeros(1), grad_gain_ffn[None], placed, zeros(4)], 0)
        late, early, d_inputs, small = last(
            count, sets, d_raw, d_logits, early, h_first, d_gate_logit, w_attn,
            jnp.pad(w_heads, ((0, 0), (0, SMALL - 3 * HEADS))), tokens[0], gain_attn[None], d_resid, extra
        )
    row = 3 * HEADS
    used = 9 * (D // UNIT)
    heads_rows = late[used : used + 9].reshape(3, SMALL, 256).transpose(1, 0, 2).reshape(SMALL, D).astype(f32)
    return (
        output[None].astype(bf16),
        d_inputs[None],
        small[0],
        unpack(D, 3, (late, 0, 9), (early, 27, 3)),
        heads_rows[:row].T,
        small[4, :HEADS],
        small[2],
        small[3],
        unpack(D, 1, (early, 24, 3)),
        small[1],
        unpack(D, 2, (early, 0, 16)),
        unpack(FF, 1, (early, 6, 3)),
    )


def solution(mesh):
    rows = P("group", "seq", None)
    return jax.shard_map(
        local,
        mesh=mesh,
        in_specs=(rows, rows, P("group", None, None)) + (P(),) * 10,
        out_specs=(rows, rows) + (P(),) * 10,
        check_vma=False,
    )
```
